32 devices in a mesh: grp: 2 (over x), row: 16 (over z, y, core).
Axes of the slice: x: 2, y: 2, z: 4, core: 2. Of those that a mesh axis runs over, the one named last changes fastest.
Arguments:
- q_latent: bfloat16 [128, 1536], P(('grp', 'row')), parts along dimension 0, may hold values from -96 to 96
- new_latent: bfloat16 [128, 576], P(('grp', 'row')), parts along dimension 0, may hold values from -18 to 18
- cache: bfloat16 [128, 1536, 576], P(('grp', 'row')), parts along dimension 0, may hold values from -6 to 6
- lengths: int32 [128], P(('grp', 'row')), parts along dimension 0, may hold values from 128 to 1536, as said below
- w_uq: bfloat16 [1536, 24576], P(None, 'row'), may hold values from -0.15625 to 0.15625
- w_uk: bfloat16 [128, 128, 512], P('row'), may hold values from -0.5 to 0.5
- w_uv: bfloat16 [128, 512, 128], P('row'), may hold values from -0.25 to 0.25
- w_o: bfloat16 [16384, 7168], P('row'), may hold values from -0.046875 to 0.046875
Outputs:
- attended: bfloat16 [128, 7168], P(('grp', 'row')), parts along dimension 0
The draws below stay inside these ranges and needn't reach their ends.
There are 2 independent parts, one for each index of `grp`. The reference program is written for one: setup_inputs(seed, part) draws one part's arguments, and reference() takes and returns one part's arrays. A program takes and returns all parts, laid end to end along the dimension named above; an argument that names none is the same for every part. Nothing has to cross between parts.
Inputs may be any that keep to these rules, and one draw needn't show every extreme that they name: `lengths`: each is a multiple of 128.
All inputs are finite; a program needn't handle non-finite values.
Results may differ from the reference program's by a relative error of at most 0.013.
The reference program's roundings to bfloat16 on the way (of `projected`, `absorbed`, `rotated`, `query`, `weights`, `latent_out` and `values`) count: a program that leaves them out, or rounds other values in their place, can miss the bound.
Values may be sent and summed in bfloat16 or wider, within the bound.
No kernel may reach another device: no remote copies, remote signals or barrier semaphores. Data moves between devices by JAX's collectives and lax.ppermute only.
A program may use at most 128 MiB of HBM per device.

```python
import math
import jax
import jax.numpy as jnp
from jax import lax

D = 7168
H = 128
QL = 1536
LAT = 512
ROPE = 64
NOPE = 128
VD = 128
MAXLEN = 1536
UNIT = 128
ROWS = 64


def draw_lengths(key, part):
    key = jax.random.fold_in(key, 11)
    key_counts, key_chosen = jax.random.split(key)
    block_count = MAXLEN // UNIT
    counts = jax.random.randint(key_counts, (ROWS,), 1, block_count + 1)
    chosen = jax.random.randint(key_chosen, (), 0, ROWS)
    counts = jnp.where(jnp.arange(ROWS) == chosen, block_count, counts)
    return (counts * UNIT).astype(jnp.int32)


def draw_q_latent(key, part):
    key = jax.random.fold_in(key, 5)
    key_values = jax.random.fold_in(key, 0)
    drawn = jnp.clip(jax.random.normal(key_values, (ROWS, QL), jnp.float32), -6.0, 6.0)
    return drawn.astype(jnp.bfloat16)


def level_of(own_key, extent, pieces, smallest, largest):
    def one(axis_at, blocks):
        heights = jax.random.uniform(jax.random.fold_in(jax.random.fold_in(own_key, 6), axis_at), (blocks,), jnp.float32, smallest / len(pieces), largest / len(pieces))
        return jnp.repeat(jnp.exp(heights), extent[axis_at] // blocks).reshape((-1,) + (1,) * (len(extent) - axis_at - 1))

    gain = one(*pieces[0])
    for cut in pieces[1:]:
        gain = gain * one(*cut)
    return gain


def gaussian(stream_key, dims, scale, reach, cuts=(), kind=jnp.bfloat16):
    factor_of = level_of(stream_key, dims, cuts, -0.22, 0.18) if cuts else 1.0
    entries = jax.random.normal(stream_key, dims, jnp.float32) * scale * factor_of
    return jnp.minimum(jnp.maximum(entries, -reach), reach).astype(kind)


def setup_inputs(seed: int = 0, part: int = 0) -> dict:
    streams_of = jax.random.split(jax.random.key(seed), 9)
    part_keys = jax.random.split(jax.random.fold_in(streams_of[8], part), 9)
    q_latent = draw_q_latent(jax.random.fold_in(jax.random.fold_in(streams_of[8], part), 71), part)
    new_latent = gaussian(part_keys[1], (ROWS, LAT + ROPE), 3.0, 18.0, ((0, 16),))
    cache = gaussian(part_keys[2], (ROWS, MAXLEN, LAT + ROPE), 1.0, 6.0, ((0, 16),))
    lengths = draw_lengths(jax.random.fold_in(jax.random.fold_in(streams_of[8], part), 71), part)
    w_uq = gaussian(streams_of[4], (QL, H * (NOPE + ROPE)), QL ** -0.5, 0.15625, ((1, 16),))
    w_uk = gaussian(streams_of[5], (H, NOPE, LAT), NOPE ** -0.5, 0.5, ((0, 16),))
    w_uv = gaussian(streams_of[6], (H, LAT, VD), LAT ** -0.5, 0.25, ((0, 16),))
    w_o = gaussian(streams_of[7], (H * VD, D), (H * VD) ** -0.5, 0.046875, ((0, 16),))
    return dict(q_latent=q_latent, new_latent=new_latent, cache=cache, lengths=lengths, w_uq=w_uq, w_uk=w_uk, w_uv=w_uv, w_o=w_o)


def rotate(pe_part, lengths):
    half = pe_part.shape[-1] // 2
    steps = jnp.arange(half, dtype=jnp.float32)
    frequency = jnp.exp(steps * (-math.log(10000.0) / half))
    angles = lengths.astype(jnp.float32)[:, None] * frequency[None, :]
    cosine = jnp.cos(angles)[:, None, :]
    sine_part = jnp.sin(angles)[:, None, :]
    values_in = pe_part.astype(jnp.float32)
    first_half = values_in[..., :half]
    second_half = values_in[..., half:]
    joined = jnp.concatenate([first_half * cosine - second_half * sine_part, second_half * cosine + first_half * sine_part], axis=-1)
    return joined.astype(jnp.bfloat16)


def attend_row(packed):
    query, row_cache, newest, length = packed
    factor = (NOPE + ROPE) ** -0.5
    scores = jnp.einsum('hc,tc->ht', query.astype(jnp.float32), row_cache.astype(jnp.float32)) * factor
    position = jnp.arange(MAXLEN)
    scores = jnp.where(position[None, :] < length, scores, -jnp.inf)
    own = jnp.einsum('hc,c->h', query.astype(jnp.float32), newest.astype(jnp.float32)) * factor
    peak = jnp.maximum(jnp.max(scores, axis=-1), own)
    expo = jnp.exp(scores - peak[:, None])
    own_expo = jnp.exp(own - peak)
    total = jnp.sum(expo, axis=-1) + own_expo
    weights = (expo / total[:, None]).astype(jnp.bfloat16)
    own_weight = (own_expo / total).astype(jnp.bfloat16)
    summed = jnp.einsum('ht,tc->hc', weights.astype(jnp.float32), row_cache[:, :LAT].astype(jnp.float32))
    summed = summed + own_weight.astype(jnp.float32)[:, None] * newest[None, :LAT].astype(jnp.float32)
    return summed.astype(jnp.bfloat16)


def reference(q_latent, new_latent, cache, lengths, w_uq, w_uk, w_uv, w_o):
    projected = jnp.dot(q_latent, w_uq, preferred_element_type=jnp.float32).astype(jnp.bfloat16)
    projected = projected.reshape(ROWS, H, NOPE + ROPE)
    absorbed = jnp.einsum('rhn,hnc->rhc', projected[..., :NOPE].astype(jnp.float32), w_uk.astype(jnp.float32)).astype(jnp.bfloat16)
    rotated = rotate(projected[..., NOPE:], lengths)
    query = jnp.concatenate([absorbed, rotated], axis=-1)
    latent_out = lax.map(attend_row, (query, cache, new_latent, lengths))
    values = jnp.einsum('rhc,hcv->rhv', latent_out.astype(jnp.float32), w_uv.astype(jnp.float32)).astype(jnp.bfloat16)
    values = values.reshape(ROWS, H * VD)
    return jnp.dot(values, w_o, preferred_element_type=jnp.float32).astype(jnp.bfloat16)
```

```python
import functools
import math

import jax
import jax.numpy as jnp
from jax import lax
from jax.experimental import pallas as pl
from jax.experimental.pallas import tpu as pltpu
from jax.sharding import PartitionSpec as P

LAT = 512
ROPE = 64
NOPE = 128
VD = 128
LANES = 128
FACTOR = (NOPE + ROPE) ** -0.5


def resident(x):
    return pltpu.with_memory_space_constraint(x, pltpu.VMEM)


def in_vmem():
    return pl.BlockSpec(memory_space=pltpu.VMEM)


def project_kernel(q_ref, wq_ref, wk_ref, out_ref, lat_ref, rot_ref):
    heads = wk_ref.shape[0]
    devices = out_ref.shape[0]
    count = q_ref.shape[0]
    rows = count // devices
    wide = rows * heads
    width = NOPE + ROPE
    projected = jnp.dot(q_ref[...], wq_ref[...], preferred_element_type=jnp.float32)
    for h in range(heads):
        mine = projected[:, h * width : (h + 1) * width]
        absorbed = jnp.dot(
            mine[:, :NOPE].astype(jnp.bfloat16), wk_ref[h], preferred_element_type=jnp.float32
        )
        for c in range(LAT // LANES):
            lat_ref[c, pl.ds(h, count, stride=heads), :] = absorbed[:, c * LANES : (c + 1) * LANES]
        pe = mine[:, NOPE:]
        rot_ref[pl.ds(h, count, stride=heads), :] = jnp.concatenate([pe, pe], axis=-1)
    for c in range(LAT // LANES):
        piece = lat_ref[c].reshape(devices, wide, LANES)
        out_ref[:, c * wide : (c + 1) * wide, :] = piece.astype(jnp.bfloat16)
    pair = rot_ref[...].reshape(devices, wide, LANES)
    lane = lax.broadcasted_iota(jnp.int32, (devices, wide // 2, LANES), 2)
    packed = jnp.where(lane < ROPE, pair[:, : wide // 2], pair[:, wide // 2 :])
    out_ref[:, LAT // LANES * wide :, :] = packed.astype(jnp.bfloat16)


def project(piece, w_uq, w_uk, devices):
    count = piece.shape[0]
    heads = w_uk.shape[0]
    wide = count // devices * heads
    return pl.pallas_call(
        project_kernel,
        out_shape=jax.ShapeDtypeStruct((devices, LAT // LANES * wide + wide // 2, LANES), jnp.bfloat16),
        in_specs=[in_vmem()] * 3,
        out_specs=in_vmem(),
        scratch_shapes=[
            pltpu.VMEM((LAT // LANES, count * heads, LANES), jnp.float32),
            pltpu.VMEM((count * heads, LANES), jnp.float32),
        ],
        compiler_params=pltpu.CompilerParams(vmem_limit_bytes=16 * 2**20),
        name="project",
    )(piece, resident(w_uq), resident(w_uk))


def attend_kernel(len_ref, q_ref, key_ref, new_ref, cos_ref, sin_ref, out_ref):
    devices = q_ref.shape[0]
    rows, _, maxlen = key_ref.shape
    wide = out_ref.shape[1]
    heads = wide // rows
    total_heads = devices * heads
    half = ROPE // 2
    pieces = LAT // LANES
    for r in range(rows):
        parts = []
        for c in range(pieces):
            first = c * wide + r * heads
            part = q_ref[:, first : first + heads, :].astype(jnp.float32)
            parts.append(part.reshape(total_heads, LANES))
        latent = jnp.concatenate(parts, axis=-1)
        first = pieces * wide + (r % (rows // 2)) * heads
        pe = q_ref[:, first : first + heads, :].astype(jnp.float32).reshape(total_heads, LANES)
        side = r // (rows // 2) * ROPE
        pe = pe[:, side : side + ROPE]
        swapped = jnp.concatenate([pe[:, half:], pe[:, :half]], axis=-1)
        rotated = (pe * cos_ref[r : r + 1, :] + swapped * sin_ref[r : r + 1, :]).astype(jnp.bfloat16)
        newest = new_ref[r : r + 1, :].astype(jnp.float32)
        own = (
            jnp.sum(latent * newest[:, :LAT], axis=-1, keepdims=True)
            + jnp.sum(rotated.astype(jnp.float32) * newest[:, LAT:], axis=-1, keepdims=True)
        ) * FACTOR
        scores = jnp.dot(
            latent.astype(jnp.bfloat16), key_ref[r, :LAT, :], preferred_element_type=jnp.float32
        )
        scores += jnp.dot(rotated, key_ref[r, LAT:, :], preferred_element_type=jnp.float32)
        position = lax.broadcasted_iota(jnp.int32, (1, maxlen), 1)
        scores = jnp.where(position < len_ref[r], scores * FACTOR, -jnp.inf)
        peak = jnp.maximum(jnp.max(scores, axis=-1, keepdims=True), own)
        expo = jnp.exp(scores - peak)
        own_expo = jnp.exp(own - peak)
        total = jnp.sum(expo, axis=-1, keepdims=True) + own_expo
        weights = (expo / total).astype(jnp.bfloat16)
        own_weight = (own_expo / total).astype(jnp.bfloat16).astype(jnp.float32)
        summed = lax.dot_general(
            weights,
            key_ref[r, :LAT, :],
            (((1,), (1,)), ((), ())),
            preferred_element_type=jnp.float32,
        )
        summed += own_weight * newest[:, :LAT]
        out_ref[:, r * heads : (r + 1) * heads, :] = summed.reshape(devices, heads, LAT).astype(
            jnp.bfloat16
        )


def attend(lengths, queries, keys, new_latent, cosine, sine, heads):
    devices = queries.shape[0]
    rows = keys.shape[0]
    return pl.pallas_call(
        attend_kernel,
        out_shape=jax.ShapeDtypeStruct((devices, rows * heads, LAT), jnp.bfloat16),
        in_specs=[pl.BlockSpec(memory_space=pltpu.SMEM)] + [in_vmem()] * 5,
        out_specs=in_vmem(),
        compiler_params=pltpu.CompilerParams(vmem_limit_bytes=16 * 2**20),
        name="attend",
    )(lengths, queries, resident(keys), new_latent, cosine, sine)


def output_kernel(core_ref, y_ref, wv_ref, wo_ref, mine_ref, other_ref, rows_ref, val_ref, block):
    heads = wv_ref.shape[0]
    devices, wide, _ = y_ref.shape
    core = core_ref[0]
    half = devices // 2 * wide
    for place in range(devices // 2):
        for side in range(2):
            device = 2 * place + (core if side == 0 else 1 - core)
            first = side * half + place * wide
            received = y_ref[device].astype(jnp.float32)
            for c in range(LAT // LANES):
                rows_ref[c, first : first + wide, :] = received[:, c * LANES : (c + 1) * LANES]
    count = devices * wide // heads
    for h in range(heads):
        chosen = jnp.concatenate(
            [rows_ref[c, pl.ds(h, count, stride=heads), :] for c in range(LAT // LANES)],
            axis=-1,
        )
        val_ref[:, h * VD : (h + 1) * VD] = jnp.dot(
            chosen.astype(jnp.bfloat16), wv_ref[h], preferred_element_type=jnp.float32
        ).astype(jnp.bfloat16)

    def step(index, carry):
        columns = pl.ds(pl.multiple_of(index * block, block), block)
        terms = jnp.dot(val_ref[...], wo_ref[:, columns], preferred_element_type=jnp.float32)
        mine_ref[:, columns] = terms[: count // 2]
        other_ref[:, columns] = terms[count // 2 :].astype(jnp.bfloat16)
        return carry

    lax.fori_loop(0, wo_ref.shape[1] // block, step, 0)


def output_terms(core, received, w_uv, w_o):
    devices, wide, _ = received.shape
    heads = w_uv.shape[0]
    count = devices * wide // heads
    depth = w_o.shape[1]
    return pl.pallas_call(
        functools.partial(output_kernel, block=1024),
        out_shape=(
            jax.ShapeDtypeStruct((count // 2, depth), jnp.float32),
            jax.ShapeDtypeStruct((count // 2, depth), jnp.bfloat16),
        ),
        in_specs=[pl.BlockSpec(memory_space=pltpu.SMEM)] + [in_vmem()] * 3,
        out_specs=(in_vmem(), in_vmem()),
        scratch_shapes=[
            pltpu.VMEM((LAT // LANES, devices * wide, LANES), jnp.float32),
            pltpu.VMEM((count, heads * VD), jnp.bfloat16),
        ],
        compiler_params=pltpu.CompilerParams(vmem_limit_bytes=16 * 2**20),
        name="output_terms",
    )(core, received, resident(w_uv), resident(w_o))


def on_device(q_latent, new_latent, cache, lengths, w_uq, w_uk, w_uv, w_o, devices):
    heads = w_uk.shape[0]
    rows = cache.shape[0]
    me = lax.axis_index("row")
    half = ROPE // 2
    frequency = jnp.exp(jnp.arange(half, dtype=jnp.float32) * (-math.log(10000.0) / half))
    angles = lengths.astype(jnp.float32)[:, None] * frequency[None, :]
    cosine = jnp.cos(angles)
    sine = jnp.sin(angles)
    cosine = jnp.concatenate([cosine, cosine], axis=-1)
    sine = jnp.concatenate([-sine, sine], axis=-1)

    copies = jnp.broadcast_to(q_latent[None], (devices,) + q_latent.shape)
    gathered = lax.all_to_all(copies, "row", split_axis=0, concat_axis=0, tiled=True)
    piece = gathered.reshape(devices * rows, -1)

    queries = project(piece, w_uq, w_uk, devices)
    queries = lax.all_to_all(queries, "row", split_axis=0, concat_axis=0, tiled=True)
    keys = jnp.swapaxes(cache, 1, 2)
    latents = attend(lengths, queries, keys, new_latent, cosine, sine, heads)
    latents = lax.all_to_all(latents, "row", split_axis=0, concat_axis=0, tiled=True)

    core = lax.rem(me, 2).astype(jnp.int32).reshape(1)
    mine, other = output_terms(core, latents, w_uv, w_o)
    partner = [(i, i ^ 1) for i in range(devices)]
    summed = mine + lax.ppermute(other, "row", partner).astype(jnp.float32)
    summed = summed.astype(jnp.bfloat16).reshape(devices // 2, rows, -1)
    groups = [list(range(c, devices, 2)) for c in range(2)]
    shares = lax.all_to_all(
        summed, "row", split_axis=0, concat_axis=0, tiled=True, axis_index_groups=groups
    )
    return jnp.sum(shares.astype(jnp.float32), axis=0).astype(jnp.bfloat16)


def solution(mesh):
    placed = (
        P(("grp", "row"), None),
        P(("grp", "row"), None),
        P(("grp", "row"), None, None),
        P(("grp", "row")),
        P(None, "row"),
        P("row", None, None),
        P("row", None, None),
        P("row", None),
    )
    body = functools.partial(on_device, devices=mesh.shape["row"])
    return jax.shard_map(
        body, mesh=mesh, in_specs=placed, out_specs=P(("grp", "row"), None), check_vma=False
    )
```

```python
import functools
import math

import jax
import jax.numpy as jnp
from jax import lax
from jax.experimental import pallas as pl
from jax.experimental.pallas import tpu as pltpu
from jax.sharding import PartitionSpec as P

LAT = 512
ROPE = 64
NOPE = 128
VD = 128
LANES = 128
PIECES = LAT // LANES
FACTOR = (NOPE + ROPE) ** -0.5
LIMIT = 16 * 2**20


def resident(x):
    return pltpu.with_memory_space_constraint(x, pltpu.VMEM)


def in_vmem():
    return pl.BlockSpec(memory_space=pltpu.VMEM)


def params():
    return pltpu.CompilerParams(vmem_limit_bytes=LIMIT)


def cost(microseconds):
    return pl.CostEstimate(
        flops=int(microseconds * 1.15e9), bytes_accessed=0, transcendentals=0
    )


def project_kernel(devices, *refs):
    q_refs = refs[:devices]
    wq_ref, wk_ref = refs[devices : devices + 2]
    out_refs = refs[devices + 2 : 2 * devices + 2]
    all_ref, lat_ref, rot_ref = refs[2 * devices + 2 :]
    heads = wk_ref.shape[0]
    rows = q_refs[0].shape[0]
    count = devices * rows
    wide = rows * heads
    width = NOPE + ROPE
    for k in range(devices):
        all_ref[k * rows : (k + 1) * rows, :] = q_refs[k][...].astype(jnp.float32)
    projected = jnp.dot(
        all_ref[...].astype(jnp.bfloat16), wq_ref[...], preferred_element_type=jnp.float32
    )
    for h in range(heads):
        mine = projected[:, h * width : (h + 1) * width]
        absorbed = jnp.dot(
            mine[:, :NOPE].astype(jnp.bfloat16), wk_ref[h], preferred_element_type=jnp.float32
        )
        for c in range(PIECES):
            lat_ref[c, pl.ds(h, count, stride=heads), :] = absorbed[:, c * LANES : (c + 1) * LANES]
        pe = mine[:, NOPE:]
        rot_ref[pl.ds(h, count, stride=heads), :] = jnp.concatenate([pe, pe], axis=-1)
    lane = lax.broadcasted_iota(jnp.int32, (wide // 2, LANES), 1)
    for k in range(devices):
        for c in range(PIECES):
            out_refs[k][c * wide : (c + 1) * wide, :] = lat_ref[
                c, k * wide : (k + 1) * wide, :
            ].astype(jnp.bfloat16)
        low = rot_ref[k * wide : k * wide + wide // 2, :]
        high = rot_ref[k * wide + wide // 2 : (k + 1) * wide, :]
        out_refs[k][PIECES * wide :, :] = jnp.where(lane < ROPE, low, high).astype(jnp.bfloat16)


def project(pieces, w_uq, w_uk):
    devices = len(pieces)
    rows, depth = pieces[0].shape
    heads = w_uk.shape[0]
    wide = rows * heads
    block = jax.ShapeDtypeStruct((PIECES * wide + wide // 2, LANES), jnp.bfloat16)
    return pl.pallas_call(
        functools.partial(project_kernel, devices),
        out_shape=[block] * devices,
        in_specs=[in_vmem()] * (devices + 2),
        out_specs=[in_vmem()] * devices,
        scratch_shapes=[
            pltpu.VMEM((devices * rows, depth), jnp.float32),
            pltpu.VMEM((PIECES, devices * wide, LANES), jnp.float32),
            pltpu.VMEM((devices * wide, LANES), jnp.float32),
        ],
        compiler_params=params(),
        cost_estimate=cost(20),
        name="project",
    )(*pieces, resident(w_uq), resident(w_uk))


def attend_kernel(devices, len_ref, *refs):
    q_refs = refs[:devices]
    key_ref, new_ref = refs[devices : devices + 2]
    out_refs = refs[devices + 2 :]
    rows, _, maxlen = key_ref.shape
    wide = out_refs[0].shape[0]
    heads = wide // rows
    half = ROPE // 2

    lane = lax.broadcasted_iota(jnp.int32, (rows, ROPE), 1)
    place = lax.broadcasted_iota(jnp.int32, (rows, ROPE), 0)
    step = jnp.where(lane < half, lane, lane - half).astype(jnp.float32)
    frequency = jnp.exp(step * (-math.log(10000.0) / half))
    length = jnp.zeros((rows, ROPE), jnp.float32)
    for r in range(rows):
        length = jnp.where(place == r, len_ref[r].astype(jnp.float32), length)
    cosine = jnp.cos(length * frequency)
    sine = jnp.sin(length * frequency)
    sine = jnp.where(lane < half, -sine, sine)

    def query_block(first):
        blocks = [ref[first : first + heads, :].astype(jnp.float32) for ref in q_refs]
        return jnp.concatenate(blocks, axis=0)

    for r in range(rows):
        latent = jnp.concatenate(
            [query_block(c * wide + r * heads) for c in range(PIECES)], axis=-1
        )
        pe = query_block(PIECES * wide + (r % (rows // 2)) * heads)
        side = r // (rows // 2) * ROPE
        pe = pe[:, side : side + ROPE]
        swapped = jnp.concatenate([pe[:, half:], pe[:, :half]], axis=-1)
        rotated = (pe * cosine[r : r + 1, :] + swapped * sine[r : r + 1, :]).astype(jnp.bfloat16)
        newest = new_ref[r : r + 1, :].astype(jnp.float32)
        own = (
            jnp.sum(latent * newest[:, :LAT], axis=-1, keepdims=True)
            + jnp.sum(rotated.astype(jnp.float32) * newest[:, LAT:], axis=-1, keepdims=True)
        ) * FACTOR
        scores = jnp.dot(
            latent.astype(jnp.bfloat16), key_ref[r, :LAT, :], preferred_element_type=jnp.float32
        )
        scores += jnp.dot(rotated, key_ref[r, LAT:, :], preferred_element_type=jnp.float32)
        position = lax.broadcasted_iota(jnp.int32, (1, maxlen), 1)
        scores = jnp.where(position < len_ref[r], scores * FACTOR, -jnp.inf)
        peak = jnp.maximum(jnp.max(scores, axis=-1, keepdims=True), own)
        expo = jnp.exp(scores - peak)
        own_expo = jnp.exp(own - peak)
        total = jnp.sum(expo, axis=-1, keepdims=True) + own_expo
        weights = (expo / total).astype(jnp.bfloat16)
        own_weight = (own_expo / total).astype(jnp.bfloat16).astype(jnp.float32)
        summed = lax.dot_general(
            weights,
            key_ref[r, :LAT, :],
            (((1,), (1,)), ((), ())),
            preferred_element_type=jnp.float32,
        )
        summed += own_weight * newest[:, :LAT]
        for k in range(devices):
            out_refs[k][r * heads : (r + 1) * heads, :] = summed[
                k * heads : (k + 1) * heads, :
            ].astype(jnp.bfloat16)


def attend(lengths, queries, keys, new_latent, heads):
    devices = len(queries)
    rows = keys.shape[0]
    block = jax.ShapeDtypeStruct((rows * heads, LAT), jnp.bfloat16)
    return pl.pallas_call(
        functools.partial(attend_kernel, devices),
        out_shape=[block] * devices,
        in_specs=[pl.BlockSpec(memory_space=pltpu.SMEM)] + [in_vmem()] * (devices + 2),
        out_specs=[in_vmem()] * devices,
        compiler_params=params(),
        cost_estimate=cost(20),
        name="attend",
    )(lengths, *queries, resident(keys), new_latent)


def output_kernel(devices, block, *refs):
    y_refs = refs[:devices]
    wv_ref, wo_ref, mine_ref, other_ref, rows_ref, val_ref = refs[devices:]
    heads = wv_ref.shape[0]
    wide = y_refs[0].shape[0]
    for place, k in enumerate([*range(0, devices, 2), *range(1, devices, 2)]):
        received = y_refs[k][...].astype(jnp.float32)
        for c in range(PIECES):
            rows_ref[c, place * wide : (place + 1) * wide, :] = received[:, c * LANES : (c + 1) * LANES]
    count = devices * wide // heads
    for h in range(heads):
        chosen = jnp.concatenate(
            [rows_ref[c, pl.ds(h, count, stride=heads), :] for c in range(PIECES)], axis=-1
        )
        val_ref[:, h * VD : (h + 1) * VD] = jnp.dot(
            chosen.astype(jnp.bfloat16), wv_ref[h], preferred_element_type=jnp.float32
        ).astype(jnp.bfloat16)

    def step(index, carry):
        columns = pl.ds(pl.multiple_of(index * block, block), block)
        terms = jnp.dot(val_ref[...], wo_ref[:, columns], preferred_element_type=jnp.float32)
        mine_ref[:, columns] = terms[: count // 2]
        other_ref[:, columns] = terms[count // 2 :].astype(jnp.bfloat16)
        return carry

    lax.fori_loop(0, wo_ref.shape[1] // block, step, 0)


def output_terms(received, w_uv, w_o):
    devices = len(received)
    wide = received[0].shape[0]
    heads = w_uv.shape[0]
    count = devices * wide // heads
    depth = w_o.shape[1]
    return pl.pallas_call(
        functools.partial(output_kernel, devices, 1024),
        out_shape=(
            jax.ShapeDtypeStruct((count // 2, depth), jnp.float32),
            jax.ShapeDtypeStruct((count // 2, depth), jnp.bfloat16),
        ),
        in_specs=[in_vmem()] * (devices + 2),
        out_specs=(in_vmem(), in_vmem()),
        scratch_shapes=[
            pltpu.VMEM((PIECES, devices * wide, LANES), jnp.float32),
            pltpu.VMEM((count, heads * VD), jnp.bfloat16),
        ],
        compiler_params=params(),
        cost_estimate=cost(20),
        name="output_terms",
    )(*received, resident(w_uv), resident(w_o))


def pair_kernel(rows, mine_ref, other_ref, *out_refs):
    total = mine_ref[...] + other_ref[...].astype(jnp.float32)
    for j, out_ref in enumerate(out_refs):
        out_ref[...] = total[j * rows : (j + 1) * rows].astype(out_ref.dtype)


def pair_sum(mine, other, rows):
    count, depth = mine.shape
    shapes = [jax.ShapeDtypeStruct((rows, depth), jnp.float32)]
    shapes += [jax.ShapeDtypeStruct((rows, depth), jnp.bfloat16)] * (count // rows - 1)
    return pl.pallas_call(
        functools.partial(pair_kernel, rows),
        out_shape=shapes,
        in_specs=[in_vmem()] * 2,
        out_specs=[in_vmem()] * len(shapes),
        compiler_params=params(),
        cost_estimate=cost(1),
        name="pair_sum",
    )(mine, other)


def on_device(q_latent, new_latent, cache, lengths, w_uq, w_uk, w_uv, w_o, devices):
    heads = w_uk.shape[0]
    rows = cache.shape[0]
    def swap(block, k):
        if k == 0:
            return block
        return lax.ppermute(block, "row", [(i, i ^ k) for i in range(devices)])

    pieces = [swap(q_latent, k) for k in range(devices)]
    queries = project(pieces, w_uq, w_uk)
    queries = [swap(block, k) for k, block in enumerate(queries)]
    keys = jnp.swapaxes(cache, 1, 2)
    latents = attend(lengths, queries, keys, new_latent, heads)
    latents = [swap(block, k) for k, block in enumerate(latents)]
    mine, other = output_terms(latents, w_uv, w_o)
    shares = pair_sum(mine, swap(other, 1), rows)
    shares = [swap(block, 2 * j).astype(jnp.float32) for j, block in enumerate(shares)]
    return sum(shares[1:], shares[0]).astype(jnp.bfloat16)


def solution(mesh):
    placed = (
        P(("grp", "row"), None),
        P(("grp", "row"), None),
        P(("grp", "row"), None, None),
        P(("grp", "row")),
        P(None, "row"),
        P("row", None, None),
        P("row", None, None),
        P("row", None),
    )
    body = functools.partial(on_device, devices=mesh.shape["row"])
    return jax.shard_map(
        body, mesh=mesh, in_specs=placed, out_specs=P(("grp", "row"), None), check_vma=False
    )
```

```python
import functools
import math

import jax
import jax.numpy as jnp
from jax import lax
from jax.experimental import pallas as pl
from jax.experimental.pallas import tpu as pltpu
from jax.sharding import PartitionSpec as P

LAT = 512
ROPE = 64
NOPE = 128
VD = 128
LANES = 128
PIECES = LAT // LANES
FACTOR = (NOPE + ROPE) ** -0.5
LIMIT = 16 * 2**20
GROUPS = 2


def resident(x):
    return pltpu.with_memory_space_constraint(x, pltpu.VMEM)


def in_vmem():
    return pl.BlockSpec(memory_space=pltpu.VMEM)


def params():
    return pltpu.CompilerParams(vmem_limit_bytes=LIMIT)


def cost(microseconds):
    return pl.CostEstimate(
        flops=int(microseconds * 1.15e9), bytes_accessed=0, transcendentals=0
    )


def join_kernel(*refs):
    *in_refs, out_ref = refs
    out_ref[...] = jnp.concatenate(
        [ref[...].astype(jnp.float32) for ref in in_refs], axis=0
    ).astype(out_ref.dtype)


def join(blocks):
    rows, depth = blocks[0].shape
    return pl.pallas_call(
        join_kernel,
        out_shape=jax.ShapeDtypeStruct((len(blocks) * rows, depth), blocks[0].dtype),
        in_specs=[in_vmem()] * len(blocks),
        out_specs=in_vmem(),
        compiler_params=params(),
        cost_estimate=cost(10),
        name="join",
    )(*blocks)


def gathered_order(devices):
    return [z + y + c for c in range(2) for z in range(0, devices, 4) for y in (0, 2)]


def project_kernel(devices, groups, q_ref, far_ref, wq_ref, wk_ref, *refs):
    out_refs = refs[:groups]
    lat_ref, rot_ref = refs[groups:]
    heads = wk_ref.shape[0]
    count = 2 * q_ref.shape[0]
    rows = count // devices // groups
    wide = rows * heads
    width = NOPE + ROPE
    me = lax.axis_index("row")
    piece = jnp.concatenate([q_ref[...], far_ref[...]], axis=0)
    projected = jnp.dot(piece, wq_ref[...], preferred_element_type=jnp.float32)
    for h in range(heads):
        mine = projected[:, h * width : (h + 1) * width]
        absorbed = jnp.dot(
            mine[:, :NOPE].astype(jnp.bfloat16), wk_ref[h], preferred_element_type=jnp.float32
        )
        for c in range(PIECES):
            lat_ref[c, pl.ds(h, count, stride=heads), :] = absorbed[:, c * LANES : (c + 1) * LANES]
        pe = mine[:, NOPE:]
        rot_ref[pl.ds(h, count, stride=heads), :] = jnp.concatenate([pe, pe], axis=-1)
    lane = lax.broadcasted_iota(jnp.int32, (wide // 2, LANES), 1)
    for place, k in enumerate(gathered_order(devices)):
        owner = jnp.bitwise_xor(me, k)
        for g, out_ref in enumerate(out_refs):
            first = (place * groups + g) * wide
            for c in range(PIECES):
                out_ref[owner, c * wide : (c + 1) * wide, :] = lat_ref[
                    c, first : first + wide, :
                ].astype(jnp.bfloat16)
            low = rot_ref[first : first + wide // 2, :]
            high = rot_ref[first + wide // 2 : first + wide, :]
            out_ref[owner, PIECES * wide :, :] = jnp.where(lane < ROPE, low, high).astype(
                jnp.bfloat16
            )


def project(near, far, w_uq, w_uk, devices, groups):
    heads = w_uk.shape[0]
    count = 2 * near.shape[0]
    wide = count // devices // groups * heads
    block = jax.ShapeDtypeStruct((devices, PIECES * wide + wide // 2, LANES), jnp.bfloat16)
    return pl.pallas_call(
        functools.partial(project_kernel, devices, groups),
        out_shape=[block] * groups,
        in_specs=[in_vmem()] * 4,
        out_specs=[in_vmem()] * groups,
        scratch_shapes=[
            pltpu.VMEM((PIECES, count * heads, LANES), jnp.float32),
            pltpu.VMEM((count * heads, LANES), jnp.float32),
        ],
        compiler_params=params(),
        cost_estimate=cost(20),
        name="project",
    )(near, far, resident(w_uq), resident(w_uk))


def attend_kernel(start, rows, len_ref, q_ref, key_ref, new_ref, out_ref):
    devices, wide, _ = out_ref.shape
    maxlen = key_ref.shape[2]
    heads = wide // rows
    half = ROPE // 2
    total_heads = devices * heads
    lane = lax.broadcasted_iota(jnp.int32, (rows, ROPE), 1)
    place = lax.broadcasted_iota(jnp.int32, (rows, ROPE), 0)
    step = jnp.where(lane < half, lane, lane - half).astype(jnp.float32)
    frequency = jnp.exp(step * (-math.log(10000.0) / half))
    length = jnp.zeros((rows, ROPE), jnp.float32)
    for r in range(rows):
        length = jnp.where(place == r, len_ref[start + r].astype(jnp.float32), length)
    cosine = jnp.cos(length * frequency)
    sine = jnp.sin(length * frequency)
    sine = jnp.where(lane < half, -sine, sine)

    def query_block(first):
        block = q_ref[:, first : first + heads, :].astype(jnp.float32)
        return block.reshape(total_heads, LANES)

    for r in range(rows):
        latent = jnp.concatenate(
            [query_block(c * wide + r * heads) for c in range(PIECES)], axis=-1
        )
        pe = query_block(PIECES * wide + (r % (rows // 2)) * heads)
        side = r // (rows // 2) * ROPE
        pe = pe[:, side : side + ROPE]
        swapped = jnp.concatenate([pe[:, half:], pe[:, :half]], axis=-1)
        rotated = (pe * cosine[r : r + 1, :] + swapped * sine[r : r + 1, :]).astype(jnp.bfloat16)
        newest = new_ref[start + r : start + r + 1, :].astype(jnp.float32)
        own = (
            jnp.sum(latent * newest[:, :LAT], axis=-1, keepdims=True)
            + jnp.sum(rotated.astype(jnp.float32) * newest[:, LAT:], axis=-1, keepdims=True)
        ) * FACTOR
        scores = jnp.dot(
            latent.astype(jnp.bfloat16),
            key_ref[start + r, :LAT, :],
            preferred_element_type=jnp.float32,
        )
        scores += jnp.dot(rotated, key_ref[start + r, LAT:, :], preferred_element_type=jnp.float32)
        position = lax.broadcasted_iota(jnp.int32, (1, maxlen), 1)
        scores = jnp.where(position < len_ref[start + r], scores * FACTOR, -jnp.inf)
        peak = jnp.maximum(jnp.max(scores, axis=-1, keepdims=True), own)
        expo = jnp.exp(scores - peak)
        own_expo = jnp.exp(own - peak)
        total = jnp.sum(expo, axis=-1, keepdims=True) + own_expo
        weights = (expo / total).astype(jnp.bfloat16)
        own_weight = (own_expo / total).astype(jnp.bfloat16).astype(jnp.float32)
        summed = lax.dot_general(
            weights,
            key_ref[start + r, :LAT, :],
            (((1,), (1,)), ((), ())),
            preferred_element_type=jnp.float32,
        )
        summed += own_weight * newest[:, :LAT]
        out_ref[:, r * heads : (r + 1) * heads, :] = summed.reshape(devices, heads, LAT).astype(
            jnp.bfloat16
        )


def attend(lengths, queries, keys, new_latent, heads, start, rows):
    devices = queries.shape[0]
    return pl.pallas_call(
        functools.partial(attend_kernel, start, rows),
        out_shape=jax.ShapeDtypeStruct((devices, rows * heads, LAT), jnp.bfloat16),
        in_specs=[pl.BlockSpec(memory_space=pltpu.SMEM)] + [in_vmem()] * 3,
        out_specs=in_vmem(),
        compiler_params=params(),
        cost_estimate=cost(10),
        name="attend",
    )(lengths, queries, resident(keys), new_latent)


def output_kernel(groups, block, *refs):
    y_refs = refs[:groups]
    wv_ref, wo_ref, mine_ref, other_ref, rows_ref, val_ref = refs[groups:]
    heads = wv_ref.shape[0]
    devices, wide, _ = y_refs[0].shape
    me = lax.axis_index("row")
    for place, k in enumerate([*range(0, devices, 2), *range(1, devices, 2)]):
        for g, y_ref in enumerate(y_refs):
            first = (place * groups + g) * wide
            received = y_ref[jnp.bitwise_xor(me, k)].astype(jnp.float32)
            for c in range(PIECES):
                rows_ref[c, first : first + wide, :] = received[:, c * LANES : (c + 1) * LANES]
    count = rows_ref.shape[1] // heads
    for h in range(heads):
        chosen = jnp.concatenate(
            [rows_ref[c, pl.ds(h, count, stride=heads), :] for c in range(PIECES)], axis=-1
        )
        val_ref[:, h * VD : (h + 1) * VD] = jnp.dot(
            chosen.astype(jnp.bfloat16), wv_ref[h], preferred_element_type=jnp.float32
        ).astype(jnp.bfloat16)

    def step(index, carry):
        columns = pl.ds(pl.multiple_of(index * block, block), block)
        terms = jnp.dot(val_ref[...], wo_ref[:, columns], preferred_element_type=jnp.float32)
        mine_ref[:, columns] = terms[: count // 2]
        other_ref[:, columns] = terms[count // 2 :].astype(jnp.bfloat16)
        return carry

    lax.fori_loop(0, wo_ref.shape[1] // block, step, 0)


def output_terms(received, w_uv, w_o):
    groups = len(received)
    devices, wide, _ = received[0].shape
    heads = w_uv.shape[0]
    count = devices * groups * wide // heads
    depth = w_o.shape[1]
    return pl.pallas_call(
        functools.partial(output_kernel, groups, 1024),
        out_shape=(
            jax.ShapeDtypeStruct((count // 2, depth), jnp.float32),
            jax.ShapeDtypeStruct((count // 2, depth), jnp.bfloat16),
        ),
        in_specs=[in_vmem()] * (groups + 2),
        out_specs=(in_vmem(), in_vmem()),
        scratch_shapes=[
            pltpu.VMEM((PIECES, count * heads, LANES), jnp.float32),
            pltpu.VMEM((count, heads * VD), jnp.bfloat16),
        ],
        compiler_params=params(),
        cost_estimate=cost(20),
        name="output_terms",
    )(*received, resident(w_uv), resident(w_o))


def pair_kernel(rows, mine_ref, other_ref, *out_refs):
    total = mine_ref[...] + other_ref[...].astype(jnp.float32)
    for j, out_ref in enumerate(out_refs):
        out_ref[...] = total[j * rows : (j + 1) * rows].astype(out_ref.dtype)


def pair_sum(mine, other, rows):
    count, depth = mine.shape
    shapes = [jax.ShapeDtypeStruct((rows, depth), jnp.float32)]
    shapes += [jax.ShapeDtypeStruct((rows, depth), jnp.bfloat16)] * (count // rows - 1)
    return pl.pallas_call(
        functools.partial(pair_kernel, rows),
        out_shape=shapes,
        in_specs=[in_vmem()] * 2,
        out_specs=[in_vmem()] * len(shapes),
        compiler_params=params(),
        cost_estimate=cost(1),
        name="pair_sum",
    )(mine, other)


def on_device(q_latent, new_latent, cache, lengths, w_uq, w_uk, w_uv, w_o, devices):
    heads = w_uk.shape[0]
    rows = cache.shape[0]
    def swap(block, k):
        if k == 0:
            return block
        return lax.ppermute(block, "row", [(i, i ^ k) for i in range(devices)])

    def exchange(block):
        return lax.all_to_all(block, "row", split_axis=0, concat_axis=0, tiled=True)

    near = join([q_latent, swap(q_latent, 2)])
    near = join([swap(near, z) for z in range(0, devices, 4)])
    queries = project(near, swap(near, 1), w_uq, w_uk, devices, GROUPS)
    queries = [exchange(block) for block in queries]
    keys = jnp.swapaxes(cache, 1, 2)
    part = rows // GROUPS
    latents = [
        exchange(attend(lengths, block, keys, new_latent, heads, g * part, part))
        for g, block in enumerate(queries)
    ]
    mine, other = output_terms(latents, w_uv, w_o)
    shares = pair_sum(mine, swap(other, 1), rows)
    shares = [swap(block, 2 * j).astype(jnp.float32) for j, block in enumerate(shares)]
    return sum(shares[1:], shares[0]).astype(jnp.bfloat16)


def solution(mesh):
    placed = (
        P(("grp", "row"), None),
        P(("grp", "row"), None),
        P(("grp", "row"), None, None),
        P(("grp", "row")),
        P(None, "row"),
        P("row", None, None),
        P("row", None, None),
        P("row", None),
    )
    body = functools.partial(on_device, devices=mesh.shape["row"])
    return jax.shard_map(
        body, mesh=mesh, in_specs=placed, out_specs=P(("grp", "row"), None), check_vma=False
    )
```

```python
import functools
import math

import jax
import jax.numpy as jnp
from jax import lax
from jax.experimental import pallas as pl
from jax.experimental.pallas import tpu as pltpu
from jax.sharding import PartitionSpec as P

LAT = 512
ROPE = 64
HALF = ROPE // 2
NOPE = 128
VD = 128
LANES = 128
PIECES = LAT // LANES
FACTOR = (NOPE + ROPE) ** -0.5
LIMIT = 16 * 2**20
PARTS = 2
BLOCK = 512


def resident(x):
    return pltpu.with_memory_space_constraint(x, pltpu.VMEM)


def in_vmem():
    return pl.BlockSpec(memory_space=pltpu.VMEM)


def call(kernel, out_shape, microseconds, name, scratch=(), scalars=0):
    def run(*args):
        smem = [pl.BlockSpec(memory_space=pltpu.SMEM)] * scalars
        return pl.pallas_call(
            kernel,
            out_shape=out_shape,
            in_specs=smem + [in_vmem()] * (len(args) - scalars),
            out_specs=jax.tree.map(lambda _: in_vmem(), out_shape),
            scratch_shapes=list(scratch),
            compiler_params=pltpu.CompilerParams(vmem_limit_bytes=LIMIT),
            cost_estimate=pl.CostEstimate(
                flops=int(microseconds * 1.15e9), bytes_accessed=0, transcendentals=0
            ),
            name=name,
        )(*args)

    return run


def shape(*dims, dtype=jnp.bfloat16):
    return jax.ShapeDtypeStruct(dims, dtype)


def chip_order(devices):
    return sorted(range(0, devices, 2), key=lambda k: -k.bit_length())


def gathered_order(devices):
    return [z + y + c for c in range(2) for z in range(0, devices, 4) for y in (0, 2)]


def rotary_kernel(len_ref, cos_ref, sin_ref):
    rows, width = cos_ref.shape
    lane = lax.broadcasted_iota(jnp.int32, (rows, width), 1)
    place = lax.broadcasted_iota(jnp.int32, (rows, width), 0)
    step = jnp.where(lane < HALF, lane, lane - HALF).astype(jnp.float32)
    frequency = jnp.exp(step * (-math.log(10000.0) / HALF))
    length = jnp.zeros((rows, width), jnp.float32)
    for r in range(rows):
        length = jnp.where(place == r, len_ref[r].astype(jnp.float32), length)
    angle = length * frequency
    sine = jnp.sin(angle)
    cos_ref[...] = jnp.cos(angle)
    sin_ref[...] = jnp.where(lane < HALF, -sine, sine)


def rotary(lengths):
    table = shape(lengths.shape[0], ROPE, dtype=jnp.float32)
    return call(rotary_kernel, (table, table), 3, "rotary", scalars=1)(lengths)


def join_kernel(*refs):
    *in_refs, out_ref = refs
    out_ref[...] = jnp.concatenate(
        [ref[...].astype(jnp.float32) for ref in in_refs], axis=0
    ).astype(out_ref.dtype)


def join(blocks):
    rows, depth = blocks[0].shape
    return call(join_kernel, shape(len(blocks) * rows, depth), 5, "join")(*blocks)


def project_kernel(devices, q_ref, far_ref, wq_ref, wk_ref, mine_ref, other_ref, lat_ref, rot_ref):
    heads = wk_ref.shape[0]
    count = 2 * q_ref.shape[0]
    wide = count // devices * heads
    width = NOPE + ROPE
    piece = jnp.concatenate([q_ref[...], far_ref[...]], axis=0)
    projected = jnp.dot(piece, wq_ref[...], preferred_element_type=jnp.float32)
    for h in range(heads):
        mine = projected[:, h * width : (h + 1) * width]
        absorbed = jnp.dot(
            mine[:, :NOPE].astype(jnp.bfloat16), wk_ref[h], preferred_element_type=jnp.float32
        )
        for c in range(PIECES):
            lat_ref[c, pl.ds(h, count, stride=heads), :] = absorbed[:, c * LANES : (c + 1) * LANES]
        pe = mine[:, NOPE:]
        rot_ref[pl.ds(h, count, stride=heads), :] = jnp.concatenate([pe, pe], axis=-1)
    lane = lax.broadcasted_iota(jnp.int32, (wide // 2, LANES), 1)
    order = chip_order(devices)
    for place, k in enumerate(gathered_order(devices)):
        out_ref = other_ref if k % 2 else mine_ref
        at = order.index(k - k % 2)
        first = place * wide
        for c in range(PIECES):
            out_ref[at, c * wide : (c + 1) * wide, :] = lat_ref[c, first : first + wide, :].astype(
                jnp.bfloat16
            )
        low = rot_ref[first : first + wide // 2, :]
        high = rot_ref[first + wide // 2 : first + wide, :]
        out_ref[at, PIECES * wide :, :] = jnp.where(lane < ROPE, low, high).astype(jnp.bfloat16)


def project(near, far, w_uq, w_uk, devices):
    heads = w_uk.shape[0]
    count = 2 * near.shape[0]
    wide = count // devices * heads
    half = shape(devices // 2, PIECES * wide + wide // 2, LANES)
    scratch = [
        pltpu.VMEM((PIECES, count * heads, LANES), jnp.float32),
        pltpu.VMEM((count * heads, LANES), jnp.float32),
    ]
    kernel = functools.partial(project_kernel, devices)
    return call(kernel, (half, half), 20, "project", scratch)(
        near, far, resident(w_uq), resident(w_uk)
    )


def pack_kernel(mine_ref, other_ref, *out_refs):
    for j, out_ref in enumerate(out_refs):
        out_ref[0] = mine_ref[j]
        out_ref[1] = other_ref[j]


def pack(mine, other):
    chips, count, width = mine.shape
    return call(pack_kernel, [shape(2, count, width)] * chips, 1, "pack")(mine, other)


def attend_kernel(chips, len_ref, cos_ref, sin_ref, key_ref, new_ref, *refs):
    q_refs = refs[:chips]
    out_refs = refs[chips:]
    rows, _, maxlen = key_ref.shape
    wide = out_refs[0].shape[1]
    heads = wide // rows

    def query_block(first):
        blocks = [
            ref[core, first : first + heads, :].astype(jnp.float32)
            for ref in q_refs
            for core in range(2)
        ]
        return jnp.concatenate(blocks, axis=0)

    for r in range(rows):
        latent = jnp.concatenate(
            [query_block(c * wide + r * heads) for c in range(PIECES)], axis=-1
        )
        pe = query_block(PIECES * wide + (r % (rows // 2)) * heads)
        side = r // (rows // 2) * ROPE
        pe = pe[:, side : side + ROPE]
        swapped = jnp.concatenate([pe[:, HALF:], pe[:, :HALF]], axis=-1)
        rotated = (pe * cos_ref[r : r + 1, :] + swapped * sin_ref[r : r + 1, :]).astype(jnp.bfloat16)
        newest = new_ref[r : r + 1, :].astype(jnp.float32)
        own = (
            jnp.sum(latent * newest[:, :LAT], axis=-1, keepdims=True)
            + jnp.sum(rotated.astype(jnp.float32) * newest[:, LAT:], axis=-1, keepdims=True)
        ) * FACTOR
        scores = jnp.dot(
            latent.astype(jnp.bfloat16), key_ref[r, :LAT, :], preferred_element_type=jnp.float32
        )
        scores += jnp.dot(rotated, key_ref[r, LAT:, :], preferred_element_type=jnp.float32)
        position = lax.broadcasted_iota(jnp.int32, (1, maxlen), 1)
        scores = jnp.where(position < len_ref[r], scores * FACTOR, -jnp.inf)
        peak = jnp.maximum(jnp.max(scores, axis=-1, keepdims=True), own)
        expo = jnp.exp(scores - peak)
        own_expo = jnp.exp(own - peak)
        total = jnp.sum(expo, axis=-1, keepdims=True) + own_expo
        weights = (expo / total).astype(jnp.bfloat16)
        own_weight = (own_expo / total).astype(jnp.bfloat16).astype(jnp.float32)
        summed = lax.dot_general(
            weights,
            key_ref[r, :LAT, :],
            (((1,), (1,)), ((), ())),
            preferred_element_type=jnp.float32,
        )
        summed += own_weight * newest[:, :LAT]
        for k in range(2 * chips):
            out_refs[k // 2][k % 2, r * heads : (r + 1) * heads, :] = summed[
                k * heads : (k + 1) * heads, :
            ].astype(jnp.bfloat16)


def attend(lengths, tables, keys, new_latent, messages, heads):
    chips = len(messages)
    kernel = functools.partial(attend_kernel, chips)
    block = shape(2, keys.shape[0] * heads, LAT)
    return call(kernel, [block] * chips, 2 + chips, "attend", scalars=1)(
        lengths, *tables, resident(keys), new_latent, *messages
    )


def regroup_kernel(*refs):
    *in_refs, out_ref = refs
    for j, ref in enumerate(in_refs):
        out_ref[j] = ref[1]


def regroup(messages):
    _, wide, width = messages[0].shape
    return call(regroup_kernel, shape(len(messages), wide, width), 1, "regroup")(*messages)


def values_kernel(chips, *refs):
    mine_refs = refs[:chips]
    other_ref, wv_ref, val_ref, rows_ref = refs[chips:]
    heads = wv_ref.shape[0]
    wide = other_ref.shape[1]
    for place in range(2 * chips):
        block = mine_refs[place][0] if place < chips else other_ref[place - chips]
        block = block.astype(jnp.float32)
        for c in range(PIECES):
            rows_ref[c, place * wide : (place + 1) * wide, :] = block[:, c * LANES : (c + 1) * LANES]
    count = val_ref.shape[0]
    for h in range(heads):
        chosen = jnp.concatenate(
            [rows_ref[c, pl.ds(h, count, stride=heads), :] for c in range(PIECES)], axis=-1
        )
        val_ref[:, h * VD : (h + 1) * VD] = jnp.dot(
            chosen.astype(jnp.bfloat16), wv_ref[h], preferred_element_type=jnp.float32
        ).astype(jnp.bfloat16)


def head_values(messages, other, w_uv):
    chips, wide, _ = other.shape
    heads = w_uv.shape[0]
    count = 2 * chips * wide // heads
    scratch = [pltpu.VMEM((PIECES, count * heads, LANES), jnp.float32)]
    kernel = functools.partial(values_kernel, chips)
    return call(kernel, shape(count, heads * VD), 3, "values", scratch)(
        *messages, other, resident(w_uv)
    )


def terms_kernel(start, val_ref, wo_ref, mine_ref, other_ref):
    half, width = mine_ref.shape

    def step(index, carry):
        here = pl.ds(pl.multiple_of(index * BLOCK, BLOCK), BLOCK)
        there = pl.ds(pl.multiple_of(start + index * BLOCK, BLOCK), BLOCK)
        terms = jnp.dot(val_ref[...], wo_ref[:, there], preferred_element_type=jnp.float32)
        mine_ref[:, here] = terms[:half]
        other_ref[:, here] = terms[half:].astype(jnp.bfloat16)
        return carry

    lax.fori_loop(0, width // BLOCK, step, 0)


def output_terms(values, w_o, part):
    half = values.shape[0] // 2
    width = w_o.shape[1] // PARTS
    out = (shape(half, width, dtype=jnp.float32), shape(half, width))
    kernel = functools.partial(terms_kernel, part * width)
    return call(kernel, out, 6, "terms")(values, resident(w_o))


def pair_kernel(rows, *refs):
    mine_refs = refs[:PARTS]
    other_refs = refs[PARTS : 2 * PARTS]
    out_refs = refs[2 * PARTS :]
    for p, (mine_ref, other_ref) in enumerate(zip(mine_refs, other_refs)):
        width = mine_ref.shape[1]
        total = mine_ref[...] + other_ref[...].astype(jnp.float32)
        for j, out_ref in enumerate(out_refs):
            out_ref[:, p * width : (p + 1) * width] = total[j * rows : (j + 1) * rows].astype(
                out_ref.dtype
            )


def pair_sum(mine, other, rows):
    count, width = mine[0].shape
    chips = count // rows
    out = [shape(rows, PARTS * width)] * (chips - 1)
    out += [shape(rows, PARTS * width, dtype=jnp.float32)]
    return call(functools.partial(pair_kernel, rows), out, 1, "pair_sum")(*mine, *other)


def on_device(q_latent, new_latent, cache, lengths, w_uq, w_uk, w_uv, w_o, devices):
    heads = w_uk.shape[0]
    rows = cache.shape[0]
    order = chip_order(devices)
    chips = len(order)
    quarter = chips // 4

    def swap(block, k):
        if k == 0:
            return block
        return lax.ppermute(block, "row", [(i, i ^ k) for i in range(devices)])

    near = join([q_latent, swap(q_latent, 2)])
    tables = rotary(lengths)
    near = join([swap(near, z) for z in range(0, devices, 4)])
    mine, other = project(near, swap(near, 1), w_uq, w_uk, devices)
    messages = pack(mine, swap(other, 1))
    messages = [swap(block, k) for k, block in zip(order, messages)]
    keys = jnp.swapaxes(cache, 1, 2)
    latents = []
    for first, last in ((0, quarter), (quarter, 2 * quarter), (2 * quarter, chips)):
        done = attend(lengths, tables, keys, new_latent, messages[first:last], heads)
        latents += [swap(block, k) for k, block in zip(order[first:last], done)]
    values = head_values(latents, swap(regroup(latents), 1), w_uv)
    terms = [output_terms(values, w_o, part) for part in range(PARTS)]
    shares = pair_sum([a for a, _ in terms], [swap(b, 1) for _, b in terms], rows)
    shares = [swap(block, k).astype(jnp.float32) for k, block in zip(order, shares)]
    return sum(shares[:-1], shares[-1]).astype(jnp.bfloat16)


def solution(mesh):
    placed = (
        P(("grp", "row"), None),
        P(("grp", "row"), None),
        P(("grp", "row"), None, None),
        P(("grp", "row")),
        P(None, "row"),
        P("row", None, None),
        P("row", None, None),
        P("row", None),
    )
    body = functools.partial(on_device, devices=mesh.shape["row"])
    return jax.shard_map(
        body, mesh=mesh, in_specs=placed, out_specs=P(("grp", "row"), None), check_vma=False
    )
```

```python
import functools
import math

import jax
import jax.numpy as jnp
from jax import lax
from jax.experimental import pallas as pl
from jax.experimental.pallas import tpu as pltpu
from jax.sharding import PartitionSpec as P

LAT = 512
ROPE = 64
HALF = ROPE // 2
NOPE = 128
VD = 128
LANES = 128
PIECES = LAT // LANES
FACTOR = (NOPE + ROPE) ** -0.5
LIMIT = 16 * 2**20
PARTS = 2
BLOCK = 512


def resident(x):
    return pltpu.with_memory_space_constraint(x, pltpu.VMEM)


def in_vmem():
    return pl.BlockSpec(memory_space=pltpu.VMEM)


def call(kernel, out_shape, microseconds, name, scratch=(), scalars=0):
    def run(*args):
        smem = [pl.BlockSpec(memory_space=pltpu.SMEM)] * scalars
        return pl.pallas_call(
            kernel,
            out_shape=out_shape,
            in_specs=smem + [in_vmem()] * (len(args) - scalars),
            out_specs=jax.tree.map(lambda _: in_vmem(), out_shape),
            scratch_shapes=list(scratch),
            compiler_params=pltpu.CompilerParams(vmem_limit_bytes=LIMIT),
            cost_estimate=pl.CostEstimate(
                flops=int(microseconds * 1.15e9), bytes_accessed=0, transcendentals=0
            ),
            name=name,
        )(*args)

    return run


def shape(*dims, dtype=jnp.bfloat16):
    return jax.ShapeDtypeStruct(dims, dtype)


def far_first(devices, step):
    return sorted(range(0, devices, step), key=lambda k: -k.bit_length())


def gathered_order(devices):
    return [z + y for z in range(0, devices, 4) for y in (0, 2)]


def rotary_kernel(len_ref, cos_ref, sin_ref):
    rows, width = cos_ref.shape
    lane = lax.broadcasted_iota(jnp.int32, (rows, width), 1)
    place = lax.broadcasted_iota(jnp.int32, (rows, width), 0)
    step = jnp.where(lane < HALF, lane, lane - HALF).astype(jnp.float32)
    frequency = jnp.exp(step * (-math.log(10000.0) / HALF))
    length = jnp.zeros((rows, width), jnp.float32)
    for r in range(rows):
        length = jnp.where(place == r, len_ref[r].astype(jnp.float32), length)
    angle = length * frequency
    sine = jnp.sin(angle)
    cos_ref[...] = jnp.cos(angle)
    sin_ref[...] = jnp.where(lane < HALF, -sine, sine)


def rotary(lengths):
    table = shape(lengths.shape[0], ROPE, dtype=jnp.float32)
    return call(rotary_kernel, (table, table), 3, "rotary", scalars=1)(lengths)


def join_kernel(*refs):
    *in_refs, out_ref = refs
    out_ref[...] = jnp.concatenate(
        [ref[...].astype(jnp.float32) for ref in in_refs], axis=0
    ).astype(out_ref.dtype)


def join(blocks):
    rows, depth = blocks[0].shape
    return call(join_kernel, shape(len(blocks) * rows, depth), 5, "join")(*blocks)


def project_kernel(devices, q_ref, *refs):
    weights = (refs[0:2], refs[2:4])
    lat_ref, rot_ref = refs[-2:]
    out_refs = refs[4:-2]
    heads = weights[0][1].shape[0]
    count = q_ref.shape[0]
    wide = 2 * count // devices * heads
    width = NOPE + ROPE
    lane = lax.broadcasted_iota(jnp.int32, (wide // 2, LANES), 1)
    order = far_first(devices, 2)
    for core, (wq_ref, wk_ref) in enumerate(weights):
        projected = jnp.dot(q_ref[...], wq_ref[...], preferred_element_type=jnp.float32)
        for h in range(heads):
            mine = projected[:, h * width : (h + 1) * width]
            absorbed = jnp.dot(
                mine[:, :NOPE].astype(jnp.bfloat16), wk_ref[h], preferred_element_type=jnp.float32
            )
            at = pl.ds(h, count, stride=heads)
            for c in range(PIECES):
                lat_ref[core * PIECES + c, at, :] = absorbed[:, c * LANES : (c + 1) * LANES]
            pe = mine[:, NOPE:]
            rot_ref[core, at, :] = jnp.concatenate([pe, pe], axis=-1)
        for place, k in enumerate(gathered_order(devices)):
            out_ref = out_refs[order.index(k)]
            first = place * wide
            for c in range(PIECES):
                out_ref[core, c * wide : (c + 1) * wide, :] = lat_ref[
                    core * PIECES + c, first : first + wide, :
                ].astype(jnp.bfloat16)
            low = rot_ref[core, first : first + wide // 2, :]
            high = rot_ref[core, first + wide // 2 : first + wide, :]
            out_ref[core, PIECES * wide :, :] = jnp.where(lane < ROPE, low, high).astype(
                jnp.bfloat16
            )


def project(piece, weights, devices):
    heads = weights[1].shape[0]
    count = piece.shape[0]
    wide = 2 * count // devices * heads
    scratch = [
        pltpu.VMEM((2 * PIECES, count * heads, LANES), jnp.float32),
        pltpu.VMEM((2, count * heads, LANES), jnp.float32),
    ]
    out = [shape(2, PIECES * wide + wide // 2, LANES)] * (devices // 2)
    kernel = functools.partial(project_kernel, devices)
    return call(kernel, out, 20, "project", scratch)(piece, *[resident(w) for w in weights])


def attend_kernel(chips, len_ref, cos_ref, sin_ref, key_ref, new_ref, *refs):
    q_refs = refs[:chips]
    out_refs = refs[chips:]
    rows, _, maxlen = key_ref.shape
    wide = out_refs[0].shape[1]
    heads = wide // rows

    def query_block(first):
        blocks = [
            ref[core, first : first + heads, :].astype(jnp.float32)
            for ref in q_refs
            for core in range(2)
        ]
        return jnp.concatenate(blocks, axis=0)

    for r in range(rows):
        latent = jnp.concatenate(
            [query_block(c * wide + r * heads) for c in range(PIECES)], axis=-1
        )
        pe = query_block(PIECES * wide + (r % (rows // 2)) * heads)
        side = r // (rows // 2) * ROPE
        pe = pe[:, side : side + ROPE]
        swapped = jnp.concatenate([pe[:, HALF:], pe[:, :HALF]], axis=-1)
        rotated = (pe * cos_ref[r : r + 1, :] + swapped * sin_ref[r : r + 1, :]).astype(jnp.bfloat16)
        newest = new_ref[r : r + 1, :].astype(jnp.float32)
        own = (
            jnp.sum(latent * newest[:, :LAT], axis=-1, keepdims=True)
            + jnp.sum(rotated.astype(jnp.float32) * newest[:, LAT:], axis=-1, keepdims=True)
        ) * FACTOR
        scores = jnp.dot(
            latent.astype(jnp.bfloat16), key_ref[r, :LAT, :], preferred_element_type=jnp.float32
        )
        scores += jnp.dot(rotated, key_ref[r, LAT:, :], preferred_element_type=jnp.float32)
        position = lax.broadcasted_iota(jnp.int32, (1, maxlen), 1)
        scores = jnp.where(position < len_ref[r], scores * FACTOR, -jnp.inf)
        peak = jnp.maximum(jnp.max(scores, axis=-1, keepdims=True), own)
        expo = jnp.exp(scores - peak)
        own_expo = jnp.exp(own - peak)
        total = jnp.sum(expo, axis=-1, keepdims=True) + own_expo
        weights = (expo / total).astype(jnp.bfloat16)
        own_weight = (own_expo / total).astype(jnp.bfloat16).astype(jnp.float32)
        summed = lax.dot_general(
            weights,
            key_ref[r, :LAT, :],
            (((1,), (1,)), ((), ())),
            preferred_element_type=jnp.float32,
        )
        summed += own_weight * newest[:, :LAT]
        for k in range(2 * chips):
            out_refs[k // 2][k % 2, r * heads : (r + 1) * heads, :] = summed[
                k * heads : (k + 1) * heads, :
            ].astype(jnp.bfloat16)


def attend(lengths, tables, keys, new_latent, messages, heads):
    chips = len(messages)
    kernel = functools.partial(attend_kernel, chips)
    block = shape(2, keys.shape[0] * heads, LAT)
    return call(kernel, [block] * chips, 2 + chips, "attend", scalars=1)(
        lengths, *tables, resident(keys), new_latent, *messages
    )


def regroup_kernel(*refs):
    *in_refs, out_ref = refs
    for j, ref in enumerate(in_refs):
        out_ref[j] = ref[1]


def regroup(messages):
    _, wide, width = messages[0].shape
    return call(regroup_kernel, shape(len(messages), wide, width), 1, "regroup")(*messages)


def values_kernel(chips, *refs):
    mine_refs = refs[:chips]
    other_ref, wv_ref, val_ref, rows_ref = refs[chips:]
    heads = wv_ref.shape[0]
    wide = other_ref.shape[1]
    for place in range(2 * chips):
        block = mine_refs[place][0] if place < chips else other_ref[place - chips]
        block = block.astype(jnp.float32)
        for c in range(PIECES):
            rows_ref[c, place * wide : (place + 1) * wide, :] = block[:, c * LANES : (c + 1) * LANES]
    count = val_ref.shape[0]
    for h in range(heads):
        chosen = jnp.concatenate(
            [rows_ref[c, pl.ds(h, count, stride=heads), :] for c in range(PIECES)], axis=-1
        )
        val_ref[:, h * VD : (h + 1) * VD] = jnp.dot(
            chosen.astype(jnp.bfloat16), wv_ref[h], preferred_element_type=jnp.float32
        ).astype(jnp.bfloat16)


def head_values(messages, other, w_uv):
    chips, wide, _ = other.shape
    heads = w_uv.shape[0]
    count = 2 * chips * wide // heads
    scratch = [pltpu.VMEM((PIECES, count * heads, LANES), jnp.float32)]
    kernel = functools.partial(values_kernel, chips)
    return call(kernel, shape(count, heads * VD), 3, "values", scratch)(
        *messages, other, resident(w_uv)
    )


def terms_kernel(start, val_ref, wo_ref, mine_ref, other_ref):
    half, width = mine_ref.shape

    def step(index, carry):
        here = pl.ds(pl.multiple_of(index * BLOCK, BLOCK), BLOCK)
        there = pl.ds(pl.multiple_of(start + index * BLOCK, BLOCK), BLOCK)
        terms = jnp.dot(val_ref[...], wo_ref[:, there], preferred_element_type=jnp.float32)
        mine_ref[:, here] = terms[:half]
        other_ref[:, here] = terms[half:].astype(jnp.bfloat16)
        return carry

    lax.fori_loop(0, width // BLOCK, step, 0)


def output_terms(values, w_o, part):
    half = values.shape[0] // 2
    width = w_o.shape[1] // PARTS
    out = (shape(half, width, dtype=jnp.float32), shape(half, width))
    kernel = functools.partial(terms_kernel, part * width)
    return call(kernel, out, 6, "terms")(values, resident(w_o))


def core_sum_kernel(keep, give, mine_ref, other_ref, keep_ref, give_ref):
    rows = keep_ref.shape[0] // len(keep)
    total = mine_ref[...] + other_ref[...].astype(jnp.float32)
    for out_ref, places in ((keep_ref, keep), (give_ref, give)):
        blocks = [total[j * rows : (j + 1) * rows] for j in places]
        out_ref[...] = jnp.concatenate(blocks, axis=0).astype(out_ref.dtype)


def core_sum(mine, other, devices):
    count, width = mine.shape
    order = far_first(devices, 2)
    zs = far_first(devices, 4)
    keep = [order.index(z) for z in zs]
    give = [order.index(z + 2) for z in zs]
    out = (shape(count // 2, width, dtype=jnp.float32), shape(count // 2, width))
    return call(functools.partial(core_sum_kernel, keep, give), out, 1, "core_sum")(mine, other)


def chip_sum_kernel(mine_ref, other_ref, *out_refs):
    rows = out_refs[0].shape[0]
    total = mine_ref[...] + other_ref[...].astype(jnp.float32)
    for j, out_ref in enumerate(out_refs):
        out_ref[...] = total[j * rows : (j + 1) * rows].astype(out_ref.dtype)


def chip_sum(mine, other, rows):
    count, width = mine.shape
    out = [shape(rows, width)] * (count // rows - 1) + [shape(rows, width, dtype=jnp.float32)]
    return call(chip_sum_kernel, out, 1, "chip_sum")(mine, other)


def last_sum_kernel(*refs):
    *in_refs, out_ref = refs
    each = len(in_refs) // PARTS
    width = out_ref.shape[1] // PARTS
    for p in range(PARTS):
        terms = [ref[...].astype(jnp.float32) for ref in in_refs[p * each : (p + 1) * each]]
        out_ref[:, p * width : (p + 1) * width] = sum(terms[1:], terms[0]).astype(out_ref.dtype)


def last_sum(shares):
    rows, width = shares[0][0].shape
    blocks = [block for part in shares for block in part]
    return call(last_sum_kernel, shape(rows, PARTS * width), 1, "last_sum")(*blocks)


def on_device(q_latent, new_latent, cache, lengths, w_uq, w_uk, w_uv, w_o, devices):
    heads = w_uk.shape[0]
    rows = cache.shape[0]
    order = far_first(devices, 2)
    zs = far_first(devices, 4)

    def swap(block, k):
        if k == 0:
            return block
        return lax.ppermute(block, "row", [(i, i ^ k) for i in range(devices)])

    far_weights = [swap(w_uq, 1), swap(w_uk, 1)]
    near = join([q_latent, swap(q_latent, 2)])
    tables = rotary(lengths)
    near = join([swap(near, z) for z in range(0, devices, 4)])
    messages = project(near, [w_uq, w_uk, *far_weights], devices)
    messages = [swap(block, k) for k, block in zip(order, messages)]
    keys = jnp.swapaxes(cache, 1, 2)
    latents = attend(lengths, tables, keys, new_latent, messages, heads)
    latents = [swap(block, k) for k, block in zip(order, latents)]
    values = head_values(latents, swap(regroup(latents), 1), w_uv)
    shares = []
    for part in range(PARTS):
        mine, other = output_terms(values, w_o, part)
        mine, other = core_sum(mine, swap(other, 1), devices)
        blocks = chip_sum(mine, swap(other, 2), rows)
        shares.append([swap(block, z) for z, block in zip(zs, blocks)])
    return last_sum(shares)


def solution(mesh):
    placed = (
        P(("grp", "row"), None),
        P(("grp", "row"), None),
        P(("grp", "row"), None, None),
        P(("grp", "row")),
        P(None, "row"),
        P("row", None, None),
        P("row", None, None),
        P("row", None),
    )
    body = functools.partial(on_device, devices=mesh.shape["row"])
    return jax.shard_map(
        body, mesh=mesh, in_specs=placed, out_specs=P(("grp", "row"), None), check_vma=False
    )
```

```python
import functools
import math

import jax
import jax.numpy as jnp
from jax import lax
from jax.experimental import pallas as pl
from jax.experimental.pallas import tpu as pltpu
from jax.sharding import PartitionSpec as P

LAT = 512
ROPE = 64
HALF = ROPE // 2
NOPE = 128
VD = 128
LANES = 128
PIECES = LAT // LANES
FACTOR = (NOPE + ROPE) ** -0.5
LIMIT = 16 * 2**20
PARTS = 2
BLOCK = 512


def resident(x):
    return pltpu.with_memory_space_constraint(x, pltpu.VMEM)


def in_vmem():
    return pl.BlockSpec(memory_space=pltpu.VMEM)


def call(kernel, out_shape, microseconds, name, scratch=(), scalars=0):
    def run(*args):
        smem = [pl.BlockSpec(memory_space=pltpu.SMEM)] * scalars
        return pl.pallas_call(
            kernel,
            out_shape=out_shape,
            in_specs=smem + [in_vmem()] * (len(args) - scalars),
            out_specs=jax.tree.map(lambda _: in_vmem(), out_shape),
            scratch_shapes=list(scratch),
            compiler_params=pltpu.CompilerParams(vmem_limit_bytes=LIMIT),
            cost_estimate=pl.CostEstimate(
                flops=int(microseconds * 1.15e9), bytes_accessed=0, transcendentals=0
            ),
            name=name,
        )(*args)

    return run


def shape(*dims, dtype=jnp.bfloat16):
    return jax.ShapeDtypeStruct(dims, dtype)


def far_first(devices, step):
    return sorted(range(0, devices, step), key=lambda k: -k.bit_length())


def gathered_order(devices):
    return [z + y for y in (0, 2) for z in far_first(devices, 4)]


def rotary_kernel(len_ref, cos_ref, sin_ref):
    rows, width = cos_ref.shape
    lane = lax.broadcasted_iota(jnp.int32, (rows, width), 1)
    place = lax.broadcasted_iota(jnp.int32, (rows, width), 0)
    step = jnp.where(lane < HALF, lane, lane - HALF).astype(jnp.float32)
    frequency = jnp.exp(step * (-math.log(10000.0) / HALF))
    length = jnp.zeros((rows, width), jnp.float32)
    for r in range(rows):
        length = jnp.where(place == r, len_ref[r].astype(jnp.float32), length)
    angle = length * frequency
    sine = jnp.sin(angle)
    cos_ref[...] = jnp.cos(angle)
    sin_ref[...] = jnp.where(lane < HALF, -sine, sine)


def rotary(lengths):
    table = shape(lengths.shape[0], ROPE, dtype=jnp.float32)
    return call(rotary_kernel, (table, table), 3, "rotary", scalars=1)(lengths)


def join_kernel(cos_ref, sin_ref, *refs):
    *in_refs, cos_out_ref, sin_out_ref, out_ref = refs
    cos_out_ref[...] = cos_ref[...]
    sin_out_ref[...] = sin_ref[...]
    out_ref[...] = jnp.concatenate(
        [ref[...].astype(jnp.float32) for ref in in_refs], axis=0
    ).astype(out_ref.dtype)


def join(tables, blocks):
    rows, depth = blocks[0].shape
    out = (*[shape(*t.shape, dtype=t.dtype) for t in tables], shape(len(blocks) * rows, depth))
    cosine, sine, joined = call(join_kernel, out, 3, "join")(*tables, *blocks)
    return (cosine, sine), joined


def project_kernel(devices, q_ref, far_ref, *refs):
    weights = (refs[0:2], refs[2:4])
    lat_ref, rot_ref = refs[-2:]
    out_refs = refs[4:-2]
    heads = weights[0][1].shape[0]
    piece = jnp.concatenate([q_ref[...], far_ref[...]], axis=0)
    count = piece.shape[0]
    wide = 2 * count // devices * heads
    width = NOPE + ROPE
    lane = lax.broadcasted_iota(jnp.int32, (wide // 2, LANES), 1)
    order = far_first(devices, 2)
    for core, (wq_ref, wk_ref) in enumerate(weights):
        projected = jnp.dot(piece, wq_ref[...], preferred_element_type=jnp.float32)
        for h in range(heads):
            mine = projected[:, h * width : (h + 1) * width]
            absorbed = jnp.dot(
                mine[:, :NOPE].astype(jnp.bfloat16), wk_ref[h], preferred_element_type=jnp.float32
            )
            at = pl.ds(h, count, stride=heads)
            for c in range(PIECES):
                lat_ref[core * PIECES + c, at, :] = absorbed[:, c * LANES : (c + 1) * LANES]
            pe = mine[:, NOPE:]
            rot_ref[core, at, :] = jnp.concatenate([pe, pe], axis=-1)
        for place, k in enumerate(gathered_order(devices)):
            out_ref = out_refs[order.index(k)]
            first = place * wide
            for c in range(PIECES):
                out_ref[core, c * wide : (c + 1) * wide, :] = lat_ref[
                    core * PIECES + c, first : first + wide, :
                ].astype(jnp.bfloat16)
            low = rot_ref[core, first : first + wide // 2, :]
            high = rot_ref[core, first + wide // 2 : first + wide, :]
            out_ref[core, PIECES * wide :, :] = jnp.where(lane < ROPE, low, high).astype(
                jnp.bfloat16
            )


def project(near, far, weights, devices):
    heads = weights[1].shape[0]
    count = 2 * near.shape[0]
    wide = 2 * count // devices * heads
    scratch = [
        pltpu.VMEM((2 * PIECES, count * heads, LANES), jnp.float32),
        pltpu.VMEM((2, count * heads, LANES), jnp.float32),
    ]
    out = [shape(2, PIECES * wide + wide // 2, LANES)] * (devices // 2)
    kernel = functools.partial(project_kernel, devices)
    return call(kernel, out, 20, "project", scratch)(near, far, *[resident(w) for w in weights])


def attend_kernel(chips, len_ref, cos_ref, sin_ref, key_ref, new_ref, *refs):
    q_refs = refs[:chips]
    out_refs = refs[chips:]
    rows, _, maxlen = key_ref.shape
    wide = out_refs[0].shape[1]
    heads = wide // rows

    def query_block(first):
        blocks = [
            ref[core, first : first + heads, :].astype(jnp.float32)
            for ref in q_refs
            for core in range(2)
        ]
        return jnp.concatenate(blocks, axis=0)

    for r in range(rows):
        latent = jnp.concatenate(
            [query_block(c * wide + r * heads) for c in range(PIECES)], axis=-1
        )
        pe = query_block(PIECES * wide + (r % (rows // 2)) * heads)
        side = r // (rows // 2) * ROPE
        pe = pe[:, side : side + ROPE]
        swapped = jnp.concatenate([pe[:, HALF:], pe[:, :HALF]], axis=-1)
        rotated = (pe * cos_ref[r : r + 1, :] + swapped * sin_ref[r : r + 1, :]).astype(jnp.bfloat16)
        newest = new_ref[r : r + 1, :].astype(jnp.float32)
        own = (
            jnp.sum(latent * newest[:, :LAT], axis=-1, keepdims=True)
            + jnp.sum(rotated.astype(jnp.float32) * newest[:, LAT:], axis=-1, keepdims=True)
        ) * FACTOR
        scores = jnp.dot(
            latent.astype(jnp.bfloat16), key_ref[r, :LAT, :], preferred_element_type=jnp.float32
        )
        scores += jnp.dot(rotated, key_ref[r, LAT:, :], preferred_element_type=jnp.float32)
        position = lax.broadcasted_iota(jnp.int32, (1, maxlen), 1)
        scores = jnp.where(position < len_ref[r], scores * FACTOR, -jnp.inf)
        peak = jnp.maximum(jnp.max(scores, axis=-1, keepdims=True), own)
        expo = jnp.exp(scores - peak)
        own_expo = jnp.exp(own - peak)
        total = jnp.sum(expo, axis=-1, keepdims=True) + own_expo
        weights = (expo / total).astype(jnp.bfloat16)
        own_weight = (own_expo / total).astype(jnp.bfloat16).astype(jnp.float32)
        summed = lax.dot_general(
            weights,
            key_ref[r, :LAT, :],
            (((1,), (1,)), ((), ())),
            preferred_element_type=jnp.float32,
        )
        summed += own_weight * newest[:, :LAT]
        for k in range(2 * chips):
            out_refs[k // 2][k % 2, r * heads : (r + 1) * heads, :] = summed[
                k * heads : (k + 1) * heads, :
            ].astype(jnp.bfloat16)


def attend(lengths, tables, keys, new_latent, messages, heads):
    chips = len(messages)
    kernel = functools.partial(attend_kernel, chips)
    block = shape(2, keys.shape[0] * heads, LAT)
    return call(kernel, [block] * chips, 2 + chips, "attend", scalars=1)(
        lengths, *tables, resident(keys), new_latent, *messages
    )


def regroup_kernel(*refs):
    *in_refs, out_ref = refs
    for j, ref in enumerate(in_refs):
        out_ref[j] = ref[1]


def regroup(messages):
    _, wide, width = messages[0].shape
    return call(regroup_kernel, shape(len(messages), wide, width), 1, "regroup")(*messages)


def values_kernel(chips, *refs):
    mine_refs = refs[:chips]
    other_ref, wv_ref, val_ref, rows_ref = refs[chips:]
    heads = wv_ref.shape[0]
    wide = other_ref.shape[1]
    for place in range(2 * chips):
        block = mine_refs[place][0] if place < chips else other_ref[place - chips]
        block = block.astype(jnp.float32)
        for c in range(PIECES):
            rows_ref[c, place * wide : (place + 1) * wide, :] = block[:, c * LANES : (c + 1) * LANES]
    count = val_ref.shape[0]
    for h in range(heads):
        chosen = jnp.concatenate(
            [rows_ref[c, pl.ds(h, count, stride=heads), :] for c in range(PIECES)], axis=-1
        )
        val_ref[:, h * VD : (h + 1) * VD] = jnp.dot(
            chosen.astype(jnp.bfloat16), wv_ref[h], preferred_element_type=jnp.float32
        ).astype(jnp.bfloat16)


def head_values(messages, other, w_uv):
    chips, wide, _ = other.shape
    heads = w_uv.shape[0]
    count = 2 * chips * wide // heads
    scratch = [pltpu.VMEM((PIECES, count * heads, LANES), jnp.float32)]
    kernel = functools.partial(values_kernel, chips)
    return call(kernel, shape(count, heads * VD), 3, "values", scratch)(
        *messages, other, resident(w_uv)
    )


def terms_kernel(start, val_ref, wo_ref, mine_ref, other_ref):
    half, width = mine_ref.shape

    def step(index, carry):
        here = pl.ds(pl.multiple_of(index * BLOCK, BLOCK), BLOCK)
        there = pl.ds(pl.multiple_of(start + index * BLOCK, BLOCK), BLOCK)
        terms = jnp.dot(val_ref[...], wo_ref[:, there], preferred_element_type=jnp.float32)
        mine_ref[:, here] = terms[:half]
        other_ref[:, here] = terms[half:].astype(jnp.bfloat16)
        return carry

    lax.fori_loop(0, width // BLOCK, step, 0)


def output_terms(values, w_o, part):
    half = values.shape[0] // 2
    width = w_o.shape[1] // PARTS
    out = (shape(half, width, dtype=jnp.float32), shape(half, width))
    kernel = functools.partial(terms_kernel, part * width)
    return call(kernel, out, 6, "terms")(values, resident(w_o))


def core_sum_kernel(keep, give, mine_ref, other_ref, keep_ref, give_ref):
    rows = keep_ref.shape[0] // len(keep)
    total = mine_ref[...] + other_ref[...].astype(jnp.float32)
    for out_ref, places in ((keep_ref, keep), (give_ref, give)):
        blocks = [total[j * rows : (j + 1) * rows] for j in places]
        out_ref[...] = jnp.concatenate(blocks, axis=0).astype(out_ref.dtype)


def core_sum(mine, other, devices):
    count, width = mine.shape
    order = far_first(devices, 2)
    zs = far_first(devices, 4)
    keep = [order.index(z) for z in zs]
    give = [order.index(z + 2) for z in zs]
    out = (shape(count // 2, width, dtype=jnp.float32), shape(count // 2, width))
    return call(functools.partial(core_sum_kernel, keep, give), out, 1, "core_sum")(mine, other)


def chip_sum_kernel(*refs):
    mine_refs = refs[:PARTS]
    other_refs = refs[PARTS : 2 * PARTS]
    out_refs = refs[2 * PARTS :]
    rows = out_refs[0].shape[0]
    for p, (mine_ref, other_ref) in enumerate(zip(mine_refs, other_refs)):
        width = mine_ref.shape[1]
        total = mine_ref[...] + other_ref[...].astype(jnp.float32)
        for j, out_ref in enumerate(out_refs):
            out_ref[:, p * width : (p + 1) * width] = total[j * rows : (j + 1) * rows].astype(
                out_ref.dtype
            )


def chip_sum(mine, other, rows):
    count, width = mine[0].shape
    width *= PARTS
    out = [shape(rows, width)] * (count // rows - 1) + [shape(rows, width, dtype=jnp.float32)]
    return call(chip_sum_kernel, out, 1, "chip_sum")(*mine, *other)


def last_sum_kernel(*refs):
    *in_refs, out_ref = refs
    terms = [ref[...].astype(jnp.float32) for ref in in_refs]
    out_ref[...] = sum(terms[1:], terms[0]).astype(out_ref.dtype)


def last_sum(blocks):
    return call(last_sum_kernel, shape(*blocks[0].shape), 1, "last_sum")(*blocks)


def on_device(q_latent, new_latent, cache, lengths, w_uq, w_uk, w_uv, w_o, devices):
    heads = w_uk.shape[0]
    rows = cache.shape[0]
    order = far_first(devices, 2)
    zs = far_first(devices, 4)

    def swap(block, k):
        if k == 0:
            return block
        return lax.ppermute(block, "row", [(i, i ^ k) for i in range(devices)])

    far_weights = [swap(w_uq, 1), swap(w_uk, 1)]
    tables, near = join(rotary(lengths), [swap(q_latent, z) for z in zs])
    messages = project(near, swap(near, 2), [w_uq, w_uk, *far_weights], devices)
    messages = [swap(block, k) for k, block in zip(order, messages)]
    keys = jnp.swapaxes(cache, 1, 2)
    latents = attend(lengths, tables, keys, new_latent, messages, heads)
    latents = [swap(block, k) for k, block in zip(order, latents)]
    values = head_values(latents, swap(regroup(latents), 1), w_uv)
    keep, got = [], []
    for part in range(PARTS):
        mine, other = output_terms(values, w_o, part)
        mine, other = core_sum(mine, swap(other, 1), devices)
        keep.append(mine)
        got.append(swap(other, 2))
    blocks = chip_sum(keep, got, rows)
    return last_sum([swap(block, z) for z, block in zip(zs, blocks)])


def solution(mesh):
    placed = (
        P(("grp", "row"), None),
        P(("grp", "row"), None),
        P(("grp", "row"), None, None),
        P(("grp", "row")),
        P(None, "row"),
        P("row", None, None),
        P("row", None, None),
        P("row", None),
    )
    body = functools.partial(on_device, devices=mesh.shape["row"])
    return jax.shard_map(
        body, mesh=mesh, in_specs=placed, out_specs=P(("grp", "row"), None), check_vma=False
    )
```

```python
import functools
import math

import jax
import jax.numpy as jnp
from jax import lax
from jax.experimental import pallas as pl
from jax.experimental.pallas import tpu as pltpu
from jax.sharding import PartitionSpec as P

LAT = 512
ROPE = 64
HALF = ROPE // 2
NOPE = 128
VD = 128
LANES = 128
PIECES = LAT // LANES
FACTOR = (NOPE + ROPE) ** -0.5
LIMIT = 16 * 2**20
PARTS = 2
Y = 2
Z1 = 4


def resident(x):
    return pltpu.with_memory_space_constraint(x, pltpu.VMEM)


def in_vmem():
    return pl.BlockSpec(memory_space=pltpu.VMEM)


def call(kernel, out_shape, microseconds, name, scratch=(), scalars=0):
    def run(*args):
        smem = [pl.BlockSpec(memory_space=pltpu.SMEM)] * scalars
        return pl.pallas_call(
            kernel,
            out_shape=out_shape,
            in_specs=smem + [in_vmem()] * (len(args) - scalars),
            out_specs=jax.tree.map(lambda _: in_vmem(), out_shape),
            scratch_shapes=list(scratch),
            compiler_params=pltpu.CompilerParams(vmem_limit_bytes=LIMIT),
            cost_estimate=pl.CostEstimate(
                flops=int(microseconds * 1.15e9), bytes_accessed=0, transcendentals=0
            ),
            name=name,
        )(*args)

    return run


def shape(*dims, dtype=jnp.bfloat16):
    return jax.ShapeDtypeStruct(dims, dtype)


def far_first(devices, step):
    return sorted(range(0, devices, step), key=lambda k: -k.bit_length())


def gathered_order(devices):
    return [z + y for z in far_first(devices, 4) for y in (0, 2)]


def rotary_kernel(len_ref, cos_ref, sin_ref):
    rows, width = cos_ref.shape
    lane = lax.broadcasted_iota(jnp.int32, (rows, width), 1)
    place = lax.broadcasted_iota(jnp.int32, (rows, width), 0)
    step = jnp.where(lane < HALF, lane, lane - HALF).astype(jnp.float32)
    frequency = jnp.exp(step * (-math.log(10000.0) / HALF))
    length = jnp.zeros((rows, width), jnp.float32)
    for r in range(rows):
        length = jnp.where(place == r, len_ref[r].astype(jnp.float32), length)
    angle = length * frequency
    sine = jnp.sin(angle)
    cos_ref[...] = jnp.cos(angle)
    sin_ref[...] = jnp.where(lane < HALF, -sine, sine)


def rotary(lengths):
    table = shape(lengths.shape[0], ROPE, dtype=jnp.float32)
    return call(rotary_kernel, (table, table), 3, "rotary", scalars=1)(lengths)


def join_kernel(cos_ref, sin_ref, *refs):
    *in_refs, cos_out_ref, sin_out_ref, out_ref = refs
    cos_out_ref[...] = cos_ref[...]
    sin_out_ref[...] = sin_ref[...]
    out_ref[...] = jnp.concatenate(
        [ref[...].astype(jnp.float32) for ref in in_refs], axis=0
    ).astype(out_ref.dtype)


def join(tables, blocks):
    rows, depth = blocks[0].shape
    out = (*[shape(*t.shape, dtype=t.dtype) for t in tables], shape(len(blocks) * rows, depth))
    cosine, sine, joined = call(join_kernel, out, 3, "join")(*tables, *blocks)
    return (cosine, sine), joined


def project_kernel(devices, *refs):
    pieces = devices // 4
    q_refs = refs[:pieces]
    weights = (refs[pieces : pieces + 2], refs[pieces + 2 : pieces + 4])
    lat_ref, rot_ref = refs[-2:]
    out_refs = refs[pieces + 4 : -2]
    heads = weights[0][1].shape[0]
    piece = jnp.concatenate([ref[...].astype(jnp.float32) for ref in q_refs], axis=0)
    piece = piece.astype(jnp.bfloat16)
    count = piece.shape[0]
    wide = 2 * count // devices * heads
    width = NOPE + ROPE
    lane = lax.broadcasted_iota(jnp.int32, (wide // 2, LANES), 1)
    order = far_first(devices, 2)
    for core, (wq_ref, wk_ref) in enumerate(weights):
        projected = jnp.dot(piece, wq_ref[...], preferred_element_type=jnp.float32)
        for h in range(heads):
            mine = projected[:, h * width : (h + 1) * width]
            absorbed = jnp.dot(
                mine[:, :NOPE].astype(jnp.bfloat16), wk_ref[h], preferred_element_type=jnp.float32
            )
            at = pl.ds(h, count, stride=heads)
            for c in range(PIECES):
                lat_ref[core * PIECES + c, at, :] = absorbed[:, c * LANES : (c + 1) * LANES]
            pe = mine[:, NOPE:]
            rot_ref[core, at, :] = jnp.concatenate([pe, pe], axis=-1)
        for place, k in enumerate(gathered_order(devices)):
            out_ref = out_refs[order.index(k)]
            first = place * wide
            for c in range(PIECES):
                out_ref[core, c * wide : (c + 1) * wide, :] = lat_ref[
                    core * PIECES + c, first : first + wide, :
                ].astype(jnp.bfloat16)
            low = rot_ref[core, first : first + wide // 2, :]
            high = rot_ref[core, first + wide // 2 : first + wide, :]
            out_ref[core, PIECES * wide :, :] = jnp.where(lane < ROPE, low, high).astype(
                jnp.bfloat16
            )


def project(pieces, weights, devices):
    heads = weights[1].shape[0]
    count = len(pieces) * pieces[0].shape[0]
    wide = 2 * count // devices * heads
    scratch = [
        pltpu.VMEM((2 * PIECES, count * heads, LANES), jnp.float32),
        pltpu.VMEM((2, count * heads, LANES), jnp.float32),
    ]
    out = [shape(2, PIECES * wide + wide // 2, LANES)] * (devices // 2)
    kernel = functools.partial(project_kernel, devices)
    return call(kernel, out, 20, "project", scratch)(*pieces, *[resident(w) for w in weights])


def attend_kernel(chips, len_ref, cos_ref, sin_ref, key_ref, new_ref, *refs):
    q_refs = refs[:chips]
    out_refs = refs[chips:]
    rows, _, maxlen = key_ref.shape
    wide = out_refs[0].shape[1]
    heads = wide // rows

    def query_block(first):
        blocks = [
            ref[core, first : first + heads, :].astype(jnp.float32)
            for ref in q_refs
            for core in range(2)
        ]
        return jnp.concatenate(blocks, axis=0)

    for r in range(rows):
        latent = jnp.concatenate(
            [query_block(c * wide + r * heads) for c in range(PIECES)], axis=-1
        )
        pe = query_block(PIECES * wide + (r % (rows // 2)) * heads)
        side = r // (rows // 2) * ROPE
        pe = pe[:, side : side + ROPE]
        swapped = jnp.concatenate([pe[:, HALF:], pe[:, :HALF]], axis=-1)
        rotated = (pe * cos_ref[r : r + 1, :] + swapped * sin_ref[r : r + 1, :]).astype(jnp.bfloat16)
        newest = new_ref[r : r + 1, :].astype(jnp.float32)
        own = (
            jnp.sum(latent * newest[:, :LAT], axis=-1, keepdims=True)
            + jnp.sum(rotated.astype(jnp.float32) * newest[:, LAT:], axis=-1, keepdims=True)
        ) * FACTOR
        scores = jnp.dot(
            latent.astype(jnp.bfloat16), key_ref[r, :LAT, :], preferred_element_type=jnp.float32
        )
        scores += jnp.dot(rotated, key_ref[r, LAT:, :], preferred_element_type=jnp.float32)
        position = lax.broadcasted_iota(jnp.int32, (1, maxlen), 1)
        scores = jnp.where(position < len_ref[r], scores * FACTOR, -jnp.inf)
        peak = jnp.maximum(jnp.max(scores, axis=-1, keepdims=True), own)
        expo = jnp.exp(scores - peak)
        own_expo = jnp.exp(own - peak)
        total = jnp.sum(expo, axis=-1, keepdims=True) + own_expo
        weights = (expo / total).astype(jnp.bfloat16)
        own_weight = (own_expo / total).astype(jnp.bfloat16).astype(jnp.float32)
        summed = lax.dot_general(
            weights,
            key_ref[r, :LAT, :],
            (((1,), (1,)), ((), ())),
            preferred_element_type=jnp.float32,
        )
        summed += own_weight * newest[:, :LAT]
        for k in range(2 * chips):
            out_refs[k // 2][k % 2, r * heads : (r + 1) * heads, :] = summed[
                k * heads : (k + 1) * heads, :
            ].astype(jnp.bfloat16)


def attend(lengths, tables, keys, new_latent, messages, heads):
    chips = len(messages)
    kernel = functools.partial(attend_kernel, chips)
    block = shape(2, keys.shape[0] * heads, LAT)
    return call(kernel, [block] * chips, 2 + chips, "attend", scalars=1)(
        lengths, *tables, resident(keys), new_latent, *messages
    )


def regroup_kernel(*refs):
    *in_refs, out_ref = refs
    for j, ref in enumerate(in_refs):
        out_ref[j] = ref[1]


def regroup(messages):
    _, wide, width = messages[0].shape
    return call(regroup_kernel, shape(len(messages), wide, width), 1, "regroup")(*messages)


def values_kernel(chips, *refs):
    mine_refs = refs[:chips]
    other_ref, wv_ref, val_ref, rows_ref = refs[chips:]
    heads = wv_ref.shape[0]
    wide = other_ref.shape[1]
    for place in range(2 * chips):
        block = mine_refs[place][0] if place < chips else other_ref[place - chips]
        block = block.astype(jnp.float32)
        for c in range(PIECES):
            rows_ref[c, place * wide : (place + 1) * wide, :] = block[:, c * LANES : (c + 1) * LANES]
    count = val_ref.shape[0]
    for h in range(heads):
        chosen = jnp.concatenate(
            [rows_ref[c, pl.ds(h, count, stride=heads), :] for c in range(PIECES)], axis=-1
        )
        val_ref[:, h * VD : (h + 1) * VD] = jnp.dot(
            chosen.astype(jnp.bfloat16), wv_ref[h], preferred_element_type=jnp.float32
        ).astype(jnp.bfloat16)


def head_values(messages, other, w_uv):
    chips, wide, _ = other.shape
    heads = w_uv.shape[0]
    count = 2 * chips * wide // heads
    scratch = [pltpu.VMEM((PIECES, count * heads, LANES), jnp.float32)]
    kernel = functools.partial(values_kernel, chips)
    return call(kernel, shape(count, heads * VD), 3, "values", scratch)(
        *messages, other, resident(w_uv)
    )


def terms_kernel(start, val_ref, wo_ref, mine_ref, other_ref):
    half, width = mine_ref.shape
    terms = jnp.dot(
        val_ref[...], wo_ref[:, start : start + width], preferred_element_type=jnp.float32
    )
    mine_ref[...] = terms[:half]
    other_ref[...] = terms[half:].astype(jnp.bfloat16)


def output_terms(values, w_o, part):
    half = values.shape[0] // 2
    width = w_o.shape[1] // PARTS
    out = (shape(half, width, dtype=jnp.float32), shape(half, width))
    kernel = functools.partial(terms_kernel, part * width)
    return call(kernel, out, 6, "terms")(values, resident(w_o))


def far_z(devices):
    return [z for z in far_first(devices, Z1) if z > Z1]


def places(devices, chips):
    order = far_first(devices, 2)
    return [order.index(k) for k in chips]


def pick(total, rows, where):
    return jnp.concatenate([total[j * rows : (j + 1) * rows] for j in where], axis=0)


def first_sum_kernel(rows, keep, give, near, mine_ref, other_ref, keep_ref, give_ref, near_ref):
    total = mine_ref[...] + other_ref[...].astype(jnp.float32)
    keep_ref[...] = pick(total, rows, keep)
    give_ref[...] = pick(total, rows, give).astype(give_ref.dtype)
    near_ref[...] = pick(total, rows, near)


def last_part_kernel(rows, keep, give, near, mine_ref, other_ref, before_ref, *out_refs):
    keep_ref, give_ref, local_ref, pair_ref = out_refs
    total = mine_ref[...] + other_ref[...].astype(jnp.float32)
    keep_ref[...] = pick(total, rows, keep)
    give_ref[...] = pick(total, rows, give).astype(give_ref.dtype)
    here = pick(total, rows, near)
    half, width = local_ref.shape[0], before_ref.shape[1]
    for columns, block in ((slice(0, width), before_ref[...]), (slice(width, None), here)):
        local_ref[:, columns] = block[:half]
        pair_ref[:, columns] = block[half:].astype(pair_ref.dtype)


def core_sum(mine, other, before, rows, devices):
    count, width = mine.shape
    keep = places(devices, far_z(devices))
    give = places(devices, [z + Y for z in far_z(devices)])
    near = places(devices, [0, Y, Z1, Z1 + Y])
    far = len(keep) * rows
    out = (shape(far, width, dtype=jnp.float32), shape(far, width))
    if before is None:
        kernel = functools.partial(first_sum_kernel, rows, keep, give, near)
        out += (shape(4 * rows, width, dtype=jnp.float32),)
        return call(kernel, out, 1, "core_sum")(mine, other)
    kernel = functools.partial(last_part_kernel, rows, keep, give, near)
    full = before.shape[1] + width
    out += (shape(2 * rows, full, dtype=jnp.float32), shape(2 * rows, full))
    return call(kernel, out, 1, "core_sum")(mine, other, before)


def far_sum_kernel(*refs):
    mine_refs = refs[:PARTS]
    other_refs = refs[PARTS : 2 * PARTS]
    out_refs = refs[2 * PARTS :]
    rows = out_refs[0].shape[0]
    for p, (mine_ref, other_ref) in enumerate(zip(mine_refs, other_refs)):
        width = mine_ref.shape[1]
        total = mine_ref[...] + other_ref[...].astype(jnp.float32)
        for j, out_ref in enumerate(out_refs):
            out_ref[:, p * width : (p + 1) * width] = total[j * rows : (j + 1) * rows].astype(
                out_ref.dtype
            )


def far_sum(mine, other, rows):
    count, width = mine[0].shape
    out = [shape(rows, PARTS * width)] * (count // rows)
    return call(far_sum_kernel, out, 1, "far_sum")(*mine, *other)


def near_sum_kernel(mine_ref, other_ref, keep_ref, give_ref):
    total = mine_ref[...] + other_ref[...].astype(jnp.float32)
    rows = keep_ref.shape[0]
    keep_ref[...] = total[:rows]
    give_ref[...] = total[rows:].astype(give_ref.dtype)


def near_sum(mine, other):
    rows, width = mine.shape[0] // 2, mine.shape[1]
    out = (shape(rows, width, dtype=jnp.float32), shape(rows, width))
    return call(near_sum_kernel, out, 1, "near_sum")(mine, other)


def last_sum_kernel(*refs):
    *in_refs, out_ref = refs
    terms = [ref[...].astype(jnp.float32) for ref in in_refs]
    out_ref[...] = sum(terms[1:], terms[0]).astype(out_ref.dtype)


def last_sum(blocks):
    return call(last_sum_kernel, shape(*blocks[0].shape), 1, "last_sum")(*blocks)


def on_device(q_latent, new_latent, cache, lengths, w_uq, w_uk, w_uv, w_o, devices):
    heads = w_uk.shape[0]
    rows = cache.shape[0]
    order = far_first(devices, 2)
    zs = far_first(devices, 4)

    def swap(block, k):
        if k == 0:
            return block
        return lax.ppermute(block, "row", [(i, i ^ k) for i in range(devices)])

    far_weights = [swap(w_uq, 1), swap(w_uk, 1)]
    tables, near = join(rotary(lengths), [q_latent, swap(q_latent, 2)])
    messages = project([swap(near, z) for z in zs], [w_uq, w_uk, *far_weights], devices)
    messages = [swap(block, k) for k, block in zip(order, messages)]
    keys = jnp.swapaxes(cache, 1, 2)
    latents = attend(lengths, tables, keys, new_latent, messages, heads)
    latents = [swap(block, k) for k, block in zip(order, latents)]
    values = head_values(latents, swap(regroup(latents), 1), w_uv)
    keep, got, near = [], [], None
    for part in range(PARTS):
        mine, other = output_terms(values, w_o, part)
        far_mine, far_other, near, *pair = core_sum(mine, swap(other, 1), near, rows, devices)
        keep.append(far_mine)
        got.append(swap(far_other, Y))
    local, across = near_sum(near, swap(pair[0], Z1))
    far = far_sum(keep, got, rows)
    far = [swap(block, z) for z, block in zip(far_z(devices), far)]
    return last_sum([local, swap(across, Y), *far])


def solution(mesh):
    placed = (
        P(("grp", "row"), None),
        P(("grp", "row"), None),
        P(("grp", "row"), None, None),
        P(("grp", "row")),
        P(None, "row"),
        P("row", None, None),
        P("row", None, None),
        P("row", None),
    )
    body = functools.partial(on_device, devices=mesh.shape["row"])
    return jax.shard_map(
        body, mesh=mesh, in_specs=placed, out_specs=P(("grp", "row"), None), check_vma=False
    )
```

```python
import functools
import math

import jax
import jax.numpy as jnp
from jax import lax
from jax.experimental import pallas as pl
from jax.experimental.pallas import tpu as pltpu
from jax.sharding import PartitionSpec as P

LAT = 512
ROPE = 64
HALF = ROPE // 2
NOPE = 128
VD = 128
LANES = 128
PIECES = LAT // LANES
SCALE = (NOPE + ROPE) ** -0.5 * math.log2(math.e)
LIMIT = 16 * 2**20
PARTS = 2
Y = 2
Z1 = 4


def resident(x):
    return pltpu.with_memory_space_constraint(x, pltpu.VMEM)


def in_vmem():
    return pl.BlockSpec(memory_space=pltpu.VMEM)


def call(kernel, out_shape, microseconds, name, scratch=(), scalars=0):
    def run(*args):
        smem = [pl.BlockSpec(memory_space=pltpu.SMEM)] * scalars
        return pl.pallas_call(
            kernel,
            out_shape=out_shape,
            in_specs=smem + [in_vmem()] * (len(args) - scalars),
            out_specs=jax.tree.map(lambda _: in_vmem(), out_shape),
            scratch_shapes=list(scratch),
            compiler_params=pltpu.CompilerParams(vmem_limit_bytes=LIMIT),
            cost_estimate=pl.CostEstimate(
                flops=int(microseconds * 1.15e9), bytes_accessed=0, transcendentals=0
            ),
            name=name,
        )(*args)

    return run


def shape(*dims, dtype=jnp.bfloat16):
    return jax.ShapeDtypeStruct(dims, dtype)


def far_first(devices, step):
    return sorted(range(0, devices, step), key=lambda k: -k.bit_length())


def chip_order(devices):
    chips = far_first(devices, 2)
    far = chips[: len(chips) // 2]
    near = sorted(chips[len(chips) // 2 :])[1:]
    mixed = far[:1]
    for k, other in zip(far[1:], near):
        mixed += [k, other]
    return mixed + [0]


def gathered_order(devices):
    return [z + y for z in reversed(far_first(devices, 4)) for y in (0, 2)]


def rotary_kernel(len_ref, cos_ref, sin_ref):
    rows, width = cos_ref.shape
    lane = lax.broadcasted_iota(jnp.int32, (rows, width), 1)
    place = lax.broadcasted_iota(jnp.int32, (rows, width), 0)
    step = jnp.where(lane < HALF, lane, lane - HALF).astype(jnp.float32)
    frequency = jnp.exp(step * (-math.log(10000.0) / HALF))
    length = jnp.zeros((rows, width), jnp.float32)
    for r in range(rows):
        length = jnp.where(place == r, len_ref[r].astype(jnp.float32), length)
    angle = length * frequency
    sine = jnp.sin(angle)
    cos_ref[...] = jnp.cos(angle)
    sin_ref[...] = jnp.where(lane < HALF, -sine, sine)


def rotary(lengths):
    table = shape(lengths.shape[0], ROPE, dtype=jnp.float32)
    return call(rotary_kernel, (table, table), 3, "rotary", scalars=1)(lengths)


def join_kernel(cos_ref, sin_ref, *refs):
    *in_refs, cos_out_ref, sin_out_ref, out_ref = refs
    cos_out_ref[...] = cos_ref[...]
    sin_out_ref[...] = sin_ref[...]
    out_ref[...] = jnp.concatenate(
        [ref[...].astype(jnp.float32) for ref in in_refs], axis=0
    ).astype(out_ref.dtype)


def join(tables, blocks):
    rows, depth = blocks[0].shape
    out = (*[shape(*t.shape, dtype=t.dtype) for t in tables], shape(len(blocks) * rows, depth))
    cosine, sine, joined = call(join_kernel, out, 3, "join")(*tables, *blocks)
    return (cosine, sine), joined


def project_kernel(devices, *refs):
    pieces = devices // 4
    q_refs = refs[:pieces]
    weights = (refs[pieces : pieces + 2], refs[pieces + 2 : pieces + 4])
    lat_ref, rot_ref = refs[-2:]
    out_refs = refs[pieces + 4 : -2]
    heads = weights[0][1].shape[0]
    piece = jnp.concatenate([ref[...].astype(jnp.float32) for ref in q_refs], axis=0)
    piece = piece.astype(jnp.bfloat16)
    count = piece.shape[0]
    wide = 2 * count // devices * heads
    width = NOPE + ROPE
    lane = lax.broadcasted_iota(jnp.int32, (wide // 2, LANES), 1)
    order = chip_order(devices)
    for core, (wq_ref, wk_ref) in enumerate(weights):
        projected = jnp.dot(piece, wq_ref[...], preferred_element_type=jnp.float32)
        for h in range(heads):
            mine = projected[:, h * width : (h + 1) * width]
            absorbed = jnp.dot(
                mine[:, :NOPE].astype(jnp.bfloat16), wk_ref[h], preferred_element_type=jnp.float32
            )
            at = pl.ds(h, count, stride=heads)
            for c in range(PIECES):
                lat_ref[core * PIECES + c, at, :] = absorbed[:, c * LANES : (c + 1) * LANES]
            pe = mine[:, NOPE:]
            rot_ref[core, at, :] = jnp.concatenate([pe, pe], axis=-1)
        for place, k in enumerate(gathered_order(devices)):
            out_ref = out_refs[order.index(k)]
            first = place * wide
            for c in range(PIECES):
                out_ref[core, c * wide : (c + 1) * wide, :] = lat_ref[
                    core * PIECES + c, first : first + wide, :
                ].astype(jnp.bfloat16)
            low = rot_ref[core, first : first + wide // 2, :]
            high = rot_ref[core, first + wide // 2 : first + wide, :]
            out_ref[core, PIECES * wide :, :] = jnp.where(lane < ROPE, low, high).astype(
                jnp.bfloat16
            )


def project(pieces, weights, devices):
    heads = weights[1].shape[0]
    count = len(pieces) * pieces[0].shape[0]
    wide = 2 * count // devices * heads
    scratch = [
        pltpu.VMEM((2 * PIECES, count * heads, LANES), jnp.float32),
        pltpu.VMEM((2, count * heads, LANES), jnp.float32),
    ]
    out = [shape(2, PIECES * wide + wide // 2, LANES)] * (devices // 2)
    kernel = functools.partial(project_kernel, devices)
    return call(kernel, out, 20, "project", scratch)(*pieces, *[resident(w) for w in weights])


def flip_kernel(key_ref, after_ref, out_ref):
    for r in range(key_ref.shape[0]):
        out_ref[r] = key_ref[r, :LAT, :].T


def flip(keys, after):
    rows, _, maxlen = keys.shape
    return call(flip_kernel, shape(rows, maxlen, LAT), 4, "flip")(resident(keys), after)


def attend_kernel(chips, len_ref, cos_ref, sin_ref, key_ref, flip_ref, new_ref, *refs):
    q_refs = refs[:chips]
    out_refs = refs[chips:]
    rows, _, maxlen = key_ref.shape
    wide = out_refs[0].shape[1]
    heads = wide // rows

    def query_block(first):
        blocks = [
            ref[core, first : first + heads, :].astype(jnp.float32)
            for ref in q_refs
            for core in range(2)
        ]
        return jnp.concatenate(blocks, axis=0)

    for r in range(rows):
        latent = jnp.concatenate(
            [query_block(c * wide + r * heads) for c in range(PIECES)], axis=-1
        )
        pe = query_block(PIECES * wide + (r % (rows // 2)) * heads)
        side = r // (rows // 2) * ROPE
        pe = pe[:, side : side + ROPE]
        swapped = jnp.concatenate([pe[:, HALF:], pe[:, :HALF]], axis=-1)
        rotated = (pe * cos_ref[r : r + 1, :] + swapped * sin_ref[r : r + 1, :]).astype(jnp.bfloat16)
        newest = new_ref[r : r + 1, :].astype(jnp.float32)
        own = jnp.sum(latent * newest[:, :LAT], axis=-1, keepdims=True) + jnp.sum(
            rotated.astype(jnp.float32) * newest[:, LAT:], axis=-1, keepdims=True
        )
        scores = jnp.dot(
            latent.astype(jnp.bfloat16), key_ref[r, :LAT, :], preferred_element_type=jnp.float32
        )
        scores += jnp.dot(rotated, key_ref[r, LAT:, :], preferred_element_type=jnp.float32)
        position = lax.broadcasted_iota(jnp.int32, (1, maxlen), 1)
        scores = jnp.where(position < len_ref[r], scores, -jnp.inf)
        peak = jnp.maximum(jnp.max(scores, axis=-1, keepdims=True), own)
        expo = jnp.exp2((scores - peak) * SCALE)
        own_expo = jnp.exp2((own - peak) * SCALE)
        inverse = 1.0 / (jnp.sum(expo, axis=-1, keepdims=True) + own_expo)
        weights = (expo * inverse).astype(jnp.bfloat16)
        own_weight = (own_expo * inverse).astype(jnp.bfloat16).astype(jnp.float32)
        summed = jnp.dot(weights, flip_ref[r], preferred_element_type=jnp.float32)
        summed += own_weight * newest[:, :LAT]
        for k in range(2 * chips):
            out_refs[k // 2][k % 2, r * heads : (r + 1) * heads, :] = summed[
                k * heads : (k + 1) * heads, :
            ].astype(jnp.bfloat16)


def attend(lengths, tables, keys, flipped, new_latent, messages, heads):
    chips = len(messages)
    kernel = functools.partial(attend_kernel, chips)
    block = shape(2, keys.shape[0] * heads, LAT)
    return call(kernel, [block] * chips, 2 + chips, "attend", scalars=1)(
        lengths, *tables, resident(keys), resident(flipped), new_latent, *messages
    )


def regroup_kernel(*refs):
    *in_refs, out_ref = refs
    for j, ref in enumerate(in_refs):
        out_ref[j] = ref[1]


def regroup(messages):
    _, wide, width = messages[0].shape
    return call(regroup_kernel, shape(len(messages), wide, width), 1, "regroup")(*messages)


def values_kernel(chips, *refs):
    mine_refs = refs[:chips]
    other_ref, wv_ref, val_ref, rows_ref = refs[chips:]
    heads = wv_ref.shape[0]
    wide = other_ref.shape[1]
    for place in range(2 * chips):
        block = mine_refs[place][0] if place < chips else other_ref[place - chips]
        block = block.astype(jnp.float32)
        for c in range(PIECES):
            rows_ref[c, place * wide : (place + 1) * wide, :] = block[:, c * LANES : (c + 1) * LANES]
    count = val_ref.shape[0]
    for h in range(heads):
        chosen = jnp.concatenate(
            [rows_ref[c, pl.ds(h, count, stride=heads), :] for c in range(PIECES)], axis=-1
        )
        val_ref[:, h * VD : (h + 1) * VD] = jnp.dot(
            chosen.astype(jnp.bfloat16), wv_ref[h], preferred_element_type=jnp.float32
        ).astype(jnp.bfloat16)


def head_values(messages, other, w_uv):
    chips, wide, _ = other.shape
    heads = w_uv.shape[0]
    count = 2 * chips * wide // heads
    scratch = [pltpu.VMEM((PIECES, count * heads, LANES), jnp.float32)]
    kernel = functools.partial(values_kernel, chips)
    return call(kernel, shape(count, heads * VD), 3, "values", scratch)(
        *messages, other, resident(w_uv)
    )


def terms_kernel(start, val_ref, wo_ref, mine_ref, other_ref):
    half, width = mine_ref.shape
    terms = jnp.dot(
        val_ref[...], wo_ref[:, start : start + width], preferred_element_type=jnp.float32
    )
    mine_ref[...] = terms[:half]
    other_ref[...] = terms[half:].astype(jnp.bfloat16)


def output_terms(values, w_o, part):
    half = values.shape[0] // 2
    width = w_o.shape[1] // PARTS
    out = (shape(half, width, dtype=jnp.float32), shape(half, width))
    kernel = functools.partial(terms_kernel, part * width)
    return call(kernel, out, 6, "terms")(values, resident(w_o))


def far_z(devices):
    return [z for z in far_first(devices, Z1) if z > Z1]


def places(devices, chips):
    order = chip_order(devices)
    return [order.index(k) for k in chips]


def pick(total, rows, where):
    return jnp.concatenate([total[j * rows : (j + 1) * rows] for j in where], axis=0)


def first_sum_kernel(rows, keep, give, near, mine_ref, other_ref, keep_ref, give_ref, near_ref):
    total = mine_ref[...] + other_ref[...].astype(jnp.float32)
    keep_ref[...] = pick(total, rows, keep)
    give_ref[...] = pick(total, rows, give).astype(give_ref.dtype)
    near_ref[...] = pick(total, rows, near)


def last_part_kernel(rows, keep, give, near, mine_ref, other_ref, before_ref, *out_refs):
    keep_ref, give_ref, local_ref, pair_ref = out_refs
    total = mine_ref[...] + other_ref[...].astype(jnp.float32)
    keep_ref[...] = pick(total, rows, keep)
    give_ref[...] = pick(total, rows, give).astype(give_ref.dtype)
    here = pick(total, rows, near)
    half, width = local_ref.shape[0], before_ref.shape[1]
    for columns, block in ((slice(0, width), before_ref[...]), (slice(width, None), here)):
        local_ref[:, columns] = block[:half]
        pair_ref[:, columns] = block[half:].astype(pair_ref.dtype)


def core_sum(mine, other, before, rows, devices):
    count, width = mine.shape
    keep = places(devices, far_z(devices))
    give = places(devices, [z + Y for z in far_z(devices)])
    near = places(devices, [0, Y, Z1, Z1 + Y])
    far = len(keep) * rows
    out = (shape(far, width, dtype=jnp.float32), shape(far, width))
    if before is None:
        kernel = functools.partial(first_sum_kernel, rows, keep, give, near)
        out += (shape(4 * rows, width, dtype=jnp.float32),)
        return call(kernel, out, 1, "core_sum")(mine, other)
    kernel = functools.partial(last_part_kernel, rows, keep, give, near)
    full = before.shape[1] + width
    out += (shape(2 * rows, full, dtype=jnp.float32), shape(2 * rows, full))
    return call(kernel, out, 1, "core_sum")(mine, other, before)


def far_sum_kernel(*refs):
    mine_refs = refs[:PARTS]
    other_refs = refs[PARTS : 2 * PARTS]
    out_refs = refs[2 * PARTS :]
    rows = out_refs[0].shape[0]
    for p, (mine_ref, other_ref) in enumerate(zip(mine_refs, other_refs)):
        width = mine_ref.shape[1]
        total = mine_ref[...] + other_ref[...].astype(jnp.float32)
        for j, out_ref in enumerate(out_refs):
            out_ref[:, p * width : (p + 1) * width] = total[j * rows : (j + 1) * rows].astype(
                out_ref.dtype
            )


def far_sum(mine, other, rows):
    count, width = mine[0].shape
    out = [shape(rows, PARTS * width)] * (count // rows)
    return call(far_sum_kernel, out, 1, "far_sum")(*mine, *other)


def near_sum_kernel(mine_ref, other_ref, keep_ref, give_ref):
    total = mine_ref[...] + other_ref[...].astype(jnp.float32)
    rows = keep_ref.shape[0]
    keep_ref[...] = total[:rows]
    give_ref[...] = total[rows:].astype(give_ref.dtype)


def near_sum(mine, other):
    rows, width = mine.shape[0] // 2, mine.shape[1]
    out = (shape(rows, width, dtype=jnp.float32), shape(rows, width))
    return call(near_sum_kernel, out, 1, "near_sum")(mine, other)


def last_sum_kernel(*refs):
    *in_refs, out_ref = refs
    terms = [ref[...].astype(jnp.float32) for ref in in_refs]
    out_ref[...] = sum(terms[1:], terms[0]).astype(out_ref.dtype)


def last_sum(blocks):
    return call(last_sum_kernel, shape(*blocks[0].shape), 1, "last_sum")(*blocks)


def on_device(q_latent, new_latent, cache, lengths, w_uq, w_uk, w_uv, w_o, devices):
    heads = w_uk.shape[0]
    rows = cache.shape[0]
    order = chip_order(devices)
    zs = far_first(devices, 4)[::-1]

    def swap(block, k):
        if k == 0:
            return block
        return lax.ppermute(block, "row", [(i, i ^ k) for i in range(devices)])

    far_weights = [swap(w_uq, 1), swap(w_uk, 1)]
    tables, near = join(rotary(lengths), [q_latent, swap(q_latent, 2)])
    messages = project([swap(near, z) for z in zs], [w_uq, w_uk, *far_weights], devices)
    keys = jnp.swapaxes(cache, 1, 2)
    flipped = flip(keys, messages[-1])
    messages = [swap(block, k) for k, block in zip(order, messages)]
    latents = attend(lengths, tables, keys, flipped, new_latent, messages, heads)
    latents = [swap(block, k) for k, block in zip(order, latents)]
    values = head_values(latents, swap(regroup(latents), 1), w_uv)
    keep, got, near = [], [], None
    for part in range(PARTS):
        mine, other = output_terms(values, w_o, part)
        far_mine, far_other, near, *pair = core_sum(mine, swap(other, 1), near, rows, devices)
        keep.append(far_mine)
        got.append(swap(far_other, Y))
    local, across = near_sum(near, swap(pair[0], Z1))
    far = far_sum(keep, got, rows)
    far = [swap(block, z) for z, block in zip(far_z(devices), far)]
    return last_sum([local, swap(across, Y), *far])


def solution(mesh):
    placed = (
        P(("grp", "row"), None),
        P(("grp", "row"), None),
        P(("grp", "row"), None, None),
        P(("grp", "row")),
        P(None, "row"),
        P("row", None, None),
        P("row", None, None),
        P("row", None),
    )
    body = functools.partial(on_device, devices=mesh.shape["row"])
    return jax.shard_map(
        body, mesh=mesh, in_specs=placed, out_specs=P(("grp", "row"), None), check_vma=False
    )
```

```python
import functools
import math

import jax
import jax.numpy as jnp
from jax import lax
from jax.experimental import pallas as pl
from jax.experimental.pallas import tpu as pltpu
from jax.sharding import PartitionSpec as P

LAT = 512
ROPE = 64
HALF = ROPE // 2
NOPE = 128
VD = 128
LANES = 128
PIECES = LAT // LANES
SCALE = (NOPE + ROPE) ** -0.5 * math.log2(math.e)
LIMIT = 16 * 2**20
PARTS = 2
Y = 2
Z1 = 4


def resident(x):
    return pltpu.with_memory_space_constraint(x, pltpu.VMEM)


def in_vmem():
    return pl.BlockSpec(memory_space=pltpu.VMEM)


def call(kernel, out_shape, microseconds, name, scratch=(), scalars=0):
    def run(*args):
        smem = [pl.BlockSpec(memory_space=pltpu.SMEM)] * scalars
        return pl.pallas_call(
            kernel,
            out_shape=out_shape,
            in_specs=smem + [in_vmem()] * (len(args) - scalars),
            out_specs=jax.tree.map(lambda _: in_vmem(), out_shape),
            scratch_shapes=list(scratch),
            compiler_params=pltpu.CompilerParams(vmem_limit_bytes=LIMIT),
            cost_estimate=pl.CostEstimate(
                flops=int(microseconds * 1.15e9), bytes_accessed=0, transcendentals=0
            ),
            name=name,
        )(*args)

    return run


def shape(*dims, dtype=jnp.bfloat16):
    return jax.ShapeDtypeStruct(dims, dtype)


def mask(k):
    return k ^ (k.bit_count() & 1)


def far_first(devices, step):
    return sorted(range(0, devices, step), key=lambda k: -k.bit_length())


def chip_order(devices):
    chips = far_first(devices, 2)
    far = chips[: len(chips) // 2]
    near = sorted(chips[len(chips) // 2 :])[1:]
    mixed = far[:1]
    for k, other in zip(far[1:], near):
        mixed += [k, other]
    return mixed + [0]


def gathered_order(devices):
    return [z + y for z in reversed(far_first(devices, 4)) for y in (0, 2)]


def rotary_kernel(len_ref, cos_ref, sin_ref):
    rows, width = cos_ref.shape
    lane = lax.broadcasted_iota(jnp.int32, (rows, width), 1)
    place = lax.broadcasted_iota(jnp.int32, (rows, width), 0)
    step = jnp.where(lane < HALF, lane, lane - HALF).astype(jnp.float32)
    frequency = jnp.exp(step * (-math.log(10000.0) / HALF))
    length = jnp.zeros((rows, width), jnp.float32)
    for r in range(rows):
        length = jnp.where(place == r, len_ref[r].astype(jnp.float32), length)
    angle = length * frequency
    sine = jnp.sin(angle)
    cos_ref[...] = jnp.cos(angle)
    sin_ref[...] = jnp.where(lane < HALF, -sine, sine)


def rotary(lengths):
    table = shape(lengths.shape[0], ROPE, dtype=jnp.float32)
    return call(rotary_kernel, (table, table), 3, "rotary", scalars=1)(lengths)


def join_kernel(cos_ref, sin_ref, *refs):
    *in_refs, cos_out_ref, sin_out_ref, out_ref = refs
    cos_out_ref[...] = cos_ref[...]
    sin_out_ref[...] = sin_ref[...]
    out_ref[...] = jnp.concatenate(
        [ref[...].astype(jnp.float32) for ref in in_refs], axis=0
    ).astype(out_ref.dtype)


def join(tables, blocks):
    rows, depth = blocks[0].shape
    out = (*[shape(*t.shape, dtype=t.dtype) for t in tables], shape(len(blocks) * rows, depth))
    cosine, sine, joined = call(join_kernel, out, 3, "join")(*tables, *blocks)
    return (cosine, sine), joined


def project_kernel(devices, *refs):
    pieces = devices // 4
    q_refs = refs[:pieces]
    weights = (refs[pieces : pieces + 2], refs[pieces + 2 : pieces + 4])
    lat_ref, rot_ref = refs[-2:]
    out_refs = refs[pieces + 4 : -2]
    heads = weights[0][1].shape[0]
    piece = jnp.concatenate([ref[...].astype(jnp.float32) for ref in q_refs], axis=0)
    piece = piece.astype(jnp.bfloat16)
    count = piece.shape[0]
    wide = 2 * count // devices * heads
    width = NOPE + ROPE
    lane = lax.broadcasted_iota(jnp.int32, (wide // 2, LANES), 1)
    order = chip_order(devices)
    for core, (wq_ref, wk_ref) in enumerate(weights):
        projected = jnp.dot(piece, wq_ref[...], preferred_element_type=jnp.float32)
        for h in range(heads):
            mine = projected[:, h * width : (h + 1) * width]
            absorbed = jnp.dot(
                mine[:, :NOPE].astype(jnp.bfloat16), wk_ref[h], preferred_element_type=jnp.float32
            )
            at = pl.ds(h, count, stride=heads)
            for c in range(PIECES):
                lat_ref[core * PIECES + c, at, :] = absorbed[:, c * LANES : (c + 1) * LANES]
            pe = mine[:, NOPE:]
            rot_ref[core, at, :] = jnp.concatenate([pe, pe], axis=-1)
        for place, k in enumerate(gathered_order(devices)):
            out_ref = out_refs[order.index(k)]
            first = place * wide
            for c in range(PIECES):
                out_ref[core, c * wide : (c + 1) * wide, :] = lat_ref[
                    core * PIECES + c, first : first + wide, :
                ].astype(jnp.bfloat16)
            low = rot_ref[core, first : first + wide // 2, :]
            high = rot_ref[core, first + wide // 2 : first + wide, :]
            out_ref[core, PIECES * wide :, :] = jnp.where(lane < ROPE, low, high).astype(
                jnp.bfloat16
            )


def project(pieces, weights, devices):
    heads = weights[1].shape[0]
    count = len(pieces) * pieces[0].shape[0]
    wide = 2 * count // devices * heads
    scratch = [
        pltpu.VMEM((2 * PIECES, count * heads, LANES), jnp.float32),
        pltpu.VMEM((2, count * heads, LANES), jnp.float32),
    ]
    out = [shape(2, PIECES * wide + wide // 2, LANES)] * (devices // 2)
    kernel = functools.partial(project_kernel, devices)
    return call(kernel, out, 20, "project", scratch)(*pieces, *[resident(w) for w in weights])


def flip_kernel(key_ref, after_ref, out_ref):
    for r in range(key_ref.shape[0]):
        out_ref[r] = key_ref[r, :LAT, :].T


def flip(keys, after):
    rows, _, maxlen = keys.shape
    return call(flip_kernel, shape(rows, maxlen, LAT), 4, "flip")(resident(keys), after)


def attend_kernel(chips, len_ref, cos_ref, sin_ref, key_ref, flip_ref, new_ref, *refs):
    q_refs = refs[:chips]
    out_refs = refs[chips:]
    rows, _, maxlen = key_ref.shape
    wide = out_refs[0].shape[1]
    heads = wide // rows

    def query_block(first):
        blocks = [
            ref[core, first : first + heads, :].astype(jnp.float32)
            for ref in q_refs
            for core in range(2)
        ]
        return jnp.concatenate(blocks, axis=0)

    for r in range(rows):
        latent = jnp.concatenate(
            [query_block(c * wide + r * heads) for c in range(PIECES)], axis=-1
        )
        pe = query_block(PIECES * wide + (r % (rows // 2)) * heads)
        side = r // (rows // 2) * ROPE
        pe = pe[:, side : side + ROPE]
        swapped = jnp.concatenate([pe[:, HALF:], pe[:, :HALF]], axis=-1)
        rotated = (pe * cos_ref[r : r + 1, :] + swapped * sin_ref[r : r + 1, :]).astype(jnp.bfloat16)
        newest = new_ref[r : r + 1, :].astype(jnp.float32)
        own = jnp.sum(latent * newest[:, :LAT], axis=-1, keepdims=True) + jnp.sum(
            rotated.astype(jnp.float32) * newest[:, LAT:], axis=-1, keepdims=True
        )
        scores = jnp.dot(
            latent.astype(jnp.bfloat16), key_ref[r, :LAT, :], preferred_element_type=jnp.float32
        )
        scores += jnp.dot(rotated, key_ref[r, LAT:, :], preferred_element_type=jnp.float32)
        position = lax.broadcasted_iota(jnp.int32, (1, maxlen), 1)
        scores = jnp.where(position < len_ref[r], scores, -jnp.inf)
        peak = jnp.maximum(jnp.max(scores, axis=-1, keepdims=True), own)
        expo = jnp.exp2((scores - peak) * SCALE)
        own_expo = jnp.exp2((own - peak) * SCALE)
        inverse = 1.0 / (jnp.sum(expo, axis=-1, keepdims=True) + own_expo)
        weights = (expo * inverse).astype(jnp.bfloat16)
        own_weight = (own_expo * inverse).astype(jnp.bfloat16).astype(jnp.float32)
        summed = jnp.dot(weights, flip_ref[r], preferred_element_type=jnp.float32)
        summed += own_weight * newest[:, :LAT]
        for k in range(2 * chips):
            out_refs[k // 2][k % 2, r * heads : (r + 1) * heads, :] = summed[
                k * heads : (k + 1) * heads, :
            ].astype(jnp.bfloat16)


def attend(lengths, tables, keys, flipped, new_latent, messages, heads):
    chips = len(messages)
    kernel = functools.partial(attend_kernel, chips)
    block = shape(2, keys.shape[0] * heads, LAT)
    return call(kernel, [block] * chips, 2 + chips, "attend", scalars=1)(
        lengths, *tables, resident(keys), resident(flipped), new_latent, *messages
    )


def regroup_kernel(*refs):
    *in_refs, out_ref = refs
    for j, ref in enumerate(in_refs):
        out_ref[j] = ref[1]


def regroup(messages):
    _, wide, width = messages[0].shape
    return call(regroup_kernel, shape(len(messages), wide, width), 1, "regroup")(*messages)


def values_kernel(chips, *refs):
    mine_refs = refs[:chips]
    other_ref, wv_ref, val_ref, rows_ref = refs[chips:]
    heads = wv_ref.shape[0]
    wide = other_ref.shape[1]
    for place in range(2 * chips):
        block = mine_refs[place][0] if place < chips else other_ref[place - chips]
        block = block.astype(jnp.float32)
        for c in range(PIECES):
            rows_ref[c, place * wide : (place + 1) * wide, :] = block[:, c * LANES : (c + 1) * LANES]
    count = val_ref.shape[0]
    for h in range(heads):
        chosen = jnp.concatenate(
            [rows_ref[c, pl.ds(h, count, stride=heads), :] for c in range(PIECES)], axis=-1
        )
        val_ref[:, h * VD : (h + 1) * VD] = jnp.dot(
            chosen.astype(jnp.bfloat16), wv_ref[h], preferred_element_type=jnp.float32
        ).astype(jnp.bfloat16)


def head_values(messages, other, w_uv):
    chips, wide, _ = other.shape
    heads = w_uv.shape[0]
    count = 2 * chips * wide // heads
    scratch = [pltpu.VMEM((PIECES, count * heads, LANES), jnp.float32)]
    kernel = functools.partial(values_kernel, chips)
    return call(kernel, shape(count, heads * VD), 3, "values", scratch)(
        *messages, other, resident(w_uv)
    )


def terms_kernel(start, val_ref, wo_ref, mine_ref, other_ref):
    half, width = mine_ref.shape
    terms = jnp.dot(
        val_ref[...], wo_ref[:, start : start + width], preferred_element_type=jnp.float32
    )
    mine_ref[...] = terms[:half]
    other_ref[...] = terms[half:].astype(jnp.bfloat16)


def output_terms(values, w_o, part):
    half = values.shape[0] // 2
    width = w_o.shape[1] // PARTS
    out = (shape(half, width, dtype=jnp.float32), shape(half, width))
    kernel = functools.partial(terms_kernel, part * width)
    return call(kernel, out, 6, "terms")(values, resident(w_o))


def far_z(devices):
    return [z for z in far_first(devices, Z1) if z > Z1]


def places(devices, chips):
    order = chip_order(devices)
    return [order.index(k) for k in chips]


def pick(total, rows, where):
    return jnp.concatenate([total[j * rows : (j + 1) * rows] for j in where], axis=0)


def first_sum_kernel(rows, keep, give, near, mine_ref, other_ref, keep_ref, give_ref, near_ref):
    total = mine_ref[...] + other_ref[...].astype(jnp.float32)
    keep_ref[...] = pick(total, rows, keep)
    give_ref[...] = pick(total, rows, give).astype(give_ref.dtype)
    near_ref[...] = pick(total, rows, near)


def last_part_kernel(rows, keep, give, near, mine_ref, other_ref, before_ref, *out_refs):
    keep_ref, give_ref, local_ref, pair_ref = out_refs
    total = mine_ref[...] + other_ref[...].astype(jnp.float32)
    keep_ref[...] = pick(total, rows, keep)
    give_ref[...] = pick(total, rows, give).astype(give_ref.dtype)
    here = pick(total, rows, near)
    half, width = local_ref.shape[0], before_ref.shape[1]
    for columns, block in ((slice(0, width), before_ref[...]), (slice(width, None), here)):
        local_ref[:, columns] = block[:half]
        pair_ref[:, columns] = block[half:].astype(pair_ref.dtype)


def core_sum(mine, other, before, rows, devices):
    count, width = mine.shape
    keep = places(devices, far_z(devices))
    give = places(devices, [z + Y for z in far_z(devices)])
    near = places(devices, [0, Y, Z1, Z1 + Y])
    far = len(keep) * rows
    out = (shape(far, width, dtype=jnp.float32), shape(far, width))
    if before is None:
        kernel = functools.partial(first_sum_kernel, rows, keep, give, near)
        out += (shape(4 * rows, width, dtype=jnp.float32),)
        return call(kernel, out, 1, "core_sum")(mine, other)
    kernel = functools.partial(last_part_kernel, rows, keep, give, near)
    full = before.shape[1] + width
    out += (shape(2 * rows, full, dtype=jnp.float32), shape(2 * rows, full))
    return call(kernel, out, 1, "core_sum")(mine, other, before)


def far_sum_kernel(*refs):
    mine_refs = refs[:PARTS]
    other_refs = refs[PARTS : 2 * PARTS]
    out_refs = refs[2 * PARTS :]
    rows = out_refs[0].shape[0]
    for p, (mine_ref, other_ref) in enumerate(zip(mine_refs, other_refs)):
        width = mine_ref.shape[1]
        total = mine_ref[...] + other_ref[...].astype(jnp.float32)
        for j, out_ref in enumerate(out_refs):
            out_ref[:, p * width : (p + 1) * width] = total[j * rows : (j + 1) * rows].astype(
                out_ref.dtype
            )


def far_sum(mine, other, rows):
    count, width = mine[0].shape
    out = [shape(rows, PARTS * width)] * (count // rows)
    return call(far_sum_kernel, out, 1, "far_sum")(*mine, *other)


def near_sum_kernel(mine_ref, other_ref, keep_ref, give_ref):
    total = mine_ref[...] + other_ref[...].astype(jnp.float32)
    rows = keep_ref.shape[0]
    keep_ref[...] = total[:rows]
    give_ref[...] = total[rows:].astype(give_ref.dtype)


def near_sum(mine, other):
    rows, width = mine.shape[0] // 2, mine.shape[1]
    out = (shape(rows, width, dtype=jnp.float32), shape(rows, width))
    return call(near_sum_kernel, out, 1, "near_sum")(mine, other)


def last_sum_kernel(*refs):
    *in_refs, out_ref = refs
    terms = [ref[...].astype(jnp.float32) for ref in in_refs]
    out_ref[...] = sum(terms[1:], terms[0]).astype(out_ref.dtype)


def last_sum(blocks):
    return call(last_sum_kernel, shape(*blocks[0].shape), 1, "last_sum")(*blocks)


def on_device(q_latent, new_latent, cache, lengths, w_uq, w_uk, w_uv, w_o, devices):
    heads = w_uk.shape[0]
    rows = cache.shape[0]
    order = chip_order(devices)
    zs = far_first(devices, 4)[::-1]

    def swap(block, k):
        if k == 0:
            return block
        flip_bits = k if k == 1 else mask(k)
        return lax.ppermute(block, "row", [(i, i ^ flip_bits) for i in range(devices)])

    far_weights = [swap(w_uq, 1), swap(w_uk, 1)]
    tables, near = join(rotary(lengths), [q_latent, swap(q_latent, 2)])
    messages = project([swap(near, z) for z in zs], [w_uq, w_uk, *far_weights], devices)
    keys = jnp.swapaxes(cache, 1, 2)
    flipped = flip(keys, messages[-1])
    messages = [swap(block, k) for k, block in zip(order, messages)]
    latents = attend(lengths, tables, keys, flipped, new_latent, messages, heads)
    latents = [swap(block, k) for k, block in zip(order, latents)]
    values = head_values(latents, swap(regroup(latents), 1), w_uv)
    keep, got, near = [], [], None
    for part in range(PARTS):
        mine, other = output_terms(values, w_o, part)
        far_mine, far_other, near, *pair = core_sum(mine, swap(other, 1), near, rows, devices)
        keep.append(far_mine)
        got.append(swap(far_other, Y))
    local, across = near_sum(near, swap(pair[0], Z1))
    far = far_sum(keep, got, rows)
    far = [swap(block, z) for z, block in zip(far_z(devices), far)]
    return last_sum([local, swap(across, Y), *far])


def solution(mesh):
    placed = (
        P(("grp", "row"), None),
        P(("grp", "row"), None),
        P(("grp", "row"), None, None),
        P(("grp", "row")),
        P(None, "row"),
        P("row", None, None),
        P("row", None, None),
        P("row", None),
    )
    body = functools.partial(on_device, devices=mesh.shape["row"])
    return jax.shard_map(
        body, mesh=mesh, in_specs=placed, out_specs=P(("grp", "row"), None), check_vma=False
    )
```

```python
import functools
import math

import jax
import jax.numpy as jnp
from jax import lax
from jax.experimental import pallas as pl
from jax.experimental.pallas import tpu as pltpu
from jax.sharding import PartitionSpec as P

LAT = 512
ROPE = 64
HALF = ROPE // 2
NOPE = 128
VD = 128
LANES = 128
PIECES = LAT // LANES
SCALE = (NOPE + ROPE) ** -0.5 * math.log2(math.e)
LIMIT = 16 * 2**20
PARTS = 2
Y = 2
Z1 = 4


def resident(x):
    return pltpu.with_memory_space_constraint(x, pltpu.VMEM)


def in_vmem():
    return pl.BlockSpec(memory_space=pltpu.VMEM)


def call(kernel, out_shape, microseconds, name, scratch=(), scalars=0):
    def run(*args):
        smem = [pl.BlockSpec(memory_space=pltpu.SMEM)] * scalars
        return pl.pallas_call(
            kernel,
            out_shape=out_shape,
            in_specs=smem + [in_vmem()] * (len(args) - scalars),
            out_specs=jax.tree.map(lambda _: in_vmem(), out_shape),
            scratch_shapes=list(scratch),
            compiler_params=pltpu.CompilerParams(vmem_limit_bytes=LIMIT),
            cost_estimate=pl.CostEstimate(
                flops=int(microseconds * 1.15e9), bytes_accessed=0, transcendentals=0
            ),
            name=name,
        )(*args)

    return run


def shape(*dims, dtype=jnp.bfloat16):
    return jax.ShapeDtypeStruct(dims, dtype)


def mask(k):
    return k ^ (k.bit_count() & 1)


def far_first(devices, step):
    return sorted(range(0, devices, step), key=lambda k: -k.bit_length())


def far_chips(devices):
    return [k for k in far_first(devices, 2) if k > Y + Z1]


def chip_order(devices):
    return [*far_chips(devices), Y, Y + Z1, Z1, 0]


def message_sizes(devices):
    return [1] * len(far_chips(devices)) + [2, 1, 1]


def gathered_order(devices):
    return [z + y for z in reversed(far_first(devices, 4)) for y in (0, 2)]


def rotary_kernel(len_ref, cos_ref, sin_ref):
    rows, width = cos_ref.shape
    lane = lax.broadcasted_iota(jnp.int32, (rows, width), 1)
    place = lax.broadcasted_iota(jnp.int32, (rows, width), 0)
    step = jnp.where(lane < HALF, lane, lane - HALF).astype(jnp.float32)
    frequency = jnp.exp(step * (-math.log(10000.0) / HALF))
    length = jnp.zeros((rows, width), jnp.float32)
    for r in range(rows):
        length = jnp.where(place == r, len_ref[r].astype(jnp.float32), length)
    angle = length * frequency
    sine = jnp.sin(angle)
    cos_ref[...] = jnp.cos(angle)
    sin_ref[...] = jnp.where(lane < HALF, -sine, sine)


def rotary(lengths):
    table = shape(lengths.shape[0], ROPE, dtype=jnp.float32)
    return call(rotary_kernel, (table, table), 3, "rotary", scalars=1)(lengths)


def join_kernel(cos_ref, sin_ref, *refs):
    *in_refs, cos_out_ref, sin_out_ref, out_ref = refs
    cos_out_ref[...] = cos_ref[...]
    sin_out_ref[...] = sin_ref[...]
    out_ref[...] = jnp.concatenate(
        [ref[...].astype(jnp.float32) for ref in in_refs], axis=0
    ).astype(out_ref.dtype)


def join(tables, blocks):
    rows, depth = blocks[0].shape
    out = (*[shape(*t.shape, dtype=t.dtype) for t in tables], shape(len(blocks) * rows, depth))
    cosine, sine, joined = call(join_kernel, out, 3, "join")(*tables, *blocks)
    return (cosine, sine), joined


def project_kernel(devices, *refs):
    pieces = devices // 4
    q_refs = refs[:pieces]
    weights = (refs[pieces : pieces + 2], refs[pieces + 2 : pieces + 4])
    lat_ref, rot_ref = refs[-2:]
    out_refs = refs[pieces + 4 : -2]
    heads = weights[0][1].shape[0]
    piece = jnp.concatenate([ref[...].astype(jnp.float32) for ref in q_refs], axis=0)
    piece = piece.astype(jnp.bfloat16)
    count = piece.shape[0]
    wide = 2 * count // devices * heads
    width = NOPE + ROPE
    lane = lax.broadcasted_iota(jnp.int32, (wide // 2, LANES), 1)
    blocks = [(ref, 2 * i) for ref in out_refs for i in range(ref.shape[0] // 2)]
    blocks = dict(zip(chip_order(devices), blocks))
    for core, (wq_ref, wk_ref) in enumerate(weights):
        projected = jnp.dot(piece, wq_ref[...], preferred_element_type=jnp.float32)
        for h in range(heads):
            mine = projected[:, h * width : (h + 1) * width]
            absorbed = jnp.dot(
                mine[:, :NOPE].astype(jnp.bfloat16), wk_ref[h], preferred_element_type=jnp.float32
            )
            spread = pl.ds(h, count, stride=heads)
            for c in range(PIECES):
                lat_ref[core * PIECES + c, spread, :] = absorbed[:, c * LANES : (c + 1) * LANES]
            pe = mine[:, NOPE:]
            rot_ref[core, spread, :] = jnp.concatenate([pe, pe], axis=-1)
        for place, k in enumerate(gathered_order(devices)):
            out_ref, at = blocks[k]
            at += core
            first = place * wide
            for c in range(PIECES):
                out_ref[at, c * wide : (c + 1) * wide, :] = lat_ref[
                    core * PIECES + c, first : first + wide, :
                ].astype(jnp.bfloat16)
            low = rot_ref[core, first : first + wide // 2, :]
            high = rot_ref[core, first + wide // 2 : first + wide, :]
            out_ref[at, PIECES * wide :, :] = jnp.where(lane < ROPE, low, high).astype(
                jnp.bfloat16
            )


def project(pieces, weights, devices):
    heads = weights[1].shape[0]
    count = len(pieces) * pieces[0].shape[0]
    wide = 2 * count // devices * heads
    scratch = [
        pltpu.VMEM((2 * PIECES, count * heads, LANES), jnp.float32),
        pltpu.VMEM((2, count * heads, LANES), jnp.float32),
    ]
    tall = PIECES * wide + wide // 2
    out = [shape(2 * size, tall, LANES) for size in message_sizes(devices)]
    kernel = functools.partial(project_kernel, devices)
    return call(kernel, out, 20, "project", scratch)(*pieces, *[resident(w) for w in weights])


def flip_kernel(key_ref, after_ref, out_ref):
    for r in range(key_ref.shape[0]):
        out_ref[r] = key_ref[r, :LAT, :].T


def flip(keys, after):
    rows, _, maxlen = keys.shape
    return call(flip_kernel, shape(rows, maxlen, LAT), 4, "flip")(resident(keys), after)


def forward_kernel(own_ref, passing_ref, out_ref):
    out_ref[:2] = own_ref[...]
    out_ref[2:] = passing_ref[2:]


def forward(own, passing):
    return call(forward_kernel, shape(4, *own.shape[1:]), 1, "forward")(own, passing)


def arrived(refs):
    blocks = []
    for i, ref in enumerate(refs):
        count = 2 if i == len(refs) - 3 else ref.shape[0]
        blocks += [(ref, core) for core in range(count)]
    return blocks


def attend_kernel(sizes, len_ref, cos_ref, sin_ref, key_ref, flip_ref, new_ref, *refs):
    blocks = arrived(refs[: len(sizes)])
    out_refs = refs[len(sizes) :]
    rows, _, maxlen = key_ref.shape
    wide = out_refs[0].shape[1]
    heads = wide // rows

    def query_block(first):
        parts = [ref[i, first : first + heads, :].astype(jnp.float32) for ref, i in blocks]
        return jnp.concatenate(parts, axis=0)

    def score(r):
        latent = jnp.concatenate(
            [query_block(c * wide + r * heads) for c in range(PIECES)], axis=-1
        )
        pe = query_block(PIECES * wide + (r % (rows // 2)) * heads)
        side = r // (rows // 2) * ROPE
        pe = pe[:, side : side + ROPE]
        swapped = jnp.concatenate([pe[:, HALF:], pe[:, :HALF]], axis=-1)
        rotated = (pe * cos_ref[r : r + 1, :] + swapped * sin_ref[r : r + 1, :]).astype(jnp.bfloat16)
        newest = new_ref[r : r + 1, :].astype(jnp.float32)
        own = jnp.sum(latent * newest[:, :LAT], axis=-1, keepdims=True) + jnp.sum(
            rotated.astype(jnp.float32) * newest[:, LAT:], axis=-1, keepdims=True
        )
        scores = jnp.dot(
            latent.astype(jnp.bfloat16), key_ref[r, :LAT, :], preferred_element_type=jnp.float32
        )
        scores += jnp.dot(rotated, key_ref[r, LAT:, :], preferred_element_type=jnp.float32)
        position = lax.broadcasted_iota(jnp.int32, (1, maxlen), 1)
        return jnp.where(position < len_ref[r], scores, -jnp.inf), own

    back = [(ref, i) for ref in out_refs for i in range(ref.shape[0])]
    y_at = len(back) - 8
    back = back[: y_at + 2] + back[y_at + 4 : y_at + 6] + back[y_at + 2 : y_at + 4] + back[-2:]
    ahead = score(0)
    for r in range(rows):
        scores, own = ahead
        if r + 1 < rows:
            ahead = score(r + 1)
        peak = jnp.maximum(jnp.max(scores, axis=-1, keepdims=True), own)
        expo = jnp.exp2((scores - peak) * SCALE)
        own_expo = jnp.exp2((own - peak) * SCALE)
        inverse = 1.0 / (jnp.sum(expo, axis=-1, keepdims=True) + own_expo)
        weights = (expo * inverse).astype(jnp.bfloat16)
        own_weight = (own_expo * inverse).astype(jnp.bfloat16).astype(jnp.float32)
        summed = jnp.dot(weights, flip_ref[r], preferred_element_type=jnp.float32)
        summed += own_weight * new_ref[r : r + 1, :LAT].astype(jnp.float32)
        for k, (out_ref, i) in enumerate(back):
            out_ref[i, r * heads : (r + 1) * heads, :] = summed[
                k * heads : (k + 1) * heads, :
            ].astype(jnp.bfloat16)


def attend(lengths, tables, keys, flipped, new_latent, messages, heads, devices):
    sizes = message_sizes(devices)
    out = [shape(2 * size, keys.shape[0] * heads, LAT) for size in sizes]
    return call(functools.partial(attend_kernel, sizes), out, 10, "attend", scalars=1)(
        lengths, *tables, resident(keys), resident(flipped), new_latent, *messages
    )


def early_kernel(passing_ref, own_ref, after_ref, out_ref):
    out_ref[0] = passing_ref[1]
    out_ref[1] = own_ref[1]


def early(passing, own, after):
    return call(early_kernel, shape(2, *own.shape[1:]), 4, "early")(passing, own, after)


def regroup_kernel(*refs):
    *in_refs, early_ref, out_ref = refs
    blocks = arrived(in_refs)[1::2]
    blocks = [*blocks[:-4], (early_ref, 0), *blocks[-3:-1], (early_ref, 1)]
    for j, (ref, i) in enumerate(blocks):
        out_ref[j] = ref[i]


def regroup(messages, ready, chips):
    _, wide, width = messages[0].shape
    return call(regroup_kernel, shape(chips, wide, width), 1, "regroup")(*messages, ready)


def values_kernel(*refs):
    *in_refs, other_ref, wv_ref, val_ref, rows_ref = refs
    mine = arrived(in_refs)[::2]
    chips = len(mine)
    heads = wv_ref.shape[0]
    wide = other_ref.shape[1]
    for place in range(2 * chips):
        ref, i = mine[place] if place < chips else (other_ref, place - chips)
        block = ref[i].astype(jnp.float32)
        for c in range(PIECES):
            rows_ref[c, place * wide : (place + 1) * wide, :] = block[:, c * LANES : (c + 1) * LANES]
    count = val_ref.shape[0]
    for h in range(heads):
        chosen = jnp.concatenate(
            [rows_ref[c, pl.ds(h, count, stride=heads), :] for c in range(PIECES)], axis=-1
        )
        val_ref[:, h * VD : (h + 1) * VD] = jnp.dot(
            chosen.astype(jnp.bfloat16), wv_ref[h], preferred_element_type=jnp.float32
        ).astype(jnp.bfloat16)


def head_values(messages, other, w_uv):
    chips, wide, _ = other.shape
    heads = w_uv.shape[0]
    count = 2 * chips * wide // heads
    scratch = [pltpu.VMEM((PIECES, count * heads, LANES), jnp.float32)]
    return call(values_kernel, shape(count, heads * VD), 3, "values", scratch)(
        *messages, other, resident(w_uv)
    )


def terms_kernel(start, val_ref, wo_ref, mine_ref, other_ref):
    half, width = mine_ref.shape
    terms = jnp.dot(
        val_ref[...], wo_ref[:, start : start + width], preferred_element_type=jnp.float32
    )
    mine_ref[...] = terms[:half]
    other_ref[...] = terms[half:].astype(jnp.bfloat16)


def output_terms(values, w_o, part):
    half = values.shape[0] // 2
    width = w_o.shape[1] // PARTS
    out = (shape(half, width, dtype=jnp.float32), shape(half, width))
    kernel = functools.partial(terms_kernel, part * width)
    return call(kernel, out, 6, "terms")(values, resident(w_o))


def far_z(devices):
    return [z for z in far_first(devices, Z1) if z > Z1]


def places(devices, chips):
    order = [*far_chips(devices), Y, Z1, Y + Z1, 0]
    return [order.index(k) for k in chips]


def pick(total, rows, where):
    return jnp.concatenate([total[j * rows : (j + 1) * rows] for j in where], axis=0)


def first_sum_kernel(rows, keep, give, near, mine_ref, other_ref, keep_ref, give_ref, near_ref):
    total = mine_ref[...] + other_ref[...].astype(jnp.float32)
    keep_ref[...] = pick(total, rows, keep)
    give_ref[...] = pick(total, rows, give).astype(give_ref.dtype)
    near_ref[...] = pick(total, rows, near)


def last_part_kernel(rows, keep, give, near, mine_ref, other_ref, before_ref, *out_refs):
    keep_ref, give_ref, local_ref, pair_ref = out_refs
    total = mine_ref[...] + other_ref[...].astype(jnp.float32)
    keep_ref[...] = pick(total, rows, keep)
    give_ref[...] = pick(total, rows, give).astype(give_ref.dtype)
    here = pick(total, rows, near)
    half, width = local_ref.shape[0], before_ref.shape[1]
    for columns, block in ((slice(0, width), before_ref[...]), (slice(width, None), here)):
        local_ref[:, columns] = block[:half]
        pair_ref[:, columns] = block[half:].astype(pair_ref.dtype)


def core_sum(mine, other, before, rows, devices):
    count, width = mine.shape
    keep = places(devices, far_z(devices))
    give = places(devices, [z + Y for z in far_z(devices)])
    near = places(devices, [0, Y, Z1, Z1 + Y])
    far = len(keep) * rows
    out = (shape(far, width, dtype=jnp.float32), shape(far, width))
    if before is None:
        kernel = functools.partial(first_sum_kernel, rows, keep, give, near)
        out += (shape(4 * rows, width, dtype=jnp.float32),)
        return call(kernel, out, 1, "core_sum")(mine, other)
    kernel = functools.partial(last_part_kernel, rows, keep, give, near)
    full = before.shape[1] + width
    out += (shape(2 * rows, full, dtype=jnp.float32), shape(2 * rows, full))
    return call(kernel, out, 1, "core_sum")(mine, other, before)


def far_sum_kernel(*refs):
    mine_refs = refs[:PARTS]
    other_refs = refs[PARTS : 2 * PARTS]
    out_refs = refs[2 * PARTS :]
    rows = out_refs[0].shape[0]
    for p, (mine_ref, other_ref) in enumerate(zip(mine_refs, other_refs)):
        width = mine_ref.shape[1]
        total = mine_ref[...] + other_ref[...].astype(jnp.float32)
        for j, out_ref in enumerate(out_refs):
            out_ref[:, p * width : (p + 1) * width] = total[j * rows : (j + 1) * rows].astype(
                out_ref.dtype
            )


def far_sum(mine, other, rows):
    count, width = mine[0].shape
    out = [shape(rows, PARTS * width)] * (count // rows)
    return call(far_sum_kernel, out, 1, "far_sum")(*mine, *other)


def near_sum_kernel(mine_ref, other_ref, keep_ref, give_ref):
    total = mine_ref[...] + other_ref[...].astype(jnp.float32)
    rows = keep_ref.shape[0]
    keep_ref[...] = total[:rows]
    give_ref[...] = total[rows:].astype(give_ref.dtype)


def near_sum(mine, other):
    rows, width = mine.shape[0] // 2, mine.shape[1]
    out = (shape(rows, width, dtype=jnp.float32), shape(rows, width))
    return call(near_sum_kernel, out, 1, "near_sum")(mine, other)


def last_sum_kernel(*refs):
    *in_refs, out_ref = refs
    terms = [ref[...].astype(jnp.float32) for ref in in_refs]
    out_ref[...] = sum(terms[1:], terms[0]).astype(out_ref.dtype)


def last_sum(blocks):
    return call(last_sum_kernel, shape(*blocks[0].shape), 1, "last_sum")(*blocks)


def on_device(q_latent, new_latent, cache, lengths, w_uq, w_uk, w_uv, w_o, devices):
    heads = w_uk.shape[0]
    rows = cache.shape[0]
    zs = far_first(devices, 4)[::-1]

    def swap(block, k):
        if k == 0:
            return block
        flip_bits = k if k == 1 else mask(k)
        return lax.ppermute(block, "row", [(i, i ^ flip_bits) for i in range(devices)])

    far_weights = [swap(w_uq, 1), swap(w_uk, 1)]
    tables, near = join(rotary(lengths), [q_latent, swap(q_latent, 2)])
    def exchange(messages):
        *far, across, pair, own = messages
        early = len(far) // 2
        got = [swap(block, k) for block, k in zip(far[:early], far_k)]
        passing = swap(across, Y)
        got += [swap(block, k) for block, k in zip(far[early:], far_k[early:])]
        sent = forward(pair, passing)
        return [*got, passing, swap(sent, Z1), own], sent

    far_k = far_chips(devices)
    messages = project([swap(near, z) for z in zs], [w_uq, w_uk, *far_weights], devices)
    messages, sent = exchange(messages)
    keys = jnp.swapaxes(cache, 1, 2)
    flipped = flip(keys, sent)
    latents = attend(lengths, tables, keys, flipped, new_latent, messages, heads, devices)
    latents, sent = exchange(latents)
    ready = early(latents[-3], latents[-1], sent)
    values = head_values(latents, swap(regroup(latents, ready, devices // 2), 1), w_uv)
    keep, got, near = [], [], None
    for part in range(PARTS):
        mine, other = output_terms(values, w_o, part)
        far_mine, far_other, near, *pair = core_sum(mine, swap(other, 1), near, rows, devices)
        keep.append(far_mine)
        got.append(swap(far_other, Y))
    local, across = near_sum(near, swap(pair[0], Z1))
    far = far_sum(keep, got, rows)
    far = [swap(block, z) for z, block in zip(far_z(devices), far)]
    return last_sum([local, swap(across, Y), *far])


def solution(mesh):
    placed = (
        P(("grp", "row"), None),
        P(("grp", "row"), None),
        P(("grp", "row"), None, None),
        P(("grp", "row")),
        P(None, "row"),
        P("row", None, None),
        P("row", None, None),
        P("row", None),
    )
    body = functools.partial(on_device, devices=mesh.shape["row"])
    return jax.shard_map(
        body, mesh=mesh, in_specs=placed, out_specs=P(("grp", "row"), None), check_vma=False
    )
```

```python
import functools
import math

import jax
import jax.numpy as jnp
from jax import lax
from jax.experimental import pallas as pl
from jax.experimental.pallas import tpu as pltpu
from jax.sharding import PartitionSpec as P

LAT = 512
ROPE = 64
HALF = ROPE // 2
NOPE = 128
VD = 128
LANES = 128
PIECES = LAT // LANES
SCALE = (NOPE + ROPE) ** -0.5 * math.log2(math.e)
LIMIT = 16 * 2**20
PARTS = 2
Y = 2
Z1 = 4


def resident(x):
    return pltpu.with_memory_space_constraint(x, pltpu.VMEM)


def in_vmem():
    return pl.BlockSpec(memory_space=pltpu.VMEM)


def call(kernel, out_shape, microseconds, name, scratch=(), scalars=0):
    def run(*args):
        smem = [pl.BlockSpec(memory_space=pltpu.SMEM)] * scalars
        return pl.pallas_call(
            kernel,
            out_shape=out_shape,
            in_specs=smem + [in_vmem()] * (len(args) - scalars),
            out_specs=jax.tree.map(lambda _: in_vmem(), out_shape),
            scratch_shapes=list(scratch),
            compiler_params=pltpu.CompilerParams(vmem_limit_bytes=LIMIT),
            cost_estimate=pl.CostEstimate(
                flops=int(microseconds * 1.15e9), bytes_accessed=0, transcendentals=0
            ),
            name=name,
        )(*args)

    return run


def shape(*dims, dtype=jnp.bfloat16):
    return jax.ShapeDtypeStruct(dims, dtype)


def far_first(devices, step):
    return sorted(range(0, devices, step), key=lambda k: -k.bit_length())


def far_chips(devices):
    return [k for k in far_first(devices, 2) if k > Y + Z1]


def chip_order(devices):
    return [*far_chips(devices), Y, Y + Z1, Z1, 0]


def message_sizes(devices):
    return [1] * len(far_chips(devices)) + [2, 1, 1]


def gathered_order(devices):
    return [z + y for z in reversed(far_first(devices, 4)) for y in (0, 2)]


def rotary_kernel(len_ref, cos_ref, sin_ref):
    rows, width = cos_ref.shape
    lane = lax.broadcasted_iota(jnp.int32, (rows, width), 1)
    place = lax.broadcasted_iota(jnp.int32, (rows, width), 0)
    step = jnp.where(lane < HALF, lane, lane - HALF).astype(jnp.float32)
    frequency = jnp.exp(step * (-math.log(10000.0) / HALF))
    length = jnp.zeros((rows, width), jnp.float32)
    for r in range(rows):
        length = jnp.where(place == r, len_ref[r].astype(jnp.float32), length)
    angle = length * frequency
    sine = jnp.sin(angle)
    cos_ref[...] = jnp.cos(angle)
    sin_ref[...] = jnp.where(lane < HALF, -sine, sine)


def rotary(lengths):
    table = shape(lengths.shape[0], ROPE, dtype=jnp.float32)
    return call(rotary_kernel, (table, table), 3, "rotary", scalars=1)(lengths)


def join_kernel(cos_ref, sin_ref, *refs):
    *in_refs, cos_out_ref, sin_out_ref, out_ref = refs
    cos_out_ref[...] = cos_ref[...]
    sin_out_ref[...] = sin_ref[...]
    out_ref[...] = jnp.concatenate(
        [ref[...].astype(jnp.float32) for ref in in_refs], axis=0
    ).astype(out_ref.dtype)


def join(tables, blocks):
    rows, depth = blocks[0].shape
    out = (*[shape(*t.shape, dtype=t.dtype) for t in tables], shape(len(blocks) * rows, depth))
    cosine, sine, joined = call(join_kernel, out, 3, "join")(*tables, *blocks)
    return (cosine, sine), joined


def project_kernel(devices, *refs):
    pieces = devices // 4
    q_refs = refs[:pieces]
    weights = (refs[pieces : pieces + 2], refs[pieces + 2 : pieces + 4])
    lat_ref, rot_ref = refs[-2:]
    out_refs = refs[pieces + 4 : -2]
    heads = weights[0][1].shape[0]
    piece = jnp.concatenate([ref[...].astype(jnp.float32) for ref in q_refs], axis=0)
    piece = piece.astype(jnp.bfloat16)
    count = piece.shape[0]
    wide = 2 * count // devices * heads
    width = NOPE + ROPE
    lane = lax.broadcasted_iota(jnp.int32, (wide // 2, LANES), 1)
    blocks = [(ref, 2 * i) for ref in out_refs for i in range(ref.shape[0] // 2)]
    blocks = dict(zip(chip_order(devices), blocks))
    for core, (wq_ref, wk_ref) in enumerate(weights):
        projected = jnp.dot(piece, wq_ref[...], preferred_element_type=jnp.float32)
        for h in range(heads):
            mine = projected[:, h * width : (h + 1) * width]
            absorbed = jnp.dot(
                mine[:, :NOPE].astype(jnp.bfloat16), wk_ref[h], preferred_element_type=jnp.float32
            )
            spread = pl.ds(h, count, stride=heads)
            for c in range(PIECES):
                lat_ref[core * PIECES + c, spread, :] = absorbed[:, c * LANES : (c + 1) * LANES]
            pe = mine[:, NOPE:]
            rot_ref[core, spread, :] = jnp.concatenate([pe, pe], axis=-1)
        for place, k in enumerate(gathered_order(devices)):
            out_ref, at = blocks[k]
            at += core
            first = place * wide
            for c in range(PIECES):
                out_ref[at, c * wide : (c + 1) * wide, :] = lat_ref[
                    core * PIECES + c, first : first + wide, :
                ].astype(jnp.bfloat16)
            low = rot_ref[core, first : first + wide // 2, :]
            high = rot_ref[core, first + wide // 2 : first + wide, :]
            out_ref[at, PIECES * wide :, :] = jnp.where(lane < ROPE, low, high).astype(
                jnp.bfloat16
            )


def project(pieces, weights, devices):
    heads = weights[1].shape[0]
    count = len(pieces) * pieces[0].shape[0]
    wide = 2 * count // devices * heads
    scratch = [
        pltpu.VMEM((2 * PIECES, count * heads, LANES), jnp.float32),
        pltpu.VMEM((2, count * heads, LANES), jnp.float32),
    ]
    tall = PIECES * wide + wide // 2
    out = [shape(2 * size, tall, LANES) for size in message_sizes(devices)]
    kernel = functools.partial(project_kernel, devices)
    return call(kernel, out, 20, "project", scratch)(*pieces, *[resident(w) for w in weights])


def flip_kernel(key_ref, after_ref, out_ref):
    for r in range(key_ref.shape[0]):
        out_ref[r] = key_ref[r, :LAT, :].T


def flip(keys, after):
    rows, _, maxlen = keys.shape
    return call(flip_kernel, shape(rows, maxlen, LAT), 4, "flip")(resident(keys), after)


def forward_kernel(own_ref, passing_ref, out_ref):
    out_ref[:2] = own_ref[...]
    out_ref[2:] = passing_ref[2:]


def forward(own, passing):
    return call(forward_kernel, shape(4, *own.shape[1:]), 1, "forward")(own, passing)


def arrived(refs):
    blocks = []
    for i, ref in enumerate(refs):
        count = 2 if i == len(refs) - 3 else ref.shape[0]
        blocks += [(ref, core) for core in range(count)]
    return blocks


def attend_kernel(sizes, len_ref, cos_ref, sin_ref, key_ref, flip_ref, new_ref, *refs):
    blocks = arrived(refs[: len(sizes)])
    out_refs = refs[len(sizes) :]
    rows, _, maxlen = key_ref.shape
    wide = out_refs[0].shape[1]
    heads = wide // rows

    def query_block(first):
        parts = [ref[i, first : first + heads, :].astype(jnp.float32) for ref, i in blocks]
        return jnp.concatenate(parts, axis=0)

    def score(r):
        latent = jnp.concatenate(
            [query_block(c * wide + r * heads) for c in range(PIECES)], axis=-1
        )
        pe = query_block(PIECES * wide + (r % (rows // 2)) * heads)
        side = r // (rows // 2) * ROPE
        pe = pe[:, side : side + ROPE]
        swapped = jnp.concatenate([pe[:, HALF:], pe[:, :HALF]], axis=-1)
        rotated = (pe * cos_ref[r : r + 1, :] + swapped * sin_ref[r : r + 1, :]).astype(jnp.bfloat16)
        newest = new_ref[r : r + 1, :].astype(jnp.float32)
        own = jnp.sum(latent * newest[:, :LAT], axis=-1, keepdims=True) + jnp.sum(
            rotated.astype(jnp.float32) * newest[:, LAT:], axis=-1, keepdims=True
        )
        scores = jnp.dot(
            latent.astype(jnp.bfloat16), key_ref[r, :LAT, :], preferred_element_type=jnp.float32
        )
        scores += jnp.dot(rotated, key_ref[r, LAT:, :], preferred_element_type=jnp.float32)
        position = lax.broadcasted_iota(jnp.int32, (1, maxlen), 1)
        return jnp.where(position < len_ref[r], scores, -jnp.inf), own

    back = [(ref, i) for ref in out_refs for i in range(ref.shape[0])]
    y_at = len(back) - 8
    back = back[: y_at + 2] + back[y_at + 4 : y_at + 6] + back[y_at + 2 : y_at + 4] + back[-2:]
    ahead = score(0)
    for r in range(rows):
        scores, own = ahead
        if r + 1 < rows:
            ahead = score(r + 1)
        peak = jnp.maximum(jnp.max(scores, axis=-1, keepdims=True), own)
        expo = jnp.exp2((scores - peak) * SCALE)
        own_expo = jnp.exp2((own - peak) * SCALE)
        inverse = 1.0 / (jnp.sum(expo, axis=-1, keepdims=True) + own_expo)
        weights = (expo * inverse).astype(jnp.bfloat16)
        own_weight = (own_expo * inverse).astype(jnp.bfloat16).astype(jnp.float32)
        summed = jnp.dot(weights, flip_ref[r], preferred_element_type=jnp.float32)
        summed += own_weight * new_ref[r : r + 1, :LAT].astype(jnp.float32)
        for k, (out_ref, i) in enumerate(back):
            out_ref[i, r * heads : (r + 1) * heads, :] = summed[
                k * heads : (k + 1) * heads, :
            ].astype(jnp.bfloat16)


def attend(lengths, tables, keys, flipped, new_latent, messages, heads, devices):
    sizes = message_sizes(devices)
    out = [shape(2 * size, keys.shape[0] * heads, LAT) for size in sizes]
    return call(functools.partial(attend_kernel, sizes), out, 10, "attend", scalars=1)(
        lengths, *tables, resident(keys), resident(flipped), new_latent, *messages
    )


def early_kernel(passing_ref, own_ref, after_ref, out_ref):
    out_ref[0] = passing_ref[1]
    out_ref[1] = own_ref[1]


def early(passing, own, after):
    return call(early_kernel, shape(2, *own.shape[1:]), 4, "early")(passing, own, after)


def regroup_kernel(*refs):
    *in_refs, early_ref, out_ref = refs
    blocks = arrived(in_refs)[1::2]
    blocks = [*blocks[:-4], (early_ref, 0), *blocks[-3:-1], (early_ref, 1)]
    for j, (ref, i) in enumerate(blocks):
        out_ref[j] = ref[i]


def regroup(messages, ready, chips):
    _, wide, width = messages[0].shape
    return call(regroup_kernel, shape(chips, wide, width), 1, "regroup")(*messages, ready)


def values_kernel(*refs):
    *in_refs, other_ref, wv_ref, val_ref, rows_ref = refs
    mine = arrived(in_refs)[::2]
    chips = len(mine)
    heads = wv_ref.shape[0]
    wide = other_ref.shape[1]
    for place in range(2 * chips):
        ref, i = mine[place] if place < chips else (other_ref, place - chips)
        block = ref[i].astype(jnp.float32)
        for c in range(PIECES):
            rows_ref[c, place * wide : (place + 1) * wide, :] = block[:, c * LANES : (c + 1) * LANES]
    count = val_ref.shape[0]
    for h in range(heads):
        chosen = jnp.concatenate(
            [rows_ref[c, pl.ds(h, count, stride=heads), :] for c in range(PIECES)], axis=-1
        )
        val_ref[:, h * VD : (h + 1) * VD] = jnp.dot(
            chosen.astype(jnp.bfloat16), wv_ref[h], preferred_element_type=jnp.float32
        ).astype(jnp.bfloat16)


def head_values(messages, other, w_uv):
    chips, wide, _ = other.shape
    heads = w_uv.shape[0]
    count = 2 * chips * wide // heads
    scratch = [pltpu.VMEM((PIECES, count * heads, LANES), jnp.float32)]
    return call(values_kernel, shape(count, heads * VD), 3, "values", scratch)(
        *messages, other, resident(w_uv)
    )


def terms_kernel(start, val_ref, wo_ref, mine_ref, other_ref):
    half, width = mine_ref.shape
    terms = jnp.dot(
        val_ref[...], wo_ref[:, start : start + width], preferred_element_type=jnp.float32
    )
    mine_ref[...] = terms[:half]
    other_ref[...] = terms[half:].astype(jnp.bfloat16)


def output_terms(values, w_o, part):
    half = values.shape[0] // 2
    width = w_o.shape[1] // PARTS
    out = (shape(half, width, dtype=jnp.float32), shape(half, width))
    kernel = functools.partial(terms_kernel, part * width)
    return call(kernel, out, 6, "terms")(values, resident(w_o))


def far_z(devices):
    return [z for z in far_first(devices, Z1) if z > Z1]


def places(devices, chips):
    order = [*far_chips(devices), Y, Z1, Y + Z1, 0]
    return [order.index(k) for k in chips]


def pick(total, rows, where):
    return jnp.concatenate([total[j * rows : (j + 1) * rows] for j in where], axis=0)


def first_sum_kernel(rows, keep, give, near, mine_ref, other_ref, keep_ref, give_ref, near_ref):
    total = mine_ref[...] + other_ref[...].astype(jnp.float32)
    keep_ref[...] = pick(total, rows, keep)
    give_ref[...] = pick(total, rows, give).astype(give_ref.dtype)
    near_ref[...] = pick(total, rows, near)


def last_part_kernel(rows, keep, give, near, mine_ref, other_ref, before_ref, *out_refs):
    keep_ref, give_ref, local_ref, pair_ref = out_refs
    total = mine_ref[...] + other_ref[...].astype(jnp.float32)
    keep_ref[...] = pick(total, rows, keep)
    give_ref[...] = pick(total, rows, give).astype(give_ref.dtype)
    here = pick(total, rows, near)
    half, width = local_ref.shape[0], before_ref.shape[1]
    for columns, block in ((slice(0, width), before_ref[...]), (slice(width, None), here)):
        local_ref[:, columns] = block[:half]
        pair_ref[:, columns] = block[half:].astype(pair_ref.dtype)


def core_sum(mine, other, before, rows, devices):
    count, width = mine.shape
    keep = places(devices, far_z(devices))
    give = places(devices, [z + Y for z in far_z(devices)])
    near = places(devices, [0, Y, Z1, Z1 + Y])
    far = len(keep) * rows
    out = (shape(far, width, dtype=jnp.float32), shape(far, width))
    if before is None:
        kernel = functools.partial(first_sum_kernel, rows, keep, give, near)
        out += (shape(4 * rows, width, dtype=jnp.float32),)
        return call(kernel, out, 1, "core_sum")(mine, other)
    kernel = functools.partial(last_part_kernel, rows, keep, give, near)
    full = before.shape[1] + width
    out += (shape(2 * rows, full, dtype=jnp.float32), shape(2 * rows, full))
    return call(kernel, out, 1, "core_sum")(mine, other, before)


def far_sum_kernel(*refs):
    mine_refs = refs[:PARTS]
    other_refs = refs[PARTS : 2 * PARTS]
    out_refs = refs[2 * PARTS :]
    rows = out_refs[0].shape[0]
    for p, (mine_ref, other_ref) in enumerate(zip(mine_refs, other_refs)):
        width = mine_ref.shape[1]
        total = mine_ref[...] + other_ref[...].astype(jnp.float32)
        for j, out_ref in enumerate(out_refs):
            out_ref[:, p * width : (p + 1) * width] = total[j * rows : (j + 1) * rows].astype(
                out_ref.dtype
            )


def far_sum(mine, other, rows):
    count, width = mine[0].shape
    out = [shape(rows, PARTS * width)] * (count // rows)
    return call(far_sum_kernel, out, 1, "far_sum")(*mine, *other)


def near_sum_kernel(mine_ref, other_ref, keep_ref, give_ref):
    total = mine_ref[...] + other_ref[...].astype(jnp.float32)
    rows = keep_ref.shape[0]
    keep_ref[...] = total[:rows]
    give_ref[...] = total[rows:].astype(give_ref.dtype)


def near_sum(mine, other):
    rows, width = mine.shape[0] // 2, mine.shape[1]
    out = (shape(rows, width, dtype=jnp.float32), shape(rows, width))
    return call(near_sum_kernel, out, 1, "near_sum")(mine, other)


def last_sum_kernel(*refs):
    *in_refs, out_ref = refs
    terms = [ref[...].astype(jnp.float32) for ref in in_refs]
    out_ref[...] = sum(terms[1:], terms[0]).astype(out_ref.dtype)


def last_sum(blocks):
    return call(last_sum_kernel, shape(*blocks[0].shape), 1, "last_sum")(*blocks)


def on_device(q_latent, new_latent, cache, lengths, w_uq, w_uk, w_uv, w_o, devices):
    heads = w_uk.shape[0]
    rows = cache.shape[0]
    zs = far_first(devices, 4)[::-1]

    def swap(block, k):
        if k == 0:
            return block
        return lax.ppermute(block, "row", [(i, i ^ k) for i in range(devices)])

    across = swap(q_latent, Y)
    far_weights = [swap(w_uq, 1), swap(w_uk, 1)]
    tables, near = join(rotary(lengths), [q_latent, across])
    def exchange(messages):
        *far, across, pair, own = messages
        early = len(far) // 2
        got = [swap(block, k) for block, k in zip(far[:early], far_k)]
        passing = swap(across, Y)
        got += [swap(block, k) for block, k in zip(far[early:], far_k[early:])]
        sent = forward(pair, passing)
        return [*got, passing, swap(sent, Z1), own], sent

    far_k = far_chips(devices)
    messages = project([swap(near, z) for z in zs], [w_uq, w_uk, *far_weights], devices)
    messages, sent = exchange(messages)
    keys = jnp.swapaxes(cache, 1, 2)
    flipped = flip(keys, sent)
    latents = attend(lengths, tables, keys, flipped, new_latent, messages, heads, devices)
    latents, sent = exchange(latents)
    ready = early(latents[-3], latents[-1], sent)
    values = head_values(latents, swap(regroup(latents, ready, devices // 2), 1), w_uv)
    keep, got, near = [], [], None
    for part in range(PARTS):
        mine, other = output_terms(values, w_o, part)
        far_mine, far_other, near, *pair = core_sum(mine, swap(other, 1), near, rows, devices)
        keep.append(far_mine)
        got.append(swap(far_other, Y))
    local, across = near_sum(near, swap(pair[0], Z1))
    far = far_sum(keep, got, rows)
    far = [swap(block, z) for z, block in zip(far_z(devices), far)]
    return last_sum([local, swap(across, Y), *far])


def solution(mesh):
    placed = (
        P(("grp", "row"), None),
        P(("grp", "row"), None),
        P(("grp", "row"), None, None),
        P(("grp", "row")),
        P(None, "row"),
        P("row", None, None),
        P("row", None, None),
        P("row", None),
    )
    body = functools.partial(on_device, devices=mesh.shape["row"])
    return jax.shard_map(
        body, mesh=mesh, in_specs=placed, out_specs=P(("grp", "row"), None), check_vma=False
    )
```

```python
import functools
import math

import jax
import jax.numpy as jnp
from jax import lax
from jax.experimental import pallas as pl
from jax.experimental.pallas import tpu as pltpu
from jax.sharding import PartitionSpec as P

LAT = 512
ROPE = 64
HALF = ROPE // 2
NOPE = 128
VD = 128
LANES = 128
PIECES = LAT // LANES
SCALE = (NOPE + ROPE) ** -0.5 * math.log2(math.e)
LIMIT = 16 * 2**20
PARTS = 2
Y = 2
Z1 = 4


def resident(x):
    return pltpu.with_memory_space_constraint(x, pltpu.VMEM)


def in_vmem():
    return pl.BlockSpec(memory_space=pltpu.VMEM)


def call(kernel, out_shape, microseconds, name, scratch=(), scalars=0):
    def run(*args):
        smem = [pl.BlockSpec(memory_space=pltpu.SMEM)] * scalars
        return pl.pallas_call(
            kernel,
            out_shape=out_shape,
            in_specs=smem + [in_vmem()] * (len(args) - scalars),
            out_specs=jax.tree.map(lambda _: in_vmem(), out_shape),
            scratch_shapes=list(scratch),
            compiler_params=pltpu.CompilerParams(vmem_limit_bytes=LIMIT),
            cost_estimate=pl.CostEstimate(
                flops=int(microseconds * 1.15e9), bytes_accessed=0, transcendentals=0
            ),
            name=name,
        )(*args)

    return run


def shape(*dims, dtype=jnp.bfloat16):
    return jax.ShapeDtypeStruct(dims, dtype)


def far_first(devices, step):
    return sorted(range(0, devices, step), key=lambda k: -k.bit_length())


def far_chips(devices):
    return [k for k in far_first(devices, 2) if k > Y + Z1]


def chip_orders(devices):
    far, near = far_chips(devices), [Y, Z1, Y + Z1]
    return [*near, *far, 0], [*far, *near, 0]


def on_odd_core():
    return lax.rem(lax.axis_index("row"), 2) == 1


def block_at(odd, even_place, odd_place, size):
    return pl.ds(pl.multiple_of(jnp.where(odd, odd_place, even_place) * size, size), size)


def gathered_order(devices):
    return [z + y for z in reversed(far_first(devices, 4)) for y in (0, 2)]


def rotary_kernel(len_ref, cos_ref, sin_ref):
    rows, width = cos_ref.shape
    lane = lax.broadcasted_iota(jnp.int32, (rows, width), 1)
    place = lax.broadcasted_iota(jnp.int32, (rows, width), 0)
    step = jnp.where(lane < HALF, lane, lane - HALF).astype(jnp.float32)
    frequency = jnp.exp(step * (-math.log(10000.0) / HALF))
    length = jnp.zeros((rows, width), jnp.float32)
    for r in range(rows):
        length = jnp.where(place == r, len_ref[r].astype(jnp.float32), length)
    angle = length * frequency
    sine = jnp.sin(angle)
    cos_ref[...] = jnp.cos(angle)
    sin_ref[...] = jnp.where(lane < HALF, -sine, sine)


def rotary(lengths):
    table = shape(lengths.shape[0], ROPE, dtype=jnp.float32)
    return call(rotary_kernel, (table, table), 3, "rotary", scalars=1)(lengths)


def join_kernel(cos_ref, sin_ref, *refs):
    *in_refs, cos_out_ref, sin_out_ref, out_ref = refs
    cos_out_ref[...] = cos_ref[...]
    sin_out_ref[...] = sin_ref[...]
    out_ref[...] = jnp.concatenate(
        [ref[...].astype(jnp.float32) for ref in in_refs], axis=0
    ).astype(out_ref.dtype)


def join(tables, blocks):
    rows, depth = blocks[0].shape
    out = (*[shape(*t.shape, dtype=t.dtype) for t in tables], shape(len(blocks) * rows, depth))
    cosine, sine, joined = call(join_kernel, out, 3, "join")(*tables, *blocks)
    return (cosine, sine), joined


def project_kernel(devices, *refs):
    pieces = devices // 4
    q_refs = refs[:pieces]
    weights = (refs[pieces : pieces + 2], refs[pieces + 2 : pieces + 4])
    lat_ref, rot_ref = refs[-2:]
    out_refs = refs[pieces + 4 : -2]
    heads = weights[0][1].shape[0]
    piece = jnp.concatenate([ref[...].astype(jnp.float32) for ref in q_refs], axis=0)
    piece = piece.astype(jnp.bfloat16)
    count = piece.shape[0]
    wide = 2 * count // devices * heads
    width = NOPE + ROPE
    lane = lax.broadcasted_iota(jnp.int32, (wide // 2, LANES), 1)
    odd = on_odd_core()
    gathered = gathered_order(devices)
    orders = zip(*[[gathered.index(k) for k in order] for order in chip_orders(devices)])
    for core, (wq_ref, wk_ref) in enumerate(weights):
        projected = jnp.dot(piece, wq_ref[...], preferred_element_type=jnp.float32)
        for h in range(heads):
            mine = projected[:, h * width : (h + 1) * width]
            absorbed = jnp.dot(
                mine[:, :NOPE].astype(jnp.bfloat16), wk_ref[h], preferred_element_type=jnp.float32
            )
            spread = pl.ds(h, count, stride=heads)
            for c in range(PIECES):
                lat_ref[core * PIECES + c, spread, :] = absorbed[:, c * LANES : (c + 1) * LANES]
            pe = mine[:, NOPE:]
            rot_ref[core, spread, :] = jnp.concatenate([pe, pe], axis=-1)
    for out_ref, (even_place, odd_place) in zip(out_refs, orders):
        here = block_at(odd, even_place, odd_place, wide)
        for core in range(2):
            for c in range(PIECES):
                out_ref[core, c * wide : (c + 1) * wide, :] = lat_ref[
                    core * PIECES + c, here, :
                ].astype(jnp.bfloat16)
            pair = rot_ref[core, here, :]
            packed = jnp.where(lane < ROPE, pair[: wide // 2], pair[wide // 2 :])
            out_ref[core, PIECES * wide :, :] = packed.astype(jnp.bfloat16)


def project(pieces, weights, devices):
    heads = weights[1].shape[0]
    count = len(pieces) * pieces[0].shape[0]
    wide = 2 * count // devices * heads
    scratch = [
        pltpu.VMEM((2 * PIECES, count * heads, LANES), jnp.float32),
        pltpu.VMEM((2, count * heads, LANES), jnp.float32),
    ]
    out = [shape(2, PIECES * wide + wide // 2, LANES)] * (devices // 2)
    kernel = functools.partial(project_kernel, devices)
    return call(kernel, out, 20, "project", scratch)(*pieces, *[resident(w) for w in weights])


def flip_kernel(key_ref, after_ref, out_ref):
    for r in range(key_ref.shape[0]):
        out_ref[r] = key_ref[r, :LAT, :].T


def flip(keys, after):
    rows, _, maxlen = keys.shape
    return call(flip_kernel, shape(rows, maxlen, LAT), 4, "flip")(resident(keys), after)


def attend_kernel(chips, len_ref, cos_ref, sin_ref, key_ref, flip_ref, new_ref, *refs):
    blocks = [(ref, core) for ref in refs[:chips] for core in range(2)]
    out_refs = refs[chips:]
    rows, _, maxlen = key_ref.shape
    wide = out_refs[0].shape[1]
    heads = wide // rows

    def query_block(first):
        parts = [ref[i, first : first + heads, :].astype(jnp.float32) for ref, i in blocks]
        return jnp.concatenate(parts, axis=0)

    def score(r):
        latent = jnp.concatenate(
            [query_block(c * wide + r * heads) for c in range(PIECES)], axis=-1
        )
        pe = query_block(PIECES * wide + (r % (rows // 2)) * heads)
        side = r // (rows // 2) * ROPE
        pe = pe[:, side : side + ROPE]
        swapped = jnp.concatenate([pe[:, HALF:], pe[:, :HALF]], axis=-1)
        rotated = (pe * cos_ref[r : r + 1, :] + swapped * sin_ref[r : r + 1, :]).astype(jnp.bfloat16)
        newest = new_ref[r : r + 1, :].astype(jnp.float32)
        own = jnp.sum(latent * newest[:, :LAT], axis=-1, keepdims=True) + jnp.sum(
            rotated.astype(jnp.float32) * newest[:, LAT:], axis=-1, keepdims=True
        )
        scores = jnp.dot(
            latent.astype(jnp.bfloat16), key_ref[r, :LAT, :], preferred_element_type=jnp.float32
        )
        scores += jnp.dot(rotated, key_ref[r, LAT:, :], preferred_element_type=jnp.float32)
        position = lax.broadcasted_iota(jnp.int32, (1, maxlen), 1)
        return jnp.where(position < len_ref[r], scores, -jnp.inf), own

    ahead = score(0)
    for r in range(rows):
        scores, own = ahead
        if r + 1 < rows:
            ahead = score(r + 1)
        peak = jnp.maximum(jnp.max(scores, axis=-1, keepdims=True), own)
        expo = jnp.exp2((scores - peak) * SCALE)
        own_expo = jnp.exp2((own - peak) * SCALE)
        inverse = 1.0 / (jnp.sum(expo, axis=-1, keepdims=True) + own_expo)
        weights = (expo * inverse).astype(jnp.bfloat16)
        own_weight = (own_expo * inverse).astype(jnp.bfloat16).astype(jnp.float32)
        summed = jnp.dot(weights, flip_ref[r], preferred_element_type=jnp.float32)
        summed += own_weight * new_ref[r : r + 1, :LAT].astype(jnp.float32)
        for k in range(2 * chips):
            out_refs[k // 2][k % 2, r * heads : (r + 1) * heads, :] = summed[
                k * heads : (k + 1) * heads, :
            ].astype(jnp.bfloat16)


def attend(lengths, tables, keys, flipped, new_latent, messages, heads):
    chips = len(messages)
    out = [shape(2, keys.shape[0] * heads, LAT)] * chips
    return call(functools.partial(attend_kernel, chips), out, 10, "attend", scalars=1)(
        lengths, *tables, resident(keys), resident(flipped), new_latent, *messages
    )


def regroup_kernel(*refs):
    *in_refs, out_ref = refs
    for j, ref in enumerate(in_refs):
        out_ref[j] = ref[1]


def regroup(messages):
    _, wide, width = messages[0].shape
    return call(regroup_kernel, shape(len(messages), wide, width), 1, "regroup")(*messages)


def values_kernel(devices, *refs):
    chips = devices // 2
    mine_refs = refs[:chips]
    other_ref, wv_ref, val_ref, rows_ref = refs[chips:]
    heads = wv_ref.shape[0]
    wide = other_ref.shape[1]
    odd = on_odd_core()
    orders = [places(devices, order) for order in chip_orders(devices)]
    for i, (even_place, odd_place) in enumerate(zip(*orders)):
        mine = block_at(odd, even_place, odd_place, wide)
        other = block_at(odd, chips + odd_place, chips + even_place, wide)
        for where, block in ((mine, mine_refs[i][0]), (other, other_ref[i])):
            block = block.astype(jnp.float32)
            for c in range(PIECES):
                rows_ref[c, where, :] = block[:, c * LANES : (c + 1) * LANES]
    count = val_ref.shape[0]
    for h in range(heads):
        chosen = jnp.concatenate(
            [rows_ref[c, pl.ds(h, count, stride=heads), :] for c in range(PIECES)], axis=-1
        )
        val_ref[:, h * VD : (h + 1) * VD] = jnp.dot(
            chosen.astype(jnp.bfloat16), wv_ref[h], preferred_element_type=jnp.float32
        ).astype(jnp.bfloat16)


def head_values(messages, other, w_uv, devices):
    chips, wide, _ = other.shape
    heads = w_uv.shape[0]
    count = 2 * chips * wide // heads
    scratch = [pltpu.VMEM((PIECES, count * heads, LANES), jnp.float32)]
    kernel = functools.partial(values_kernel, devices)
    return call(kernel, shape(count, heads * VD), 3, "values", scratch)(
        *messages, other, resident(w_uv)
    )


def terms_kernel(start, val_ref, wo_ref, mine_ref, other_ref):
    half, width = mine_ref.shape
    terms = jnp.dot(
        val_ref[...], wo_ref[:, start : start + width], preferred_element_type=jnp.float32
    )
    mine_ref[...] = terms[:half]
    other_ref[...] = terms[half:].astype(jnp.bfloat16)


def output_terms(values, w_o, part):
    half = values.shape[0] // 2
    width = w_o.shape[1] // PARTS
    out = (shape(half, width, dtype=jnp.float32), shape(half, width))
    kernel = functools.partial(terms_kernel, part * width)
    return call(kernel, out, 6, "terms")(values, resident(w_o))


def far_z(devices):
    return [z for z in far_first(devices, Z1) if z > Z1]


def places(devices, chips):
    order = far_first(devices, 2)
    return [order.index(k) for k in chips]


def pick(total, rows, where):
    return jnp.concatenate([total[j * rows : (j + 1) * rows] for j in where], axis=0)


def first_sum_kernel(rows, keep, give, near, mine_ref, other_ref, keep_ref, give_ref, near_ref):
    total = mine_ref[...] + other_ref[...].astype(jnp.float32)
    keep_ref[...] = pick(total, rows, keep)
    give_ref[...] = pick(total, rows, give).astype(give_ref.dtype)
    near_ref[...] = pick(total, rows, near)


def last_part_kernel(rows, keep, give, near, mine_ref, other_ref, before_ref, *out_refs):
    keep_ref, give_ref, local_ref, pair_ref = out_refs
    total = mine_ref[...] + other_ref[...].astype(jnp.float32)
    keep_ref[...] = pick(total, rows, keep)
    give_ref[...] = pick(total, rows, give).astype(give_ref.dtype)
    here = pick(total, rows, near)
    half, width = local_ref.shape[0], before_ref.shape[1]
    for columns, block in ((slice(0, width), before_ref[...]), (slice(width, None), here)):
        local_ref[:, columns] = block[:half]
        pair_ref[:, columns] = block[half:].astype(pair_ref.dtype)


def core_sum(mine, other, before, rows, devices):
    count, width = mine.shape
    keep = places(devices, far_z(devices))
    give = places(devices, [z + Y for z in far_z(devices)])
    near = places(devices, [0, Y, Z1, Z1 + Y])
    far = len(keep) * rows
    out = (shape(far, width, dtype=jnp.float32), shape(far, width))
    if before is None:
        kernel = functools.partial(first_sum_kernel, rows, keep, give, near)
        out += (shape(4 * rows, width, dtype=jnp.float32),)
        return call(kernel, out, 1, "core_sum")(mine, other)
    kernel = functools.partial(last_part_kernel, rows, keep, give, near)
    full = before.shape[1] + width
    out += (shape(2 * rows, full, dtype=jnp.float32), shape(2 * rows, full))
    return call(kernel, out, 1, "core_sum")(mine, other, before)


def far_sum_kernel(*refs):
    mine_refs = refs[:PARTS]
    other_refs = refs[PARTS : 2 * PARTS]
    out_refs = refs[2 * PARTS :]
    rows = out_refs[0].shape[0]
    for p, (mine_ref, other_ref) in enumerate(zip(mine_refs, other_refs)):
        width = mine_ref.shape[1]
        total = mine_ref[...] + other_ref[...].astype(jnp.float32)
        for j, out_ref in enumerate(out_refs):
            out_ref[:, p * width : (p + 1) * width] = total[j * rows : (j + 1) * rows].astype(
                out_ref.dtype
            )


def far_sum(mine, other, rows):
    count, width = mine[0].shape
    out = [shape(rows, PARTS * width)] * (count // rows)
    return call(far_sum_kernel, out, 1, "far_sum")(*mine, *other)


def near_sum_kernel(mine_ref, other_ref, keep_ref, give_ref):
    total = mine_ref[...] + other_ref[...].astype(jnp.float32)
    rows = keep_ref.shape[0]
    keep_ref[...] = total[:rows]
    give_ref[...] = total[rows:].astype(give_ref.dtype)


def near_sum(mine, other):
    rows, width = mine.shape[0] // 2, mine.shape[1]
    out = (shape(rows, width, dtype=jnp.float32), shape(rows, width))
    return call(near_sum_kernel, out, 1, "near_sum")(mine, other)


def last_sum_kernel(*refs):
    *in_refs, out_ref = refs
    terms = [ref[...].astype(jnp.float32) for ref in in_refs]
    out_ref[...] = sum(terms[1:], terms[0]).astype(out_ref.dtype)


def last_sum(blocks):
    return call(last_sum_kernel, shape(*blocks[0].shape), 1, "last_sum")(*blocks)


def on_device(q_latent, new_latent, cache, lengths, w_uq, w_uk, w_uv, w_o, devices):
    heads = w_uk.shape[0]
    rows = cache.shape[0]
    zs = far_first(devices, 4)[::-1]

    def swap(block, k):
        if k == 0:
            return block
        return lax.ppermute(block, "row", [(i, i ^ k) for i in range(devices)])

    across = swap(q_latent, Y)
    far_weights = [swap(w_uq, 1), swap(w_uk, 1)]
    tables, near = join(rotary(lengths), [q_latent, across])
    def exchange(messages):
        got = []
        for block, flips in zip(messages, zip(*chip_orders(devices))):
            pairs = [(i, i ^ flips[i % 2]) for i in range(devices)]
            got.append(lax.ppermute(block, "row", pairs) if any(flips) else block)
        return got

    messages = project([swap(near, z) for z in zs], [w_uq, w_uk, *far_weights], devices)
    keys = jnp.swapaxes(cache, 1, 2)
    flipped = flip(keys, messages[-1])
    messages = exchange(messages)
    latents = attend(lengths, tables, keys, flipped, new_latent, messages, heads)
    latents = exchange(latents)
    values = head_values(latents, swap(regroup(latents), 1), w_uv, devices)
    keep, got, near = [], [], None
    for part in range(PARTS):
        mine, other = output_terms(values, w_o, part)
        far_mine, far_other, near, *pair = core_sum(mine, swap(other, 1), near, rows, devices)
        keep.append(far_mine)
        got.append(swap(far_other, Y))
    local, across = near_sum(near, swap(pair[0], Z1))
    far = far_sum(keep, got, rows)
    far = [swap(block, z) for z, block in zip(far_z(devices), far)]
    return last_sum([local, swap(across, Y), *far])


def solution(mesh):
    placed = (
        P(("grp", "row"), None),
        P(("grp", "row"), None),
        P(("grp", "row"), None, None),
        P(("grp", "row")),
        P(None, "row"),
        P("row", None, None),
        P("row", None, None),
        P("row", None),
    )
    body = functools.partial(on_device, devices=mesh.shape["row"])
    return jax.shard_map(
        body, mesh=mesh, in_specs=placed, out_specs=P(("grp", "row"), None), check_vma=False
    )
```

```python
import functools
import math

import jax
import jax.numpy as jnp
from jax import lax
from jax.experimental import pallas as pl
from jax.experimental.pallas import tpu as pltpu
from jax.sharding import PartitionSpec as P

LAT = 512
ROPE = 64
HALF = ROPE // 2
NOPE = 128
VD = 128
LANES = 128
PIECES = LAT // LANES
SCALE = (NOPE + ROPE) ** -0.5 * math.log2(math.e)
LIMIT = 16 * 2**20
PARTS = 2
Y = 2
Z1 = 4
NEAR = (Z1, Y + Z1, Y)


def resident(x):
    return pltpu.with_memory_space_constraint(x, pltpu.VMEM)


def in_vmem():
    return pl.BlockSpec(memory_space=pltpu.VMEM)


def call(kernel, out_shape, microseconds, name, scratch=(), scalars=0):
    def run(*args):
        smem = [pl.BlockSpec(memory_space=pltpu.SMEM)] * scalars
        return pl.pallas_call(
            kernel,
            out_shape=out_shape,
            in_specs=smem + [in_vmem()] * (len(args) - scalars),
            out_specs=jax.tree.map(lambda _: in_vmem(), out_shape),
            scratch_shapes=list(scratch),
            compiler_params=pltpu.CompilerParams(vmem_limit_bytes=LIMIT),
            cost_estimate=pl.CostEstimate(
                flops=int(microseconds * 1.15e9), bytes_accessed=0, transcendentals=0
            ),
            name=name,
        )(*args)

    return run


def shape(*dims, dtype=jnp.bfloat16):
    return jax.ShapeDtypeStruct(dims, dtype)


def far_first(devices, step):
    return sorted(range(0, devices, step), key=lambda k: -k.bit_length())


def far_chips(devices):
    chips = [k for k in far_first(devices, 2) if k > Y + Z1]
    return chips[:1] + chips[:0:-1]


def chip_order(devices):
    return [*far_chips(devices), Y, Y + Z1, Z1, 0]


def message_sizes(devices):
    return [1] * len(far_chips(devices)) + [2, 1, 1]


def gathered_order(devices):
    return [z + y for z in reversed(far_first(devices, 4)) for y in (0, 2)]


def rotary_kernel(len_ref, cos_ref, sin_ref):
    rows, width = cos_ref.shape
    lane = lax.broadcasted_iota(jnp.int32, (rows, width), 1)
    place = lax.broadcasted_iota(jnp.int32, (rows, width), 0)
    step = jnp.where(lane < HALF, lane, lane - HALF).astype(jnp.float32)
    frequency = jnp.exp(step * (-math.log(10000.0) / HALF))
    length = jnp.zeros((rows, width), jnp.float32)
    for r in range(rows):
        length = jnp.where(place == r, len_ref[r].astype(jnp.float32), length)
    angle = length * frequency
    sine = jnp.sin(angle)
    cos_ref[...] = jnp.cos(angle)
    sin_ref[...] = jnp.where(lane < HALF, -sine, sine)


def rotary(lengths):
    table = shape(lengths.shape[0], ROPE, dtype=jnp.float32)
    return call(rotary_kernel, (table, table), 3, "rotary", scalars=1)(lengths)


def join_kernel(cos_ref, sin_ref, *refs):
    *in_refs, cos_out_ref, sin_out_ref, out_ref = refs
    cos_out_ref[...] = cos_ref[...]
    sin_out_ref[...] = sin_ref[...]
    out_ref[...] = jnp.concatenate(
        [ref[...].astype(jnp.float32) for ref in in_refs], axis=0
    ).astype(out_ref.dtype)


def join(tables, blocks):
    rows, depth = blocks[0].shape
    out = (*[shape(*t.shape, dtype=t.dtype) for t in tables], shape(len(blocks) * rows, depth))
    cosine, sine, joined = call(join_kernel, out, 3, "join")(*tables, *blocks)
    return (cosine, sine), joined


def project_kernel(devices, *refs):
    pieces = devices // 4
    q_refs = refs[:pieces]
    weights = (refs[pieces : pieces + 2], refs[pieces + 2 : pieces + 4])
    lat_ref, rot_ref = refs[-2:]
    out_refs = refs[pieces + 4 : -2]
    heads = weights[0][1].shape[0]
    piece = jnp.concatenate([ref[...].astype(jnp.float32) for ref in q_refs], axis=0)
    piece = piece.astype(jnp.bfloat16)
    count = piece.shape[0]
    wide = 2 * count // devices * heads
    width = NOPE + ROPE
    lane = lax.broadcasted_iota(jnp.int32, (wide // 2, LANES), 1)
    blocks = [(ref, 2 * i) for ref in out_refs for i in range(ref.shape[0] // 2)]
    blocks = dict(zip(chip_order(devices), blocks))
    for core, (wq_ref, wk_ref) in enumerate(weights):
        projected = jnp.dot(piece, wq_ref[...], preferred_element_type=jnp.float32)
        for h in range(heads):
            mine = projected[:, h * width : (h + 1) * width]
            absorbed = jnp.dot(
                mine[:, :NOPE].astype(jnp.bfloat16), wk_ref[h], preferred_element_type=jnp.float32
            )
            spread = pl.ds(h, count, stride=heads)
            for c in range(PIECES):
                lat_ref[core * PIECES + c, spread, :] = absorbed[:, c * LANES : (c + 1) * LANES]
            pe = mine[:, NOPE:]
            rot_ref[core, spread, :] = jnp.concatenate([pe, pe], axis=-1)
        for place, k in enumerate(gathered_order(devices)):
            out_ref, at = blocks[k]
            at += core
            first = place * wide
            for c in range(PIECES):
                out_ref[at, c * wide : (c + 1) * wide, :] = lat_ref[
                    core * PIECES + c, first : first + wide, :
                ].astype(jnp.bfloat16)
            low = rot_ref[core, first : first + wide // 2, :]
            high = rot_ref[core, first + wide // 2 : first + wide, :]
            out_ref[at, PIECES * wide :, :] = jnp.where(lane < ROPE, low, high).astype(
                jnp.bfloat16
            )


def project(pieces, weights, devices):
    heads = weights[1].shape[0]
    count = len(pieces) * pieces[0].shape[0]
    wide = 2 * count // devices * heads
    scratch = [
        pltpu.VMEM((2 * PIECES, count * heads, LANES), jnp.float32),
        pltpu.VMEM((2, count * heads, LANES), jnp.float32),
    ]
    tall = PIECES * wide + wide // 2
    out = [shape(2 * size, tall, LANES) for size in message_sizes(devices)]
    kernel = functools.partial(project_kernel, devices)
    return call(kernel, out, 20, "project", scratch)(*pieces, *[resident(w) for w in weights])


def flip_kernel(key_ref, after_ref, out_ref):
    for r in range(key_ref.shape[0]):
        out_ref[r] = key_ref[r, :LAT, :].T


def flip(keys, after):
    rows, _, maxlen = keys.shape
    return call(flip_kernel, shape(rows, maxlen, LAT), 4, "flip")(resident(keys), after)


def forward_kernel(own_ref, passing_ref, out_ref):
    out_ref[:2] = own_ref[...]
    out_ref[2:] = passing_ref[2:]


def forward(own, passing):
    return call(forward_kernel, shape(4, *own.shape[1:]), 1, "forward")(own, passing)


def arrived(refs):
    blocks = []
    for i, ref in enumerate(refs):
        count = 2 if i == len(refs) - 3 else ref.shape[0]
        blocks += [(ref, core) for core in range(count)]
    return blocks


def attend_kernel(sizes, len_ref, cos_ref, sin_ref, key_ref, flip_ref, new_ref, *refs):
    blocks = arrived(refs[: len(sizes)])
    out_refs = refs[len(sizes) :]
    rows, _, maxlen = key_ref.shape
    wide = out_refs[0].shape[1]
    heads = wide // rows

    def query_block(first):
        parts = [ref[i, first : first + heads, :].astype(jnp.float32) for ref, i in blocks]
        return jnp.concatenate(parts, axis=0)

    def score(r):
        latent = jnp.concatenate(
            [query_block(c * wide + r * heads) for c in range(PIECES)], axis=-1
        )
        pe = query_block(PIECES * wide + (r % (rows // 2)) * heads)
        side = r // (rows // 2) * ROPE
        pe = pe[:, side : side + ROPE]
        swapped = jnp.concatenate([pe[:, HALF:], pe[:, :HALF]], axis=-1)
        rotated = (pe * cos_ref[r : r + 1, :] + swapped * sin_ref[r : r + 1, :]).astype(jnp.bfloat16)
        newest = new_ref[r : r + 1, :].astype(jnp.float32)
        own = jnp.sum(latent * newest[:, :LAT], axis=-1, keepdims=True) + jnp.sum(
            rotated.astype(jnp.float32) * newest[:, LAT:], axis=-1, keepdims=True
        )
        scores = jnp.dot(
            latent.astype(jnp.bfloat16), key_ref[r, :LAT, :], preferred_element_type=jnp.float32
        )
        scores += jnp.dot(rotated, key_ref[r, LAT:, :], preferred_element_type=jnp.float32)
        position = lax.broadcasted_iota(jnp.int32, (1, maxlen), 1)
        return jnp.where(position < len_ref[r], scores, -jnp.inf), own

    back = [(ref, i) for ref in out_refs for i in range(ref.shape[0])]
    y_at = len(back) - 8
    back = back[: y_at + 2] + back[y_at + 4 : y_at + 6] + back[y_at + 2 : y_at + 4] + back[-2:]
    ahead = score(0)
    for r in range(rows):
        scores, own = ahead
        if r + 1 < rows:
            ahead = score(r + 1)
        peak = jnp.maximum(jnp.max(scores, axis=-1, keepdims=True), own)
        expo = jnp.exp2((scores - peak) * SCALE)
        own_expo = jnp.exp2((own - peak) * SCALE)
        inverse = 1.0 / (jnp.sum(expo, axis=-1, keepdims=True) + own_expo)
        weights = (expo * inverse).astype(jnp.bfloat16)
        own_weight = (own_expo * inverse).astype(jnp.bfloat16).astype(jnp.float32)
        summed = jnp.dot(weights, flip_ref[r], preferred_element_type=jnp.float32)
        summed += own_weight * new_ref[r : r + 1, :LAT].astype(jnp.float32)
        for k, (out_ref, i) in enumerate(back):
            out_ref[i, r * heads : (r + 1) * heads, :] = summed[
                k * heads : (k + 1) * heads, :
            ].astype(jnp.bfloat16)


def attend(lengths, tables, keys, flipped, new_latent, messages, heads, devices):
    sizes = message_sizes(devices)
    out = [shape(2 * size, keys.shape[0] * heads, LAT) for size in sizes]
    return call(functools.partial(attend_kernel, sizes), out, 10, "attend", scalars=1)(
        lengths, *tables, resident(keys), resident(flipped), new_latent, *messages
    )


def early_kernel(passing_ref, own_ref, after_ref, out_ref):
    out_ref[0] = passing_ref[1]
    out_ref[1] = own_ref[1]


def early(passing, own, after):
    return call(early_kernel, shape(2, *own.shape[1:]), 4, "early")(passing, own, after)


def regroup_kernel(*refs):
    *in_refs, early_ref, out_ref = refs
    blocks = arrived(in_refs)[1::2]
    blocks = [*blocks[:-4], (early_ref, 0), *blocks[-3:-1], (early_ref, 1)]
    for j, (ref, i) in enumerate(blocks):
        out_ref[j] = ref[i]


def regroup(messages, ready, chips):
    _, wide, width = messages[0].shape
    return call(regroup_kernel, shape(chips, wide, width), 1, "regroup")(*messages, ready)


def values_kernel(*refs):
    *in_refs, other_ref, wv_ref, val_ref, rows_ref = refs
    mine = arrived(in_refs)[::2]
    chips = len(mine)
    heads = wv_ref.shape[0]
    wide = other_ref.shape[1]
    for place in range(2 * chips):
        ref, i = mine[place] if place < chips else (other_ref, place - chips)
        block = ref[i].astype(jnp.float32)
        for c in range(PIECES):
            rows_ref[c, place * wide : (place + 1) * wide, :] = block[:, c * LANES : (c + 1) * LANES]
    count = val_ref.shape[0]
    for h in range(heads):
        chosen = jnp.concatenate(
            [rows_ref[c, pl.ds(h, count, stride=heads), :] for c in range(PIECES)], axis=-1
        )
        val_ref[:, h * VD : (h + 1) * VD] = jnp.dot(
            chosen.astype(jnp.bfloat16), wv_ref[h], preferred_element_type=jnp.float32
        ).astype(jnp.bfloat16)


def head_values(messages, other, w_uv):
    chips, wide, _ = other.shape
    heads = w_uv.shape[0]
    count = 2 * chips * wide // heads
    scratch = [pltpu.VMEM((PIECES, count * heads, LANES), jnp.float32)]
    return call(values_kernel, shape(count, heads * VD), 3, "values", scratch)(
        *messages, other, resident(w_uv)
    )


def terms_kernel(start, val_ref, wo_ref, mine_ref, other_ref):
    half, width = mine_ref.shape
    terms = jnp.dot(
        val_ref[...], wo_ref[:, start : start + width], preferred_element_type=jnp.float32
    )
    mine_ref[...] = terms[:half]
    other_ref[...] = terms[half:].astype(jnp.bfloat16)


def output_terms(values, w_o, part):
    half = values.shape[0] // 2
    width = w_o.shape[1] // PARTS
    out = (shape(half, width, dtype=jnp.float32), shape(half, width))
    kernel = functools.partial(terms_kernel, part * width)
    return call(kernel, out, 6, "terms")(values, resident(w_o))


def far_z(devices):
    return [z for z in far_first(devices, Z1) if z > Z1][::-1]


def places(devices, chips):
    order = [*far_chips(devices), Y, Z1, Y + Z1, 0]
    return [order.index(k) for k in chips]


def pick(total, rows, where):
    return jnp.concatenate([total[j * rows : (j + 1) * rows] for j in where], axis=0)


def first_sum_kernel(rows, keep, give, near, mine_ref, other_ref, keep_ref, give_ref, near_ref):
    total = mine_ref[...] + other_ref[...].astype(jnp.float32)
    keep_ref[...] = pick(total, rows, keep)
    give_ref[...] = pick(total, rows, give).astype(give_ref.dtype)
    near_ref[...] = pick(total, rows, near)


def last_part_kernel(rows, keep, give, near, mine_ref, other_ref, before_ref, *out_refs):
    keep_ref, give_ref, *near_refs = out_refs
    total = mine_ref[...] + other_ref[...].astype(jnp.float32)
    keep_ref[...] = pick(total, rows, keep)
    give_ref[...] = pick(total, rows, give).astype(give_ref.dtype)
    width = before_ref.shape[1]
    for i, (j, out_ref) in enumerate(zip(near, near_refs)):
        out_ref[:, :width] = before_ref[i * rows : (i + 1) * rows].astype(out_ref.dtype)
        out_ref[:, width:] = total[j * rows : (j + 1) * rows].astype(out_ref.dtype)


def core_sum(mine, other, before, rows, devices):
    count, width = mine.shape
    keep = places(devices, far_z(devices))
    give = places(devices, [z + Y for z in far_z(devices)])
    near = places(devices, [0, *NEAR])
    far = len(keep) * rows
    out = (shape(far, width, dtype=jnp.float32), shape(far, width))
    if before is None:
        kernel = functools.partial(first_sum_kernel, rows, keep, give, near)
        out += (shape(4 * rows, width, dtype=jnp.float32),)
        return call(kernel, out, 1, "core_sum")(mine, other)
    kernel = functools.partial(last_part_kernel, rows, keep, give, near)
    full = before.shape[1] + width
    out += (shape(rows, full, dtype=jnp.float32), *[shape(rows, full)] * len(NEAR))
    return call(kernel, out, 1, "core_sum")(mine, other, before)


def far_sum_kernel(*refs):
    mine_refs = refs[:PARTS]
    other_refs = refs[PARTS : 2 * PARTS]
    out_refs = refs[2 * PARTS :]
    rows = out_refs[0].shape[0]
    for p, (mine_ref, other_ref) in enumerate(zip(mine_refs, other_refs)):
        width = mine_ref.shape[1]
        total = mine_ref[...] + other_ref[...].astype(jnp.float32)
        for j, out_ref in enumerate(out_refs):
            out_ref[:, p * width : (p + 1) * width] = total[j * rows : (j + 1) * rows].astype(
                out_ref.dtype
            )


def far_sum(mine, other, rows):
    count, width = mine[0].shape
    out = [shape(rows, PARTS * width)] * (count // rows)
    return call(far_sum_kernel, out, 1, "far_sum")(*mine, *other)


def last_sum_kernel(*refs):
    *in_refs, out_ref = refs
    terms = [ref[...].astype(jnp.float32) for ref in in_refs]
    out_ref[...] = sum(terms[1:], terms[0]).astype(out_ref.dtype)


def last_sum(blocks):
    return call(last_sum_kernel, shape(*blocks[0].shape), 1, "last_sum")(*blocks)


def on_device(q_latent, new_latent, cache, lengths, w_uq, w_uk, w_uv, w_o, devices):
    heads = w_uk.shape[0]
    rows = cache.shape[0]
    zs = far_first(devices, 4)[::-1]

    def swap(block, k):
        if k == 0:
            return block
        return lax.ppermute(block, "row", [(i, i ^ k) for i in range(devices)])

    across = swap(q_latent, Y)
    far_weights = [swap(w_uq, 1), swap(w_uk, 1)]
    tables, near = join(rotary(lengths), [q_latent, across])
    def exchange(messages):
        *far, across, pair, own = messages
        early = len(far) // 2
        got = [swap(block, k) for block, k in zip(far[:early], far_k)]
        passing = swap(across, Y)
        got += [swap(block, k) for block, k in zip(far[early:], far_k[early:])]
        sent = forward(pair, passing)
        return [*got, passing, swap(sent, Z1), own], sent

    far_k = far_chips(devices)
    messages = project([swap(near, z) for z in zs], [w_uq, w_uk, *far_weights], devices)
    messages, sent = exchange(messages)
    keys = jnp.swapaxes(cache, 1, 2)
    flipped = flip(keys, sent)
    latents = attend(lengths, tables, keys, flipped, new_latent, messages, heads, devices)
    latents, sent = exchange(latents)
    ready = early(latents[-3], latents[-1], sent)
    values = head_values(latents, swap(regroup(latents, ready, devices // 2), 1), w_uv)
    keep, got, near = [], [], None
    for part in range(PARTS):
        mine, other = output_terms(values, w_o, part)
        far_mine, far_other, near, *given = core_sum(mine, swap(other, 1), near, rows, devices)
        keep.append(far_mine)
        got.append(swap(far_other, Y))
    given = [swap(block, k) for block, k in zip(given, NEAR)]
    far = far_sum(keep, got, rows)
    far = [swap(block, z) for z, block in zip(far_z(devices), far)]
    return last_sum([near, *given, *far])


def solution(mesh):
    placed = (
        P(("grp", "row"), None),
        P(("grp", "row"), None),
        P(("grp", "row"), None, None),
        P(("grp", "row")),
        P(None, "row"),
        P("row", None, None),
        P("row", None, None),
        P("row", None),
    )
    body = functools.partial(on_device, devices=mesh.shape["row"])
    return jax.shard_map(
        body, mesh=mesh, in_specs=placed, out_specs=P(("grp", "row"), None), check_vma=False
    )
```

```python
import functools
import math

import jax
import jax.numpy as jnp
from jax import lax
from jax.experimental import pallas as pl
from jax.experimental.pallas import tpu as pltpu
from jax.sharding import PartitionSpec as P

LAT = 512
ROPE = 64
HALF = ROPE // 2
NOPE = 128
VD = 128
LANES = 128
PIECES = LAT // LANES
SCALE = (NOPE + ROPE) ** -0.5 * math.log2(math.e)
LIMIT = 16 * 2**20
PARTS = 2
Y = 2
Z1 = 4
PASSED = Y + Z1
NEAR = (Z1, PASSED, Y)


def resident(x):
    return pltpu.with_memory_space_constraint(x, pltpu.VMEM)


def in_vmem():
    return pl.BlockSpec(memory_space=pltpu.VMEM)


def call(kernel, out_shape, microseconds, name, scratch=(), scalars=0):
    def run(*args):
        smem = [pl.BlockSpec(memory_space=pltpu.SMEM)] * scalars
        return pl.pallas_call(
            kernel,
            out_shape=out_shape,
            in_specs=smem + [in_vmem()] * (len(args) - scalars),
            out_specs=jax.tree.map(lambda _: in_vmem(), out_shape),
            scratch_shapes=list(scratch),
            compiler_params=pltpu.CompilerParams(vmem_limit_bytes=LIMIT),
            cost_estimate=pl.CostEstimate(
                flops=int(microseconds * 1.15e9), bytes_accessed=0, transcendentals=0
            ),
            name=name,
        )(*args)

    return run


def shape(*dims, dtype=jnp.bfloat16):
    return jax.ShapeDtypeStruct(dims, dtype)


def far_first(devices, step):
    return sorted(range(0, devices, step), key=lambda k: -k.bit_length())


def far_chips(devices):
    return [k for k in far_first(devices, 2) if k > Y + Z1]


def sent_orders(devices):
    far = far_chips(devices)
    even = [PASSED, Y, *far]
    odd = [far[0], PASSED, far[1], Y, *far[2:]]
    return [*even, Z1, 0], [*odd, Z1, 0]


def arrived_orders(devices):
    even, odd = sent_orders(devices)
    return [*even[1:-1], PASSED, 0], [odd[0], *odd[2:-1], PASSED, 0]


def on_odd_core():
    return lax.rem(lax.axis_index("row"), 2) == 1


def block_at(odd, even_place, odd_place, size):
    return pl.ds(pl.multiple_of(jnp.where(odd, odd_place, even_place) * size, size), size)


def gathered_order(devices):
    return [z + y for z in reversed(far_first(devices, 4)) for y in (0, 2)]


def rotary_kernel(len_ref, cos_ref, sin_ref):
    rows, width = cos_ref.shape
    lane = lax.broadcasted_iota(jnp.int32, (rows, width), 1)
    place = lax.broadcasted_iota(jnp.int32, (rows, width), 0)
    step = jnp.where(lane < HALF, lane, lane - HALF).astype(jnp.float32)
    frequency = jnp.exp(step * (-math.log(10000.0) / HALF))
    length = jnp.zeros((rows, width), jnp.float32)
    for r in range(rows):
        length = jnp.where(place == r, len_ref[r].astype(jnp.float32), length)
    angle = length * frequency
    sine = jnp.sin(angle)
    cos_ref[...] = jnp.cos(angle)
    sin_ref[...] = jnp.where(lane < HALF, -sine, sine)


def rotary(lengths):
    table = shape(lengths.shape[0], ROPE, dtype=jnp.float32)
    return call(rotary_kernel, (table, table), 3, "rotary", scalars=1)(lengths)


def join_kernel(cos_ref, sin_ref, *refs):
    *in_refs, cos_out_ref, sin_out_ref, out_ref = refs
    cos_out_ref[...] = cos_ref[...]
    sin_out_ref[...] = sin_ref[...]
    out_ref[...] = jnp.concatenate(
        [ref[...].astype(jnp.float32) for ref in in_refs], axis=0
    ).astype(out_ref.dtype)


def join(tables, blocks):
    rows, depth = blocks[0].shape
    out = (*[shape(*t.shape, dtype=t.dtype) for t in tables], shape(len(blocks) * rows, depth))
    cosine, sine, joined = call(join_kernel, out, 3, "join")(*tables, *blocks)
    return (cosine, sine), joined


def project_kernel(devices, *refs):
    pieces = devices // 4
    q_refs = refs[:pieces]
    weights = (refs[pieces : pieces + 2], refs[pieces + 2 : pieces + 4])
    lat_ref, rot_ref = refs[-2:]
    out_refs = refs[pieces + 4 : -2]
    heads = weights[0][1].shape[0]
    piece = jnp.concatenate([ref[...].astype(jnp.float32) for ref in q_refs], axis=0)
    piece = piece.astype(jnp.bfloat16)
    count = piece.shape[0]
    wide = 2 * count // devices * heads
    width = NOPE + ROPE
    lane = lax.broadcasted_iota(jnp.int32, (wide // 2, LANES), 1)
    odd = on_odd_core()
    gathered = gathered_order(devices)
    orders = zip(*[[gathered.index(k) for k in order] for order in sent_orders(devices)])
    for core, (wq_ref, wk_ref) in enumerate(weights):
        projected = jnp.dot(piece, wq_ref[...], preferred_element_type=jnp.float32)
        for h in range(heads):
            mine = projected[:, h * width : (h + 1) * width]
            absorbed = jnp.dot(
                mine[:, :NOPE].astype(jnp.bfloat16), wk_ref[h], preferred_element_type=jnp.float32
            )
            spread = pl.ds(h, count, stride=heads)
            for c in range(PIECES):
                lat_ref[core * PIECES + c, spread, :] = absorbed[:, c * LANES : (c + 1) * LANES]
            pe = mine[:, NOPE:]
            rot_ref[core, spread, :] = jnp.concatenate([pe, pe], axis=-1)
    for out_ref, (even_place, odd_place) in zip(out_refs, orders):
        here = block_at(odd, even_place, odd_place, wide)
        for core in range(2):
            for c in range(PIECES):
                out_ref[core, c * wide : (c + 1) * wide, :] = lat_ref[
                    core * PIECES + c, here, :
                ].astype(jnp.bfloat16)
            pair = rot_ref[core, here, :]
            packed = jnp.where(lane < ROPE, pair[: wide // 2], pair[wide // 2 :])
            out_ref[core, PIECES * wide :, :] = packed.astype(jnp.bfloat16)


def project(pieces, weights, devices):
    heads = weights[1].shape[0]
    count = len(pieces) * pieces[0].shape[0]
    wide = 2 * count // devices * heads
    scratch = [
        pltpu.VMEM((2 * PIECES, count * heads, LANES), jnp.float32),
        pltpu.VMEM((2, count * heads, LANES), jnp.float32),
    ]
    out = [shape(2, PIECES * wide + wide // 2, LANES)] * (devices // 2)
    kernel = functools.partial(project_kernel, devices)
    return call(kernel, out, 20, "project", scratch)(*pieces, *[resident(w) for w in weights])


def flip_kernel(key_ref, after_ref, out_ref):
    for r in range(key_ref.shape[0]):
        out_ref[r] = key_ref[r, :LAT, :].T


def flip(keys, after):
    rows, _, maxlen = keys.shape
    return call(flip_kernel, shape(rows, maxlen, LAT), 4, "flip")(resident(keys), after)


def forward_kernel(pair_ref, first_ref, second_ref, sent_ref, kept_ref):
    odd = on_odd_core()
    first, second = first_ref[...], second_ref[...]
    sent_ref[:2] = pair_ref[...]
    sent_ref[2:] = jnp.where(odd, second, first)
    kept_ref[...] = jnp.where(odd, first, second)


def forward(pair, first, second):
    out = (shape(4, *pair.shape[1:]), shape(*pair.shape))
    return call(forward_kernel, out, 1, "forward")(pair, first, second)


def arrived(refs):
    return [(ref, i) for ref in refs for i in range(ref.shape[0])]


def attend_kernel(count, len_ref, cos_ref, sin_ref, key_ref, flip_ref, new_ref, *refs):
    blocks = arrived(refs[:count])
    out_refs = refs[count:]
    odd = on_odd_core()
    rows, _, maxlen = key_ref.shape
    wide = out_refs[0].shape[1]
    heads = wide // rows

    def query_block(first):
        parts = [ref[i, first : first + heads, :].astype(jnp.float32) for ref, i in blocks]
        return jnp.concatenate(parts, axis=0)

    def score(r):
        latent = jnp.concatenate(
            [query_block(c * wide + r * heads) for c in range(PIECES)], axis=-1
        )
        pe = query_block(PIECES * wide + (r % (rows // 2)) * heads)
        side = r // (rows // 2) * ROPE
        pe = pe[:, side : side + ROPE]
        swapped = jnp.concatenate([pe[:, HALF:], pe[:, :HALF]], axis=-1)
        rotated = (pe * cos_ref[r : r + 1, :] + swapped * sin_ref[r : r + 1, :]).astype(jnp.bfloat16)
        newest = new_ref[r : r + 1, :].astype(jnp.float32)
        own = jnp.sum(latent * newest[:, :LAT], axis=-1, keepdims=True) + jnp.sum(
            rotated.astype(jnp.float32) * newest[:, LAT:], axis=-1, keepdims=True
        )
        scores = jnp.dot(
            latent.astype(jnp.bfloat16), key_ref[r, :LAT, :], preferred_element_type=jnp.float32
        )
        scores += jnp.dot(rotated, key_ref[r, LAT:, :], preferred_element_type=jnp.float32)
        position = lax.broadcasted_iota(jnp.int32, (1, maxlen), 1)
        return jnp.where(position < len_ref[r], scores, -jnp.inf), own

    straight = [(1 + i, out_ref) for i, out_ref in enumerate(out_refs[2:-1])]
    straight.append((len(out_refs) - 1, out_refs[-1]))
    passed = len(out_refs) - 2
    ahead = score(0)
    for r in range(rows):
        scores, own = ahead
        if r + 1 < rows:
            ahead = score(r + 1)
        peak = jnp.maximum(jnp.max(scores, axis=-1, keepdims=True), own)
        expo = jnp.exp2((scores - peak) * SCALE)
        own_expo = jnp.exp2((own - peak) * SCALE)
        inverse = 1.0 / (jnp.sum(expo, axis=-1, keepdims=True) + own_expo)
        weights = (expo * inverse).astype(jnp.bfloat16)
        own_weight = (own_expo * inverse).astype(jnp.bfloat16).astype(jnp.float32)
        summed = jnp.dot(weights, flip_ref[r], preferred_element_type=jnp.float32)
        summed += own_weight * new_ref[r : r + 1, :LAT].astype(jnp.float32)
        summed = summed.astype(jnp.bfloat16)
        for core in range(2):
            at = slice(r * heads, (r + 1) * heads)
            chip = [summed[k * heads : (k + 1) * heads, :] for k in range(core, len(blocks), 2)]
            for k, out_ref in straight:
                out_ref[core, at, :] = chip[k]
            out_refs[0][core, at, :] = jnp.where(odd, chip[0], chip[passed])
            out_refs[1][core, at, :] = jnp.where(odd, chip[passed], chip[0])


def attend(lengths, tables, keys, flipped, new_latent, messages, heads, devices):
    out = [shape(2, keys.shape[0] * heads, LAT)] * (devices // 2)
    return call(functools.partial(attend_kernel, len(messages)), out, 10, "attend", scalars=1)(
        lengths, *tables, resident(keys), resident(flipped), new_latent, *messages
    )


def early_kernel(own_ref, after_ref, out_ref):
    out_ref[...] = own_ref[1]


def early(own, after):
    return call(early_kernel, shape(*own.shape[1:]), 4, "early")(own, after)


def regroup_kernel(*refs):
    *in_refs, early_ref, out_ref = refs
    blocks = arrived(in_refs)[1::2]
    for j, (ref, i) in enumerate(blocks[:-1]):
        out_ref[j] = ref[i]
    out_ref[len(blocks) - 1] = early_ref[...]


def regroup(messages, ready, chips):
    _, wide, width = messages[0].shape
    return call(regroup_kernel, shape(chips, wide, width), 1, "regroup")(*messages, ready)


def values_kernel(devices, *refs):
    *in_refs, other_ref, wv_ref, val_ref, rows_ref = refs
    chips = devices // 2
    heads = wv_ref.shape[0]
    wide = other_ref.shape[1]
    odd = on_odd_core()
    orders = [places(devices, order) for order in arrived_orders(devices)]
    mine_blocks = arrived(in_refs)[::2]
    for i, (even_place, odd_place) in enumerate(zip(*orders)):
        ref, at = mine_blocks[i]
        mine = block_at(odd, even_place, odd_place, wide)
        other = block_at(odd, chips + odd_place, chips + even_place, wide)
        for where, block in ((mine, ref[at]), (other, other_ref[i])):
            block = block.astype(jnp.float32)
            for c in range(PIECES):
                rows_ref[c, where, :] = block[:, c * LANES : (c + 1) * LANES]
    count = val_ref.shape[0]
    for h in range(heads):
        chosen = jnp.concatenate(
            [rows_ref[c, pl.ds(h, count, stride=heads), :] for c in range(PIECES)], axis=-1
        )
        val_ref[:, h * VD : (h + 1) * VD] = jnp.dot(
            chosen.astype(jnp.bfloat16), wv_ref[h], preferred_element_type=jnp.float32
        ).astype(jnp.bfloat16)


def head_values(messages, other, w_uv, devices):
    chips, wide, _ = other.shape
    heads = w_uv.shape[0]
    count = 2 * chips * wide // heads
    scratch = [pltpu.VMEM((PIECES, count * heads, LANES), jnp.float32)]
    kernel = functools.partial(values_kernel, devices)
    return call(kernel, shape(count, heads * VD), 3, "values", scratch)(
        *messages, other, resident(w_uv)
    )


def terms_kernel(start, val_ref, wo_ref, mine_ref, other_ref):
    half, width = mine_ref.shape
    terms = jnp.dot(
        val_ref[...], wo_ref[:, start : start + width], preferred_element_type=jnp.float32
    )
    mine_ref[...] = terms[:half]
    other_ref[...] = terms[half:].astype(jnp.bfloat16)


def output_terms(values, w_o, part):
    half = values.shape[0] // 2
    width = w_o.shape[1] // PARTS
    out = (shape(half, width, dtype=jnp.float32), shape(half, width))
    kernel = functools.partial(terms_kernel, part * width)
    return call(kernel, out, 6, "terms")(values, resident(w_o))


def far_z(devices):
    return [z for z in far_first(devices, Z1) if z > Z1][::-1]


def places(devices, chips):
    order = far_first(devices, 2)
    return [order.index(k) for k in chips]


def pick(total, rows, where):
    return jnp.concatenate([total[j * rows : (j + 1) * rows] for j in where], axis=0)


def first_sum_kernel(rows, keep, give, near, mine_ref, other_ref, keep_ref, give_ref, near_ref):
    total = mine_ref[...] + other_ref[...].astype(jnp.float32)
    keep_ref[...] = pick(total, rows, keep)
    give_ref[...] = pick(total, rows, give).astype(give_ref.dtype)
    near_ref[...] = pick(total, rows, near)


def last_part_kernel(rows, keep, give, near, mine_ref, other_ref, before_ref, *out_refs):
    keep_ref, give_ref, *near_refs = out_refs
    total = mine_ref[...] + other_ref[...].astype(jnp.float32)
    keep_ref[...] = pick(total, rows, keep)
    give_ref[...] = pick(total, rows, give).astype(give_ref.dtype)
    width = before_ref.shape[1]
    for i, (j, out_ref) in enumerate(zip(near, near_refs)):
        out_ref[:, :width] = before_ref[i * rows : (i + 1) * rows].astype(out_ref.dtype)
        out_ref[:, width:] = total[j * rows : (j + 1) * rows].astype(out_ref.dtype)


def core_sum(mine, other, before, rows, devices):
    count, width = mine.shape
    keep = places(devices, far_z(devices))
    give = places(devices, [z + Y for z in far_z(devices)])
    near = places(devices, [0, *NEAR])
    far = len(keep) * rows
    out = (shape(far, width, dtype=jnp.float32), shape(far, width))
    if before is None:
        kernel = functools.partial(first_sum_kernel, rows, keep, give, near)
        out += (shape(4 * rows, width, dtype=jnp.float32),)
        return call(kernel, out, 1, "core_sum")(mine, other)
    kernel = functools.partial(last_part_kernel, rows, keep, give, near)
    full = before.shape[1] + width
    out += (shape(rows, full, dtype=jnp.float32), *[shape(rows, full)] * len(NEAR))
    return call(kernel, out, 1, "core_sum")(mine, other, before)


def far_sum_kernel(*refs):
    mine_refs = refs[:PARTS]
    other_refs = refs[PARTS : 2 * PARTS]
    out_refs = refs[2 * PARTS :]
    rows = out_refs[0].shape[0]
    for p, (mine_ref, other_ref) in enumerate(zip(mine_refs, other_refs)):
        width = mine_ref.shape[1]
        total = mine_ref[...] + other_ref[...].astype(jnp.float32)
        for j, out_ref in enumerate(out_refs):
            out_ref[:, p * width : (p + 1) * width] = total[j * rows : (j + 1) * rows].astype(
                out_ref.dtype
            )


def far_sum(mine, other, rows):
    count, width = mine[0].shape
    out = [shape(rows, PARTS * width)] * (count // rows)
    return call(far_sum_kernel, out, 1, "far_sum")(*mine, *other)


def last_sum_kernel(*refs):
    *in_refs, out_ref = refs
    terms = [ref[...].astype(jnp.float32) for ref in in_refs]
    out_ref[...] = sum(terms[1:], terms[0]).astype(out_ref.dtype)


def last_sum(blocks):
    return call(last_sum_kernel, shape(*blocks[0].shape), 1, "last_sum")(*blocks)


def on_device(q_latent, new_latent, cache, lengths, w_uq, w_uk, w_uv, w_o, devices):
    heads = w_uk.shape[0]
    rows = cache.shape[0]
    zs = far_first(devices, 4)[::-1]

    def swap(block, k):
        if k == 0:
            return block
        return lax.ppermute(block, "row", [(i, i ^ k) for i in range(devices)])

    across = swap(q_latent, Y)
    far_weights = [swap(w_uq, 1), swap(w_uk, 1)]
    tables, near = join(rotary(lengths), [q_latent, across])
    def exchange(messages):
        *first, pair, own = messages
        got = []
        for block, chips in zip(first, zip(*sent_orders(devices))):
            flips = [Y if k == PASSED else k for k in chips]
            pairs = [(i, i ^ flips[i % 2]) for i in range(devices)]
            got.append(lax.ppermute(block, "row", pairs))
        sent, kept = forward(pair, *got[:2])
        return [kept, *got[2:], swap(sent, Z1), own], sent

    messages = project([swap(near, z) for z in zs], [w_uq, w_uk, *far_weights], devices)
    messages, sent = exchange(messages)
    keys = jnp.swapaxes(cache, 1, 2)
    flipped = flip(keys, sent)
    latents = attend(lengths, tables, keys, flipped, new_latent, messages, heads, devices)
    latents, sent = exchange(latents)
    other = swap(regroup(latents, early(latents[-1], sent), devices // 2), 1)
    values = head_values(latents, other, w_uv, devices)
    keep, got, near = [], [], None
    for part in range(PARTS):
        mine, other = output_terms(values, w_o, part)
        far_mine, far_other, near, *given = core_sum(mine, swap(other, 1), near, rows, devices)
        keep.append(far_mine)
        got.append(swap(far_other, Y))
    given = [swap(block, k) for block, k in zip(given, NEAR)]
    far = far_sum(keep, got, rows)
    far = [swap(block, z) for z, block in zip(far_z(devices), far)]
    return last_sum([near, *given, *far])


def solution(mesh):
    placed = (
        P(("grp", "row"), None),
        P(("grp", "row"), None),
        P(("grp", "row"), None, None),
        P(("grp", "row")),
        P(None, "row"),
        P("row", None, None),
        P("row", None, None),
        P("row", None),
    )
    body = functools.partial(on_device, devices=mesh.shape["row"])
    return jax.shard_map(
        body, mesh=mesh, in_specs=placed, out_specs=P(("grp", "row"), None), check_vma=False
    )
```

```python
import functools
import math

import jax
import jax.numpy as jnp
from jax import lax
from jax.experimental import pallas as pl
from jax.experimental.pallas import tpu as pltpu
from jax.sharding import PartitionSpec as P

LAT = 512
ROPE = 64
HALF = ROPE // 2
NOPE = 128
VD = 128
LANES = 128
PIECES = LAT // LANES
SCALE = (NOPE + ROPE) ** -0.5 * math.log2(math.e)
LIMIT = 16 * 2**20
PARTS = 2
Y = 2
Z1 = 4
NEAR = (Z1, Y + Z1, Y)


def resident(x):
    return pltpu.with_memory_space_constraint(x, pltpu.VMEM)


def in_vmem():
    return pl.BlockSpec(memory_space=pltpu.VMEM)


def call(kernel, out_shape, microseconds, name, scratch=(), scalars=0):
    def run(*args):
        smem = [pl.BlockSpec(memory_space=pltpu.SMEM)] * scalars
        return pl.pallas_call(
            kernel,
            out_shape=out_shape,
            in_specs=smem + [in_vmem()] * (len(args) - scalars),
            out_specs=jax.tree.map(lambda _: in_vmem(), out_shape),
            scratch_shapes=list(scratch),
            compiler_params=pltpu.CompilerParams(vmem_limit_bytes=LIMIT),
            cost_estimate=pl.CostEstimate(
                flops=int(microseconds * 1.15e9), bytes_accessed=0, transcendentals=0
            ),
            name=name,
        )(*args)

    return run


def shape(*dims, dtype=jnp.bfloat16):
    return jax.ShapeDtypeStruct(dims, dtype)


def far_first(devices, step):
    return sorted(range(0, devices, step), key=lambda k: -k.bit_length())


def far_chips(devices):
    return [k for k in far_first(devices, 2) if k > Y + Z1]


def chip_order(devices):
    return [*far_chips(devices), Y, Y + Z1, Z1, 0]


def message_sizes(devices):
    return [1] * len(far_chips(devices)) + [2, 1, 1]


def gathered_order(devices):
    return [z + y for z in reversed(far_first(devices, 4)) for y in (0, 2)]


def rotary_kernel(len_ref, cos_ref, sin_ref):
    rows, width = cos_ref.shape
    lane = lax.broadcasted_iota(jnp.int32, (rows, width), 1)
    place = lax.broadcasted_iota(jnp.int32, (rows, width), 0)
    step = jnp.where(lane < HALF, lane, lane - HALF).astype(jnp.float32)
    frequency = jnp.exp(step * (-math.log(10000.0) / HALF))
    length = jnp.zeros((rows, width), jnp.float32)
    for r in range(rows):
        length = jnp.where(place == r, len_ref[r].astype(jnp.float32), length)
    angle = length * frequency
    sine = jnp.sin(angle)
    cos_ref[...] = jnp.cos(angle)
    sin_ref[...] = jnp.where(lane < HALF, -sine, sine)


def rotary(lengths):
    table = shape(lengths.shape[0], ROPE, dtype=jnp.float32)
    return call(rotary_kernel, (table, table), 3, "rotary", scalars=1)(lengths)


def join_kernel(cos_ref, sin_ref, *refs):
    *in_refs, cos_out_ref, sin_out_ref, out_ref = refs
    cos_out_ref[...] = cos_ref[...]
    sin_out_ref[...] = sin_ref[...]
    out_ref[...] = jnp.concatenate(
        [ref[...].astype(jnp.float32) for ref in in_refs], axis=0
    ).astype(out_ref.dtype)


def join(tables, blocks):
    rows, depth = blocks[0].shape
    out = (*[shape(*t.shape, dtype=t.dtype) for t in tables], shape(len(blocks) * rows, depth))
    cosine, sine, joined = call(join_kernel, out, 3, "join")(*tables, *blocks)
    return (cosine, sine), joined


def project_kernel(devices, *refs):
    pieces = devices // 4
    q_refs = refs[:pieces]
    weights = (refs[pieces : pieces + 2], refs[pieces + 2 : pieces + 4])
    lat_ref, rot_ref = refs[-2:]
    out_refs = refs[pieces + 4 : -2]
    heads = weights[0][1].shape[0]
    piece = jnp.concatenate([ref[...].astype(jnp.float32) for ref in q_refs], axis=0)
    piece = piece.astype(jnp.bfloat16)
    count = piece.shape[0]
    wide = 2 * count // devices * heads
    width = NOPE + ROPE
    lane = lax.broadcasted_iota(jnp.int32, (wide // 2, LANES), 1)
    blocks = [(ref, 2 * i) for ref in out_refs for i in range(ref.shape[0] // 2)]
    blocks = dict(zip(chip_order(devices), blocks))
    for core, (wq_ref, wk_ref) in enumerate(weights):
        projected = jnp.dot(piece, wq_ref[...], preferred_element_type=jnp.float32)
        for h in range(heads):
            mine = projected[:, h * width : (h + 1) * width]
            absorbed = jnp.dot(
                mine[:, :NOPE].astype(jnp.bfloat16), wk_ref[h], preferred_element_type=jnp.float32
            )
            spread = pl.ds(h, count, stride=heads)
            for c in range(PIECES):
                lat_ref[core * PIECES + c, spread, :] = absorbed[:, c * LANES : (c + 1) * LANES]
            pe = mine[:, NOPE:]
            rot_ref[core, spread, :] = jnp.concatenate([pe, pe], axis=-1)
        for place, k in enumerate(gathered_order(devices)):
            out_ref, at = blocks[k]
            at += core
            first = place * wide
            for c in range(PIECES):
                out_ref[at, c * wide : (c + 1) * wide, :] = lat_ref[
                    core * PIECES + c, first : first + wide, :
                ].astype(jnp.bfloat16)
            low = rot_ref[core, first : first + wide // 2, :]
            high = rot_ref[core, first + wide // 2 : first + wide, :]
            out_ref[at, PIECES * wide :, :] = jnp.where(lane < ROPE, low, high).astype(
                jnp.bfloat16
            )


def project(pieces, weights, devices):
    heads = weights[1].shape[0]
    count = len(pieces) * pieces[0].shape[0]
    wide = 2 * count // devices * heads
    scratch = [
        pltpu.VMEM((2 * PIECES, count * heads, LANES), jnp.float32),
        pltpu.VMEM((2, count * heads, LANES), jnp.float32),
    ]
    tall = PIECES * wide + wide // 2
    out = [shape(2 * size, tall, LANES) for size in message_sizes(devices)]
    kernel = functools.partial(project_kernel, devices)
    return call(kernel, out, 20, "project", scratch)(*pieces, *[resident(w) for w in weights])


def flip_kernel(key_ref, after_ref, out_ref):
    for r in range(key_ref.shape[0]):
        out_ref[r] = key_ref[r, :LAT, :].T


def flip(keys, after):
    rows, _, maxlen = keys.shape
    return call(flip_kernel, shape(rows, maxlen, LAT), 4, "flip")(resident(keys), after)


def forward_kernel(own_ref, passing_ref, out_ref):
    out_ref[:2] = own_ref[...]
    out_ref[2:] = passing_ref[2:]


def forward(own, passing):
    return call(forward_kernel, shape(4, *own.shape[1:]), 1, "forward")(own, passing)


def arrived(refs):
    blocks = []
    for i, ref in enumerate(refs):
        count = 2 if i == len(refs) - 3 else ref.shape[0]
        blocks += [(ref, core) for core in range(count)]
    return blocks


def attend_kernel(sizes, len_ref, cos_ref, sin_ref, key_ref, flip_ref, new_ref, *refs):
    blocks = arrived(refs[: len(sizes)])
    out_refs = refs[len(sizes) :]
    rows, _, maxlen = key_ref.shape
    wide = out_refs[0].shape[1]
    heads = wide // rows

    def query_block(first):
        parts = [ref[i, first : first + heads, :].astype(jnp.float32) for ref, i in blocks]
        return jnp.concatenate(parts, axis=0)

    def score(r):
        latent = jnp.concatenate(
            [query_block(c * wide + r * heads) for c in range(PIECES)], axis=-1
        )
        pe = query_block(PIECES * wide + (r % (rows // 2)) * heads)
        side = r // (rows // 2) * ROPE
        pe = pe[:, side : side + ROPE]
        swapped = jnp.concatenate([pe[:, HALF:], pe[:, :HALF]], axis=-1)
        rotated = (pe * cos_ref[r : r + 1, :] + swapped * sin_ref[r : r + 1, :]).astype(jnp.bfloat16)
        newest = new_ref[r : r + 1, :].astype(jnp.float32)
        own = jnp.sum(latent * newest[:, :LAT], axis=-1, keepdims=True) + jnp.sum(
            rotated.astype(jnp.float32) * newest[:, LAT:], axis=-1, keepdims=True
        )
        scores = jnp.dot(
            latent.astype(jnp.bfloat16), key_ref[r, :LAT, :], preferred_element_type=jnp.float32
        )
        scores += jnp.dot(rotated, key_ref[r, LAT:, :], preferred_element_type=jnp.float32)
        position = lax.broadcasted_iota(jnp.int32, (1, maxlen), 1)
        return jnp.where(position < len_ref[r], scores, -jnp.inf), own

    back = [(ref, i) for ref in out_refs for i in range(ref.shape[0])]
    y_at = len(back) - 8
    back = back[: y_at + 2] + back[y_at + 4 : y_at + 6] + back[y_at + 2 : y_at + 4] + back[-2:]
    ahead = score(0)
    for r in range(rows):
        scores, own = ahead
        if r + 1 < rows:
            ahead = score(r + 1)
        peak = jnp.maximum(jnp.max(scores, axis=-1, keepdims=True), own)
        expo = jnp.exp2((scores - peak) * SCALE)
        own_expo = jnp.exp2((own - peak) * SCALE)
        inverse = 1.0 / (jnp.sum(expo, axis=-1, keepdims=True) + own_expo)
        weights = (expo * inverse).astype(jnp.bfloat16)
        own_weight = (own_expo * inverse).astype(jnp.bfloat16).astype(jnp.float32)
        summed = jnp.dot(weights, flip_ref[r], preferred_element_type=jnp.float32)
        summed += own_weight * new_ref[r : r + 1, :LAT].astype(jnp.float32)
        for k, (out_ref, i) in enumerate(back):
            out_ref[i, r * heads : (r + 1) * heads, :] = summed[
                k * heads : (k + 1) * heads, :
            ].astype(jnp.bfloat16)


def attend(lengths, tables, keys, flipped, new_latent, messages, heads, devices):
    sizes = message_sizes(devices)
    out = [shape(2 * size, keys.shape[0] * heads, LAT) for size in sizes]
    return call(functools.partial(attend_kernel, sizes), out, 10, "attend", scalars=1)(
        lengths, *tables, resident(keys), resident(flipped), new_latent, *messages
    )


def early_kernel(passing_ref, own_ref, after_ref, out_ref):
    out_ref[0] = passing_ref[1]
    out_ref[1] = own_ref[1]


def early(passing, own, after):
    return call(early_kernel, shape(2, *own.shape[1:]), 4, "early")(passing, own, after)


def regroup_kernel(*refs):
    *in_refs, early_ref, out_ref = refs
    blocks = arrived(in_refs)[1::2]
    blocks = [*blocks[:-4], (early_ref, 0), *blocks[-3:-1], (early_ref, 1)]
    for j, (ref, i) in enumerate(blocks):
        out_ref[j] = ref[i]


def regroup(messages, ready, chips):
    _, wide, width = messages[0].shape
    return call(regroup_kernel, shape(chips, wide, width), 1, "regroup")(*messages, ready)


def values_kernel(count, *refs):
    blocks = arrived(refs[:count])
    blocks = blocks[::2] if count > 1 else blocks
    wv_ref, val_ref, rows_ref = refs[count], *refs[-2:]
    heads = wv_ref.shape[0]
    for place, (ref, i) in enumerate(blocks):
        block = ref[i].astype(jnp.float32)
        wide = block.shape[0]
        for c in range(PIECES):
            rows_ref[c, place * wide : (place + 1) * wide, :] = block[:, c * LANES : (c + 1) * LANES]
    total = val_ref.shape[0]
    for h in range(heads):
        chosen = jnp.concatenate(
            [rows_ref[c, pl.ds(h, total, stride=heads), :] for c in range(PIECES)], axis=-1
        )
        val_ref[:, h * VD : (h + 1) * VD] = jnp.dot(
            chosen.astype(jnp.bfloat16), wv_ref[h], preferred_element_type=jnp.float32
        ).astype(jnp.bfloat16)


def head_values(messages, w_uv, chips, *after):
    heads = w_uv.shape[0]
    count = chips * messages[0].shape[1] // heads
    scratch = [pltpu.VMEM((PIECES, count * heads, LANES), jnp.float32)]
    kernel = functools.partial(values_kernel, len(messages))
    return call(kernel, shape(count, heads * VD), 2, "values", scratch)(
        *messages, resident(w_uv), *after
    )


def terms_kernel(start, *refs):
    *val_refs, wo_ref = refs[: len(refs) // 2 + 1]
    out_refs = refs[len(refs) // 2 + 1 :]
    half, width = out_refs[0].shape
    values = jnp.concatenate([ref[...] for ref in val_refs], axis=0)
    terms = jnp.dot(values, wo_ref[:, start : start + width], preferred_element_type=jnp.float32)
    for i, out_ref in enumerate(out_refs):
        out_ref[...] = terms[i * half : (i + 1) * half].astype(out_ref.dtype)


def output_terms(values, types, w_o, part):
    width = w_o.shape[1] // PARTS
    out = [shape(v.shape[0], width, dtype=t) for v, t in zip(values, types)]
    kernel = functools.partial(terms_kernel, part * width)
    return call(kernel, out, 3 * len(values), "terms")(*values, resident(w_o))


def far_z(devices):
    return [z for z in far_first(devices, Z1) if z > Z1][::-1]


def places(devices, chips):
    order = [*far_chips(devices), Y, Z1, Y + Z1, 0]
    return [order.index(k) for k in chips]


def pick(total, rows, where):
    return jnp.concatenate([total[j * rows : (j + 1) * rows] for j in where], axis=0)


def first_sum_kernel(rows, keep, give, near, mine_ref, other_ref, keep_ref, give_ref, near_ref):
    total = mine_ref[...] + other_ref[...].astype(jnp.float32)
    keep_ref[...] = pick(total, rows, keep)
    give_ref[...] = pick(total, rows, give).astype(give_ref.dtype)
    near_ref[...] = pick(total, rows, near)


def last_part_kernel(rows, keep, give, near, mine_ref, other_ref, before_ref, *out_refs):
    keep_ref, give_ref, *near_refs = out_refs
    total = mine_ref[...] + other_ref[...].astype(jnp.float32)
    keep_ref[...] = pick(total, rows, keep)
    give_ref[...] = pick(total, rows, give).astype(give_ref.dtype)
    width = before_ref.shape[1]
    for i, (j, out_ref) in enumerate(zip(near, near_refs)):
        out_ref[:, :width] = before_ref[i * rows : (i + 1) * rows].astype(out_ref.dtype)
        out_ref[:, width:] = total[j * rows : (j + 1) * rows].astype(out_ref.dtype)


def core_sum(mine, other, before, rows, devices):
    count, width = mine.shape
    keep = places(devices, far_z(devices))
    give = places(devices, [z + Y for z in far_z(devices)])
    near = places(devices, [0, *NEAR])
    far = len(keep) * rows
    out = (shape(far, width, dtype=jnp.float32), shape(far, width))
    if before is None:
        kernel = functools.partial(first_sum_kernel, rows, keep, give, near)
        out += (shape(4 * rows, width, dtype=jnp.float32),)
        return call(kernel, out, 1, "core_sum")(mine, other)
    kernel = functools.partial(last_part_kernel, rows, keep, give, near)
    full = before.shape[1] + width
    out += (shape(rows, full, dtype=jnp.float32), *[shape(rows, full)] * len(NEAR))
    return call(kernel, out, 1, "core_sum")(mine, other, before)


def far_sum_kernel(*refs):
    mine_refs = refs[:PARTS]
    other_refs = refs[PARTS : 2 * PARTS]
    out_refs = refs[2 * PARTS :]
    rows = out_refs[0].shape[0]
    for p, (mine_ref, other_ref) in enumerate(zip(mine_refs, other_refs)):
        width = mine_ref.shape[1]
        total = mine_ref[...] + other_ref[...].astype(jnp.float32)
        for j, out_ref in enumerate(out_refs):
            out_ref[:, p * width : (p + 1) * width] = total[j * rows : (j + 1) * rows].astype(
                out_ref.dtype
            )


def far_sum(mine, other, rows):
    count, width = mine[0].shape
    out = [shape(rows, PARTS * width)] * (count // rows)
    return call(far_sum_kernel, out, 1, "far_sum")(*mine, *other)


def last_sum_kernel(*refs):
    *in_refs, out_ref = refs
    terms = [ref[...].astype(jnp.float32) for ref in in_refs]
    out_ref[...] = sum(terms[1:], terms[0]).astype(out_ref.dtype)


def last_sum(blocks):
    return call(last_sum_kernel, shape(*blocks[0].shape), 1, "last_sum")(*blocks)


def on_device(q_latent, new_latent, cache, lengths, w_uq, w_uk, w_uv, w_o, devices):
    heads = w_uk.shape[0]
    rows = cache.shape[0]
    zs = far_first(devices, 4)[::-1]

    def swap(block, k):
        if k == 0:
            return block
        return lax.ppermute(block, "row", [(i, i ^ k) for i in range(devices)])

    across = swap(q_latent, Y)
    far_weights = [swap(w_uq, 1), swap(w_uk, 1)]
    tables, near = join(rotary(lengths), [q_latent, across])
    def exchange(messages):
        *far, across, pair, own = messages
        early = len(far) // 2
        got = [swap(block, k) for block, k in zip(far[:early], far_k)]
        passing = swap(across, Y)
        got += [swap(block, k) for block, k in zip(far[early:], far_k[early:])]
        sent = forward(pair, passing)
        return [*got, passing, swap(sent, Z1), own], sent

    far_k = far_chips(devices)
    messages = project([swap(near, z) for z in zs], [w_uq, w_uk, *far_weights], devices)
    messages, sent = exchange(messages)
    keys = jnp.swapaxes(cache, 1, 2)
    flipped = flip(keys, sent)
    latents = attend(lengths, tables, keys, flipped, new_latent, messages, heads, devices)
    latents, sent = exchange(latents)
    ready = early(latents[-3], latents[-1], sent)
    other = swap(regroup(latents, ready, devices // 2), 1)
    here, there = jnp.float32, jnp.bfloat16
    mine_values = head_values(latents, w_uv, devices // 2)
    early_mine = output_terms([mine_values], [here], w_o, 0)
    other_values = head_values([other], w_uv, devices // 2, *early_mine)
    keep, got, near = [], [], None
    for part in range(PARTS):
        if part == 0:
            mine, other = *early_mine, *output_terms([other_values], [there], w_o, 0)
        else:
            mine, other = output_terms([mine_values, other_values], [here, there], w_o, part)
        far_mine, far_other, near, *given = core_sum(mine, swap(other, 1), near, rows, devices)
        keep.append(far_mine)
        got.append(swap(far_other, Y))
    given = [swap(block, k) for block, k in zip(given, NEAR)]
    far = far_sum(keep, got, rows)
    far = [swap(block, z) for z, block in zip(far_z(devices), far)]
    return last_sum([near, *given, *far])


def solution(mesh):
    placed = (
        P(("grp", "row"), None),
        P(("grp", "row"), None),
        P(("grp", "row"), None, None),
        P(("grp", "row")),
        P(None, "row"),
        P("row", None, None),
        P("row", None, None),
        P("row", None),
    )
    body = functools.partial(on_device, devices=mesh.shape["row"])
    return jax.shard_map(
        body, mesh=mesh, in_specs=placed, out_specs=P(("grp", "row"), None), check_vma=False
    )
```

```python
import functools
import math

import jax
import jax.numpy as jnp
from jax import lax
from jax.experimental import pallas as pl
from jax.experimental.pallas import tpu as pltpu
from jax.sharding import PartitionSpec as P

LAT = 512
ROPE = 64
HALF = ROPE // 2
NOPE = 128
VD = 128
LANES = 128
PIECES = LAT // LANES
SCALE = (NOPE + ROPE) ** -0.5 * math.log2(math.e)
LIMIT = 16 * 2**20
PARTS = 2
Y = 2
Z1 = 4
NEAR = (Z1, Y + Z1, Y)


def resident(x):
    return pltpu.with_memory_space_constraint(x, pltpu.VMEM)


def in_vmem():
    return pl.BlockSpec(memory_space=pltpu.VMEM)


def call(kernel, out_shape, microseconds, name, scratch=(), scalars=0):
    def run(*args):
        smem = [pl.BlockSpec(memory_space=pltpu.SMEM)] * scalars
        return pl.pallas_call(
            kernel,
            out_shape=out_shape,
            in_specs=smem + [in_vmem()] * (len(args) - scalars),
            out_specs=jax.tree.map(lambda _: in_vmem(), out_shape),
            scratch_shapes=list(scratch),
            compiler_params=pltpu.CompilerParams(vmem_limit_bytes=LIMIT),
            cost_estimate=pl.CostEstimate(
                flops=int(microseconds * 1.15e9), bytes_accessed=0, transcendentals=0
            ),
            name=name,
        )(*args)

    return run


def shape(*dims, dtype=jnp.bfloat16):
    return jax.ShapeDtypeStruct(dims, dtype)


def far_first(devices, step):
    return sorted(range(0, devices, step), key=lambda k: -k.bit_length())


def far_chips(devices):
    return [k for k in far_first(devices, 2) if k > Y + Z1]


def chip_order(devices):
    return [*far_chips(devices), Y, Y + Z1, Z1, 0]


def message_sizes(devices):
    return [1] * len(far_chips(devices)) + [2, 1, 1]


def gathered_order(devices):
    return [z + y for z in reversed(far_first(devices, 4)) for y in (0, 2)]


def rotary_kernel(len_ref, cos_ref, sin_ref):
    rows, width = cos_ref.shape
    lane = lax.broadcasted_iota(jnp.int32, (rows, width), 1)
    place = lax.broadcasted_iota(jnp.int32, (rows, width), 0)
    step = jnp.where(lane < HALF, lane, lane - HALF).astype(jnp.float32)
    frequency = jnp.exp(step * (-math.log(10000.0) / HALF))
    length = jnp.zeros((rows, width), jnp.float32)
    for r in range(rows):
        length = jnp.where(place == r, len_ref[r].astype(jnp.float32), length)
    angle = length * frequency
    sine = jnp.sin(angle)
    cos_ref[...] = jnp.cos(angle)
    sin_ref[...] = jnp.where(lane < HALF, -sine, sine)


def rotary(lengths):
    table = shape(lengths.shape[0], ROPE, dtype=jnp.float32)
    return call(rotary_kernel, (table, table), 3, "rotary", scalars=1)(lengths)


def stage_kernel(in_ref, out_ref):
    out_ref[...] = in_ref[...]


def stage(block):
    return call(stage_kernel, shape(*block.shape), 1, "stage")(block)


def join_kernel(cos_ref, sin_ref, *refs):
    *in_refs, cos_out_ref, sin_out_ref, out_ref = refs
    cos_out_ref[...] = cos_ref[...]
    sin_out_ref[...] = sin_ref[...]
    out_ref[...] = jnp.concatenate(
        [ref[...].astype(jnp.float32) for ref in in_refs], axis=0
    ).astype(out_ref.dtype)


def join(tables, blocks):
    rows, depth = blocks[0].shape
    out = (*[shape(*t.shape, dtype=t.dtype) for t in tables], shape(len(blocks) * rows, depth))
    cosine, sine, joined = call(join_kernel, out, 3, "join")(*tables, *blocks)
    return (cosine, sine), joined


def project_kernel(devices, *refs):
    pieces = devices // 4
    q_refs = refs[:pieces]
    weights = (refs[pieces : pieces + 2], refs[pieces + 2 : pieces + 4])
    lat_ref, rot_ref = refs[-2:]
    out_refs = refs[pieces + 4 : -2]
    heads = weights[0][1].shape[0]
    piece = jnp.concatenate([ref[...].astype(jnp.float32) for ref in q_refs], axis=0)
    piece = piece.astype(jnp.bfloat16)
    count = piece.shape[0]
    wide = 2 * count // devices * heads
    width = NOPE + ROPE
    lane = lax.broadcasted_iota(jnp.int32, (wide // 2, LANES), 1)
    blocks = [(ref, 2 * i) for ref in out_refs for i in range(ref.shape[0] // 2)]
    blocks = dict(zip(chip_order(devices), blocks))
    for core, (wq_ref, wk_ref) in enumerate(weights):
        projected = jnp.dot(piece, wq_ref[...], preferred_element_type=jnp.float32)
        for h in range(heads):
            mine = projected[:, h * width : (h + 1) * width]
            absorbed = jnp.dot(
                mine[:, :NOPE].astype(jnp.bfloat16), wk_ref[h], preferred_element_type=jnp.float32
            )
            spread = pl.ds(h, count, stride=heads)
            for c in range(PIECES):
                lat_ref[core * PIECES + c, spread, :] = absorbed[:, c * LANES : (c + 1) * LANES]
            pe = mine[:, NOPE:]
            rot_ref[core, spread, :] = jnp.concatenate([pe, pe], axis=-1)
        for place, k in enumerate(gathered_order(devices)):
            out_ref, at = blocks[k]
            at += core
            first = place * wide
            for c in range(PIECES):
                out_ref[at, c * wide : (c + 1) * wide, :] = lat_ref[
                    core * PIECES + c, first : first + wide, :
                ].astype(jnp.bfloat16)
            low = rot_ref[core, first : first + wide // 2, :]
            high = rot_ref[core, first + wide // 2 : first + wide, :]
            out_ref[at, PIECES * wide :, :] = jnp.where(lane < ROPE, low, high).astype(
                jnp.bfloat16
            )


def project(pieces, weights, devices):
    heads = weights[1].shape[0]
    count = len(pieces) * pieces[0].shape[0]
    wide = 2 * count // devices * heads
    scratch = [
        pltpu.VMEM((2 * PIECES, count * heads, LANES), jnp.float32),
        pltpu.VMEM((2, count * heads, LANES), jnp.float32),
    ]
    tall = PIECES * wide + wide // 2
    out = [shape(2 * size, tall, LANES) for size in message_sizes(devices)]
    kernel = functools.partial(project_kernel, devices)
    return call(kernel, out, 20, "project", scratch)(*pieces, *[resident(w) for w in weights])


def flip_kernel(key_ref, after_ref, out_ref):
    for r in range(key_ref.shape[0]):
        out_ref[r] = key_ref[r, :LAT, :].T


def flip(keys, after):
    rows, _, maxlen = keys.shape
    return call(flip_kernel, shape(rows, maxlen, LAT), 4, "flip")(resident(keys), after)


def forward_kernel(own_ref, passing_ref, out_ref):
    out_ref[:2] = own_ref[...]
    out_ref[2:] = passing_ref[2:]


def forward(own, passing):
    return call(forward_kernel, shape(4, *own.shape[1:]), 1, "forward")(own, passing)


def arrived(refs):
    blocks = []
    for i, ref in enumerate(refs):
        count = 2 if i == len(refs) - 3 else ref.shape[0]
        blocks += [(ref, core) for core in range(count)]
    return blocks


def attend_kernel(sizes, len_ref, cos_ref, sin_ref, key_ref, flip_ref, new_ref, *refs):
    blocks = arrived(refs[: len(sizes)])
    out_refs = refs[len(sizes) :]
    rows, _, maxlen = key_ref.shape
    wide = out_refs[0].shape[1]
    heads = wide // rows

    def query_block(first):
        parts = [ref[i, first : first + heads, :].astype(jnp.float32) for ref, i in blocks]
        return jnp.concatenate(parts, axis=0)

    def score(r):
        latent = jnp.concatenate(
            [query_block(c * wide + r * heads) for c in range(PIECES)], axis=-1
        )
        pe = query_block(PIECES * wide + (r % (rows // 2)) * heads)
        side = r // (rows // 2) * ROPE
        pe = pe[:, side : side + ROPE]
        swapped = jnp.concatenate([pe[:, HALF:], pe[:, :HALF]], axis=-1)
        rotated = (pe * cos_ref[r : r + 1, :] + swapped * sin_ref[r : r + 1, :]).astype(jnp.bfloat16)
        newest = new_ref[r : r + 1, :].astype(jnp.float32)
        own = jnp.sum(latent * newest[:, :LAT], axis=-1, keepdims=True) + jnp.sum(
            rotated.astype(jnp.float32) * newest[:, LAT:], axis=-1, keepdims=True
        )
        scores = jnp.dot(
            latent.astype(jnp.bfloat16), key_ref[r, :LAT, :], preferred_element_type=jnp.float32
        )
        scores += jnp.dot(rotated, key_ref[r, LAT:, :], preferred_element_type=jnp.float32)
        position = lax.broadcasted_iota(jnp.int32, (1, maxlen), 1)
        return jnp.where(position < len_ref[r], scores, -jnp.inf), own

    back = [(ref, i) for ref in out_refs for i in range(ref.shape[0])]
    y_at = len(back) - 8
    back = back[: y_at + 2] + back[y_at + 4 : y_at + 6] + back[y_at + 2 : y_at + 4] + back[-2:]
    ahead = score(0)
    for r in range(rows):
        scores, own = ahead
        if r + 1 < rows:
            ahead = score(r + 1)
        peak = jnp.maximum(jnp.max(scores, axis=-1, keepdims=True), own)
        expo = jnp.exp2((scores - peak) * SCALE)
        own_expo = jnp.exp2((own - peak) * SCALE)
        inverse = 1.0 / (jnp.sum(expo, axis=-1, keepdims=True) + own_expo)
        weights = (expo * inverse).astype(jnp.bfloat16)
        own_weight = (own_expo * inverse).astype(jnp.bfloat16).astype(jnp.float32)
        summed = jnp.dot(weights, flip_ref[r], preferred_element_type=jnp.float32)
        summed += own_weight * new_ref[r : r + 1, :LAT].astype(jnp.float32)
        for k, (out_ref, i) in enumerate(back):
            out_ref[i, r * heads : (r + 1) * heads, :] = summed[
                k * heads : (k + 1) * heads, :
            ].astype(jnp.bfloat16)


def attend(lengths, tables, keys, flipped, new_latent, messages, heads, devices):
    sizes = message_sizes(devices)
    out = [shape(2 * size, keys.shape[0] * heads, LAT) for size in sizes]
    return call(functools.partial(attend_kernel, sizes), out, 10, "attend", scalars=1)(
        lengths, *tables, resident(keys), resident(flipped), new_latent, *messages
    )


def early_kernel(passing_ref, own_ref, after_ref, out_ref):
    out_ref[0] = passing_ref[1]
    out_ref[1] = own_ref[1]


def early(passing, own, after):
    return call(early_kernel, shape(2, *own.shape[1:]), 4, "early")(passing, own, after)


def regroup_kernel(*refs):
    *in_refs, early_ref, out_ref = refs
    blocks = arrived(in_refs)[1::2]
    blocks = [*blocks[:-4], (early_ref, 0), *blocks[-3:-1], (early_ref, 1)]
    for j, (ref, i) in enumerate(blocks):
        out_ref[j] = ref[i]


def regroup(messages, ready, chips):
    _, wide, width = messages[0].shape
    return call(regroup_kernel, shape(chips, wide, width), 1, "regroup")(*messages, ready)


def values_kernel(*refs):
    *in_refs, other_ref, wv_ref, val_ref, rows_ref = refs
    mine = arrived(in_refs)[::2]
    chips = len(mine)
    heads = wv_ref.shape[0]
    wide = other_ref.shape[1]
    for place in range(2 * chips):
        ref, i = mine[place] if place < chips else (other_ref, place - chips)
        block = ref[i].astype(jnp.float32)
        for c in range(PIECES):
            rows_ref[c, place * wide : (place + 1) * wide, :] = block[:, c * LANES : (c + 1) * LANES]
    count = val_ref.shape[0]
    for h in range(heads):
        chosen = jnp.concatenate(
            [rows_ref[c, pl.ds(h, count, stride=heads), :] for c in range(PIECES)], axis=-1
        )
        val_ref[:, h * VD : (h + 1) * VD] = jnp.dot(
            chosen.astype(jnp.bfloat16), wv_ref[h], preferred_element_type=jnp.float32
        ).astype(jnp.bfloat16)


def head_values(messages, other, w_uv):
    chips, wide, _ = other.shape
    heads = w_uv.shape[0]
    count = 2 * chips * wide // heads
    scratch = [pltpu.VMEM((PIECES, count * heads, LANES), jnp.float32)]
    return call(values_kernel, shape(count, heads * VD), 3, "values", scratch)(
        *messages, other, resident(w_uv)
    )


def terms_kernel(start, val_ref, wo_ref, mine_ref, other_ref):
    half, width = mine_ref.shape
    terms = jnp.dot(
        val_ref[...], wo_ref[:, start : start + width], preferred_element_type=jnp.float32
    )
    mine_ref[...] = terms[:half]
    other_ref[...] = terms[half:].astype(jnp.bfloat16)


def output_terms(values, w_o, part):
    half = values.shape[0] // 2
    width = w_o.shape[1] // PARTS
    out = (shape(half, width, dtype=jnp.float32), shape(half, width))
    kernel = functools.partial(terms_kernel, part * width)
    return call(kernel, out, 6, "terms")(values, resident(w_o))


def far_z(devices):
    return [z for z in far_first(devices, Z1) if z > Z1][::-1]


def places(devices, chips):
    order = [*far_chips(devices), Y, Z1, Y + Z1, 0]
    return [order.index(k) for k in chips]


def pick(total, rows, where):
    return jnp.concatenate([total[j * rows : (j + 1) * rows] for j in where], axis=0)


def first_sum_kernel(rows, keep, give, near, mine_ref, other_ref, keep_ref, give_ref, near_ref):
    total = mine_ref[...] + other_ref[...].astype(jnp.float32)
    keep_ref[...] = pick(total, rows, keep)
    give_ref[...] = pick(total, rows, give).astype(give_ref.dtype)
    near_ref[...] = pick(total, rows, near)


def last_part_kernel(rows, keep, give, near, mine_ref, other_ref, before_ref, *out_refs):
    keep_ref, give_ref, *near_refs = out_refs
    total = mine_ref[...] + other_ref[...].astype(jnp.float32)
    keep_ref[...] = pick(total, rows, keep)
    give_ref[...] = pick(total, rows, give).astype(give_ref.dtype)
    width = before_ref.shape[1]
    for i, (j, out_ref) in enumerate(zip(near, near_refs)):
        out_ref[:, :width] = before_ref[i * rows : (i + 1) * rows].astype(out_ref.dtype)
        out_ref[:, width:] = total[j * rows : (j + 1) * rows].astype(out_ref.dtype)


def core_sum(mine, other, before, rows, devices):
    count, width = mine.shape
    keep = places(devices, far_z(devices))
    give = places(devices, [z + Y for z in far_z(devices)])
    near = places(devices, [0, *NEAR])
    far = len(keep) * rows
    out = (shape(far, width, dtype=jnp.float32), shape(far, width))
    if before is None:
        kernel = functools.partial(first_sum_kernel, rows, keep, give, near)
        out += (shape(4 * rows, width, dtype=jnp.float32),)
        return call(kernel, out, 1, "core_sum")(mine, other)
    kernel = functools.partial(last_part_kernel, rows, keep, give, near)
    full = before.shape[1] + width
    out += (shape(rows, full, dtype=jnp.float32), *[shape(rows, full)] * len(NEAR))
    return call(kernel, out, 1, "core_sum")(mine, other, before)


def far_sum_kernel(*refs):
    mine_refs = refs[:PARTS]
    other_refs = refs[PARTS : 2 * PARTS]
    out_refs = refs[2 * PARTS :]
    rows = out_refs[0].shape[0]
    for p, (mine_ref, other_ref) in enumerate(zip(mine_refs, other_refs)):
        width = mine_ref.shape[1]
        total = mine_ref[...] + other_ref[...].astype(jnp.float32)
        for j, out_ref in enumerate(out_refs):
            out_ref[:, p * width : (p + 1) * width] = total[j * rows : (j + 1) * rows].astype(
                out_ref.dtype
            )


def far_sum(mine, other, rows):
    count, width = mine[0].shape
    out = [shape(rows, PARTS * width)] * (count // rows)
    return call(far_sum_kernel, out, 1, "far_sum")(*mine, *other)


def last_sum_kernel(*refs):
    *in_refs, out_ref = refs
    terms = [ref[...].astype(jnp.float32) for ref in in_refs]
    out_ref[...] = sum(terms[1:], terms[0]).astype(out_ref.dtype)


def last_sum(blocks):
    return call(last_sum_kernel, shape(*blocks[0].shape), 1, "last_sum")(*blocks)


def on_device(q_latent, new_latent, cache, lengths, w_uq, w_uk, w_uv, w_o, devices):
    heads = w_uk.shape[0]
    rows = cache.shape[0]
    zs = far_first(devices, 4)[::-1]

    def swap(block, k):
        if k == 0:
            return block
        return lax.ppermute(block, "row", [(i, i ^ k) for i in range(devices)])

    own_rows = stage(q_latent)
    across = swap(own_rows, Y)
    far_weights = [swap(w_uq, 1), swap(w_uk, 1)]
    tables, near = join(rotary(lengths), [own_rows, across])
    def exchange(messages):
        *far, across, pair, own = messages
        early = len(far) // 2
        got = [swap(block, k) for block, k in zip(far[:early], far_k)]
        passing = swap(across, Y)
        got += [swap(block, k) for block, k in zip(far[early:], far_k[early:])]
        sent = forward(pair, passing)
        return [*got, passing, swap(sent, Z1), own], sent

    far_k = far_chips(devices)
    messages = project([swap(near, z) for z in zs], [w_uq, w_uk, *far_weights], devices)
    messages, sent = exchange(messages)
    keys = jnp.swapaxes(cache, 1, 2)
    flipped = flip(keys, sent)
    latents = attend(lengths, tables, keys, flipped, new_latent, messages, heads, devices)
    latents, sent = exchange(latents)
    ready = early(latents[-3], latents[-1], sent)
    values = head_values(latents, swap(regroup(latents, ready, devices // 2), 1), w_uv)
    keep, got, near = [], [], None
    for part in range(PARTS):
        mine, other = output_terms(values, w_o, part)
        far_mine, far_other, near, *given = core_sum(mine, swap(other, 1), near, rows, devices)
        keep.append(far_mine)
        got.append(swap(far_other, Y))
    given = [swap(block, k) for block, k in zip(given, NEAR)]
    far = far_sum(keep, got, rows)
    far = [swap(block, z) for z, block in zip(far_z(devices), far)]
    return last_sum([near, *given, *far])


def solution(mesh):
    placed = (
        P(("grp", "row"), None),
        P(("grp", "row"), None),
        P(("grp", "row"), None, None),
        P(("grp", "row")),
        P(None, "row"),
        P("row", None, None),
        P("row", None, None),
        P("row", None),
    )
    body = functools.partial(on_device, devices=mesh.shape["row"])
    return jax.shard_map(
        body, mesh=mesh, in_specs=placed, out_specs=P(("grp", "row"), None), check_vma=False
    )
```

```python
import functools
import math

import jax
import jax.numpy as jnp
from jax import lax
from jax.experimental import pallas as pl
from jax.experimental.pallas import tpu as pltpu
from jax.sharding import PartitionSpec as P

LAT = 512
ROPE = 64
HALF = ROPE // 2
NOPE = 128
VD = 128
LANES = 128
PIECES = LAT // LANES
SCALE = (NOPE + ROPE) ** -0.5 * math.log2(math.e)
LIMIT = 16 * 2**20
PARTS = 2
Y = 2
Z1 = 4
NEAR = (Z1, Y + Z1, Y)


def resident(x):
    return pltpu.with_memory_space_constraint(x, pltpu.VMEM)


def in_vmem():
    return pl.BlockSpec(memory_space=pltpu.VMEM)


def call(kernel, out_shape, microseconds, name, scratch=(), scalars=0):
    def run(*args):
        smem = [pl.BlockSpec(memory_space=pltpu.SMEM)] * scalars
        return pl.pallas_call(
            kernel,
            out_shape=out_shape,
            in_specs=smem + [in_vmem()] * (len(args) - scalars),
            out_specs=jax.tree.map(lambda _: in_vmem(), out_shape),
            scratch_shapes=list(scratch),
            compiler_params=pltpu.CompilerParams(vmem_limit_bytes=LIMIT),
            cost_estimate=pl.CostEstimate(
                flops=int(microseconds * 1.15e9), bytes_accessed=0, transcendentals=0
            ),
            name=name,
        )(*args)

    return run


def shape(*dims, dtype=jnp.bfloat16):
    return jax.ShapeDtypeStruct(dims, dtype)


def far_first(devices, step):
    return sorted(range(0, devices, step), key=lambda k: -k.bit_length())


def far_chips(devices):
    return [k for k in far_first(devices, 2) if k > Y + Z1]


def chip_order(devices):
    return [*far_chips(devices), Y, Y + Z1, Z1, 0]


def message_sizes(devices):
    return [1] * len(far_chips(devices)) + [2, 1, 1]


def on_odd_core():
    return lax.rem(lax.axis_index("row"), 2) == 1


def flip_rows(key_ref, out_ref):
    for r in range(key_ref.shape[0]):
        out_ref[r] = key_ref[r, :LAT, :].T


def gathered_order(devices):
    return [z + y for z in reversed(far_first(devices, 4)) for y in (0, 2)]


def rotary_kernel(len_ref, cos_ref, sin_ref):
    rows, width = cos_ref.shape
    lane = lax.broadcasted_iota(jnp.int32, (rows, width), 1)
    place = lax.broadcasted_iota(jnp.int32, (rows, width), 0)
    step = jnp.where(lane < HALF, lane, lane - HALF).astype(jnp.float32)
    frequency = jnp.exp(step * (-math.log(10000.0) / HALF))
    length = jnp.zeros((rows, width), jnp.float32)
    for r in range(rows):
        length = jnp.where(place == r, len_ref[r].astype(jnp.float32), length)
    angle = length * frequency
    sine = jnp.sin(angle)
    cos_ref[...] = jnp.cos(angle)
    sin_ref[...] = jnp.where(lane < HALF, -sine, sine)


def rotary(lengths):
    table = shape(lengths.shape[0], ROPE, dtype=jnp.float32)
    return call(rotary_kernel, (table, table), 3, "rotary", scalars=1)(lengths)


def join_kernel(cos_ref, sin_ref, *refs):
    *in_refs, cos_out_ref, sin_out_ref, out_ref = refs
    cos_out_ref[...] = cos_ref[...]
    sin_out_ref[...] = sin_ref[...]
    out_ref[...] = jnp.concatenate(
        [ref[...].astype(jnp.float32) for ref in in_refs], axis=0
    ).astype(out_ref.dtype)


def join(tables, blocks):
    rows, depth = blocks[0].shape
    out = (*[shape(*t.shape, dtype=t.dtype) for t in tables], shape(len(blocks) * rows, depth))
    cosine, sine, joined = call(join_kernel, out, 3, "join")(*tables, *blocks)
    return (cosine, sine), joined


def project_kernel(devices, *refs):
    pieces = devices // 4
    q_refs = refs[:pieces]
    weights = (refs[pieces : pieces + 2], refs[pieces + 2 : pieces + 4])
    key_ref = refs[pieces + 4]
    flip_ref, lat_ref, rot_ref = refs[-3:]
    out_refs = refs[pieces + 5 : -3]
    heads = weights[0][1].shape[0]

    @pl.when(jnp.logical_not(on_odd_core()))
    def _():
        flip_rows(key_ref, flip_ref)

    piece = jnp.concatenate([ref[...].astype(jnp.float32) for ref in q_refs], axis=0)
    piece = piece.astype(jnp.bfloat16)
    count = piece.shape[0]
    wide = 2 * count // devices * heads
    width = NOPE + ROPE
    lane = lax.broadcasted_iota(jnp.int32, (wide // 2, LANES), 1)
    blocks = [(ref, 2 * i) for ref in out_refs for i in range(ref.shape[0] // 2)]
    blocks = dict(zip(chip_order(devices), blocks))
    for core, (wq_ref, wk_ref) in enumerate(weights):
        projected = jnp.dot(piece, wq_ref[...], preferred_element_type=jnp.float32)
        for h in range(heads):
            mine = projected[:, h * width : (h + 1) * width]
            absorbed = jnp.dot(
                mine[:, :NOPE].astype(jnp.bfloat16), wk_ref[h], preferred_element_type=jnp.float32
            )
            spread = pl.ds(h, count, stride=heads)
            for c in range(PIECES):
                lat_ref[core * PIECES + c, spread, :] = absorbed[:, c * LANES : (c + 1) * LANES]
            pe = mine[:, NOPE:]
            rot_ref[core, spread, :] = jnp.concatenate([pe, pe], axis=-1)
        for place, k in enumerate(gathered_order(devices)):
            out_ref, at = blocks[k]
            at += core
            first = place * wide
            for c in range(PIECES):
                out_ref[at, c * wide : (c + 1) * wide, :] = lat_ref[
                    core * PIECES + c, first : first + wide, :
                ].astype(jnp.bfloat16)
            low = rot_ref[core, first : first + wide // 2, :]
            high = rot_ref[core, first + wide // 2 : first + wide, :]
            out_ref[at, PIECES * wide :, :] = jnp.where(lane < ROPE, low, high).astype(
                jnp.bfloat16
            )


def project(pieces, weights, keys, devices):
    heads = weights[1].shape[0]
    count = len(pieces) * pieces[0].shape[0]
    wide = 2 * count // devices * heads
    scratch = [
        pltpu.VMEM((2 * PIECES, count * heads, LANES), jnp.float32),
        pltpu.VMEM((2, count * heads, LANES), jnp.float32),
    ]
    tall = PIECES * wide + wide // 2
    out = [shape(2 * size, tall, LANES) for size in message_sizes(devices)]
    kernel = functools.partial(project_kernel, devices)
    out.append(shape(keys.shape[0], keys.shape[2], LAT))
    args = (*pieces, *[resident(w) for w in weights], resident(keys))
    return call(kernel, out, 20, "project", scratch)(*args)


def flip_kernel(key_ref, flipped_ref, after_ref, out_ref):
    odd = on_odd_core()

    @pl.when(odd)
    def _():
        flip_rows(key_ref, out_ref)

    @pl.when(jnp.logical_not(odd))
    def _():
        out_ref[...] = flipped_ref[...]


def flip(keys, flipped, after):
    out = shape(*flipped.shape)
    return call(flip_kernel, out, 4, "flip")(resident(keys), resident(flipped), after)


def forward_kernel(own_ref, passing_ref, out_ref):
    out_ref[:2] = own_ref[...]
    out_ref[2:] = passing_ref[2:]


def forward(own, passing):
    return call(forward_kernel, shape(4, *own.shape[1:]), 1, "forward")(own, passing)


def arrived(refs):
    blocks = []
    for i, ref in enumerate(refs):
        count = 2 if i == len(refs) - 3 else ref.shape[0]
        blocks += [(ref, core) for core in range(count)]
    return blocks


def attend_kernel(sizes, len_ref, cos_ref, sin_ref, key_ref, flip_ref, new_ref, *refs):
    blocks = arrived(refs[: len(sizes)])
    out_refs = refs[len(sizes) :]
    rows, _, maxlen = key_ref.shape
    wide = out_refs[0].shape[1]
    heads = wide // rows

    def query_block(first):
        parts = [ref[i, first : first + heads, :].astype(jnp.float32) for ref, i in blocks]
        return jnp.concatenate(parts, axis=0)

    def score(r):
        latent = jnp.concatenate(
            [query_block(c * wide + r * heads) for c in range(PIECES)], axis=-1
        )
        pe = query_block(PIECES * wide + (r % (rows // 2)) * heads)
        side = r // (rows // 2) * ROPE
        pe = pe[:, side : side + ROPE]
        swapped = jnp.concatenate([pe[:, HALF:], pe[:, :HALF]], axis=-1)
        rotated = (pe * cos_ref[r : r + 1, :] + swapped * sin_ref[r : r + 1, :]).astype(jnp.bfloat16)
        newest = new_ref[r : r + 1, :].astype(jnp.float32)
        own = jnp.sum(latent * newest[:, :LAT], axis=-1, keepdims=True) + jnp.sum(
            rotated.astype(jnp.float32) * newest[:, LAT:], axis=-1, keepdims=True
        )
        scores = jnp.dot(
            latent.astype(jnp.bfloat16), key_ref[r, :LAT, :], preferred_element_type=jnp.float32
        )
        scores += jnp.dot(rotated, key_ref[r, LAT:, :], preferred_element_type=jnp.float32)
        position = lax.broadcasted_iota(jnp.int32, (1, maxlen), 1)
        return jnp.where(position < len_ref[r], scores, -jnp.inf), own

    back = [(ref, i) for ref in out_refs for i in range(ref.shape[0])]
    y_at = len(back) - 8
    back = back[: y_at + 2] + back[y_at + 4 : y_at + 6] + back[y_at + 2 : y_at + 4] + back[-2:]
    ahead = score(0)
    for r in range(rows):
        scores, own = ahead
        if r + 1 < rows:
            ahead = score(r + 1)
        peak = jnp.maximum(jnp.max(scores, axis=-1, keepdims=True), own)
        expo = jnp.exp2((scores - peak) * SCALE)
        own_expo = jnp.exp2((own - peak) * SCALE)
        inverse = 1.0 / (jnp.sum(expo, axis=-1, keepdims=True) + own_expo)
        weights = (expo * inverse).astype(jnp.bfloat16)
        own_weight = (own_expo * inverse).astype(jnp.bfloat16).astype(jnp.float32)
        summed = jnp.dot(weights, flip_ref[r], preferred_element_type=jnp.float32)
        summed += own_weight * new_ref[r : r + 1, :LAT].astype(jnp.float32)
        for k, (out_ref, i) in enumerate(back):
            out_ref[i, r * heads : (r + 1) * heads, :] = summed[
                k * heads : (k + 1) * heads, :
            ].astype(jnp.bfloat16)


def attend(lengths, tables, keys, flipped, new_latent, messages, heads, devices):
    sizes = message_sizes(devices)
    out = [shape(2 * size, keys.shape[0] * heads, LAT) for size in sizes]
    return call(functools.partial(attend_kernel, sizes), out, 10, "attend", scalars=1)(
        lengths, *tables, resident(keys), resident(flipped), new_latent, *messages
    )


def early_kernel(passing_ref, own_ref, after_ref, out_ref):
    out_ref[0] = passing_ref[1]
    out_ref[1] = own_ref[1]


def early(passing, own, after):
    return call(early_kernel, shape(2, *own.shape[1:]), 4, "early")(passing, own, after)


def regroup_kernel(*refs):
    *in_refs, early_ref, out_ref = refs
    blocks = arrived(in_refs)[1::2]
    blocks = [*blocks[:-4], (early_ref, 0), *blocks[-3:-1], (early_ref, 1)]
    for j, (ref, i) in enumerate(blocks):
        out_ref[j] = ref[i]


def regroup(messages, ready, chips):
    _, wide, width = messages[0].shape
    return call(regroup_kernel, shape(chips, wide, width), 1, "regroup")(*messages, ready)


def values_kernel(*refs):
    *in_refs, other_ref, wv_ref, val_ref, rows_ref = refs
    mine = arrived(in_refs)[::2]
    chips = len(mine)
    heads = wv_ref.shape[0]
    wide = other_ref.shape[1]
    for place in range(2 * chips):
        ref, i = mine[place] if place < chips else (other_ref, place - chips)
        block = ref[i].astype(jnp.float32)
        for c in range(PIECES):
            rows_ref[c, place * wide : (place + 1) * wide, :] = block[:, c * LANES : (c + 1) * LANES]
    count = val_ref.shape[0]
    for h in range(heads):
        chosen = jnp.concatenate(
            [rows_ref[c, pl.ds(h, count, stride=heads), :] for c in range(PIECES)], axis=-1
        )
        val_ref[:, h * VD : (h + 1) * VD] = jnp.dot(
            chosen.astype(jnp.bfloat16), wv_ref[h], preferred_element_type=jnp.float32
        ).astype(jnp.bfloat16)


def head_values(messages, other, w_uv):
    chips, wide, _ = other.shape
    heads = w_uv.shape[0]
    count = 2 * chips * wide // heads
    scratch = [pltpu.VMEM((PIECES, count * heads, LANES), jnp.float32)]
    return call(values_kernel, shape(count, heads * VD), 3, "values", scratch)(
        *messages, other, resident(w_uv)
    )


def terms_kernel(start, val_ref, wo_ref, mine_ref, other_ref):
    half, width = mine_ref.shape
    terms = jnp.dot(
        val_ref[...], wo_ref[:, start : start + width], preferred_element_type=jnp.float32
    )
    mine_ref[...] = terms[:half]
    other_ref[...] = terms[half:].astype(jnp.bfloat16)


def output_terms(values, w_o, part):
    half = values.shape[0] // 2
    width = w_o.shape[1] // PARTS
    out = (shape(half, width, dtype=jnp.float32), shape(half, width))
    kernel = functools.partial(terms_kernel, part * width)
    return call(kernel, out, 6, "terms")(values, resident(w_o))


def far_z(devices):
    return [z for z in far_first(devices, Z1) if z > Z1][::-1]


def places(devices, chips):
    order = [*far_chips(devices), Y, Z1, Y + Z1, 0]
    return [order.index(k) for k in chips]


def pick(total, rows, where):
    return jnp.concatenate([total[j * rows : (j + 1) * rows] for j in where], axis=0)


def first_sum_kernel(rows, keep, give, near, mine_ref, other_ref, keep_ref, give_ref, near_ref):
    total = mine_ref[...] + other_ref[...].astype(jnp.float32)
    keep_ref[...] = pick(total, rows, keep)
    give_ref[...] = pick(total, rows, give).astype(give_ref.dtype)
    near_ref[...] = pick(total, rows, near)


def last_part_kernel(rows, keep, give, near, mine_ref, other_ref, before_ref, *out_refs):
    keep_ref, give_ref, *near_refs = out_refs
    total = mine_ref[...] + other_ref[...].astype(jnp.float32)
    keep_ref[...] = pick(total, rows, keep)
    give_ref[...] = pick(total, rows, give).astype(give_ref.dtype)
    width = before_ref.shape[1]
    for i, (j, out_ref) in enumerate(zip(near, near_refs)):
        out_ref[:, :width] = before_ref[i * rows : (i + 1) * rows].astype(out_ref.dtype)
        out_ref[:, width:] = total[j * rows : (j + 1) * rows].astype(out_ref.dtype)


def core_sum(mine, other, before, rows, devices):
    count, width = mine.shape
    keep = places(devices, far_z(devices))
    give = places(devices, [z + Y for z in far_z(devices)])
    near = places(devices, [0, *NEAR])
    far = len(keep) * rows
    out = (shape(far, width, dtype=jnp.float32), shape(far, width))
    if before is None:
        kernel = functools.partial(first_sum_kernel, rows, keep, give, near)
        out += (shape(4 * rows, width, dtype=jnp.float32),)
        return call(kernel, out, 1, "core_sum")(mine, other)
    kernel = functools.partial(last_part_kernel, rows, keep, give, near)
    full = before.shape[1] + width
    out += (shape(rows, full, dtype=jnp.float32), *[shape(rows, full)] * len(NEAR))
    return call(kernel, out, 1, "core_sum")(mine, other, before)


def far_sum_kernel(*refs):
    mine_refs = refs[:PARTS]
    other_refs = refs[PARTS : 2 * PARTS]
    out_refs = refs[2 * PARTS :]
    rows = out_refs[0].shape[0]
    for p, (mine_ref, other_ref) in enumerate(zip(mine_refs, other_refs)):
        width = mine_ref.shape[1]
        total = mine_ref[...] + other_ref[...].astype(jnp.float32)
        for j, out_ref in enumerate(out_refs):
            out_ref[:, p * width : (p + 1) * width] = total[j * rows : (j + 1) * rows].astype(
                out_ref.dtype
            )


def far_sum(mine, other, rows):
    count, width = mine[0].shape
    out = [shape(rows, PARTS * width)] * (count // rows)
    return call(far_sum_kernel, out, 1, "far_sum")(*mine, *other)


def last_sum_kernel(*refs):
    *in_refs, out_ref = refs
    terms = [ref[...].astype(jnp.float32) for ref in in_refs]
    out_ref[...] = sum(terms[1:], terms[0]).astype(out_ref.dtype)


def last_sum(blocks):
    return call(last_sum_kernel, shape(*blocks[0].shape), 1, "last_sum")(*blocks)


def on_device(q_latent, new_latent, cache, lengths, w_uq, w_uk, w_uv, w_o, devices):
    heads = w_uk.shape[0]
    rows = cache.shape[0]
    zs = far_first(devices, 4)[::-1]

    def swap(block, k):
        if k == 0:
            return block
        return lax.ppermute(block, "row", [(i, i ^ k) for i in range(devices)])

    across = swap(q_latent, Y)
    far_weights = [swap(w_uq, 1), swap(w_uk, 1)]
    tables, near = join(rotary(lengths), [q_latent, across])
    def exchange(messages):
        *far, across, pair, own = messages
        early = len(far) // 2
        got = [swap(block, k) for block, k in zip(far[:early], far_k)]
        passing = swap(across, Y)
        got += [swap(block, k) for block, k in zip(far[early:], far_k[early:])]
        sent = forward(pair, passing)
        return [*got, passing, swap(sent, Z1), own], sent

    far_k = far_chips(devices)
    keys = jnp.swapaxes(cache, 1, 2)
    pieces = [swap(near, z) for z in zs]
    *messages, flipped = project(pieces, [w_uq, w_uk, *far_weights], keys, devices)
    messages, sent = exchange(messages)
    flipped = flip(keys, flipped, sent)
    latents = attend(lengths, tables, keys, flipped, new_latent, messages, heads, devices)
    latents, sent = exchange(latents)
    ready = early(latents[-3], latents[-1], sent)
    values = head_values(latents, swap(regroup(latents, ready, devices // 2), 1), w_uv)
    keep, got, near = [], [], None
    for part in range(PARTS):
        mine, other = output_terms(values, w_o, part)
        far_mine, far_other, near, *given = core_sum(mine, swap(other, 1), near, rows, devices)
        keep.append(far_mine)
        got.append(swap(far_other, Y))
    given = [swap(block, k) for block, k in zip(given, NEAR)]
    far = far_sum(keep, got, rows)
    far = [swap(block, z) for z, block in zip(far_z(devices), far)]
    return last_sum([near, *given, *far])


def solution(mesh):
    placed = (
        P(("grp", "row"), None),
        P(("grp", "row"), None),
        P(("grp", "row"), None, None),
        P(("grp", "row")),
        P(None, "row"),
        P("row", None, None),
        P("row", None, None),
        P("row", None),
    )
    body = functools.partial(on_device, devices=mesh.shape["row"])
    return jax.shard_map(
        body, mesh=mesh, in_specs=placed, out_specs=P(("grp", "row"), None), check_vma=False
    )
```

```python
import functools
import math

import jax
import jax.numpy as jnp
from jax import lax
from jax.experimental import pallas as pl
from jax.experimental.pallas import tpu as pltpu
from jax.sharding import PartitionSpec as P

LAT = 512
ROPE = 64
HALF = ROPE // 2
NOPE = 128
VD = 128
LANES = 128
PIECES = LAT // LANES
SCALE = (NOPE + ROPE) ** -0.5 * math.log2(math.e)
LIMIT = 16 * 2**20
PARTS = 2
Y = 2
Z1 = 4
NEAR = (Z1, Y + Z1, Y)


def resident(x):
    return pltpu.with_memory_space_constraint(x, pltpu.VMEM)


def in_vmem():
    return pl.BlockSpec(memory_space=pltpu.VMEM)


def call(kernel, out_shape, microseconds, name, scratch=(), scalars=0):
    def run(*args):
        smem = [pl.BlockSpec(memory_space=pltpu.SMEM)] * scalars
        return pl.pallas_call(
            kernel,
            out_shape=out_shape,
            in_specs=smem + [in_vmem()] * (len(args) - scalars),
            out_specs=jax.tree.map(lambda _: in_vmem(), out_shape),
            scratch_shapes=list(scratch),
            compiler_params=pltpu.CompilerParams(vmem_limit_bytes=LIMIT),
            cost_estimate=pl.CostEstimate(
                flops=int(microseconds * 1.15e9), bytes_accessed=0, transcendentals=0
            ),
            name=name,
        )(*args)

    return run


def shape(*dims, dtype=jnp.bfloat16):
    return jax.ShapeDtypeStruct(dims, dtype)


def far_first(devices, step):
    return sorted(range(0, devices, step), key=lambda k: -k.bit_length())


def far_chips(devices):
    return [k for k in far_first(devices, 2) if k > Y + Z1]


def chip_order(devices):
    return [*far_chips(devices), Y, Y + Z1, Z1, 0]


def message_sizes(devices):
    return [1] * len(far_chips(devices)) + [2, 1, 1]


def gathered_order(devices):
    return [z + y for z in reversed(far_first(devices, 4)) for y in (0, 2)]


def rotary_kernel(len_ref, cos_ref, sin_ref):
    rows, width = cos_ref.shape
    lane = lax.broadcasted_iota(jnp.int32, (rows, width), 1)
    place = lax.broadcasted_iota(jnp.int32, (rows, width), 0)
    step = jnp.where(lane < HALF, lane, lane - HALF).astype(jnp.float32)
    frequency = jnp.exp(step * (-math.log(10000.0) / HALF))
    length = jnp.zeros((rows, width), jnp.float32)
    for r in range(rows):
        length = jnp.where(place == r, len_ref[r].astype(jnp.float32), length)
    angle = length * frequency
    sine = jnp.sin(angle)
    cos_ref[...] = jnp.cos(angle)
    sin_ref[...] = jnp.where(lane < HALF, -sine, sine)


def rotary(lengths):
    table = shape(lengths.shape[0], ROPE, dtype=jnp.float32)
    return call(rotary_kernel, (table, table), 3, "rotary", scalars=1)(lengths)


def join_kernel(cos_ref, sin_ref, *refs):
    *in_refs, cos_out_ref, sin_out_ref, out_ref = refs
    cos_out_ref[...] = cos_ref[...]
    sin_out_ref[...] = sin_ref[...]
    out_ref[...] = jnp.concatenate(
        [ref[...].astype(jnp.float32) for ref in in_refs], axis=0
    ).astype(out_ref.dtype)


def join(tables, blocks):
    rows, depth = blocks[0].shape
    out = (*[shape(*t.shape, dtype=t.dtype) for t in tables], shape(len(blocks) * rows, depth))
    cosine, sine, joined = call(join_kernel, out, 3, "join")(*tables, *blocks)
    return (cosine, sine), joined


def project_kernel(devices, *refs):
    pieces = devices // 4
    q_refs = refs[:pieces]
    weights = (refs[pieces : pieces + 2], refs[pieces + 2 : pieces + 4])
    lat_ref, rot_ref = refs[-2:]
    out_refs = refs[pieces + 4 : -2]
    heads = weights[0][1].shape[0]
    piece = jnp.concatenate([ref[...].astype(jnp.float32) for ref in q_refs], axis=0)
    piece = piece.astype(jnp.bfloat16)
    count = piece.shape[0]
    wide = 2 * count // devices * heads
    width = NOPE + ROPE
    lane = lax.broadcasted_iota(jnp.int32, (wide // 2, LANES), 1)
    blocks = [(ref, 2 * i) for ref in out_refs for i in range(ref.shape[0] // 2)]
    blocks = dict(zip(chip_order(devices), blocks))
    for core, (wq_ref, wk_ref) in enumerate(weights):
        projected = jnp.dot(piece, wq_ref[...], preferred_element_type=jnp.float32)
        for h in range(heads):
            mine = projected[:, h * width : (h + 1) * width]
            absorbed = jnp.dot(
                mine[:, :NOPE].astype(jnp.bfloat16), wk_ref[h], preferred_element_type=jnp.float32
            )
            spread = pl.ds(h, count, stride=heads)
            for c in range(PIECES):
                lat_ref[core * PIECES + c, spread, :] = absorbed[:, c * LANES : (c + 1) * LANES]
            pe = mine[:, NOPE:]
            rot_ref[core, spread, :] = jnp.concatenate([pe, pe], axis=-1)
        for place, k in enumerate(gathered_order(devices)):
            out_ref, at = blocks[k]
            at += core
            first = place * wide
            for c in range(PIECES):
                out_ref[at, c * wide : (c + 1) * wide, :] = lat_ref[
                    core * PIECES + c, first : first + wide, :
                ].astype(jnp.bfloat16)
            low = rot_ref[core, first : first + wide // 2, :]
            high = rot_ref[core, first + wide // 2 : first + wide, :]
            out_ref[at, PIECES * wide :, :] = jnp.where(lane < ROPE, low, high).astype(
                jnp.bfloat16
            )


def project(pieces, weights, devices):
    heads = weights[1].shape[0]
    count = len(pieces) * pieces[0].shape[0]
    wide = 2 * count // devices * heads
    scratch = [
        pltpu.VMEM((2 * PIECES, count * heads, LANES), jnp.float32),
        pltpu.VMEM((2, count * heads, LANES), jnp.float32),
    ]
    tall = PIECES * wide + wide // 2
    out = [shape(2 * size, tall, LANES) for size in message_sizes(devices)]
    kernel = functools.partial(project_kernel, devices)
    return call(kernel, out, 20, "project", scratch)(*pieces, *[resident(w) for w in weights])


def flip_kernel(key_ref, after_ref, out_ref):
    for r in range(key_ref.shape[0]):
        out_ref[r] = key_ref[r, :LAT, :].T


def flip(keys, after):
    rows, _, maxlen = keys.shape
    return call(flip_kernel, shape(rows, maxlen, LAT), 4, "flip")(resident(keys), after)


def forward_kernel(own_ref, passing_ref, out_ref):
    out_ref[:2] = own_ref[...]
    out_ref[2:] = passing_ref[2:]


def forward(own, passing):
    return call(forward_kernel, shape(4, *own.shape[1:]), 1, "forward")(own, passing)


def arrived(refs):
    blocks = []
    for i, ref in enumerate(refs):
        count = 2 if i == len(refs) - 3 else ref.shape[0]
        blocks += [(ref, core) for core in range(count)]
    return blocks


def attend_kernel(sizes, len_ref, cos_ref, sin_ref, key_ref, flip_ref, new_ref, *refs):
    blocks = arrived(refs[: len(sizes)])
    out_refs = refs[len(sizes) :]
    rows, _, maxlen = key_ref.shape
    wide = out_refs[0].shape[1]
    heads = wide // rows

    def query_block(first):
        parts = [ref[i, first : first + heads, :].astype(jnp.float32) for ref, i in blocks]
        return jnp.concatenate(parts, axis=0)

    def score(r):
        latent = jnp.concatenate(
            [query_block(c * wide + r * heads) for c in range(PIECES)], axis=-1
        )
        pe = query_block(PIECES * wide + (r % (rows // 2)) * heads)
        side = r // (rows // 2) * ROPE
        pe = pe[:, side : side + ROPE]
        swapped = jnp.concatenate([pe[:, HALF:], pe[:, :HALF]], axis=-1)
        rotated = (pe * cos_ref[r : r + 1, :] + swapped * sin_ref[r : r + 1, :]).astype(jnp.bfloat16)
        newest = new_ref[r : r + 1, :].astype(jnp.float32)
        own = jnp.sum(latent * newest[:, :LAT], axis=-1, keepdims=True) + jnp.sum(
            rotated.astype(jnp.float32) * newest[:, LAT:], axis=-1, keepdims=True
        )
        scores = jnp.dot(
            latent.astype(jnp.bfloat16), key_ref[r, :LAT, :], preferred_element_type=jnp.float32
        )
        scores += jnp.dot(rotated, key_ref[r, LAT:, :], preferred_element_type=jnp.float32)
        position = lax.broadcasted_iota(jnp.int32, (1, maxlen), 1)
        return jnp.where(position < len_ref[r], scores, -jnp.inf), own

    back = [(ref, i) for ref in out_refs for i in range(ref.shape[0])]
    y_at = len(back) - 8
    back = back[: y_at + 2] + back[y_at + 4 : y_at + 6] + back[y_at + 2 : y_at + 4] + back[-2:]
    ahead = score(0)
    for r in range(rows):
        scores, own = ahead
        if r + 1 < rows:
            ahead = score(r + 1)
        peak = jnp.maximum(jnp.max(scores, axis=-1, keepdims=True), own)
        expo = jnp.exp2((scores - peak) * SCALE)
        own_expo = jnp.exp2((own - peak) * SCALE)
        inverse = 1.0 / (jnp.sum(expo, axis=-1, keepdims=True) + own_expo)
        weights = (expo * inverse).astype(jnp.bfloat16)
        own_weight = (own_expo * inverse).astype(jnp.bfloat16).astype(jnp.float32)
        summed = jnp.dot(weights, flip_ref[r], preferred_element_type=jnp.float32)
        summed += own_weight * new_ref[r : r + 1, :LAT].astype(jnp.float32)
        for k, (out_ref, i) in enumerate(back):
            out_ref[i, r * heads : (r + 1) * heads, :] = summed[
                k * heads : (k + 1) * heads, :
            ].astype(jnp.bfloat16)


def attend(lengths, tables, keys, flipped, new_latent, messages, heads, devices):
    sizes = message_sizes(devices)
    out = [shape(2 * size, keys.shape[0] * heads, LAT) for size in sizes]
    return call(functools.partial(attend_kernel, sizes), out, 10, "attend", scalars=1)(
        lengths, *tables, resident(keys), resident(flipped), new_latent, *messages
    )


def early_kernel(passing_ref, own_ref, after_ref, out_ref):
    out_ref[0] = passing_ref[1]
    out_ref[1] = own_ref[1]


def early(passing, own, after):
    return call(early_kernel, shape(2, *own.shape[1:]), 4, "early")(passing, own, after)


def regroup_kernel(*refs):
    *in_refs, early_ref, out_ref = refs
    blocks = arrived(in_refs)[1::2]
    blocks = [*blocks[:-4], (early_ref, 0), *blocks[-3:-1], (early_ref, 1)]
    for j, (ref, i) in enumerate(blocks):
        out_ref[j] = ref[i]


def regroup(messages, ready, chips):
    _, wide, width = messages[0].shape
    return call(regroup_kernel, shape(chips, wide, width), 1, "regroup")(*messages, ready)


def values_kernel(*refs):
    *in_refs, other_ref, wv_ref, val_ref, rows_ref = refs
    mine = arrived(in_refs)[::2]
    chips = len(mine)
    heads = wv_ref.shape[0]
    wide = other_ref.shape[1]
    for place in range(2 * chips):
        ref, i = mine[place] if place < chips else (other_ref, place - chips)
        block = ref[i].astype(jnp.float32)
        for c in range(PIECES):
            rows_ref[c, place * wide : (place + 1) * wide, :] = block[:, c * LANES : (c + 1) * LANES]
    count = val_ref.shape[0]
    for h in range(heads):
        chosen = jnp.concatenate(
            [rows_ref[c, pl.ds(h, count, stride=heads), :] for c in range(PIECES)], axis=-1
        )
        val_ref[:, h * VD : (h + 1) * VD] = jnp.dot(
            chosen.astype(jnp.bfloat16), wv_ref[h], preferred_element_type=jnp.float32
        ).astype(jnp.bfloat16)


def head_values(messages, other, w_uv):
    chips, wide, _ = other.shape
    heads = w_uv.shape[0]
    count = 2 * chips * wide // heads
    scratch = [pltpu.VMEM((PIECES, count * heads, LANES), jnp.float32)]
    return call(values_kernel, shape(count, heads * VD), 3, "values", scratch)(
        *messages, other, resident(w_uv)
    )


def terms_kernel(start, val_ref, wo_ref, mine_ref, other_ref):
    half, width = mine_ref.shape
    terms = jnp.dot(
        val_ref[...], wo_ref[:, start : start + width], preferred_element_type=jnp.float32
    )
    mine_ref[...] = terms[:half]
    other_ref[...] = terms[half:].astype(jnp.bfloat16)


def output_terms(values, w_o, part):
    half = values.shape[0] // 2
    width = w_o.shape[1] // PARTS
    out = (shape(half, width, dtype=jnp.float32), shape(half, width))
    kernel = functools.partial(terms_kernel, part * width)
    return call(kernel, out, 6, "terms")(values, resident(w_o))


def far_z(devices):
    return [z for z in far_first(devices, Z1) if z > Z1][::-1]


def places(devices, chips):
    order = [*far_chips(devices), Y, Z1, Y + Z1, 0]
    return [order.index(k) for k in chips]


def pick(total, rows, where):
    return jnp.concatenate([total[j * rows : (j + 1) * rows] for j in where], axis=0)


def first_sum_kernel(rows, keep, give, near, mine_ref, other_ref, keep_ref, give_ref, near_ref):
    total = mine_ref[...] + other_ref[...].astype(jnp.float32)
    keep_ref[...] = pick(total, rows, keep)
    give_ref[...] = pick(total, rows, give).astype(give_ref.dtype)
    near_ref[...] = pick(total, rows, near)


def last_part_kernel(rows, keep, give, near, mine_ref, other_ref, before_ref, *out_refs):
    keep_ref, give_ref, *near_refs = out_refs
    total = mine_ref[...] + other_ref[...].astype(jnp.float32)
    keep_ref[...] = pick(total, rows, keep)
    give_ref[...] = pick(total, rows, give).astype(give_ref.dtype)
    width = before_ref.shape[1]
    for i, (j, out_ref) in enumerate(zip(near, near_refs)):
        out_ref[:, :width] = before_ref[i * rows : (i + 1) * rows].astype(out_ref.dtype)
        out_ref[:, width:] = total[j * rows : (j + 1) * rows].astype(out_ref.dtype)


def core_sum(mine, other, before, rows, devices):
    count, width = mine.shape
    keep = places(devices, far_z(devices))
    give = places(devices, [z + Y for z in far_z(devices)])
    near = places(devices, [0, *NEAR])
    far = len(keep) * rows
    out = (shape(far, width, dtype=jnp.float32), shape(far, width))
    if before is None:
        kernel = functools.partial(first_sum_kernel, rows, keep, give, near)
        out += (shape(4 * rows, width, dtype=jnp.float32),)
        return call(kernel, out, 1, "core_sum")(mine, other)
    kernel = functools.partial(last_part_kernel, rows, keep, give, near)
    full = before.shape[1] + width
    out += (shape(rows, full, dtype=jnp.float32), *[shape(rows, full)] * len(NEAR))
    return call(kernel, out, 1, "core_sum")(mine, other, before)


def far_sum_kernel(*refs):
    mine_refs = refs[:PARTS]
    other_refs = refs[PARTS : 2 * PARTS]
    out_refs = refs[2 * PARTS :]
    rows = out_refs[0].shape[0]
    for p, (mine_ref, other_ref) in enumerate(zip(mine_refs, other_refs)):
        width = mine_ref.shape[1]
        total = mine_ref[...] + other_ref[...].astype(jnp.float32)
        for j, out_ref in enumerate(out_refs):
            out_ref[:, p * width : (p + 1) * width] = total[j * rows : (j + 1) * rows].astype(
                out_ref.dtype
            )


def far_sum(mine, other, rows):
    count, width = mine[0].shape
    out = [shape(rows, PARTS * width)] * (count // rows)
    return call(far_sum_kernel, out, 1, "far_sum")(*mine, *other)


def last_sum_kernel(*refs):
    *in_refs, out_ref = refs
    terms = [ref[...].astype(jnp.float32) for ref in in_refs]
    out_ref[...] = sum(terms[1:], terms[0]).astype(out_ref.dtype)


def last_sum(blocks):
    return call(last_sum_kernel, shape(*blocks[0].shape), 1, "last_sum")(*blocks)


def on_device(q_latent, new_latent, cache, lengths, w_uq, w_uk, w_uv, w_o, devices):
    heads = w_uk.shape[0]
    rows = cache.shape[0]
    zs = far_first(devices, 4)[::-1]

    def swap(block, k):
        if k == 0:
            return block
        return lax.ppermute(block, "row", [(i, i ^ k) for i in range(devices)])

    across = swap(q_latent, Y)
    far_weights = [swap(w_uq, 1), swap(w_uk, 1)]
    tables, near = join(rotary(lengths), [q_latent, across])
    def exchange(messages):
        *far, across, pair, own = messages
        early = len(far) // 2
        got = [swap(block, k) for block, k in zip(far[:early], far_k)]
        passing = swap(across, Y)
        got += [swap(block, k) for block, k in zip(far[early:], far_k[early:])]
        sent = forward(pair, passing)
        return [*got, passing, swap(sent, Z1), own], sent

    far_k = far_chips(devices)
    messages = project([swap(near, z) for z in zs], [w_uq, w_uk, *far_weights], devices)
    messages, sent = exchange(messages)
    keys = jnp.swapaxes(cache, 1, 2)
    flipped = flip(keys, sent)
    latents = attend(lengths, tables, keys, flipped, new_latent, messages, heads, devices)
    latents, sent = exchange(latents)
    ready = early(latents[-3], latents[-1], sent)
    values = head_values(latents, swap(regroup(latents, ready, devices // 2), 1), w_uv)
    keep, got, near = [], [], None
    for part in range(PARTS):
        mine, other = output_terms(values, w_o, part)
        far_mine, far_other, near, *given = core_sum(mine, swap(other, 1), near, rows, devices)
        keep.append(far_mine)
        got.append(swap(far_other, Y))
    given = [swap(block, k) for block, k in zip(given, NEAR)]
    far = far_sum(keep, got, rows)
    far = [swap(block, z) for z, block in zip(far_z(devices), far)]
    return last_sum([near, *given, *far])


def solution(mesh):
    placed = (
        P(("grp", "row"), None),
        P(("grp", "row"), None),
        P(("grp", "row"), None, None),
        P(("grp", "row")),
        P(None, "row"),
        P("row", None, None),
        P("row", None, None),
        P("row", None),
    )
    body = functools.partial(on_device, devices=mesh.shape["row"])
    return jax.shard_map(
        body, mesh=mesh, in_specs=placed, out_specs=P(("grp", "row"), None), check_vma=False
    )
```

```python
import functools
import math

import jax
import jax.numpy as jnp
from jax import lax
from jax.experimental import pallas as pl
from jax.experimental.pallas import tpu as pltpu
from jax.sharding import PartitionSpec as P

LAT = 512
ROPE = 64
HALF = ROPE // 2
NOPE = 128
VD = 128
LANES = 128
PIECES = LAT // LANES
SCALE = (NOPE + ROPE) ** -0.5 * math.log2(math.e)
LIMIT = 16 * 2**20
PARTS = 2
Y = 2
Z1 = 4
NEAR = (Z1, Y + Z1, Y)


def resident(x):
    return pltpu.with_memory_space_constraint(x, pltpu.VMEM)


def in_vmem():
    return pl.BlockSpec(memory_space=pltpu.VMEM)


def call(kernel, out_shape, microseconds, name, scratch=(), scalars=0):
    def run(*args):
        smem = [pl.BlockSpec(memory_space=pltpu.SMEM)] * scalars
        return pl.pallas_call(
            kernel,
            out_shape=out_shape,
            in_specs=smem + [in_vmem()] * (len(args) - scalars),
            out_specs=jax.tree.map(lambda _: in_vmem(), out_shape),
            scratch_shapes=list(scratch),
            compiler_params=pltpu.CompilerParams(vmem_limit_bytes=LIMIT),
            cost_estimate=pl.CostEstimate(
                flops=int(microseconds * 1.15e9), bytes_accessed=0, transcendentals=0
            ),
            name=name,
        )(*args)

    return run


def shape(*dims, dtype=jnp.bfloat16):
    return jax.ShapeDtypeStruct(dims, dtype)


def far_first(devices, step):
    return sorted(range(0, devices, step), key=lambda k: -k.bit_length())


def far_chips(devices):
    chips = [k for k in far_first(devices, 2) if k > Y + Z1]
    return chips[:1] + chips[:0:-1]


def chip_order(devices):
    return [*far_chips(devices), Y, Y + Z1, Z1, 0]


def message_sizes(devices):
    return [1] * len(far_chips(devices)) + [2, 1, 1]


def gathered_order(devices):
    return [z + y for z in reversed(far_first(devices, 4)) for y in (0, 2)]


def rotary_kernel(len_ref, cos_ref, sin_ref):
    rows, width = cos_ref.shape
    lane = lax.broadcasted_iota(jnp.int32, (rows, width), 1)
    place = lax.broadcasted_iota(jnp.int32, (rows, width), 0)
    step = jnp.where(lane < HALF, lane, lane - HALF).astype(jnp.float32)
    frequency = jnp.exp(step * (-math.log(10000.0) / HALF))
    length = jnp.zeros((rows, width), jnp.float32)
    for r in range(rows):
        length = jnp.where(place == r, len_ref[r].astype(jnp.float32), length)
    angle = length * frequency
    sine = jnp.sin(angle)
    cos_ref[...] = jnp.cos(angle)
    sin_ref[...] = jnp.where(lane < HALF, -sine, sine)


def rotary(lengths):
    table = shape(lengths.shape[0], ROPE, dtype=jnp.float32)
    return call(rotary_kernel, (table, table), 3, "rotary", scalars=1)(lengths)


def join_kernel(cos_ref, sin_ref, *refs):
    *in_refs, cos_out_ref, sin_out_ref, out_ref = refs
    cos_out_ref[...] = cos_ref[...]
    sin_out_ref[...] = sin_ref[...]
    out_ref[...] = jnp.concatenate(
        [ref[...].astype(jnp.float32) for ref in in_refs], axis=0
    ).astype(out_ref.dtype)


def join(tables, blocks):
    rows, depth = blocks[0].shape
    out = (*[shape(*t.shape, dtype=t.dtype) for t in tables], shape(len(blocks) * rows, depth))
    cosine, sine, joined = call(join_kernel, out, 3, "join")(*tables, *blocks)
    return (cosine, sine), joined


def project_kernel(devices, *refs):
    pieces = devices // 4
    q_refs = refs[:pieces]
    weights = (refs[pieces : pieces + 2], refs[pieces + 2 : pieces + 4])
    lat_ref, rot_ref = refs[-2:]
    out_refs = refs[pieces + 4 : -2]
    heads = weights[0][1].shape[0]
    piece = jnp.concatenate([ref[...].astype(jnp.float32) for ref in q_refs], axis=0)
    piece = piece.astype(jnp.bfloat16)
    count = piece.shape[0]
    wide = 2 * count // devices * heads
    width = NOPE + ROPE
    lane = lax.broadcasted_iota(jnp.int32, (wide // 2, LANES), 1)
    blocks = [(ref, 2 * i) for ref in out_refs for i in range(ref.shape[0] // 2)]
    blocks = dict(zip(chip_order(devices), blocks))
    for core, (wq_ref, wk_ref) in enumerate(weights):
        projected = jnp.dot(piece, wq_ref[...], preferred_element_type=jnp.float32)
        for h in range(heads):
            mine = projected[:, h * width : (h + 1) * width]
            absorbed = jnp.dot(
                mine[:, :NOPE].astype(jnp.bfloat16), wk_ref[h], preferred_element_type=jnp.float32
            )
            spread = pl.ds(h, count, stride=heads)
            for c in range(PIECES):
                lat_ref[core * PIECES + c, spread, :] = absorbed[:, c * LANES : (c + 1) * LANES]
            pe = mine[:, NOPE:]
            rot_ref[core, spread, :] = jnp.concatenate([pe, pe], axis=-1)
        for place, k in enumerate(gathered_order(devices)):
            out_ref, at = blocks[k]
            at += core
            first = place * wide
            for c in range(PIECES):
                out_ref[at, c * wide : (c + 1) * wide, :] = lat_ref[
                    core * PIECES + c, first : first + wide, :
                ].astype(jnp.bfloat16)
            low = rot_ref[core, first : first + wide // 2, :]
            high = rot_ref[core, first + wide // 2 : first + wide, :]
            out_ref[at, PIECES * wide :, :] = jnp.where(lane < ROPE, low, high).astype(
                jnp.bfloat16
            )


def project(pieces, weights, devices):
    heads = weights[1].shape[0]
    count = len(pieces) * pieces[0].shape[0]
    wide = 2 * count // devices * heads
    scratch = [
        pltpu.VMEM((2 * PIECES, count * heads, LANES), jnp.float32),
        pltpu.VMEM((2, count * heads, LANES), jnp.float32),
    ]
    tall = PIECES * wide + wide // 2
    out = [shape(2 * size, tall, LANES) for size in message_sizes(devices)]
    kernel = functools.partial(project_kernel, devices)
    return call(kernel, out, 20, "project", scratch)(*pieces, *[resident(w) for w in weights])


def flip_kernel(key_ref, after_ref, out_ref):
    for r in range(key_ref.shape[0]):
        out_ref[r] = key_ref[r, :LAT, :].T


def flip(keys, after):
    rows, _, maxlen = keys.shape
    return call(flip_kernel, shape(rows, maxlen, LAT), 4, "flip")(resident(keys), after)


def forward_kernel(own_ref, passing_ref, out_ref):
    out_ref[:2] = own_ref[...]
    out_ref[2:] = passing_ref[2:]


def forward(own, passing):
    return call(forward_kernel, shape(4, *own.shape[1:]), 1, "forward")(own, passing)


def arrived(refs):
    blocks = []
    for i, ref in enumerate(refs):
        count = 2 if i == len(refs) - 3 else ref.shape[0]
        blocks += [(ref, core) for core in range(count)]
    return blocks


def attend_kernel(sizes, len_ref, cos_ref, sin_ref, key_ref, flip_ref, new_ref, *refs):
    blocks = arrived(refs[: len(sizes)])
    out_refs = refs[len(sizes) :]
    rows, _, maxlen = key_ref.shape
    wide = out_refs[0].shape[1]
    heads = wide // rows

    def query_block(first):
        parts = [ref[i, first : first + heads, :].astype(jnp.float32) for ref, i in blocks]
        return jnp.concatenate(parts, axis=0)

    def score(r):
        latent = jnp.concatenate(
            [query_block(c * wide + r * heads) for c in range(PIECES)], axis=-1
        )
        pe = query_block(PIECES * wide + (r % (rows // 2)) * heads)
        side = r // (rows // 2) * ROPE
        pe = pe[:, side : side + ROPE]
        swapped = jnp.concatenate([pe[:, HALF:], pe[:, :HALF]], axis=-1)
        rotated = (pe * cos_ref[r : r + 1, :] + swapped * sin_ref[r : r + 1, :]).astype(jnp.bfloat16)
        newest = new_ref[r : r + 1, :].astype(jnp.float32)
        own = jnp.sum(latent * newest[:, :LAT], axis=-1, keepdims=True) + jnp.sum(
            rotated.astype(jnp.float32) * newest[:, LAT:], axis=-1, keepdims=True
        )
        query = jnp.concatenate([latent.astype(jnp.bfloat16), rotated], axis=-1)
        scores = jnp.dot(query, key_ref[r], preferred_element_type=jnp.float32)
        position = lax.broadcasted_iota(jnp.int32, (1, maxlen), 1)
        return jnp.where(position < len_ref[r], scores, -jnp.inf), own

    back = [(ref, i) for ref in out_refs for i in range(ref.shape[0])]
    y_at = len(back) - 8
    back = back[: y_at + 2] + back[y_at + 4 : y_at + 6] + back[y_at + 2 : y_at + 4] + back[-2:]
    ahead = score(0)
    for r in range(rows):
        scores, own = ahead
        if r + 1 < rows:
            ahead = score(r + 1)
        peak = jnp.maximum(jnp.max(scores, axis=-1, keepdims=True), own)
        expo = jnp.exp2((scores - peak) * SCALE)
        own_expo = jnp.exp2((own - peak) * SCALE)
        inverse = 1.0 / (jnp.sum(expo, axis=-1, keepdims=True) + own_expo)
        weights = (expo * inverse).astype(jnp.bfloat16)
        own_weight = (own_expo * inverse).astype(jnp.bfloat16).astype(jnp.float32)
        summed = jnp.dot(weights, flip_ref[r], preferred_element_type=jnp.float32)
        summed += own_weight * new_ref[r : r + 1, :LAT].astype(jnp.float32)
        for k, (out_ref, i) in enumerate(back):
            out_ref[i, r * heads : (r + 1) * heads, :] = summed[
                k * heads : (k + 1) * heads, :
            ].astype(jnp.bfloat16)


def attend(lengths, tables, keys, flipped, new_latent, messages, heads, devices):
    sizes = message_sizes(devices)
    out = [shape(2 * size, keys.shape[0] * heads, LAT) for size in sizes]
    return call(functools.partial(attend_kernel, sizes), out, 10, "attend", scalars=1)(
        lengths, *tables, resident(keys), resident(flipped), new_latent, *messages
    )


def early_kernel(passing_ref, own_ref, after_ref, out_ref):
    out_ref[0] = passing_ref[1]
    out_ref[1] = own_ref[1]


def early(passing, own, after):
    return call(early_kernel, shape(2, *own.shape[1:]), 4, "early")(passing, own, after)


def regroup_kernel(*refs):
    *in_refs, early_ref, out_ref = refs
    blocks = arrived(in_refs)[1::2]
    blocks = [*blocks[:-4], (early_ref, 0), *blocks[-3:-1], (early_ref, 1)]
    for j, (ref, i) in enumerate(blocks):
        out_ref[j] = ref[i]


def regroup(messages, ready, chips):
    _, wide, width = messages[0].shape
    return call(regroup_kernel, shape(chips, wide, width), 1, "regroup")(*messages, ready)


def values_kernel(*refs):
    *in_refs, other_ref, wv_ref, val_ref, rows_ref = refs
    mine = arrived(in_refs)[::2]
    chips = len(mine)
    heads = wv_ref.shape[0]
    wide = other_ref.shape[1]
    for place in range(2 * chips):
        ref, i = mine[place] if place < chips else (other_ref, place - chips)
        block = ref[i].astype(jnp.float32)
        for c in range(PIECES):
            rows_ref[c, place * wide : (place + 1) * wide, :] = block[:, c * LANES : (c + 1) * LANES]
    count = val_ref.shape[0]
    for h in range(heads):
        chosen = jnp.concatenate(
            [rows_ref[c, pl.ds(h, count, stride=heads), :] for c in range(PIECES)], axis=-1
        )
        val_ref[:, h * VD : (h + 1) * VD] = jnp.dot(
            chosen.astype(jnp.bfloat16), wv_ref[h], preferred_element_type=jnp.float32
        ).astype(jnp.bfloat16)


def head_values(messages, other, w_uv):
    chips, wide, _ = other.shape
    heads = w_uv.shape[0]
    count = 2 * chips * wide // heads
    scratch = [pltpu.VMEM((PIECES, count * heads, LANES), jnp.float32)]
    return call(values_kernel, shape(count, heads * VD), 3, "values", scratch)(
        *messages, other, resident(w_uv)
    )


def terms_kernel(start, val_ref, wo_ref, mine_ref, other_ref):
    half, width = mine_ref.shape
    terms = jnp.dot(
        val_ref[...], wo_ref[:, start : start + width], preferred_element_type=jnp.float32
    )
    mine_ref[...] = terms[:half]
    other_ref[...] = terms[half:].astype(jnp.bfloat16)


def output_terms(values, w_o, part):
    half = values.shape[0] // 2
    width = w_o.shape[1] // PARTS
    out = (shape(half, width, dtype=jnp.float32), shape(half, width))
    kernel = functools.partial(terms_kernel, part * width)
    return call(kernel, out, 6, "terms")(values, resident(w_o))


def far_z(devices):
    return [z for z in far_first(devices, Z1) if z > Z1][::-1]


def places(devices, chips):
    order = [*far_chips(devices), Y, Z1, Y + Z1, 0]
    return [order.index(k) for k in chips]


def pick(total, rows, where):
    return jnp.concatenate([total[j * rows : (j + 1) * rows] for j in where], axis=0)


def first_sum_kernel(rows, keep, give, near, mine_ref, other_ref, keep_ref, give_ref, near_ref):
    total = mine_ref[...] + other_ref[...].astype(jnp.float32)
    keep_ref[...] = pick(total, rows, keep)
    give_ref[...] = pick(total, rows, give).astype(give_ref.dtype)
    near_ref[...] = pick(total, rows, near)


def last_part_kernel(rows, keep, give, near, mine_ref, other_ref, before_ref, *out_refs):
    keep_ref, give_ref, *near_refs = out_refs
    total = mine_ref[...] + other_ref[...].astype(jnp.float32)
    keep_ref[...] = pick(total, rows, keep)
    give_ref[...] = pick(total, rows, give).astype(give_ref.dtype)
    width = before_ref.shape[1]
    for i, (j, out_ref) in enumerate(zip(near, near_refs)):
        out_ref[:, :width] = before_ref[i * rows : (i + 1) * rows].astype(out_ref.dtype)
        out_ref[:, width:] = total[j * rows : (j + 1) * rows].astype(out_ref.dtype)


def core_sum(mine, other, before, rows, devices):
    count, width = mine.shape
    keep = places(devices, far_z(devices))
    give = places(devices, [z + Y for z in far_z(devices)])
    near = places(devices, [0, *NEAR])
    far = len(keep) * rows
    out = (shape(far, width, dtype=jnp.float32), shape(far, width))
    if before is None:
        kernel = functools.partial(first_sum_kernel, rows, keep, give, near)
        out += (shape(4 * rows, width, dtype=jnp.float32),)
        return call(kernel, out, 1, "core_sum")(mine, other)
    kernel = functools.partial(last_part_kernel, rows, keep, give, near)
    full = before.shape[1] + width
    out += (shape(rows, full, dtype=jnp.float32), *[shape(rows, full)] * len(NEAR))
    return call(kernel, out, 1, "core_sum")(mine, other, before)


def far_sum_kernel(*refs):
    mine_refs = refs[:PARTS]
    other_refs = refs[PARTS : 2 * PARTS]
    out_refs = refs[2 * PARTS :]
    rows = out_refs[0].shape[0]
    for p, (mine_ref, other_ref) in enumerate(zip(mine_refs, other_refs)):
        width = mine_ref.shape[1]
        total = mine_ref[...] + other_ref[...].astype(jnp.float32)
        for j, out_ref in enumerate(out_refs):
            out_ref[:, p * width : (p + 1) * width] = total[j * rows : (j + 1) * rows].astype(
                out_ref.dtype
            )


def far_sum(mine, other, rows):
    count, width = mine[0].shape
    out = [shape(rows, PARTS * width)] * (count // rows)
    return call(far_sum_kernel, out, 1, "far_sum")(*mine, *other)


def last_sum_kernel(*refs):
    *in_refs, out_ref = refs
    terms = [ref[...].astype(jnp.float32) for ref in in_refs]
    out_ref[...] = sum(terms[1:], terms[0]).astype(out_ref.dtype)


def last_sum(blocks):
    return call(last_sum_kernel, shape(*blocks[0].shape), 1, "last_sum")(*blocks)


def on_device(q_latent, new_latent, cache, lengths, w_uq, w_uk, w_uv, w_o, devices):
    heads = w_uk.shape[0]
    rows = cache.shape[0]
    zs = far_first(devices, 4)[::-1]

    def swap(block, k):
        if k == 0:
            return block
        return lax.ppermute(block, "row", [(i, i ^ k) for i in range(devices)])

    across = swap(q_latent, Y)
    far_weights = [swap(w_uq, 1), swap(w_uk, 1)]
    tables, near = join(rotary(lengths), [q_latent, across])
    def exchange(messages):
        *far, across, pair, own = messages
        early = len(far) // 2
        got = [swap(block, k) for block, k in zip(far[:early], far_k)]
        passing = swap(across, Y)
        got += [swap(block, k) for block, k in zip(far[early:], far_k[early:])]
        sent = forward(pair, passing)
        return [*got, passing, swap(sent, Z1), own], sent

    far_k = far_chips(devices)
    messages = project([swap(near, z) for z in zs], [w_uq, w_uk, *far_weights], devices)
    messages, sent = exchange(messages)
    keys = jnp.swapaxes(cache, 1, 2)
    flipped = flip(keys, sent)
    latents = attend(lengths, tables, keys, flipped, new_latent, messages, heads, devices)
    latents, sent = exchange(latents)
    ready = early(latents[-3], latents[-1], sent)
    values = head_values(latents, swap(regroup(latents, ready, devices // 2), 1), w_uv)
    keep, got, near = [], [], None
    for part in range(PARTS):
        mine, other = output_terms(values, w_o, part)
        far_mine, far_other, near, *given = core_sum(mine, swap(other, 1), near, rows, devices)
        keep.append(far_mine)
        got.append(swap(far_other, Y))
    given = [swap(block, k) for block, k in zip(given, NEAR)]
    far = far_sum(keep, got, rows)
    far = [swap(block, z) for z, block in zip(far_z(devices), far)]
    return last_sum([near, *given, *far])


def solution(mesh):
    placed = (
        P(("grp", "row"), None),
        P(("grp", "row"), None),
        P(("grp", "row"), None, None),
        P(("grp", "row")),
        P(None, "row"),
        P("row", None, None),
        P("row", None, None),
        P("row", None),
    )
    body = functools.partial(on_device, devices=mesh.shape["row"])
    return jax.shard_map(
        body, mesh=mesh, in_specs=placed, out_specs=P(("grp", "row"), None), check_vma=False
    )
```

```python
import functools
import math

import jax
import jax.numpy as jnp
from jax import lax
from jax.experimental import pallas as pl
from jax.experimental.pallas import tpu as pltpu
from jax.sharding import PartitionSpec as P

LAT = 512
ROPE = 64
HALF = ROPE // 2
NOPE = 128
VD = 128
LANES = 128
PIECES = LAT // LANES
SCALE = (NOPE + ROPE) ** -0.5 * math.log2(math.e)
LIMIT = 16 * 2**20
PARTS = 2
Y = 2
Z1 = 4
NEAR = (Z1, Y + Z1, Y)


def resident(x):
    return pltpu.with_memory_space_constraint(x, pltpu.VMEM)


def in_vmem():
    return pl.BlockSpec(memory_space=pltpu.VMEM)


def call(kernel, out_shape, microseconds, name, scratch=(), scalars=0):
    def run(*args):
        smem = [pl.BlockSpec(memory_space=pltpu.SMEM)] * scalars
        return pl.pallas_call(
            kernel,
            out_shape=out_shape,
            in_specs=smem + [in_vmem()] * (len(args) - scalars),
            out_specs=jax.tree.map(lambda _: in_vmem(), out_shape),
            scratch_shapes=list(scratch),
            compiler_params=pltpu.CompilerParams(vmem_limit_bytes=LIMIT),
            cost_estimate=pl.CostEstimate(
                flops=int(microseconds * 1.15e9), bytes_accessed=0, transcendentals=0
            ),
            name=name,
        )(*args)

    return run


def shape(*dims, dtype=jnp.bfloat16):
    return jax.ShapeDtypeStruct(dims, dtype)


def far_first(devices, step):
    return sorted(range(0, devices, step), key=lambda k: -k.bit_length())


def far_chips(devices):
    return [k for k in far_first(devices, 2) if k > Y + Z1]


def chip_order(devices):
    return [*far_chips(devices), Y, Y + Z1, Z1, 0]


def message_sizes(devices):
    return [1] * len(far_chips(devices)) + [2, 1, 1]


def gathered_order(devices):
    return [z + y for z in reversed(far_first(devices, 4)) for y in (0, 2)]


def rotary_kernel(len_ref, cos_ref, sin_ref):
    rows, width = cos_ref.shape
    lane = lax.broadcasted_iota(jnp.int32, (rows, width), 1)
    place = lax.broadcasted_iota(jnp.int32, (rows, width), 0)
    step = jnp.where(lane < HALF, lane, lane - HALF).astype(jnp.float32)
    frequency = jnp.exp(step * (-math.log(10000.0) / HALF))
    length = jnp.zeros((rows, width), jnp.float32)
    for r in range(rows):
        length = jnp.where(place == r, len_ref[r].astype(jnp.float32), length)
    angle = length * frequency
    sine = jnp.sin(angle)
    cos_ref[...] = jnp.cos(angle)
    sin_ref[...] = jnp.where(lane < HALF, -sine, sine)


def rotary(lengths):
    table = shape(lengths.shape[0], ROPE, dtype=jnp.float32)
    return call(rotary_kernel, (table, table), 3, "rotary", scalars=1)(lengths)


def join_kernel(cos_ref, sin_ref, *refs):
    *in_refs, cos_out_ref, sin_out_ref, out_ref = refs
    cos_out_ref[...] = cos_ref[...]
    sin_out_ref[...] = sin_ref[...]
    out_ref[...] = jnp.concatenate(
        [ref[...].astype(jnp.float32) for ref in in_refs], axis=0
    ).astype(out_ref.dtype)


def join(tables, blocks):
    rows, depth = blocks[0].shape
    out = (*[shape(*t.shape, dtype=t.dtype) for t in tables], shape(len(blocks) * rows, depth))
    cosine, sine, joined = call(join_kernel, out, 3, "join")(*tables, *blocks)
    return (cosine, sine), joined


def project_kernel(devices, *refs):
    pieces = devices // 4
    q_refs = refs[:pieces]
    weights = (refs[pieces : pieces + 2], refs[pieces + 2 : pieces + 4])
    lat_ref, rot_ref = refs[-2:]
    out_refs = refs[pieces + 4 : -2]
    heads = weights[0][1].shape[0]
    piece = jnp.concatenate([ref[...].astype(jnp.float32) for ref in q_refs], axis=0)
    piece = piece.astype(jnp.bfloat16)
    count = piece.shape[0]
    wide = 2 * count // devices * heads
    width = NOPE + ROPE
    lane = lax.broadcasted_iota(jnp.int32, (wide // 2, LANES), 1)
    blocks = [(ref, 2 * i) for ref in out_refs for i in range(ref.shape[0] // 2)]
    blocks = dict(zip(chip_order(devices), blocks))
    for core, (wq_ref, wk_ref) in enumerate(weights):
        projected = jnp.dot(piece, wq_ref[...], preferred_element_type=jnp.float32)
        for h in range(heads):
            mine = projected[:, h * width : (h + 1) * width]
            absorbed = jnp.dot(
                mine[:, :NOPE].astype(jnp.bfloat16), wk_ref[h], preferred_element_type=jnp.float32
            )
            spread = pl.ds(h, count, stride=heads)
            for c in range(PIECES):
                lat_ref[core * PIECES + c, spread, :] = absorbed[:, c * LANES : (c + 1) * LANES]
            pe = mine[:, NOPE:]
            rot_ref[core, spread, :] = jnp.concatenate([pe, pe], axis=-1)
        for place, k in enumerate(gathered_order(devices)):
            out_ref, at = blocks[k]
            at += core
            first = place * wide
            for c in range(PIECES):
                out_ref[at, c * wide : (c + 1) * wide, :] = lat_ref[
                    core * PIECES + c, first : first + wide, :
                ].astype(jnp.bfloat16)
            low = rot_ref[core, first : first + wide // 2, :]
            high = rot_ref[core, first + wide // 2 : first + wide, :]
            out_ref[at, PIECES * wide :, :] = jnp.where(lane < ROPE, low, high).astype(
                jnp.bfloat16
            )


def project(pieces, weights, devices):
    heads = weights[1].shape[0]
    count = len(pieces) * pieces[0].shape[0]
    wide = 2 * count // devices * heads
    scratch = [
        pltpu.VMEM((2 * PIECES, count * heads, LANES), jnp.float32),
        pltpu.VMEM((2, count * heads, LANES), jnp.float32),
    ]
    tall = PIECES * wide + wide // 2
    out = [shape(2 * size, tall, LANES) for size in message_sizes(devices)]
    kernel = functools.partial(project_kernel, devices)
    return call(kernel, out, 20, "project", scratch)(*pieces, *[resident(w) for w in weights])


def flip_kernel(key_ref, after_ref, out_ref):
    for r in range(key_ref.shape[0]):
        out_ref[r] = key_ref[r, :LAT, :].T


def flip(keys, after):
    rows, _, maxlen = keys.shape
    return call(flip_kernel, shape(rows, maxlen, LAT), 4, "flip")(resident(keys), after)


def forward_kernel(own_ref, passing_ref, out_ref):
    out_ref[:2] = own_ref[...]
    out_ref[2:] = passing_ref[2:]


def forward(own, passing):
    return call(forward_kernel, shape(4, *own.shape[1:]), 1, "forward")(own, passing)


def arrived(refs):
    blocks = []
    for i, ref in enumerate(refs):
        count = 2 if i == len(refs) - 3 else ref.shape[0]
        blocks += [(ref, core) for core in range(count)]
    return blocks


def attend_kernel(sizes, len_ref, cos_ref, sin_ref, key_ref, flip_ref, new_ref, *refs):
    blocks = arrived(refs[: len(sizes)])
    out_refs = refs[len(sizes) :]
    rows, _, maxlen = key_ref.shape
    wide = out_refs[0].shape[1]
    heads = wide // rows

    def query_block(first):
        parts = [ref[i, first : first + heads, :].astype(jnp.float32) for ref, i in blocks]
        return jnp.concatenate(parts, axis=0)

    def score(r):
        latent = jnp.concatenate(
            [query_block(c * wide + r * heads) for c in range(PIECES)], axis=-1
        )
        pe = query_block(PIECES * wide + (r % (rows // 2)) * heads)
        side = r // (rows // 2) * ROPE
        pe = pe[:, side : side + ROPE]
        swapped = jnp.concatenate([pe[:, HALF:], pe[:, :HALF]], axis=-1)
        rotated = (pe * cos_ref[r : r + 1, :] + swapped * sin_ref[r : r + 1, :]).astype(jnp.bfloat16)
        newest = new_ref[r : r + 1, :].astype(jnp.float32)
        own = jnp.sum(latent * newest[:, :LAT], axis=-1, keepdims=True) + jnp.sum(
            rotated.astype(jnp.float32) * newest[:, LAT:], axis=-1, keepdims=True
        )
        scores = jnp.dot(
            latent.astype(jnp.bfloat16), key_ref[r, :LAT, :], preferred_element_type=jnp.float32
        )
        scores += jnp.dot(rotated, key_ref[r, LAT:, :], preferred_element_type=jnp.float32)
        position = lax.broadcasted_iota(jnp.int32, (1, maxlen), 1)
        return jnp.where(position < len_ref[r], scores, -jnp.inf), own

    back = [(ref, i) for ref in out_refs for i in range(ref.shape[0])]
    y_at = len(back) - 8
    back = back[: y_at + 2] + back[y_at + 4 : y_at + 6] + back[y_at + 2 : y_at + 4] + back[-2:]
    ahead = score(0)
    for r in range(rows):
        scores, own = ahead
        if r + 1 < rows:
            ahead = score(r + 1)
        peak = jnp.maximum(jnp.max(scores, axis=-1, keepdims=True), own)
        expo = jnp.exp2((scores - peak) * SCALE)
        own_expo = jnp.exp2((own - peak) * SCALE)
        inverse = 1.0 / (jnp.sum(expo, axis=-1, keepdims=True) + own_expo)
        weights = (expo * inverse).astype(jnp.bfloat16)
        own_weight = (own_expo * inverse).astype(jnp.bfloat16).astype(jnp.float32)
        summed = jnp.dot(weights, flip_ref[r], preferred_element_type=jnp.float32)
        summed += own_weight * new_ref[r : r + 1, :LAT].astype(jnp.float32)
        for k, (out_ref, i) in enumerate(back):
            out_ref[i, r * heads : (r + 1) * heads, :] = summed[
                k * heads : (k + 1) * heads, :
            ].astype(jnp.bfloat16)


def attend(lengths, tables, keys, flipped, new_latent, messages, heads, devices):
    sizes = message_sizes(devices)
    out = [shape(2 * size, keys.shape[0] * heads, LAT) for size in sizes]
    return call(functools.partial(attend_kernel, sizes), out, 10, "attend", scalars=1)(
        lengths, *tables, resident(keys), resident(flipped), new_latent, *messages
    )


def early_kernel(own_ref, after_ref, out_ref):
    out_ref[...] = own_ref[...]


def early(own, after):
    return call(early_kernel, shape(*own.shape), 4, "early")(own, after)


def values_kernel(count, core, *refs):
    blocks = arrived(refs[:count])[core::2]
    wv_ref, val_ref, rows_ref = refs[count:]
    heads = wv_ref.shape[0]
    for place, (ref, i) in enumerate(blocks):
        block = ref[i].astype(jnp.float32)
        wide = block.shape[0]
        for c in range(PIECES):
            rows_ref[c, place * wide : (place + 1) * wide, :] = block[:, c * LANES : (c + 1) * LANES]
    total = val_ref.shape[0]
    for h in range(heads):
        chosen = jnp.concatenate(
            [rows_ref[c, pl.ds(h, total, stride=heads), :] for c in range(PIECES)], axis=-1
        )
        val_ref[:, h * VD : (h + 1) * VD] = jnp.dot(
            chosen.astype(jnp.bfloat16), wv_ref[h], preferred_element_type=jnp.float32
        ).astype(jnp.bfloat16)


def head_values(messages, w_uv, core, chips):
    heads = w_uv.shape[0]
    count = chips * messages[0].shape[1] // heads
    scratch = [pltpu.VMEM((PIECES, count * heads, LANES), jnp.float32)]
    kernel = functools.partial(values_kernel, len(messages), core)
    return call(kernel, shape(count, heads * VD), 2, "values", scratch)(*messages, resident(w_uv))


def terms_kernel(start, *refs):
    *val_refs, wo_ref = refs[: len(refs) // 2 + 1]
    out_refs = refs[len(refs) // 2 + 1 :]
    half, width = out_refs[0].shape
    values = jnp.concatenate([ref[...] for ref in val_refs], axis=0)
    terms = jnp.dot(values, wo_ref[:, start : start + width], preferred_element_type=jnp.float32)
    for i, out_ref in enumerate(out_refs):
        out_ref[...] = terms[i * half : (i + 1) * half].astype(out_ref.dtype)


def output_terms(values, types, w_o, part):
    width = w_o.shape[1] // PARTS
    out = [shape(v.shape[0], width, dtype=t) for v, t in zip(values, types)]
    kernel = functools.partial(terms_kernel, part * width)
    return call(kernel, out, 3 * len(values), "terms")(*values, resident(w_o))


def far_z(devices):
    return [z for z in far_first(devices, Z1) if z > Z1][::-1]


def places(devices, chips):
    order = [*far_chips(devices), Y, Z1, Y + Z1, 0]
    return [order.index(k) for k in chips]


def pick(total, rows, where):
    return jnp.concatenate([total[j * rows : (j + 1) * rows] for j in where], axis=0)


def first_sum_kernel(rows, keep, give, near, mine_ref, other_ref, keep_ref, give_ref, near_ref):
    total = mine_ref[...] + other_ref[...].astype(jnp.float32)
    keep_ref[...] = pick(total, rows, keep)
    give_ref[...] = pick(total, rows, give).astype(give_ref.dtype)
    near_ref[...] = pick(total, rows, near)


def last_part_kernel(rows, keep, give, near, mine_ref, other_ref, before_ref, *out_refs):
    keep_ref, give_ref, *near_refs = out_refs
    total = mine_ref[...] + other_ref[...].astype(jnp.float32)
    keep_ref[...] = pick(total, rows, keep)
    give_ref[...] = pick(total, rows, give).astype(give_ref.dtype)
    width = before_ref.shape[1]
    for i, (j, out_ref) in enumerate(zip(near, near_refs)):
        out_ref[:, :width] = before_ref[i * rows : (i + 1) * rows].astype(out_ref.dtype)
        out_ref[:, width:] = total[j * rows : (j + 1) * rows].astype(out_ref.dtype)


def core_sum(mine, other, before, rows, devices):
    count, width = mine.shape
    keep = places(devices, far_z(devices))
    give = places(devices, [z + Y for z in far_z(devices)])
    near = places(devices, [0, *NEAR])
    far = len(keep) * rows
    out = (shape(far, width, dtype=jnp.float32), shape(far, width))
    if before is None:
        kernel = functools.partial(first_sum_kernel, rows, keep, give, near)
        out += (shape(4 * rows, width, dtype=jnp.float32),)
        return call(kernel, out, 1, "core_sum")(mine, other)
    kernel = functools.partial(last_part_kernel, rows, keep, give, near)
    full = before.shape[1] + width
    out += (shape(rows, full, dtype=jnp.float32), *[shape(rows, full)] * len(NEAR))
    return call(kernel, out, 1, "core_sum")(mine, other, before)


def far_sum_kernel(*refs):
    mine_refs = refs[:PARTS]
    other_refs = refs[PARTS : 2 * PARTS]
    out_refs = refs[2 * PARTS :]
    rows = out_refs[0].shape[0]
    for p, (mine_ref, other_ref) in enumerate(zip(mine_refs, other_refs)):
        width = mine_ref.shape[1]
        total = mine_ref[...] + other_ref[...].astype(jnp.float32)
        for j, out_ref in enumerate(out_refs):
            out_ref[:, p * width : (p + 1) * width] = total[j * rows : (j + 1) * rows].astype(
                out_ref.dtype
            )


def far_sum(mine, other, rows):
    count, width = mine[0].shape
    out = [shape(rows, PARTS * width)] * (count // rows)
    return call(far_sum_kernel, out, 1, "far_sum")(*mine, *other)


def last_sum_kernel(*refs):
    *in_refs, out_ref = refs
    terms = [ref[...].astype(jnp.float32) for ref in in_refs]
    out_ref[...] = sum(terms[1:], terms[0]).astype(out_ref.dtype)


def last_sum(blocks):
    return call(last_sum_kernel, shape(*blocks[0].shape), 1, "last_sum")(*blocks)


def on_device(q_latent, new_latent, cache, lengths, w_uq, w_uk, w_uv, w_o, devices):
    heads = w_uk.shape[0]
    rows = cache.shape[0]
    zs = far_first(devices, 4)[::-1]

    def swap(block, k):
        if k == 0:
            return block
        return lax.ppermute(block, "row", [(i, i ^ k) for i in range(devices)])

    across = swap(q_latent, Y)
    far_weights = [swap(w_uq, 1), swap(w_uk, 1)]
    tables, near = join(rotary(lengths), [q_latent, across])
    def exchange(messages):
        *far, across, pair, own = messages
        early = len(far) // 2
        got = [swap(block, k) for block, k in zip(far[:early], far_k)]
        passing = swap(across, Y)
        got += [swap(block, k) for block, k in zip(far[early:], far_k[early:])]
        sent = forward(pair, passing)
        return [*got, passing, swap(sent, Z1), own], sent

    far_k = far_chips(devices)
    messages = project([swap(near, z) for z in zs], [w_uq, w_uk, *far_weights], devices)
    messages, sent = exchange(messages)
    keys = jnp.swapaxes(cache, 1, 2)
    flipped = flip(keys, sent)
    far_wv = swap(w_uv, 1)
    latents = attend(lengths, tables, keys, flipped, new_latent, messages, heads, devices)
    latents, sent = exchange(latents)
    latents[-1] = early(latents[-1], sent)
    other_values = head_values(latents, far_wv, 1, devices // 2)
    other_values = swap(other_values, 1)
    mine_values = head_values(latents, w_uv, 0, devices // 2)
    keep, got, near = [], [], None
    for part in range(PARTS):
        mine, other = output_terms(
            [mine_values, other_values], [jnp.float32, jnp.bfloat16], w_o, part
        )
        far_mine, far_other, near, *given = core_sum(mine, swap(other, 1), near, rows, devices)
        keep.append(far_mine)
        got.append(swap(far_other, Y))
    given = [swap(block, k) for block, k in zip(given, NEAR)]
    far = far_sum(keep, got, rows)
    far = [swap(block, z) for z, block in zip(far_z(devices), far)]
    return last_sum([near, *given, *far])


def solution(mesh):
    placed = (
        P(("grp", "row"), None),
        P(("grp", "row"), None),
        P(("grp", "row"), None, None),
        P(("grp", "row")),
        P(None, "row"),
        P("row", None, None),
        P("row", None, None),
        P("row", None),
    )
    body = functools.partial(on_device, devices=mesh.shape["row"])
    return jax.shard_map(
        body, mesh=mesh, in_specs=placed, out_specs=P(("grp", "row"), None), check_vma=False
    )
```

```python
import functools
import math

import jax
import jax.numpy as jnp
from jax import lax
from jax.experimental import pallas as pl
from jax.experimental.pallas import tpu as pltpu
from jax.sharding import PartitionSpec as P

LAT = 512
ROPE = 64
HALF = ROPE // 2
NOPE = 128
VD = 128
LANES = 128
PIECES = LAT // LANES
SCALE = (NOPE + ROPE) ** -0.5 * math.log2(math.e)
LIMIT = 16 * 2**20
PARTS = 2
Y = 2
Z1 = 4
NEAR = (Z1, Y + Z1, Y)


def resident(x):
    return pltpu.with_memory_space_constraint(x, pltpu.VMEM)


def in_vmem():
    return pl.BlockSpec(memory_space=pltpu.VMEM)


def call(kernel, out_shape, microseconds, name, scratch=(), scalars=0):
    def run(*args):
        smem = [pl.BlockSpec(memory_space=pltpu.SMEM)] * scalars
        return pl.pallas_call(
            kernel,
            out_shape=out_shape,
            in_specs=smem + [in_vmem()] * (len(args) - scalars),
            out_specs=jax.tree.map(lambda _: in_vmem(), out_shape),
            scratch_shapes=list(scratch),
            compiler_params=pltpu.CompilerParams(vmem_limit_bytes=LIMIT),
            cost_estimate=pl.CostEstimate(
                flops=int(microseconds * 1.15e9), bytes_accessed=0, transcendentals=0
            ),
            name=name,
        )(*args)

    return run


def shape(*dims, dtype=jnp.bfloat16):
    return jax.ShapeDtypeStruct(dims, dtype)


def far_first(devices, step):
    return sorted(range(0, devices, step), key=lambda k: -k.bit_length())


def far_chips(devices):
    chips = [k for k in far_first(devices, 2) if k > Y + Z1]
    return [k for k in chips if not k & Y] + [k for k in chips if k & Y]


def chip_order(devices):
    return [*far_chips(devices), Y, Y + Z1, Z1, 0]


def message_sizes(devices):
    return [1] * len(far_chips(devices)) + [2, 1, 1]


def gathered_order(devices):
    return [z + y for z in reversed(far_first(devices, 4)) for y in (0, 2)]


def rotary_kernel(len_ref, cos_ref, sin_ref):
    rows, width = cos_ref.shape
    lane = lax.broadcasted_iota(jnp.int32, (rows, width), 1)
    place = lax.broadcasted_iota(jnp.int32, (rows, width), 0)
    step = jnp.where(lane < HALF, lane, lane - HALF).astype(jnp.float32)
    frequency = jnp.exp(step * (-math.log(10000.0) / HALF))
    length = jnp.zeros((rows, width), jnp.float32)
    for r in range(rows):
        length = jnp.where(place == r, len_ref[r].astype(jnp.float32), length)
    angle = length * frequency
    sine = jnp.sin(angle)
    cos_ref[...] = jnp.cos(angle)
    sin_ref[...] = jnp.where(lane < HALF, -sine, sine)


def rotary(lengths):
    table = shape(lengths.shape[0], ROPE, dtype=jnp.float32)
    return call(rotary_kernel, (table, table), 3, "rotary", scalars=1)(lengths)


def join_kernel(cos_ref, sin_ref, *refs):
    *in_refs, cos_out_ref, sin_out_ref, out_ref = refs
    cos_out_ref[...] = cos_ref[...]
    sin_out_ref[...] = sin_ref[...]
    out_ref[...] = jnp.concatenate(
        [ref[...].astype(jnp.float32) for ref in in_refs], axis=0
    ).astype(out_ref.dtype)


def join(tables, blocks):
    rows, depth = blocks[0].shape
    out = (*[shape(*t.shape, dtype=t.dtype) for t in tables], shape(len(blocks) * rows, depth))
    cosine, sine, joined = call(join_kernel, out, 3, "join")(*tables, *blocks)
    return (cosine, sine), joined


def project_kernel(devices, *refs):
    pieces = devices // 4
    q_refs = refs[:pieces]
    weights = (refs[pieces : pieces + 2], refs[pieces + 2 : pieces + 4])
    lat_ref, rot_ref = refs[-2:]
    out_refs = refs[pieces + 4 : -2]
    heads = weights[0][1].shape[0]
    piece = jnp.concatenate([ref[...].astype(jnp.float32) for ref in q_refs], axis=0)
    piece = piece.astype(jnp.bfloat16)
    count = piece.shape[0]
    wide = 2 * count // devices * heads
    width = NOPE + ROPE
    lane = lax.broadcasted_iota(jnp.int32, (wide // 2, LANES), 1)
    blocks = [(ref, 2 * i) for ref in out_refs for i in range(ref.shape[0] // 2)]
    blocks = dict(zip(chip_order(devices), blocks))
    for core, (wq_ref, wk_ref) in enumerate(weights):
        projected = jnp.dot(piece, wq_ref[...], preferred_element_type=jnp.float32)
        for h in range(heads):
            mine = projected[:, h * width : (h + 1) * width]
            absorbed = jnp.dot(
                mine[:, :NOPE].astype(jnp.bfloat16), wk_ref[h], preferred_element_type=jnp.float32
            )
            spread = pl.ds(h, count, stride=heads)
            for c in range(PIECES):
                lat_ref[core * PIECES + c, spread, :] = absorbed[:, c * LANES : (c + 1) * LANES]
            pe = mine[:, NOPE:]
            rot_ref[core, spread, :] = jnp.concatenate([pe, pe], axis=-1)
        for place, k in enumerate(gathered_order(devices)):
            out_ref, at = blocks[k]
            at += core
            first = place * wide
            for c in range(PIECES):
                out_ref[at, c * wide : (c + 1) * wide, :] = lat_ref[
                    core * PIECES + c, first : first + wide, :
                ].astype(jnp.bfloat16)
            low = rot_ref[core, first : first + wide // 2, :]
            high = rot_ref[core, first + wide // 2 : first + wide, :]
            out_ref[at, PIECES * wide :, :] = jnp.where(lane < ROPE, low, high).astype(
                jnp.bfloat16
            )


def project(pieces, weights, devices):
    heads = weights[1].shape[0]
    count = len(pieces) * pieces[0].shape[0]
    wide = 2 * count // devices * heads
    scratch = [
        pltpu.VMEM((2 * PIECES, count * heads, LANES), jnp.float32),
        pltpu.VMEM((2, count * heads, LANES), jnp.float32),
    ]
    tall = PIECES * wide + wide // 2
    out = [shape(2 * size, tall, LANES) for size in message_sizes(devices)]
    kernel = functools.partial(project_kernel, devices)
    return call(kernel, out, 20, "project", scratch)(*pieces, *[resident(w) for w in weights])


def flip_kernel(key_ref, after_ref, out_ref):
    for r in range(key_ref.shape[0]):
        out_ref[r] = key_ref[r, :LAT, :].T


def flip(keys, after):
    rows, _, maxlen = keys.shape
    return call(flip_kernel, shape(rows, maxlen, LAT), 4, "flip")(resident(keys), after)


def forward_kernel(own_ref, passing_ref, out_ref):
    out_ref[:2] = own_ref[...]
    out_ref[2:] = passing_ref[2:]


def forward(own, passing):
    return call(forward_kernel, shape(4, *own.shape[1:]), 1, "forward")(own, passing)


def arrived(refs):
    blocks = []
    for i, ref in enumerate(refs):
        count = 2 if i == len(refs) - 3 else ref.shape[0]
        blocks += [(ref, core) for core in range(count)]
    return blocks


def attend_kernel(sizes, len_ref, cos_ref, sin_ref, key_ref, flip_ref, new_ref, *refs):
    blocks = arrived(refs[: len(sizes)])
    out_refs = refs[len(sizes) :]
    rows, _, maxlen = key_ref.shape
    wide = out_refs[0].shape[1]
    heads = wide // rows

    def query_block(first):
        parts = [ref[i, first : first + heads, :].astype(jnp.float32) for ref, i in blocks]
        return jnp.concatenate(parts, axis=0)

    def score(r):
        latent = jnp.concatenate(
            [query_block(c * wide + r * heads) for c in range(PIECES)], axis=-1
        )
        pe = query_block(PIECES * wide + (r % (rows // 2)) * heads)
        side = r // (rows // 2) * ROPE
        pe = pe[:, side : side + ROPE]
        swapped = jnp.concatenate([pe[:, HALF:], pe[:, :HALF]], axis=-1)
        rotated = (pe * cos_ref[r : r + 1, :] + swapped * sin_ref[r : r + 1, :]).astype(jnp.bfloat16)
        newest = new_ref[r : r + 1, :].astype(jnp.float32)
        own = jnp.sum(latent * newest[:, :LAT], axis=-1, keepdims=True) + jnp.sum(
            rotated.astype(jnp.float32) * newest[:, LAT:], axis=-1, keepdims=True
        )
        scores = jnp.dot(
            latent.astype(jnp.bfloat16), key_ref[r, :LAT, :], preferred_element_type=jnp.float32
        )
        scores += jnp.dot(rotated, key_ref[r, LAT:, :], preferred_element_type=jnp.float32)
        position = lax.broadcasted_iota(jnp.int32, (1, maxlen), 1)
        return jnp.where(position < len_ref[r], scores, -jnp.inf), own

    back = [(ref, i) for ref in out_refs for i in range(ref.shape[0])]
    y_at = len(back) - 8
    back = back[: y_at + 2] + back[y_at + 4 : y_at + 6] + back[y_at + 2 : y_at + 4] + back[-2:]
    ahead = score(0)
    for r in range(rows):
        scores, own = ahead
        if r + 1 < rows:
            ahead = score(r + 1)
        peak = jnp.maximum(jnp.max(scores, axis=-1, keepdims=True), own)
        expo = jnp.exp2((scores - peak) * SCALE)
        own_expo = jnp.exp2((own - peak) * SCALE)
        inverse = 1.0 / (jnp.sum(expo, axis=-1, keepdims=True) + own_expo)
        weights = (expo * inverse).astype(jnp.bfloat16)
        own_weight = (own_expo * inverse).astype(jnp.bfloat16).astype(jnp.float32)
        summed = jnp.dot(weights, flip_ref[r], preferred_element_type=jnp.float32)
        summed += own_weight * new_ref[r : r + 1, :LAT].astype(jnp.float32)
        for k, (out_ref, i) in enumerate(back):
            out_ref[i, r * heads : (r + 1) * heads, :] = summed[
                k * heads : (k + 1) * heads, :
            ].astype(jnp.bfloat16)


def attend(lengths, tables, keys, flipped, new_latent, messages, heads, devices):
    sizes = message_sizes(devices)
    out = [shape(2 * size, keys.shape[0] * heads, LAT) for size in sizes]
    return call(functools.partial(attend_kernel, sizes), out, 10, "attend", scalars=1)(
        lengths, *tables, resident(keys), resident(flipped), new_latent, *messages
    )


def early_kernel(passing_ref, own_ref, after_ref, out_ref):
    out_ref[0] = passing_ref[1]
    out_ref[1] = own_ref[1]


def early(passing, own, after):
    return call(early_kernel, shape(2, *own.shape[1:]), 4, "early")(passing, own, after)


def regroup_kernel(*refs):
    *in_refs, early_ref, out_ref = refs
    blocks = arrived(in_refs)[1::2]
    blocks = [*blocks[:-4], (early_ref, 0), *blocks[-3:-1], (early_ref, 1)]
    for j, (ref, i) in enumerate(blocks):
        out_ref[j] = ref[i]


def regroup(messages, ready, chips):
    _, wide, width = messages[0].shape
    return call(regroup_kernel, shape(chips, wide, width), 1, "regroup")(*messages, ready)


def values_kernel(*refs):
    *in_refs, other_ref, wv_ref, val_ref, rows_ref = refs
    mine = arrived(in_refs)[::2]
    chips = len(mine)
    heads = wv_ref.shape[0]
    wide = other_ref.shape[1]
    for place in range(2 * chips):
        ref, i = mine[place] if place < chips else (other_ref, place - chips)
        block = ref[i].astype(jnp.float32)
        for c in range(PIECES):
            rows_ref[c, place * wide : (place + 1) * wide, :] = block[:, c * LANES : (c + 1) * LANES]
    count = val_ref.shape[0]
    for h in range(heads):
        chosen = jnp.concatenate(
            [rows_ref[c, pl.ds(h, count, stride=heads), :] for c in range(PIECES)], axis=-1
        )
        val_ref[:, h * VD : (h + 1) * VD] = jnp.dot(
            chosen.astype(jnp.bfloat16), wv_ref[h], preferred_element_type=jnp.float32
        ).astype(jnp.bfloat16)


def head_values(messages, other, w_uv):
    chips, wide, _ = other.shape
    heads = w_uv.shape[0]
    count = 2 * chips * wide // heads
    scratch = [pltpu.VMEM((PIECES, count * heads, LANES), jnp.float32)]
    return call(values_kernel, shape(count, heads * VD), 3, "values", scratch)(
        *messages, other, resident(w_uv)
    )


def terms_kernel(start, val_ref, wo_ref, mine_ref, other_ref):
    half, width = mine_ref.shape
    terms = jnp.dot(
        val_ref[...], wo_ref[:, start : start + width], preferred_element_type=jnp.float32
    )
    mine_ref[...] = terms[:half]
    other_ref[...] = terms[half:].astype(jnp.bfloat16)


def output_terms(values, w_o, part):
    half = values.shape[0] // 2
    width = w_o.shape[1] // PARTS
    out = (shape(half, width, dtype=jnp.float32), shape(half, width))
    kernel = functools.partial(terms_kernel, part * width)
    return call(kernel, out, 6, "terms")(values, resident(w_o))


def far_z(devices):
    return [z for z in far_first(devices, Z1) if z > Z1][::-1]


def places(devices, chips):
    order = [*far_chips(devices), Y, Z1, Y + Z1, 0]
    return [order.index(k) for k in chips]


def pick(total, rows, where):
    return jnp.concatenate([total[j * rows : (j + 1) * rows] for j in where], axis=0)


def first_sum_kernel(rows, keep, give, near, mine_ref, other_ref, keep_ref, give_ref, near_ref):
    total = mine_ref[...] + other_ref[...].astype(jnp.float32)
    keep_ref[...] = pick(total, rows, keep)
    give_ref[...] = pick(total, rows, give).astype(give_ref.dtype)
    near_ref[...] = pick(total, rows, near)


def last_part_kernel(rows, keep, give, near, mine_ref, other_ref, before_ref, *out_refs):
    keep_ref, give_ref, *near_refs = out_refs
    total = mine_ref[...] + other_ref[...].astype(jnp.float32)
    keep_ref[...] = pick(total, rows, keep)
    give_ref[...] = pick(total, rows, give).astype(give_ref.dtype)
    width = before_ref.shape[1]
    for i, (j, out_ref) in enumerate(zip(near, near_refs)):
        out_ref[:, :width] = before_ref[i * rows : (i + 1) * rows].astype(out_ref.dtype)
        out_ref[:, width:] = total[j * rows : (j + 1) * rows].astype(out_ref.dtype)


def core_sum(mine, other, before, rows, devices):
    count, width = mine.shape
    keep = places(devices, far_z(devices))
    give = places(devices, [z + Y for z in far_z(devices)])
    near = places(devices, [0, *NEAR])
    far = len(keep) * rows
    out = (shape(far, width, dtype=jnp.float32), shape(far, width))
    if before is None:
        kernel = functools.partial(first_sum_kernel, rows, keep, give, near)
        out += (shape(4 * rows, width, dtype=jnp.float32),)
        return call(kernel, out, 1, "core_sum")(mine, other)
    kernel = functools.partial(last_part_kernel, rows, keep, give, near)
    full = before.shape[1] + width
    out += (shape(rows, full, dtype=jnp.float32), *[shape(rows, full)] * len(NEAR))
    return call(kernel, out, 1, "core_sum")(mine, other, before)


def far_sum_kernel(*refs):
    mine_refs = refs[:PARTS]
    other_refs = refs[PARTS : 2 * PARTS]
    out_refs = refs[2 * PARTS :]
    rows = out_refs[0].shape[0]
    for p, (mine_ref, other_ref) in enumerate(zip(mine_refs, other_refs)):
        width = mine_ref.shape[1]
        total = mine_ref[...] + other_ref[...].astype(jnp.float32)
        for j, out_ref in enumerate(out_refs):
            out_ref[:, p * width : (p + 1) * width] = total[j * rows : (j + 1) * rows].astype(
                out_ref.dtype
            )


def far_sum(mine, other, rows):
    count, width = mine[0].shape
    out = [shape(rows, PARTS * width)] * (count // rows)
    return call(far_sum_kernel, out, 1, "far_sum")(*mine, *other)


def last_sum_kernel(*refs):
    *in_refs, out_ref = refs
    terms = [ref[...].astype(jnp.float32) for ref in in_refs]
    out_ref[...] = sum(terms[1:], terms[0]).astype(out_ref.dtype)


def last_sum(blocks):
    return call(last_sum_kernel, shape(*blocks[0].shape), 1, "last_sum")(*blocks)


def on_device(q_latent, new_latent, cache, lengths, w_uq, w_uk, w_uv, w_o, devices):
    heads = w_uk.shape[0]
    rows = cache.shape[0]
    zs = far_first(devices, 4)[::-1]

    def swap(block, k):
        if k == 0:
            return block
        return lax.ppermute(block, "row", [(i, i ^ k) for i in range(devices)])

    across = swap(q_latent, Y)
    far_weights = [swap(w_uq, 1), swap(w_uk, 1)]
    tables, near = join(rotary(lengths), [q_latent, across])
    def exchange(messages):
        *far, across, pair, own = messages
        early = len(far) // 2
        got = [swap(block, k) for block, k in zip(far[:early], far_k)]
        passing = swap(across, Y)
        got += [swap(block, k) for block, k in zip(far[early:], far_k[early:])]
        sent = forward(pair, passing)
        return [*got, passing, swap(sent, Z1), own], sent

    far_k = far_chips(devices)
    messages = project([swap(near, z) for z in zs], [w_uq, w_uk, *far_weights], devices)
    messages, sent = exchange(messages)
    keys = jnp.swapaxes(cache, 1, 2)
    flipped = flip(keys, sent)
    latents = attend(lengths, tables, keys, flipped, new_latent, messages, heads, devices)
    latents, sent = exchange(latents)
    ready = early(latents[-3], latents[-1], sent)
    values = head_values(latents, swap(regroup(latents, ready, devices // 2), 1), w_uv)
    keep, got, near = [], [], None
    for part in range(PARTS):
        mine, other = output_terms(values, w_o, part)
        far_mine, far_other, near, *given = core_sum(mine, swap(other, 1), near, rows, devices)
        keep.append(far_mine)
        got.append(swap(far_other, Y))
    given = [swap(block, k) for block, k in zip(given, NEAR)]
    far = far_sum(keep, got, rows)
    far = [swap(block, z) for z, block in zip(far_z(devices), far)]
    return last_sum([near, *given, *far])


def solution(mesh):
    placed = (
        P(("grp", "row"), None),
        P(("grp", "row"), None),
        P(("grp", "row"), None, None),
        P(("grp", "row")),
        P(None, "row"),
        P("row", None, None),
        P("row", None, None),
        P("row", None),
    )
    body = functools.partial(on_device, devices=mesh.shape["row"])
    return jax.shard_map(
        body, mesh=mesh, in_specs=placed, out_specs=P(("grp", "row"), None), check_vma=False
    )
```

```python
import functools
import math

import jax
import jax.numpy as jnp
from jax import lax
from jax.experimental import pallas as pl
from jax.experimental.pallas import tpu as pltpu
from jax.sharding import PartitionSpec as P

LAT = 512
ROPE = 64
HALF = ROPE // 2
NOPE = 128
VD = 128
LANES = 128
PIECES = LAT // LANES
SCALE = (NOPE + ROPE) ** -0.5 * math.log2(math.e)
LIMIT = 16 * 2**20
PARTS = 2
Y = 2
Z1 = 4
NEAR = (Z1, Y + Z1, Y)


def resident(x):
    return pltpu.with_memory_space_constraint(x, pltpu.VMEM)


def in_vmem():
    return pl.BlockSpec(memory_space=pltpu.VMEM)


def call(kernel, out_shape, microseconds, name, scratch=(), scalars=0):
    def run(*args):
        smem = [pl.BlockSpec(memory_space=pltpu.SMEM)] * scalars
        return pl.pallas_call(
            kernel,
            out_shape=out_shape,
            in_specs=smem + [in_vmem()] * (len(args) - scalars),
            out_specs=jax.tree.map(lambda _: in_vmem(), out_shape),
            scratch_shapes=list(scratch),
            compiler_params=pltpu.CompilerParams(vmem_limit_bytes=LIMIT),
            cost_estimate=pl.CostEstimate(
                flops=int(microseconds * 1.15e9), bytes_accessed=0, transcendentals=0
            ),
            name=name,
        )(*args)

    return run


def shape(*dims, dtype=jnp.bfloat16):
    return jax.ShapeDtypeStruct(dims, dtype)


def far_first(devices, step):
    return sorted(range(0, devices, step), key=lambda k: -k.bit_length())


def far_chips(devices):
    chips = [k for k in far_first(devices, 2) if k > Y + Z1]
    return [k for k in chips if not k & Y] + [k for k in chips[::-1] if k & Y]


def chip_order(devices):
    return [*far_chips(devices), Y, Y + Z1, Z1, 0]


def message_sizes(devices):
    return [1] * len(far_chips(devices)) + [2, 1, 1]


def gathered_order(devices):
    return [z + y for z in reversed(far_first(devices, 4)) for y in (0, 2)]


def rotary_kernel(len_ref, cos_ref, sin_ref):
    rows, width = cos_ref.shape
    lane = lax.broadcasted_iota(jnp.int32, (rows, width), 1)
    place = lax.broadcasted_iota(jnp.int32, (rows, width), 0)
    step = jnp.where(lane < HALF, lane, lane - HALF).astype(jnp.float32)
    frequency = jnp.exp(step * (-math.log(10000.0) / HALF))
    length = jnp.zeros((rows, width), jnp.float32)
    for r in range(rows):
        length = jnp.where(place == r, len_ref[r].astype(jnp.float32), length)
    angle = length * frequency
    sine = jnp.sin(angle)
    cos_ref[...] = jnp.cos(angle)
    sin_ref[...] = jnp.where(lane < HALF, -sine, sine)


def rotary(lengths):
    table = shape(lengths.shape[0], ROPE, dtype=jnp.float32)
    return call(rotary_kernel, (table, table), 3, "rotary", scalars=1)(lengths)


def join_kernel(cos_ref, sin_ref, *refs):
    *in_refs, cos_out_ref, sin_out_ref, out_ref = refs
    cos_out_ref[...] = cos_ref[...]
    sin_out_ref[...] = sin_ref[...]
    out_ref[...] = jnp.concatenate(
        [ref[...].astype(jnp.float32) for ref in in_refs], axis=0
    ).astype(out_ref.dtype)


def join(tables, blocks):
    rows, depth = blocks[0].shape
    out = (*[shape(*t.shape, dtype=t.dtype) for t in tables], shape(len(blocks) * rows, depth))
    cosine, sine, joined = call(join_kernel, out, 3, "join")(*tables, *blocks)
    return (cosine, sine), joined


def project_kernel(devices, *refs):
    pieces = devices // 4
    q_refs = refs[:pieces]
    weights = (refs[pieces : pieces + 2], refs[pieces + 2 : pieces + 4])
    lat_ref, rot_ref = refs[-2:]
    out_refs = refs[pieces + 4 : -2]
    heads = weights[0][1].shape[0]
    piece = jnp.concatenate([ref[...].astype(jnp.float32) for ref in q_refs], axis=0)
    piece = piece.astype(jnp.bfloat16)
    count = piece.shape[0]
    wide = 2 * count // devices * heads
    width = NOPE + ROPE
    lane = lax.broadcasted_iota(jnp.int32, (wide // 2, LANES), 1)
    blocks = [(ref, 2 * i) for ref in out_refs for i in range(ref.shape[0] // 2)]
    blocks = dict(zip(chip_order(devices), blocks))
    for core, (wq_ref, wk_ref) in enumerate(weights):
        projected = jnp.dot(piece, wq_ref[...], preferred_element_type=jnp.float32)
        for h in range(heads):
            mine = projected[:, h * width : (h + 1) * width]
            absorbed = jnp.dot(
                mine[:, :NOPE].astype(jnp.bfloat16), wk_ref[h], preferred_element_type=jnp.float32
            )
            spread = pl.ds(h, count, stride=heads)
            for c in range(PIECES):
                lat_ref[core * PIECES + c, spread, :] = absorbed[:, c * LANES : (c + 1) * LANES]
            pe = mine[:, NOPE:]
            rot_ref[core, spread, :] = jnp.concatenate([pe, pe], axis=-1)
        for place, k in enumerate(gathered_order(devices)):
            out_ref, at = blocks[k]
            at += core
            first = place * wide
            for c in range(PIECES):
                out_ref[at, c * wide : (c + 1) * wide, :] = lat_ref[
                    core * PIECES + c, first : first + wide, :
                ].astype(jnp.bfloat16)
            low = rot_ref[core, first : first + wide // 2, :]
            high = rot_ref[core, first + wide // 2 : first + wide, :]
            out_ref[at, PIECES * wide :, :] = jnp.where(lane < ROPE, low, high).astype(
                jnp.bfloat16
            )


def project(pieces, weights, devices):
    heads = weights[1].shape[0]
    count = len(pieces) * pieces[0].shape[0]
    wide = 2 * count // devices * heads
    scratch = [
        pltpu.VMEM((2 * PIECES, count * heads, LANES), jnp.float32),
        pltpu.VMEM((2, count * heads, LANES), jnp.float32),
    ]
    tall = PIECES * wide + wide // 2
    out = [shape(2 * size, tall, LANES) for size in message_sizes(devices)]
    kernel = functools.partial(project_kernel, devices)
    return call(kernel, out, 20, "project", scratch)(*pieces, *[resident(w) for w in weights])


def flip_kernel(key_ref, after_ref, out_ref):
    for r in range(key_ref.shape[0]):
        out_ref[r] = key_ref[r, :LAT, :].T


def flip(keys, after):
    rows, _, maxlen = keys.shape
    return call(flip_kernel, shape(rows, maxlen, LAT), 4, "flip")(resident(keys), after)


def forward_kernel(own_ref, passing_ref, out_ref):
    out_ref[:2] = own_ref[...]
    out_ref[2:] = passing_ref[2:]


def forward(own, passing):
    return call(forward_kernel, shape(4, *own.shape[1:]), 1, "forward")(own, passing)


def arrived(refs):
    blocks = []
    for i, ref in enumerate(refs):
        count = 2 if i == len(refs) - 3 else ref.shape[0]
        blocks += [(ref, core) for core in range(count)]
    return blocks


def attend_kernel(sizes, len_ref, cos_ref, sin_ref, key_ref, flip_ref, new_ref, *refs):
    blocks = arrived(refs[: len(sizes)])
    out_refs = refs[len(sizes) :]
    rows, _, maxlen = key_ref.shape
    wide = out_refs[0].shape[1]
    heads = wide // rows

    def query_block(first):
        parts = [ref[i, first : first + heads, :].astype(jnp.float32) for ref, i in blocks]
        return jnp.concatenate(parts, axis=0)

    def score(r):
        latent = jnp.concatenate(
            [query_block(c * wide + r * heads) for c in range(PIECES)], axis=-1
        )
        pe = query_block(PIECES * wide + (r % (rows // 2)) * heads)
        side = r // (rows // 2) * ROPE
        pe = pe[:, side : side + ROPE]
        swapped = jnp.concatenate([pe[:, HALF:], pe[:, :HALF]], axis=-1)
        rotated = (pe * cos_ref[r : r + 1, :] + swapped * sin_ref[r : r + 1, :]).astype(jnp.bfloat16)
        newest = new_ref[r : r + 1, :].astype(jnp.float32)
        own = jnp.sum(latent * newest[:, :LAT], axis=-1, keepdims=True) + jnp.sum(
            rotated.astype(jnp.float32) * newest[:, LAT:], axis=-1, keepdims=True
        )
        scores = jnp.dot(
            latent.astype(jnp.bfloat16), key_ref[r, :LAT, :], preferred_element_type=jnp.float32
        )
        scores += jnp.dot(rotated, key_ref[r, LAT:, :], preferred_element_type=jnp.float32)
        position = lax.broadcasted_iota(jnp.int32, (1, maxlen), 1)
        return jnp.where(position < len_ref[r], scores, -jnp.inf), own

    back = [(ref, i) for ref in out_refs for i in range(ref.shape[0])]
    y_at = len(back) - 8
    back = back[: y_at + 2] + back[y_at + 4 : y_at + 6] + back[y_at + 2 : y_at + 4] + back[-2:]
    ahead = score(0)
    for r in range(rows):
        scores, own = ahead
        if r + 1 < rows:
            ahead = score(r + 1)
        peak = jnp.maximum(jnp.max(scores, axis=-1, keepdims=True), own)
        expo = jnp.exp2((scores - peak) * SCALE)
        own_expo = jnp.exp2((own - peak) * SCALE)
        inverse = 1.0 / (jnp.sum(expo, axis=-1, keepdims=True) + own_expo)
        weights = (expo * inverse).astype(jnp.bfloat16)
        own_weight = (own_expo * inverse).astype(jnp.bfloat16).astype(jnp.float32)
        summed = jnp.dot(weights, flip_ref[r], preferred_element_type=jnp.float32)
        summed += own_weight * new_ref[r : r + 1, :LAT].astype(jnp.float32)
        for k, (out_ref, i) in enumerate(back):
            out_ref[i, r * heads : (r + 1) * heads, :] = summed[
                k * heads : (k + 1) * heads, :
            ].astype(jnp.bfloat16)


def attend(lengths, tables, keys, flipped, new_latent, messages, heads, devices):
    sizes = message_sizes(devices)
    out = [shape(2 * size, keys.shape[0] * heads, LAT) for size in sizes]
    return call(functools.partial(attend_kernel, sizes), out, 10, "attend", scalars=1)(
        lengths, *tables, resident(keys), resident(flipped), new_latent, *messages
    )


def early_kernel(passing_ref, own_ref, after_ref, out_ref):
    out_ref[0] = passing_ref[1]
    out_ref[1] = own_ref[1]


def early(passing, own, after):
    return call(early_kernel, shape(2, *own.shape[1:]), 4, "early")(passing, own, after)


def regroup_kernel(*refs):
    *in_refs, early_ref, out_ref = refs
    blocks = arrived(in_refs)[1::2]
    blocks = [*blocks[:-4], (early_ref, 0), *blocks[-3:-1], (early_ref, 1)]
    for j, (ref, i) in enumerate(blocks):
        out_ref[j] = ref[i]


def regroup(messages, ready, chips):
    _, wide, width = messages[0].shape
    return call(regroup_kernel, shape(chips, wide, width), 1, "regroup")(*messages, ready)


def values_kernel(*refs):
    *in_refs, other_ref, wv_ref, val_ref, rows_ref = refs
    mine = arrived(in_refs)[::2]
    chips = len(mine)
    heads = wv_ref.shape[0]
    wide = other_ref.shape[1]
    for place in range(2 * chips):
        ref, i = mine[place] if place < chips else (other_ref, place - chips)
        block = ref[i].astype(jnp.float32)
        for c in range(PIECES):
            rows_ref[c, place * wide : (place + 1) * wide, :] = block[:, c * LANES : (c + 1) * LANES]
    count = val_ref.shape[0]
    for h in range(heads):
        chosen = jnp.concatenate(
            [rows_ref[c, pl.ds(h, count, stride=heads), :] for c in range(PIECES)], axis=-1
        )
        val_ref[:, h * VD : (h + 1) * VD] = jnp.dot(
            chosen.astype(jnp.bfloat16), wv_ref[h], preferred_element_type=jnp.float32
        ).astype(jnp.bfloat16)


def head_values(messages, other, w_uv):
    chips, wide, _ = other.shape
    heads = w_uv.shape[0]
    count = 2 * chips * wide // heads
    scratch = [pltpu.VMEM((PIECES, count * heads, LANES), jnp.float32)]
    return call(values_kernel, shape(count, heads * VD), 3, "values", scratch)(
        *messages, other, resident(w_uv)
    )


def terms_kernel(start, val_ref, wo_ref, mine_ref, other_ref):
    half, width = mine_ref.shape
    terms = jnp.dot(
        val_ref[...], wo_ref[:, start : start + width], preferred_element_type=jnp.float32
    )
    mine_ref[...] = terms[:half]
    other_ref[...] = terms[half:].astype(jnp.bfloat16)


def output_terms(values, w_o, part):
    half = values.shape[0] // 2
    width = w_o.shape[1] // PARTS
    out = (shape(half, width, dtype=jnp.float32), shape(half, width))
    kernel = functools.partial(terms_kernel, part * width)
    return call(kernel, out, 6, "terms")(values, resident(w_o))


def far_z(devices):
    return [z for z in far_first(devices, Z1) if z > Z1][::-1]


def places(devices, chips):
    order = [*far_chips(devices), Y, Z1, Y + Z1, 0]
    return [order.index(k) for k in chips]


def pick(total, rows, where):
    return jnp.concatenate([total[j * rows : (j + 1) * rows] for j in where], axis=0)


def first_sum_kernel(rows, keep, give, near, mine_ref, other_ref, keep_ref, give_ref, near_ref):
    total = mine_ref[...] + other_ref[...].astype(jnp.float32)
    keep_ref[...] = pick(total, rows, keep)
    give_ref[...] = pick(total, rows, give).astype(give_ref.dtype)
    near_ref[...] = pick(total, rows, near)


def last_part_kernel(rows, keep, give, near, mine_ref, other_ref, before_ref, *out_refs):
    keep_ref, give_ref, *near_refs = out_refs
    total = mine_ref[...] + other_ref[...].astype(jnp.float32)
    keep_ref[...] = pick(total, rows, keep)
    give_ref[...] = pick(total, rows, give).astype(give_ref.dtype)
    width = before_ref.shape[1]
    for i, (j, out_ref) in enumerate(zip(near, near_refs)):
        out_ref[:, :width] = before_ref[i * rows : (i + 1) * rows].astype(out_ref.dtype)
        out_ref[:, width:] = total[j * rows : (j + 1) * rows].astype(out_ref.dtype)


def core_sum(mine, other, before, rows, devices):
    count, width = mine.shape
    keep = places(devices, far_z(devices))
    give = places(devices, [z + Y for z in far_z(devices)])
    near = places(devices, [0, *NEAR])
    far = len(keep) * rows
    out = (shape(far, width, dtype=jnp.float32), shape(far, width))
    if before is None:
        kernel = functools.partial(first_sum_kernel, rows, keep, give, near)
        out += (shape(4 * rows, width, dtype=jnp.float32),)
        return call(kernel, out, 1, "core_sum")(mine, other)
    kernel = functools.partial(last_part_kernel, rows, keep, give, near)
    full = before.shape[1] + width
    out += (shape(rows, full, dtype=jnp.float32), *[shape(rows, full)] * len(NEAR))
    return call(kernel, out, 1, "core_sum")(mine, other, before)


def far_sum_kernel(*refs):
    mine_refs = refs[:PARTS]
    other_refs = refs[PARTS : 2 * PARTS]
    out_refs = refs[2 * PARTS :]
    rows = out_refs[0].shape[0]
    for p, (mine_ref, other_ref) in enumerate(zip(mine_refs, other_refs)):
        width = mine_ref.shape[1]
        total = mine_ref[...] + other_ref[...].astype(jnp.float32)
        for j, out_ref in enumerate(out_refs):
            out_ref[:, p * width : (p + 1) * width] = total[j * rows : (j + 1) * rows].astype(
                out_ref.dtype
            )


def far_sum(mine, other, rows):
    count, width = mine[0].shape
    out = [shape(rows, PARTS * width)] * (count // rows)
    return call(far_sum_kernel, out, 1, "far_sum")(*mine, *other)


def last_sum_kernel(*refs):
    *in_refs, out_ref = refs
    terms = [ref[...].astype(jnp.float32) for ref in in_refs]
    out_ref[...] = sum(terms[1:], terms[0]).astype(out_ref.dtype)


def last_sum(blocks):
    return call(last_sum_kernel, shape(*blocks[0].shape), 1, "last_sum")(*blocks)


def on_device(q_latent, new_latent, cache, lengths, w_uq, w_uk, w_uv, w_o, devices):
    heads = w_uk.shape[0]
    rows = cache.shape[0]
    zs = far_first(devices, 4)[::-1]

    def swap(block, k):
        if k == 0:
            return block
        return lax.ppermute(block, "row", [(i, i ^ k) for i in range(devices)])

    across = swap(q_latent, Y)
    far_weights = [swap(w_uq, 1), swap(w_uk, 1)]
    tables, near = join(rotary(lengths), [q_latent, across])
    def exchange(messages):
        *far, across, pair, own = messages
        early = len(far) // 2
        got = [swap(block, k) for block, k in zip(far[:early], far_k)]
        passing = swap(across, Y)
        got += [swap(block, k) for block, k in zip(far[early:], far_k[early:])]
        sent = forward(pair, passing)
        return [*got, passing, swap(sent, Z1), own], sent

    far_k = far_chips(devices)
    messages = project([swap(near, z) for z in zs], [w_uq, w_uk, *far_weights], devices)
    messages, sent = exchange(messages)
    keys = jnp.swapaxes(cache, 1, 2)
    flipped = flip(keys, sent)
    latents = attend(lengths, tables, keys, flipped, new_latent, messages, heads, devices)
    latents, sent = exchange(latents)
    ready = early(latents[-3], latents[-1], sent)
    values = head_values(latents, swap(regroup(latents, ready, devices // 2), 1), w_uv)
    keep, got, near = [], [], None
    for part in range(PARTS):
        mine, other = output_terms(values, w_o, part)
        far_mine, far_other, near, *given = core_sum(mine, swap(other, 1), near, rows, devices)
        keep.append(far_mine)
        got.append(swap(far_other, Y))
    given = [swap(block, k) for block, k in zip(given, NEAR)]
    far = far_sum(keep, got, rows)
    far = [swap(block, z) for z, block in zip(far_z(devices), far)]
    return last_sum([near, *given, *far])


def solution(mesh):
    placed = (
        P(("grp", "row"), None),
        P(("grp", "row"), None),
        P(("grp", "row"), None, None),
        P(("grp", "row")),
        P(None, "row"),
        P("row", None, None),
        P("row", None, None),
        P("row", None),
    )
    body = functools.partial(on_device, devices=mesh.shape["row"])
    return jax.shard_map(
        body, mesh=mesh, in_specs=placed, out_specs=P(("grp", "row"), None), check_vma=False
    )
```

```python
import functools
import math

import jax
import jax.numpy as jnp
from jax import lax
from jax.experimental import pallas as pl
from jax.experimental.pallas import tpu as pltpu
from jax.sharding import PartitionSpec as P

LAT = 512
ROPE = 64
HALF = ROPE // 2
NOPE = 128
VD = 128
LANES = 128
PIECES = LAT // LANES
SCALE = (NOPE + ROPE) ** -0.5 * math.log2(math.e)
LIMIT = 16 * 2**20
PARTS = 2
Y = 2
Z1 = 4
NEAR = (Z1, Y + Z1, Y)


def resident(x):
    return pltpu.with_memory_space_constraint(x, pltpu.VMEM)


def in_vmem():
    return pl.BlockSpec(memory_space=pltpu.VMEM)


def call(kernel, out_shape, microseconds, name, scratch=(), scalars=0):
    def run(*args):
        smem = [pl.BlockSpec(memory_space=pltpu.SMEM)] * scalars
        return pl.pallas_call(
            kernel,
            out_shape=out_shape,
            in_specs=smem + [in_vmem()] * (len(args) - scalars),
            out_specs=jax.tree.map(lambda _: in_vmem(), out_shape),
            scratch_shapes=list(scratch),
            compiler_params=pltpu.CompilerParams(vmem_limit_bytes=LIMIT),
            cost_estimate=pl.CostEstimate(
                flops=int(microseconds * 1.15e9), bytes_accessed=0, transcendentals=0
            ),
            name=name,
        )(*args)

    return run


def shape(*dims, dtype=jnp.bfloat16):
    return jax.ShapeDtypeStruct(dims, dtype)


def far_first(devices, step):
    return sorted(range(0, devices, step), key=lambda k: -k.bit_length())


def far_chips(devices):
    chips = [k for k in far_first(devices, 2) if k > Y + Z1]
    return [k for k in chips[::-1] if not k & Y] + [k for k in chips if k & Y]


def chip_order(devices):
    return [*far_chips(devices), Y, Y + Z1, Z1, 0]


def message_sizes(devices):
    return [1] * len(far_chips(devices)) + [2, 1, 1]


def gathered_order(devices):
    return [z + y for z in reversed(far_first(devices, 4)) for y in (0, 2)]


def rotary_kernel(len_ref, cos_ref, sin_ref):
    rows, width = cos_ref.shape
    lane = lax.broadcasted_iota(jnp.int32, (rows, width), 1)
    place = lax.broadcasted_iota(jnp.int32, (rows, width), 0)
    step = jnp.where(lane < HALF, lane, lane - HALF).astype(jnp.float32)
    frequency = jnp.exp(step * (-math.log(10000.0) / HALF))
    length = jnp.zeros((rows, width), jnp.float32)
    for r in range(rows):
        length = jnp.where(place == r, len_ref[r].astype(jnp.float32), length)
    angle = length * frequency
    sine = jnp.sin(angle)
    cos_ref[...] = jnp.cos(angle)
    sin_ref[...] = jnp.where(lane < HALF, -sine, sine)


def rotary(lengths):
    table = shape(lengths.shape[0], ROPE, dtype=jnp.float32)
    return call(rotary_kernel, (table, table), 3, "rotary", scalars=1)(lengths)


def join_kernel(cos_ref, sin_ref, *refs):
    *in_refs, cos_out_ref, sin_out_ref, out_ref = refs
    cos_out_ref[...] = cos_ref[...]
    sin_out_ref[...] = sin_ref[...]
    out_ref[...] = jnp.concatenate(
        [ref[...].astype(jnp.float32) for ref in in_refs], axis=0
    ).astype(out_ref.dtype)


def join(tables, blocks):
    rows, depth = blocks[0].shape
    out = (*[shape(*t.shape, dtype=t.dtype) for t in tables], shape(len(blocks) * rows, depth))
    cosine, sine, joined = call(join_kernel, out, 3, "join")(*tables, *blocks)
    return (cosine, sine), joined


def project_kernel(devices, *refs):
    pieces = devices // 4
    q_refs = refs[:pieces]
    weights = (refs[pieces : pieces + 2], refs[pieces + 2 : pieces + 4])
    lat_ref, rot_ref = refs[-2:]
    out_refs = refs[pieces + 4 : -2]
    heads = weights[0][1].shape[0]
    piece = jnp.concatenate([ref[...].astype(jnp.float32) for ref in q_refs], axis=0)
    piece = piece.astype(jnp.bfloat16)
    count = piece.shape[0]
    wide = 2 * count // devices * heads
    width = NOPE + ROPE
    lane = lax.broadcasted_iota(jnp.int32, (wide // 2, LANES), 1)
    blocks = [(ref, 2 * i) for ref in out_refs for i in range(ref.shape[0] // 2)]
    blocks = dict(zip(chip_order(devices), blocks))
    for core, (wq_ref, wk_ref) in enumerate(weights):
        projected = jnp.dot(piece, wq_ref[...], preferred_element_type=jnp.float32)
        for h in range(heads):
            mine = projected[:, h * width : (h + 1) * width]
            absorbed = jnp.dot(
                mine[:, :NOPE].astype(jnp.bfloat16), wk_ref[h], preferred_element_type=jnp.float32
            )
            spread = pl.ds(h, count, stride=heads)
            for c in range(PIECES):
                lat_ref[core * PIECES + c, spread, :] = absorbed[:, c * LANES : (c + 1) * LANES]
            pe = mine[:, NOPE:]
            rot_ref[core, spread, :] = jnp.concatenate([pe, pe], axis=-1)
        for place, k in enumerate(gathered_order(devices)):
            out_ref, at = blocks[k]
            at += core
            first = place * wide
            for c in range(PIECES):
                out_ref[at, c * wide : (c + 1) * wide, :] = lat_ref[
                    core * PIECES + c, first : first + wide, :
                ].astype(jnp.bfloat16)
            low = rot_ref[core, first : first + wide // 2, :]
            high = rot_ref[core, first + wide // 2 : first + wide, :]
            out_ref[at, PIECES * wide :, :] = jnp.where(lane < ROPE, low, high).astype(
                jnp.bfloat16
            )


def project(pieces, weights, devices):
    heads = weights[1].shape[0]
    count = len(pieces) * pieces[0].shape[0]
    wide = 2 * count // devices * heads
    scratch = [
        pltpu.VMEM((2 * PIECES, count * heads, LANES), jnp.float32),
        pltpu.VMEM((2, count * heads, LANES), jnp.float32),
    ]
    tall = PIECES * wide + wide // 2
    out = [shape(2 * size, tall, LANES) for size in message_sizes(devices)]
    kernel = functools.partial(project_kernel, devices)
    return call(kernel, out, 20, "project", scratch)(*pieces, *[resident(w) for w in weights])


def flip_kernel(key_ref, after_ref, out_ref):
    for r in range(key_ref.shape[0]):
        out_ref[r] = key_ref[r, :LAT, :].T


def flip(keys, after):
    rows, _, maxlen = keys.shape
    return call(flip_kernel, shape(rows, maxlen, LAT), 4, "flip")(resident(keys), after)


def forward_kernel(own_ref, passing_ref, out_ref):
    out_ref[:2] = own_ref[...]
    out_ref[2:] = passing_ref[2:]


def forward(own, passing):
    return call(forward_kernel, shape(4, *own.shape[1:]), 1, "forward")(own, passing)


def arrived(refs):
    blocks = []
    for i, ref in enumerate(refs):
        count = 2 if i == len(refs) - 3 else ref.shape[0]
        blocks += [(ref, core) for core in range(count)]
    return blocks


def attend_kernel(sizes, len_ref, cos_ref, sin_ref, key_ref, flip_ref, new_ref, *refs):
    blocks = arrived(refs[: len(sizes)])
    out_refs = refs[len(sizes) :]
    rows, _, maxlen = key_ref.shape
    wide = out_refs[0].shape[1]
    heads = wide // rows

    def query_block(first):
        parts = [ref[i, first : first + heads, :].astype(jnp.float32) for ref, i in blocks]
        return jnp.concatenate(parts, axis=0)

    def score(r):
        latent = jnp.concatenate(
            [query_block(c * wide + r * heads) for c in range(PIECES)], axis=-1
        )
        pe = query_block(PIECES * wide + (r % (rows // 2)) * heads)
        side = r // (rows // 2) * ROPE
        pe = pe[:, side : side + ROPE]
        swapped = jnp.concatenate([pe[:, HALF:], pe[:, :HALF]], axis=-1)
        rotated = (pe * cos_ref[r : r + 1, :] + swapped * sin_ref[r : r + 1, :]).astype(jnp.bfloat16)
        newest = new_ref[r : r + 1, :].astype(jnp.float32)
        own = jnp.sum(latent * newest[:, :LAT], axis=-1, keepdims=True) + jnp.sum(
            rotated.astype(jnp.float32) * newest[:, LAT:], axis=-1, keepdims=True
        )
        scores = jnp.dot(
            latent.astype(jnp.bfloat16), key_ref[r, :LAT, :], preferred_element_type=jnp.float32
        )
        scores += jnp.dot(rotated, key_ref[r, LAT:, :], preferred_element_type=jnp.float32)
        position = lax.broadcasted_iota(jnp.int32, (1, maxlen), 1)
        return jnp.where(position < len_ref[r], scores, -jnp.inf), own

    back = [(ref, i) for ref in out_refs for i in range(ref.shape[0])]
    y_at = len(back) - 8
    back = back[: y_at + 2] + back[y_at + 4 : y_at + 6] + back[y_at + 2 : y_at + 4] + back[-2:]
    ahead = score(0)
    for r in range(rows):
        scores, own = ahead
        if r + 1 < rows:
            ahead = score(r + 1)
        peak = jnp.maximum(jnp.max(scores, axis=-1, keepdims=True), own)
        expo = jnp.exp2((scores - peak) * SCALE)
        own_expo = jnp.exp2((own - peak) * SCALE)
        inverse = 1.0 / (jnp.sum(expo, axis=-1, keepdims=True) + own_expo)
        weights = (expo * inverse).astype(jnp.bfloat16)
        own_weight = (own_expo * inverse).astype(jnp.bfloat16).astype(jnp.float32)
        summed = jnp.dot(weights, flip_ref[r], preferred_element_type=jnp.float32)
        summed += own_weight * new_ref[r : r + 1, :LAT].astype(jnp.float32)
        for k, (out_ref, i) in enumerate(back):
            out_ref[i, r * heads : (r + 1) * heads, :] = summed[
                k * heads : (k + 1) * heads, :
            ].astype(jnp.bfloat16)


def attend(lengths, tables, keys, flipped, new_latent, messages, heads, devices):
    sizes = message_sizes(devices)
    out = [shape(2 * size, keys.shape[0] * heads, LAT) for size in sizes]
    return call(functools.partial(attend_kernel, sizes), out, 10, "attend", scalars=1)(
        lengths, *tables, resident(keys), resident(flipped), new_latent, *messages
    )


def early_kernel(passing_ref, own_ref, after_ref, out_ref):
    out_ref[0] = passing_ref[1]
    out_ref[1] = own_ref[1]


def early(passing, own, after):
    return call(early_kernel, shape(2, *own.shape[1:]), 4, "early")(passing, own, after)


def regroup_kernel(*refs):
    *in_refs, early_ref, out_ref = refs
    blocks = arrived(in_refs)[1::2]
    blocks = [*blocks[:-4], (early_ref, 0), *blocks[-3:-1], (early_ref, 1)]
    for j, (ref, i) in enumerate(blocks):
        out_ref[j] = ref[i]


def regroup(messages, ready, chips):
    _, wide, width = messages[0].shape
    return call(regroup_kernel, shape(chips, wide, width), 1, "regroup")(*messages, ready)


def values_kernel(*refs):
    *in_refs, other_ref, wv_ref, val_ref, rows_ref = refs
    mine = arrived(in_refs)[::2]
    chips = len(mine)
    heads = wv_ref.shape[0]
    wide = other_ref.shape[1]
    for place in range(2 * chips):
        ref, i = mine[place] if place < chips else (other_ref, place - chips)
        block = ref[i].astype(jnp.float32)
        for c in range(PIECES):
            rows_ref[c, place * wide : (place + 1) * wide, :] = block[:, c * LANES : (c + 1) * LANES]
    count = val_ref.shape[0]
    for h in range(heads):
        chosen = jnp.concatenate(
            [rows_ref[c, pl.ds(h, count, stride=heads), :] for c in range(PIECES)], axis=-1
        )
        val_ref[:, h * VD : (h + 1) * VD] = jnp.dot(
            chosen.astype(jnp.bfloat16), wv_ref[h], preferred_element_type=jnp.float32
        ).astype(jnp.bfloat16)


def head_values(messages, other, w_uv):
    chips, wide, _ = other.shape
    heads = w_uv.shape[0]
    count = 2 * chips * wide // heads
    scratch = [pltpu.VMEM((PIECES, count * heads, LANES), jnp.float32)]
    return call(values_kernel, shape(count, heads * VD), 3, "values", scratch)(
        *messages, other, resident(w_uv)
    )


def terms_kernel(start, val_ref, wo_ref, mine_ref, other_ref):
    half, width = mine_ref.shape
    terms = jnp.dot(
        val_ref[...], wo_ref[:, start : start + width], preferred_element_type=jnp.float32
    )
    mine_ref[...] = terms[:half]
    other_ref[...] = terms[half:].astype(jnp.bfloat16)


def output_terms(values, w_o, part):
    half = values.shape[0] // 2
    width = w_o.shape[1] // PARTS
    out = (shape(half, width, dtype=jnp.float32), shape(half, width))
    kernel = functools.partial(terms_kernel, part * width)
    return call(kernel, out, 6, "terms")(values, resident(w_o))


def far_z(devices):
    return [z for z in far_first(devices, Z1) if z > Z1][::-1]


def places(devices, chips):
    order = [*far_chips(devices), Y, Z1, Y + Z1, 0]
    return [order.index(k) for k in chips]


def pick(total, rows, where):
    return jnp.concatenate([total[j * rows : (j + 1) * rows] for j in where], axis=0)


def first_sum_kernel(rows, keep, give, near, mine_ref, other_ref, keep_ref, give_ref, near_ref):
    total = mine_ref[...] + other_ref[...].astype(jnp.float32)
    keep_ref[...] = pick(total, rows, keep)
    give_ref[...] = pick(total, rows, give).astype(give_ref.dtype)
    near_ref[...] = pick(total, rows, near)


def last_part_kernel(rows, keep, give, near, mine_ref, other_ref, before_ref, *out_refs):
    keep_ref, give_ref, *near_refs = out_refs
    total = mine_ref[...] + other_ref[...].astype(jnp.float32)
    keep_ref[...] = pick(total, rows, keep)
    give_ref[...] = pick(total, rows, give).astype(give_ref.dtype)
    width = before_ref.shape[1]
    for i, (j, out_ref) in enumerate(zip(near, near_refs)):
        out_ref[:, :width] = before_ref[i * rows : (i + 1) * rows].astype(out_ref.dtype)
        out_ref[:, width:] = total[j * rows : (j + 1) * rows].astype(out_ref.dtype)


def core_sum(mine, other, before, rows, devices):
    count, width = mine.shape
    keep = places(devices, far_z(devices))
    give = places(devices, [z + Y for z in far_z(devices)])
    near = places(devices, [0, *NEAR])
    far = len(keep) * rows
    out = (shape(far, width, dtype=jnp.float32), shape(far, width))
    if before is None:
        kernel = functools.partial(first_sum_kernel, rows, keep, give, near)
        out += (shape(4 * rows, width, dtype=jnp.float32),)
        return call(kernel, out, 1, "core_sum")(mine, other)
    kernel = functools.partial(last_part_kernel, rows, keep, give, near)
    full = before.shape[1] + width
    out += (shape(rows, full, dtype=jnp.float32), *[shape(rows, full)] * len(NEAR))
    return call(kernel, out, 1, "core_sum")(mine, other, before)


def far_sum_kernel(*refs):
    mine_refs = refs[:PARTS]
    other_refs = refs[PARTS : 2 * PARTS]
    out_refs = refs[2 * PARTS :]
    rows = out_refs[0].shape[0]
    for p, (mine_ref, other_ref) in enumerate(zip(mine_refs, other_refs)):
        width = mine_ref.shape[1]
        total = mine_ref[...] + other_ref[...].astype(jnp.float32)
        for j, out_ref in enumerate(out_refs):
            out_ref[:, p * width : (p + 1) * width] = total[j * rows : (j + 1) * rows].astype(
                out_ref.dtype
            )


def far_sum(mine, other, rows):
    count, width = mine[0].shape
    out = [shape(rows, PARTS * width)] * (count // rows)
    return call(far_sum_kernel, out, 1, "far_sum")(*mine, *other)


def last_sum_kernel(*refs):
    *in_refs, out_ref = refs
    terms = [ref[...].astype(jnp.float32) for ref in in_refs]
    out_ref[...] = sum(terms[1:], terms[0]).astype(out_ref.dtype)


def last_sum(blocks):
    return call(last_sum_kernel, shape(*blocks[0].shape), 1, "last_sum")(*blocks)


def on_device(q_latent, new_latent, cache, lengths, w_uq, w_uk, w_uv, w_o, devices):
    heads = w_uk.shape[0]
    rows = cache.shape[0]
    zs = far_first(devices, 4)[::-1]

    def swap(block, k):
        if k == 0:
            return block
        return lax.ppermute(block, "row", [(i, i ^ k) for i in range(devices)])

    across = swap(q_latent, Y)
    far_weights = [swap(w_uq, 1), swap(w_uk, 1)]
    tables, near = join(rotary(lengths), [q_latent, across])
    def exchange(messages):
        *far, across, pair, own = messages
        early = len(far) // 2
        got = [swap(block, k) for block, k in zip(far[:early], far_k)]
        passing = swap(across, Y)
        got += [swap(block, k) for block, k in zip(far[early:], far_k[early:])]
        sent = forward(pair, passing)
        return [*got, passing, swap(sent, Z1), own], sent

    far_k = far_chips(devices)
    messages = project([swap(near, z) for z in zs], [w_uq, w_uk, *far_weights], devices)
    messages, sent = exchange(messages)
    keys = jnp.swapaxes(cache, 1, 2)
    flipped = flip(keys, sent)
    latents = attend(lengths, tables, keys, flipped, new_latent, messages, heads, devices)
    latents, sent = exchange(latents)
    ready = early(latents[-3], latents[-1], sent)
    values = head_values(latents, swap(regroup(latents, ready, devices // 2), 1), w_uv)
    keep, got, near = [], [], None
    for part in range(PARTS):
        mine, other = output_terms(values, w_o, part)
        far_mine, far_other, near, *given = core_sum(mine, swap(other, 1), near, rows, devices)
        keep.append(far_mine)
        got.append(swap(far_other, Y))
    given = [swap(block, k) for block, k in zip(given, NEAR)]
    far = far_sum(keep, got, rows)
    far = [swap(block, z) for z, block in zip(far_z(devices), far)]
    return last_sum([near, *given, *far])


def solution(mesh):
    placed = (
        P(("grp", "row"), None),
        P(("grp", "row"), None),
        P(("grp", "row"), None, None),
        P(("grp", "row")),
        P(None, "row"),
        P("row", None, None),
        P("row", None, None),
        P("row", None),
    )
    body = functools.partial(on_device, devices=mesh.shape["row"])
    return jax.shard_map(
        body, mesh=mesh, in_specs=placed, out_specs=P(("grp", "row"), None), check_vma=False
    )
```
